128 devices in a mesh: dp: 4 (over x_hi, core), fsdp: 32 (over z, x_lo, y).
Axes of the slice: x: 4 (x_hi: 2, x_lo: 2; x = x_hi * 2 + x_lo), y: 4, z: 4, core: 2. Of those that a mesh axis runs over, the one named last changes fastest.
Arguments:
- tokens: bfloat16 [128, 128, 1024], P(('dp', 'fsdp')), may hold values from -6 to 6
- cotangent: bfloat16 [128, 128, 1024], P(('dp', 'fsdp')), may hold values from -6 to 6
- segment: int32 [128, 128], P(('dp', 'fsdp')), may hold values from 0 to 31, never falling along the last dimension, each value on 1 to 64 neighbouring positions
- keep_mask: int32 [128, 128], P(('dp', 'fsdp')), may hold values 0 or 1
- conv_state: float32 [128, 3, 1536], P(('dp', 'fsdp')), may hold values from -6 to 6
- lru_state: float32 [128, 1536], P(('dp', 'fsdp')), may hold values from -6 to 6
- norm1_gain: bfloat16 [1024], P(('dp', 'fsdp')), may hold values from 0.099609375 to 1.8984375
- conv_weight: bfloat16 [4, 1536], P(None, ('dp', 'fsdp')), may hold values from -3 to 3
- lru_bias: bfloat16 [3, 1536], P(None, ('dp', 'fsdp')), may hold values from -4 to 4
- decay_rate: bfloat16 [1536], P(('dp', 'fsdp')), may hold values from 0.00029945374 to 0.029907227
- gate_weight: bfloat16 [1536, 384], P(('dp', 'fsdp')), may hold values from -0.4375 to 0.4375
- branch_weight: bfloat16 [1024, 3072], P(('dp', 'fsdp')), may hold values from -0.1875 to 0.1875
- out_weight: bfloat16 [1536, 1024], P(('dp', 'fsdp')), may hold values from -0.625 to 0.625
- norm2_gain: bfloat16 [1024], P(('dp', 'fsdp')), may hold values from 0.099609375 to 1.8984375
- mlp_in_weight: bfloat16 [1024, 6144], P(('dp', 'fsdp')), may hold values from -0.1875 to 0.1875
- mlp_out_weight: bfloat16 [3072, 1024], P(('dp', 'fsdp')), may hold values from -0.15625 to 0.15625
Outputs:
- output: bfloat16 [128, 128, 1024], P(('dp', 'fsdp'))
- input_grad: bfloat16 [128, 128, 1024], P(('dp', 'fsdp'))
- final_conv: float32 [128, 3, 1536], P(('dp', 'fsdp'))
- final_state: float32 [128, 1536], P(('dp', 'fsdp'))
- norm1_gain_grad: float32 [1024], P(('dp', 'fsdp'))
- conv_weight_grad: float32 [4, 1536], P(None, ('dp', 'fsdp'))
- lru_bias_grad: float32 [3, 1536], P(None, ('dp', 'fsdp'))
- decay_rate_grad: float32 [1536], P(('dp', 'fsdp'))
- gate_weight_grad: float32 [1536, 384], P(('dp', 'fsdp'))
- branch_weight_grad: float32 [1024, 3072], P(('dp', 'fsdp'))
- out_weight_grad: float32 [1536, 1024], P(('dp', 'fsdp'))
- norm2_gain_grad: float32 [1024], P(('dp', 'fsdp'))
- mlp_in_weight_grad: float32 [1024, 6144], P(('dp', 'fsdp'))
- mlp_out_weight_grad: float32 [3072, 1024], P(('dp', 'fsdp'))
The draws below stay inside these ranges and needn't reach their ends.
Inputs may be any that keep to these rules, and one draw needn't show every extreme that they name: `segment`: segment numbers never fall along a sequence; a position whose number differs from the one before starts a new document.
All inputs are finite; a program needn't handle non-finite values. No bound on the sum of `keep_mask` on one device may be relied on, other than what follows from the above.
Results may differ from the reference program's by a relative error of at most 0.013.
Values may be sent and summed in bfloat16 or wider, within the bound.
No kernel may reach another device: no remote copies, remote signals or barrier semaphores. Data moves between devices by JAX's collectives and lax.ppermute only.
A program may use at most 256 MiB of HBM per device.

```python
import math
import jax
import jax.numpy as jnp
import numpy as np
from jax import lax

D = 1024
H = 8
HS = 192
R = 1536
F = 3072
SEQ = 128
ROWS = 128


def with_ends(values, key, least, largest):
    place = [jax.random.randint(jax.random.fold_in(key, axis), (), 0, length) for axis, length in enumerate(values.shape)]
    longest = values.shape.index(max(values.shape))
    neighbour = place[:longest] + [(place[longest] + 1) % values.shape[longest]] + place[longest + 1:]
    return values.at[tuple(place)].set(least).at[tuple(neighbour)].set(largest)


def block_levels(own_key, shape, shards, smallest, largest):
    loudness, own = 1.0, jax.random.fold_in(own_key, 6)
    for position, blocks in shards:
        heights = jnp.exp(jax.random.uniform(jax.random.fold_in(own, position), (blocks,), jnp.float32, smallest / len(shards), largest / len(shards)))
        loudness = loudness * jnp.repeat(heights, shape[position] // blocks).reshape([-1 if axis == position else 1 for axis in range(len(shape))])
    return loudness


def profile(count, total, bound, lean):
    portions = [(1 << 20) // math.isqrt(rank ** lean) + 1 for rank in range(2, count + 1)]
    spare, holding = total - bound - (count - 1), [1] * (count - 1)
    while spare > 0:
        movable = [i for i in range(count - 1) if holding[i] < bound]
        pool, budget = sum([portions[i] for i in movable]), spare
        for i in movable:
            more = min(bound - holding[i], max(1, budget * portions[i] // pool), spare)
            holding[i] = holding[i] + more
            spare = spare - more
    return np.array([bound] + holding)


def ragged(rng, number_of, total, bound, skew):
    if number_of == 2:
        one = jax.random.randint(rng, (), max(1, total - bound), min(bound, total - 1) + 1)
        return jnp.stack([one, total - one])
    tallies = jnp.asarray(profile(number_of, total, bound, skew), jnp.int32)
    couples = (number_of - 1) // 2
    source_of, taker = tallies[1:1 + 2 * couples:2], tallies[2:2 + 2 * couples:2]
    slack = jnp.minimum(source_of - 1, bound - taker)
    moved = jax.random.randint(jax.random.fold_in(rng, 1), (couples,), 0, 1 << 20) % (slack + 1)
    tallies = tallies.at[1:1 + 2 * couples:2].set(source_of - moved).at[2:2 + 2 * couples:2].set(taker + moved)
    return tallies[jax.random.permutation(jax.random.fold_in(rng, 2), number_of)]


def centred(rng, dims, scale, bound, cuts=(), held_as=jnp.bfloat16):
    values = scale * jax.random.normal(rng, dims, jnp.float32)
    if cuts:
        values = values * block_levels(rng, dims, cuts, -0.22, 0.18)
    return jnp.clip(values, -bound, bound).astype(held_as)


def setup_inputs(seed: int = 0) -> dict:
    splits = jax.random.split(jax.random.key(seed), 17)
    return {
        "tokens": centred(splits[0], (ROWS, SEQ, D), 1.0, 6.0, ((0, 128),)),
        "cotangent": centred(splits[1], (ROWS, SEQ, D), 1.0, 6.0, ((0, 128),)),
        "segment": jax.vmap(lambda own: jnp.searchsorted(jnp.cumsum(ragged(own, SEQ // 4, SEQ, SEQ // 2, 2)), jnp.arange(SEQ), side="right"))(jax.random.split(splits[2], ROWS)).reshape((ROWS, SEQ)).astype(jnp.int32),
        "keep_mask": with_ends((jax.random.randint(splits[3], (ROWS, SEQ), 0, 8) < 7).astype(jnp.int32), jax.random.fold_in(splits[3], 1), 0, 1),
        "conv_state": centred(splits[4], (ROWS, 3, R), 1.0, 6.0, ((0, 128),), jnp.float32),
        "lru_state": centred(splits[5], (ROWS, R), 1.0, 6.0, ((0, 128),), jnp.float32),
        "norm1_gain": jnp.clip(1.0 + 0.18 * jax.random.normal(splits[6], (D,), jnp.float32), 0.099609375, 1.8984375).astype(jnp.bfloat16),
        "conv_weight": centred(splits[7], (4, R), 4 ** -0.5, 3.0, ((1, 128),)),
        "lru_bias": centred(splits[8], (3, R), 1.0, 4.0, ((1, 128),)),
        "decay_rate": jnp.clip(jnp.exp(math.log(0.029907227) - 4.6038955 * jax.random.uniform(splits[9], (R,), jnp.float32) ** block_levels(splits[9], (R,), ((0, 128),), -0.2, 0.2)), 0.00029945374, 0.029907227).astype(jnp.bfloat16),
        "gate_weight": centred(splits[10], (R, 2 * HS), HS ** -0.5, 0.4375, ((0, 128),)),
        "branch_weight": centred(splits[11], (D, 2 * R), D ** -0.5, 0.1875, ((0, 128),)),
        "out_weight": centred(splits[12], (R, D), (R // 16) ** -0.5, 0.625, ((0, 128),)),
        "norm2_gain": jnp.clip(1.0 + 0.18 * jax.random.normal(splits[13], (D,), jnp.float32), 0.099609375, 1.8984375).astype(jnp.bfloat16),
        "mlp_in_weight": centred(splits[14], (D, 2 * F), D ** -0.5, 0.1875, ((0, 128),)),
        "mlp_out_weight": centred(splits[15], (F, D), (F // 2) ** -0.5, 0.15625, ((0, 128),)),
    }


@jax.custom_vjp
def low(v):
    return lax.optimization_barrier(v.astype(jnp.bfloat16)).astype(jnp.float32)

@jax.custom_vjp
def low_back(v):
    return v

def low_keep(v):
    return (low(v), None)

def low_pass(kept, grad):
    return (grad,)

def back_keep(v):
    return (v, None)

def back_low(kept, grad):
    return (low(grad),)
low.defvjp(low_keep, low_pass)
low_back.defvjp(back_keep, back_low)

def rms_scale(values, gain_row):
    return values * lax.rsqrt(lax.optimization_barrier(jnp.mean(values * values, axis=-1, keepdims=True)) + 1e-06) * gain_row

def smooth_gelu(values):
    return jax.nn.gelu(values, approximate=True)

def lru_combine(earlier, later):
    return (earlier[0] * later[0], later[0] * earlier[1] + later[1])

def row_masks(segment, keep_mask):
    keep_row = keep_mask.astype(jnp.float32)[..., None]
    changes = (segment[:, 1:] != segment[:, :-1]).astype(jnp.float32)
    starts = jnp.concatenate([jnp.zeros_like(changes[:, :1]), changes], axis=1)
    return (keep_row, starts[..., None])

def conv_piece(mixed_u, conv_weight, lru_bias, segment, keep_row, conv_state):
    inputs = mixed_u * keep_row
    length = inputs.shape[1]
    padded = jnp.concatenate([conv_state, inputs], axis=1)
    leading = jnp.broadcast_to(segment[:, :1], (segment.shape[0], 3))
    seg_padded = jnp.concatenate([leading, segment], axis=1)
    result = lru_bias[0] + conv_weight[0] * inputs
    for offset in range(1, 4):
        shifted = padded[:, 3 - offset:3 - offset + length]
        same_doc = (seg_padded[:, 3 - offset:3 - offset + length] == segment).astype(inputs.dtype)[..., None]
        result = result + conv_weight[offset] * shifted * same_doc
    return (result, inputs[:, length - 3:])

def gate_piece(logits, conv_values, gate_in, lru_bias, decay_rate, keep_row, starts, lru_state):
    full_shape = conv_values.shape
    half_cols = logits.shape[-1] // 2
    recur_gate = jax.nn.sigmoid(logits[..., :half_cols].reshape(full_shape) + lru_bias[1])
    input_gate = jax.nn.sigmoid(logits[..., half_cols:].reshape(full_shape) + lru_bias[2])
    step_decay = jnp.exp(-8.0 * recur_gate * decay_rate)
    coeff = (1.0 - starts) * (keep_row * step_decay + (1.0 - keep_row))
    scale = starts + (1.0 - starts) * jnp.sqrt(jnp.maximum(1.0 - step_decay * step_decay, 0.001))
    drive = keep_row * scale * input_gate * conv_values
    carried, states = lax.associative_scan(lru_combine, (coeff, drive), axis=1)
    states = states + carried * lru_state[:, None, :]
    return (states * smooth_gelu(gate_in), states[:, -1])

def product(values, weight):
    return jnp.einsum('gsd,de->gse', values, weight, precision=lax.Precision.HIGHEST)

def group_forward(inputs, params, segment, keep_row, starts, conv_state, lru_state):
    gain_one, conv_w, bias_rows, decay, gate_w, branch_w, out_w, gain_two, in_w, down_w = params
    normed = low(rms_scale(inputs, gain_one))
    mixed = low_back(product(normed, branch_w))
    convolved, final_conv = conv_piece(mixed[..., :R], conv_w, bias_rows, segment, keep_row, conv_state)
    convolved = low(convolved)
    blocks = convolved.reshape(convolved.shape[:2] + (H, HS))
    logits = low_back(jnp.einsum('gshi,hij->gshj', blocks, gate_w.reshape(H, HS, 2 * HS), precision=lax.Precision.HIGHEST))
    merged, final_state = gate_piece(logits, convolved, mixed[..., R:], bias_rows, decay, keep_row, starts, lru_state)
    merged = low(merged)
    residual = inputs + low_back(product(merged, out_w))
    normed2 = low(rms_scale(residual, gain_two))
    gate_up = low_back(product(normed2, in_w))
    hidden = low(smooth_gelu(gate_up[..., :F]) * gate_up[..., F:])
    output = residual + low_back(product(hidden, down_w))
    return (output, (final_conv, final_state))

def reference(tokens, cotangent, segment, keep_mask, conv_state, lru_state, norm1_gain, conv_weight, lru_bias, decay_rate, gate_weight, branch_weight, out_weight, norm2_gain, mlp_in_weight, mlp_out_weight):
    params = tuple((weight.astype(jnp.float32) for weight in (norm1_gain, conv_weight, lru_bias, decay_rate, gate_weight, branch_weight, out_weight, norm2_gain, mlp_in_weight, mlp_out_weight)))
    group_rows = math.gcd(ROWS, max(1, 4096 // SEQ))
    group_count = ROWS // group_rows

    def by_group(array):
        return array.reshape((group_count, group_rows) + array.shape[1:])

    def row_step(totals, entries):
        inputs, cot_rows, seg_rows, mask_rows, conv_rows, state_rows = entries
        keep_row, starts = row_masks(seg_rows, mask_rows)

        def forward(values, weights):
            return group_forward(values, weights, seg_rows, keep_row, starts, conv_rows, state_rows)
        output, pullback, finals = jax.vjp(forward, inputs.astype(jnp.float32), params, has_aux=True)
        grad_input, grads = pullback(cot_rows.astype(jnp.float32))
        totals = jax.tree.map(jnp.add, totals, grads)
        return (totals, (output.astype(jnp.bfloat16), grad_input.astype(jnp.bfloat16), finals[0], finals[1]))
    zero_grads = tuple((jnp.zeros_like(weight) for weight in params))
    totals, results = lax.scan(row_step, zero_grads, (by_group(tokens), by_group(cotangent), by_group(segment), by_group(keep_mask), by_group(conv_state), by_group(lru_state)))
    outputs, grad_inputs, final_convs, final_states = results
    return (outputs.reshape(ROWS, SEQ, D), grad_inputs.reshape(ROWS, SEQ, D), final_convs.reshape(ROWS, 3, R), final_states.reshape(ROWS, R), totals[0], totals[1], totals[2], totals[3], totals[4], totals[5], totals[6], totals[7], totals[8], totals[9])
```

```python
import jax
import jax.numpy as jnp
from jax import lax
from jax.sharding import PartitionSpec as P

AXES = ("dp", "fsdp")
D, R, F, SEQ = 1024, 1536, 3072, 128
RC, FC = R // 2, F // 2
HS = 192
F32, BF16 = jnp.float32, jnp.bfloat16
BRANCH, INNER = 2 * RC, 2 * FC
YIN = 768


def place_of(device):
    outer, inner = divmod(device, 32)
    x_hi, core = divmod(outer, 2)
    z, rest = divmod(inner, 8)
    x_lo, y = divmod(rest, 4)
    return dict(x=x_hi * 2 + x_lo, y=y, z=z, core=core)


def device_at(x, y, z, core):
    return ((x // 2) * 2 + core) * 32 + z * 8 + (x % 2) * 4 + y


def pairs(move):
    return [(d, device_at(**move(place_of(d)))) for d in range(128)]


def along(axis, steps):
    def move(p):
        sign = 1 if p["core"] == 0 else -1
        return {**p, axis: (p[axis] + sign * steps) % 4}

    return pairs(move)


def other_core(p):
    return {**p, "core": 1 - p["core"]}


def spread(turn):
    def move(p):
        return {**p, "y": 2 * (p["y"] // 2) + p["core"], "core": (p["y"] + turn) % 2}

    return pairs(move)


def collect(turn):
    return [(b, a) for a, b in spread(turn)]


def send(value, route):
    return lax.ppermute(value, AXES, route)


def swap(value):
    return send(value, pairs(other_core))


def my_place():
    device = lax.axis_index(AXES)
    outer, inner = device // 32, device % 32
    return dict(x=(outer // 2) * 2 + (inner // 4) % 2, y=inner % 4, z=inner // 8, core=outer % 2)


def gather_ring(block, axis, here):
    up = send(block, along(axis, 1))
    down = send(block, along(axis, -1))
    far = send(up, along(axis, 1))
    sign, at = 1 - 2 * here["core"], here[axis]
    out = jnp.zeros((4,) + block.shape, block.dtype)
    for piece, where in ((block, at), (up, at - sign), (down, at + sign), (far, at + 2)):
        out = lax.dynamic_update_slice(out, piece[None], (where % 4,) + (0,) * block.ndim)
    return out


def sum_ring(blocks, axis, here, kind):
    sign, at = 1 - 2 * here["core"], here[axis]

    def term(where):
        return lax.dynamic_index_in_dim(blocks, where % 4, 0, keepdims=False)

    far = send(term(at + 2), along(axis, 1))
    down = send(term(at - sign), along(axis, -1))
    passed = (term(at + sign).astype(F32) + far.astype(F32)).astype(BF16)
    up = send(passed, along(axis, 1))
    return (term(at).astype(F32) + down.astype(F32) + up.astype(F32)).astype(kind)


def gather_rings(block, axes, here):
    for axis in axes:
        block = gather_ring(block, axis, here)
    return block


def sum_rings(blocks, axes, here):
    for axis in axes[:-1]:
        blocks = sum_ring(blocks, axis, here, BF16)
    return sum_ring(blocks, axes[-1], here, F32)


def y_rows(blocks):
    n = blocks.shape[-1]
    v = blocks.reshape(2, 2, 2, 2, 4, 16, n)
    return v.transpose(2, 1, 4, 3, 0, 5, 6).reshape(D, n)


def z_rows(blocks):
    n = blocks.shape[-1]
    v = blocks.reshape(4, 2, 2, 2, 2, 16, n)
    return v.transpose(3, 2, 0, 4, 1, 5, 6).reshape(D, n)


def to_y_rows(weight):
    n = weight.shape[-1]
    v = weight.reshape(2, 2, 4, 2, 2, 16, n)
    return v.transpose(4, 1, 0, 3, 2, 5, 6).reshape(4, 4, 4, 16, n)


def to_z_rows(weight):
    n = weight.shape[-1]
    v = weight.reshape(2, 2, 4, 2, 2, 16, n)
    return v.transpose(2, 4, 1, 0, 3, 5, 6).reshape(4, 4, 4, 16, n)


def x_rows(blocks):
    n = blocks.shape[2:]
    v = blocks.reshape((2, 2, 4) + n)
    return v.transpose((0, 2, 1) + tuple(range(3, 3 + len(n))))


def to_x_rows(weight, rows):
    n = weight.shape[-1]
    v = weight.reshape(2, 4, 2, 4, rows, n)
    return v.transpose(0, 2, 1, 3, 4, 5).reshape(4, 4, 4, rows, n)


def core_half(array, core, blocks):
    v = array.reshape(array.shape[:-1] + (blocks, 2, array.shape[-1] // (2 * blocks)))
    v = lax.dynamic_index_in_dim(v, core, v.ndim - 2, keepdims=False)
    return v.reshape(array.shape[:-1] + (array.shape[-1] // 2,))


def dot(a, b, dims):
    return lax.dot_general(a, b, (dims, ((), ())), preferred_element_type=F32)


def nn(a, b):
    return dot(a, b, ((1,), (0,)))


def nt(a, b):
    return dot(a, b, ((1,), (1,)))


def tn(a, b):
    return dot(a, b, ((0,), (0,)))


def inv_rms(v):
    return lax.rsqrt(jnp.mean(v * v, axis=-1, keepdims=True) + 1e-6)


def rms_back(grad, v, gain):
    s = inv_rms(v)
    n = v * s
    g2 = grad * gain
    return s * (g2 - n * jnp.mean(g2 * n, axis=-1, keepdims=True)), grad * n


C0, C1 = 0.7978845608028654, 0.044715


def gelu_tanh(a):
    return jnp.tanh(C0 * (a + C1 * (a * a * a)))


def gelu(a):
    return 0.5 * a * (1.0 + gelu_tanh(a))


def gelu_both(a):
    t = gelu_tanh(a)
    half = 0.5 * (1.0 + t)
    return a * half, half + 0.5 * a * (1.0 - t * t) * (C0 * (1.0 + 3.0 * C1 * (a * a)))


def shifted(u, state, k):
    return jnp.concatenate([state[:, 3 - k :], u[:, : SEQ - k]], axis=1)


def gates(rate, inp, conv, bias, decay, keep, starts):
    rg = jax.nn.sigmoid(rate + bias[1])
    ig = jax.nn.sigmoid(inp + bias[2])
    sd = jnp.exp(-8.0 * rg * decay)
    coeff = (1.0 - starts) * (keep * sd + (1.0 - keep))
    q = 1.0 - sd * sd
    root = jnp.sqrt(jnp.maximum(q, 0.001))
    scale = starts + (1.0 - starts) * root
    return rg, ig, sd, coeff, q, root, scale


def combine(a, b):
    return a[0] * b[0], b[0] * a[1] + b[1]


def shards(
    tokens, cotangent, segment, keep_mask, conv_state, lru_state, norm1_gain, conv_weight, lru_bias, decay_rate,
    gate_weight, branch_weight, out_weight, norm2_gain, mlp_in_weight, mlp_out_weight,
):
    here = my_place()
    core = here["core"]
    odd = here["y"] % 2 == 1

    small = jnp.concatenate(
        [norm1_gain, norm2_gain, conv_weight.reshape(-1), lru_bias.reshape(-1), decay_rate, jnp.zeros(16, BF16)]
    )
    small = jnp.pad(small[None], ((0, 7), (0, 0)))
    branch = branch_weight.reshape(8, 4, 2, 384)
    inner = mlp_in_weight.reshape(8, 4, 2, 768)
    halves = [
        jnp.concatenate([branch[:, :, c].reshape(8, BRANCH), inner[:, :, c].reshape(8, INNER), small], axis=1)
        for c in range(2)
    ]
    first = send(jnp.where(odd, halves[1], halves[0]), spread(0))
    second = send(jnp.where(odd, halves[0], halves[1]), spread(1))
    low = jnp.where(core == 0, first, second)
    high = jnp.where(core == 0, second, first)
    block = jnp.concatenate([low, high], axis=0)
    y_block = jnp.concatenate([block[:, : BRANCH + YIN], block[:, BRANCH + INNER :]], axis=1)
    z_block = block[:, BRANCH + YIN : BRANCH + INNER]
    og = jnp.pad(jnp.concatenate([out_weight, gate_weight], axis=1), ((0, 0), (0, 128)))
    x_block = jnp.concatenate([mlp_out_weight, og.reshape(12, 2, 768).transpose(1, 0, 2).reshape(24, 768)], axis=1)

    x_block = gather_ring(x_block, "y", here)
    x_block = jnp.concatenate(
        [
            x_block[..., :D].reshape(96, D),
            x_block[..., D:].reshape(4, 2, 12, 768).transpose(1, 0, 2, 3).reshape(96, 768),
        ],
        axis=1,
    )
    x_full = x_rows(gather_rings(x_block, "zx", here))
    y_full = y_rows(gather_rings(y_block, "zxy", here))
    z_full = z_rows(gather_rings(z_block, "xyz", here))

    w_branch = y_full[:, :BRANCH]
    w_in = jnp.concatenate([y_full[:, BRANCH : BRANCH + YIN], z_full], axis=1)
    w_down = x_full[..., :D].reshape(FC, D)
    w_og = x_full[..., D:].reshape(16, 2, 48, 768).transpose(0, 2, 1, 3).reshape(RC, 1536)
    w_out, w_gate = w_og[:, :D], w_og[:, D : D + 384]
    smalls = y_full[:, BRANCH + YIN :].reshape(128, 8, 128)[:, 0].astype(F32)
    gain1, gain2 = smalls[:, :8].reshape(D), smalls[:, 8:16].reshape(D)

    def channels(v):
        v = v.reshape(2, 2, 32, v.shape[1], 12)
        v = lax.dynamic_index_in_dim(v, core, 1, keepdims=False)
        return v.transpose(2, 0, 1, 3).reshape(v.shape[2], RC)

    conv_w = channels(smalls[:, 16:64].reshape(128, 4, 12))
    bias = channels(smalls[:, 64:100].reshape(128, 3, 12))
    decay = channels(smalls[:, 100:112].reshape(128, 1, 12))

    def both(v):
        return jnp.concatenate([v, swap(v)], axis=0)

    tok = both(tokens).reshape(2 * SEQ, D).astype(F32)
    cot = both(cotangent).reshape(2 * SEQ, D)
    marks = both(jnp.concatenate([segment, keep_mask], axis=1).astype(F32))
    seg, keep = marks[:, :SEQ, None], marks[:, SEQ:, None]
    states = jnp.concatenate([conv_state, lru_state[:, None]], axis=1)
    states = jnp.concatenate([core_half(states, core, 2), swap(core_half(states, 1 - core, 2))], axis=0)
    conv_before, lru_before = states[:, :3], states[:, 3:]
    starts = jnp.concatenate([jnp.zeros_like(seg[:, :1]), (seg[:, 1:] != seg[:, :-1]).astype(F32)], axis=1)
    same = [None] + [
        (jnp.concatenate([jnp.broadcast_to(seg[:, :1], (2, k, 1)), seg[:, : SEQ - k]], axis=1) == seg).astype(F32)
        for k in range(1, 4)
    ]

    normed = (tok * inv_rms(tok) * gain1).astype(BF16)
    mixed = nn(normed, w_branch)
    u = mixed[:, :RC].reshape(2, SEQ, RC) * keep
    gate_in = mixed[:, RC:]
    conv = bias[0] + conv_w[0] * u
    for k in range(1, 4):
        conv = conv + conv_w[k] * (shifted(u, conv_before, k) * same[k])
    conv_low = conv.astype(BF16).reshape(2 * SEQ, RC)
    tables = w_gate.reshape(4, HS, 2 * HS)
    logits = [nn(conv_low[:, h * HS : (h + 1) * HS], tables[h]) for h in range(4)]
    rate = jnp.concatenate([v[:, :HS] for v in logits], axis=1).reshape(2, SEQ, RC)
    inp = jnp.concatenate([v[:, HS:] for v in logits], axis=1).reshape(2, SEQ, RC)
    conv_r = conv_low.astype(F32).reshape(2, SEQ, RC)
    rg, ig, sd, coeff, q, root, scale = gates(rate, inp, conv_r, bias, decay, keep, starts)
    drive = keep * scale * ig * conv_r
    carried, states = lax.associative_scan(combine, (coeff, drive), axis=1)
    states = states + carried * lru_before
    finals = jnp.concatenate([u[:, SEQ - 3 :], states[:, SEQ - 1 :]], axis=1)
    flat = states.reshape(2 * SEQ, RC)
    act, act_grad = gelu_both(gate_in)
    merged = (flat * act).astype(BF16)
    part = nn(merged, w_out)

    def across(v):
        w = swap(v)
        return v + jnp.concatenate([w[SEQ:], w[:SEQ]], axis=0)

    residual = tok + across(part)

    normed2 = (residual * inv_rms(residual) * gain2).astype(BF16)
    gate_up = nn(normed2, w_in)
    a, b = gate_up[:, :FC], gate_up[:, FC:]
    ga, da = gelu_both(a)
    hidden = (ga * b).astype(BF16)
    down = nn(hidden, w_down)
    output = (residual[:SEQ] + (down[:SEQ] + swap(down[SEQ:]))).astype(BF16)
    grad_hidden = nt(cot, w_down)
    ggu = jnp.concatenate([grad_hidden * b * da, grad_hidden * ga], axis=1).astype(BF16)
    d_down = tn(hidden, cot)
    d_in = tn(normed2, ggu)
    grad_normed2 = across(nt(ggu, w_in))
    back, gain2_term = rms_back(grad_normed2, residual, gain2)
    grad_residual = cot.astype(F32) + back
    grad_branch = grad_residual.astype(BF16)

    d_out = tn(merged, grad_branch)
    grad_merged = nt(grad_branch, w_out)
    grad_gate_in = grad_merged * flat * act_grad
    grad_states = (grad_merged * act).reshape(2, SEQ, RC)
    later = jnp.concatenate([coeff[:, 1:], jnp.zeros_like(coeff[:, :1])], axis=1)
    _, lam = lax.associative_scan(combine, (later, grad_states), axis=1, reverse=True)
    before = jnp.concatenate([lru_before, states[:, :-1]], axis=1)
    grad_coeff = lam * before
    common = lam * keep
    conv_direct = common * scale * ig
    d_ig = common * scale * conv_r
    d_scale = common * ig * conv_r
    d_sd = (1.0 - starts) * (grad_coeff * keep - d_scale * jnp.where(q > 0.001, sd / root, 0.0))
    d_rate = d_sd * sd * (-8.0 * decay) * rg * (1.0 - rg)
    d_inp = d_ig * ig * (1.0 - ig)
    d_decay = jnp.sum(d_sd * sd * (-8.0 * rg), axis=(0, 1))
    rate_low = d_rate.astype(BF16).reshape(2 * SEQ, RC)
    inp_low = d_inp.astype(BF16).reshape(2 * SEQ, RC)
    logit_low = [
        jnp.concatenate([rate_low[:, h * HS : (h + 1) * HS], inp_low[:, h * HS : (h + 1) * HS]], axis=1)
        for h in range(4)
    ]
    d_gate = jnp.concatenate([tn(conv_low[:, h * HS : (h + 1) * HS], logit_low[h]) for h in range(4)], axis=0)
    grad_conv = conv_direct + jnp.concatenate([nt(logit_low[h], tables[h]) for h in range(4)], axis=1).reshape(
        2, SEQ, RC
    )
    grad_u = conv_w[0] * grad_conv
    d_conv = [jnp.sum(grad_conv * u, axis=(0, 1))]
    for k in range(1, 4):
        masked = grad_conv * same[k]
        d_conv.append(jnp.sum(masked * shifted(u, conv_before, k), axis=(0, 1)))
        grad_u = grad_u + conv_w[k] * jnp.concatenate([masked[:, k:], jnp.zeros((2, k, RC), F32)], axis=1)
    d_bias = [jnp.sum(v, axis=(0, 1)) for v in (grad_conv, d_rate, d_inp)]
    grad_mixed = jnp.concatenate([(grad_u * keep).reshape(2 * SEQ, RC), grad_gate_in], axis=1).astype(BF16)
    d_branch = tn(normed, grad_mixed)
    part = nt(grad_mixed, w_branch)
    grad_normed = part[:SEQ] + swap(part[SEQ:])
    back, gain1_term = rms_back(grad_normed, tok[:SEQ], gain1)
    input_grad = (grad_residual[:SEQ] + back).astype(BF16)

    def owners(v):
        v = v.reshape(v.shape[0], 2, 1, 32, 12).transpose(1, 2, 3, 0, 4).reshape(2, 1, 32, -1)
        zero = jnp.zeros_like(v)
        return jnp.where(
            core == 0, jnp.concatenate([v, zero], axis=1), jnp.concatenate([zero, v], axis=1)
        ).reshape(128, -1)

    d_small = jnp.concatenate(
        [
            jnp.sum(gain1_term, axis=0).reshape(128, 8),
            jnp.sum(gain2_term[:SEQ], axis=0).reshape(128, 8),
            owners(jnp.stack(d_conv)),
            owners(jnp.stack(d_bias)),
            owners(d_decay[None]),
            jnp.zeros((128, 16), F32),
        ],
        axis=1,
    )
    d_small = jnp.pad(d_small[:, None], ((0, 0), (0, 7), (0, 0))).reshape(D, 128)
    d_y = jnp.concatenate([d_branch, d_in[:, :YIN], d_small], axis=1).astype(BF16)
    d_z = d_in[:, YIN:].astype(BF16)
    g_y = sum_rings(to_y_rows(d_y), "yxz", here)
    g_z = sum_rings(to_z_rows(d_z), "zyx", here)
    d_og = jnp.concatenate([d_out, d_gate], axis=1).astype(BF16)
    g_down = sum_rings(to_x_rows(d_down.astype(BF16), 24), "xzy", here)
    g_og = sum_rings(to_x_rows(d_og, 12), "xzy", here)

    block = jnp.concatenate([g_y[:, : BRANCH + YIN], g_z, g_y[:, BRANCH + YIN :]], axis=1)
    low, high = block[:8], block[8:]
    first = send(jnp.where(core == 0, low, high), collect(0))
    second = send(jnp.where(core == 0, high, low), collect(1))
    halves = [jnp.where(odd, second, first), jnp.where(odd, first, second)]
    branch_grad = jnp.stack([v[:, :BRANCH].reshape(8, 4, 384) for v in halves], axis=2).reshape(8, 2 * R)
    in_grad = jnp.stack([v[:, BRANCH : BRANCH + INNER].reshape(8, 4, 768) for v in halves], axis=2).reshape(8, 2 * F)
    small = halves[0][0, BRANCH + INNER :] + halves[1][0, BRANCH + INNER :]
    theirs = swap(finals[1:])
    mine = finals[:1]
    finals = jnp.stack(
        [v.reshape(1, 4, 2, 384) for v in (jnp.where(core == 0, mine, theirs), jnp.where(core == 0, theirs, mine))],
        axis=3,
    ).reshape(1, 4, R)
    return (
        output[None],
        input_grad[None],
        finals[:, :3],
        finals[:, 3],
        small[:8],
        small[16:64].reshape(4, 12),
        small[64:100].reshape(3, 12),
        small[100:112],
        g_og[:, D:],
        branch_grad,
        g_og[:, :D],
        small[8:16],
        in_grad,
        g_down,
    )


def solution(mesh):
    rows, last = P(AXES), P(None, AXES)
    specs = [rows] * 6 + [rows, last, last] + [rows] * 7
    outs = [rows] * 4 + [rows, last, last] + [rows] * 7
    return jax.shard_map(
        shards, mesh=mesh, in_specs=tuple(specs), out_specs=tuple(outs), check_vma=False
    )
```

```python
import jax
import jax.numpy as jnp
from jax import lax
from jax.experimental import pallas as pl
from jax.experimental.pallas import tpu as pltpu
from jax.sharding import PartitionSpec as P

AXES = ("dp", "fsdp")
D, R, F, SEQ = 1024, 1536, 3072, 128
RC, FC = R // 2, F // 2
HS = 192
F32, BF16 = jnp.float32, jnp.bfloat16
BRANCH, INNER = 2 * RC, 2 * FC
YB = BRANCH + 128
YIN = 768
ZIN = INNER - YIN
YN = YB + YIN


def place_of(device):
    outer, inner = divmod(device, 32)
    x_hi, core = divmod(outer, 2)
    z, rest = divmod(inner, 8)
    x_lo, y = divmod(rest, 4)
    return dict(x=x_hi * 2 + x_lo, y=y, z=z, core=core)


def device_at(x, y, z, core):
    return ((x // 2) * 2 + core) * 32 + z * 8 + (x % 2) * 4 + y


def pairs(move):
    return [(d, device_at(**move(place_of(d)))) for d in range(128)]


def along(axis, steps):
    def move(p):
        sign = 1 if p["core"] == 0 else -1
        return {**p, axis: (p[axis] + sign * steps) % 4}

    return pairs(move)


def other_core(p):
    return {**p, "core": 1 - p["core"]}


def spread(turn):
    def move(p):
        return {**p, "y": 2 * (p["y"] // 2) + p["core"], "core": (p["y"] + turn) % 2}

    return pairs(move)


def collect(turn):
    return [(b, a) for a, b in spread(turn)]


def send(value, route):
    return lax.ppermute(value, AXES, route)


def swap(value):
    return send(value, pairs(other_core))


def my_place():
    device = lax.axis_index(AXES)
    outer, inner = device // 32, device % 32
    return dict(x=(outer // 2) * 2 + (inner // 4) % 2, y=inner % 4, z=inner // 8, core=outer % 2)


def ring_pieces(block, axis):
    up = send(block, along(axis, 1))
    down = send(block, along(axis, -1))
    return block, up, down, send(up, along(axis, 1))


def ring_places(axis, here):
    sign, at = 1 - 2 * here["core"], here[axis]
    return [at, (at - sign) % 4, (at + sign) % 4, (at + 2) % 4]


def gather_ring(block, axis, here, shape=None, spot=None):
    if shape is None:
        shape, spot = (4,) + block.shape, lambda i: (i,) + (0,) * block.ndim
    out = jnp.zeros(shape, block.dtype)
    part = tuple(n if isinstance(at, int) else 1 for n, at in zip(shape, spot(here[axis])))
    for piece, where in zip(ring_pieces(block, axis), ring_places(axis, here)):
        out = lax.dynamic_update_slice(out, piece.reshape(part), spot(where))
    return out


def sum_ring(own, ahead, opposite, behind, axis):
    far = send(opposite, along(axis, 1))
    down = send(behind, along(axis, -1))
    passed = (ahead.astype(F32) + far.astype(F32)).astype(BF16)
    up = send(passed, along(axis, 1))
    return own.astype(F32) + down.astype(F32) + up.astype(F32)


def ring_terms(blocks, axis, here):
    sign, at = 1 - 2 * here["core"], here[axis]
    return [lax.dynamic_index_in_dim(blocks, (at + sign * j) % 4, 0, keepdims=False) for j in range(4)]


def sum_rings(terms, axes, here):
    total = sum_ring(*terms, axes[0])
    for axis in axes[1:]:
        total = sum_ring(*ring_terms(total.astype(BF16), axis, here), axis)
    return total


def core_half(array, core, blocks):
    v = array.reshape(array.shape[:-1] + (blocks, 2, array.shape[-1] // (2 * blocks)))
    v = lax.dynamic_index_in_dim(v, core, v.ndim - 2, keepdims=False)
    return v.reshape(array.shape[:-1] + (array.shape[-1] // 2,))


def dot(a, b, dims):
    return lax.dot_general(a, b, (dims, ((), ())), preferred_element_type=F32)


def nn(a, b):
    return dot(a, b, ((1,), (0,)))


def nt(a, b):
    return dot(a, b, ((1,), (1,)))


def tn(a, b):
    return dot(a, b, ((0,), (0,)))


def inv_rms(v):
    return lax.rsqrt(jnp.mean(v * v, axis=-1, keepdims=True) + 1e-6)


def rms_back(grad, v, gain):
    s = inv_rms(v)
    n = v * s
    g2 = grad * gain
    return s * (g2 - n * jnp.mean(g2 * n, axis=-1, keepdims=True)), grad * n


C0, C1 = 0.7978845608028654, 0.044715


def gelu_both(a):
    t = jnp.tanh(C0 * (a + C1 * (a * a * a)))
    half = 0.5 * (1.0 + t)
    return a * half, half + 0.5 * a * (1.0 - t * t) * (C0 * (1.0 + 3.0 * C1 * (a * a)))


def gates(rate, inp, bias1, bias2, decay, keep, starts):
    rg = jax.nn.sigmoid(rate + bias1)
    ig = jax.nn.sigmoid(inp + bias2)
    sd = jnp.exp(-8.0 * rg * decay)
    q = 1.0 - sd * sd
    root = jnp.sqrt(jnp.maximum(q, 0.001))
    scale = starts + (1.0 - starts) * root
    return rg, ig, sd, q, root, scale


TOK = 2 * SEQ
PAD = SEQ + 8
LANES = 128


def cols(c):
    return pl.ds(pl.multiple_of(c * LANES, LANES), LANES)


def x_copy(piece, places, j, block, sem, down):
    x = places[0, j]
    for z in range(4):
        b = (x // 2) * 8 + z * 2 + x % 2
        if down:
            rows = pl.ds(pl.multiple_of(b * 96, 32), 96)
            pltpu.make_async_copy(piece.at[z, :, pl.ds(0, D)], block.at[rows], sem).start()
        else:
            for h in range(2):
                pltpu.make_async_copy(
                    piece.at[z, pl.ds(48 * h, 48), pl.ds(D, 768)], block.at[b, :, pl.ds(768 * h, 768)], sem
                ).start()


def y_copy(piece, places, j, block, sem, first, count, to):
    y = places[1, j]

    @pl.loop(0, 16)
    def _(m):
        k = (m // 8) * 32 + (y % 2) * 16 + (m % 8) * 2 + y // 2
        pltpu.make_async_copy(
            piece.at[m // 8, (m // 2) % 4, m % 2, :, pl.ds(first, count)], block.at[k, :, pl.ds(to, count)], sem
        ).start()


def z_copy(piece, places, j, block, sem, to):
    z = places[2, j]
    for xh in range(2):
        for yl in range(2):
            k = xh * 32 + yl * 16 + z * 4
            pltpu.make_async_copy(piece.at[xh, yl], block.at[pl.ds(k, 4), :, pl.ds(to, ZIN)], sem).start()


def landed(block, sem):
    pltpu.make_async_copy(block, block, sem).wait()


def turn_matrix():
    i = lax.broadcasted_iota(jnp.int32, (2 * HS, 2 * HS), 0)
    j = lax.broadcasted_iota(jnp.int32, (2 * HS, 2 * HS), 1)
    return jnp.where((i == j + HS) | (j == i + HS), 1.0, 0.0).astype(BF16)


def quarter_masks():
    i = lax.broadcasted_iota(jnp.int32, (2 * HS, 2 * HS), 0) < HS
    j = lax.broadcasted_iota(jnp.int32, (2 * HS, 2 * HS), 1) < HS
    return i, j


def rec_forward(
    places, tok, masks, conv_before, lru_before, y0, y1, y2, y3, x0, x1, x2, x3,
    part, merged, normed, u_out, gate_in, conv_low, rate, inp, st_out, coeff, gains, chans, tables, finals,
    wb, wog, drive, sems,
):
    for j, piece in enumerate((y0, y1, y2, y3)):
        y_copy(piece, places, j, wb, sems.at[0], 0, YB, 0)
    for j, piece in enumerate((x0, x1, x2, x3)):
        x_copy(piece, places, j, wog, sems.at[1], False)
    t = tok[...].astype(F32)
    scaled = t * inv_rms(t)
    landed(wb, sems.at[0])
    gains[...] = wb[:, :, BRANCH:YB].reshape(D, LANES).astype(F32).T[:8]
    normed[...] = (scaled * gains[0:1]).astype(BF16)
    for s in range(2):
        u_out[s, 5:8] = conv_before[s]
        st_out[s, 7:8] = lru_before[s]

    @pl.loop(0, 3)
    def _(c):
        at = pl.ds(pl.multiple_of(c * 256, 256), 256)
        v = nn(normed[...], wb[:, :, at].reshape(D, 256))
        for s in range(2):
            for half in range(2):
                to = pl.ds(pl.multiple_of(c * 256 + half * LANES, LANES), LANES)
                u_out[s, 8:, to] = (
                    v[s * SEQ : (s + 1) * SEQ, half * LANES : (half + 1) * LANES] * masks[0, s * SEQ : (s + 1) * SEQ]
                )

    @pl.loop(0, 3)
    def _(c):
        at = pl.ds(pl.multiple_of(RC + c * 256, 256), 256)
        gate_in[:, pl.ds(pl.multiple_of(c * 256, 256), 256)] = nn(normed[...], wb[:, :, at].reshape(D, 256))

    landed(wog, sems.at[1])
    chans[...] = wog[:, :, 1408:].reshape(RC, LANES).astype(F32).T[:8]

    @pl.loop(0, 6)
    def _(c):
        at = cols(c)
        for s in range(2):
            rows = slice(s * SEQ, (s + 1) * SEQ)
            v = chans[4:5, at] + chans[0:1, at] * u_out[s, 8:, at]
            for k in range(1, 4):
                v = v + chans[k : k + 1, at] * (u_out[s, 8 - k : PAD - k, at] * masks[1 + k, rows])
            conv_low[rows, at] = v.astype(BF16)

    turn = turn_matrix()
    top, left = quarter_masks()
    for p in range(2):
        g = wog[8 * p : 8 * p + 8, :, D : D + 384].reshape(2 * HS, 2 * HS)
        turned = nn(g, turn).astype(BF16)
        zero = jnp.zeros_like(g)
        tables[2 * p] = jnp.where(left, jnp.where(top, g, zero), jnp.where(top, zero, turned))
        tables[2 * p + 1] = jnp.where(left, jnp.where(top, turned, zero), jnp.where(top, zero, g))
        at = slice(2 * HS * p, 2 * HS * (p + 1))
        rate[:, at] = nn(conv_low[:, at], tables[2 * p])
        inp[:, at] = nn(conv_low[:, at], tables[2 * p + 1])

    @pl.loop(0, 6)
    def _(c):
        at = cols(c)
        keep, starts = masks[0], masks[1]
        _, ig, sd, _, _, scale = gates(
            rate[:, at], inp[:, at], chans[5:6, at], chans[6:7, at], chans[7:8, at], keep, starts
        )
        coeff[:, at] = (1.0 - starts) * (keep * sd + (1.0 - keep))
        drive[:, at] = keep * scale * ig * conv_low[:, at].astype(F32)

    row = lax.broadcasted_iota(jnp.int32, (8, RC), 0)

    def forward(i, carry):
        new = []
        for s in range(2):
            at = pl.ds(pl.multiple_of(s * SEQ + i * 8, 8), 8)
            a, b = coeff[at], drive[at]
            for k in (1, 2, 4):
                later = row >= k
                b = jnp.where(later, a * pltpu.roll(b, k, 0) + b, b)
                a = jnp.where(later, a * pltpu.roll(a, k, 0), a)
            h = a * carry[s] + b
            st_out[s, pl.ds(pl.multiple_of(8 + i * 8, 8), 8)] = h
            new.append(h[7:8])
        return tuple(new)

    last = lax.fori_loop(0, SEQ // 8, forward, (lru_before[0], lru_before[1]))
    for s in range(2):
        finals[s, 0:3] = u_out[s, PAD - 3 :]
        finals[s, 3:4] = last[s]

    @pl.loop(0, 6)
    def _(c):
        at = cols(c)
        act, _ = gelu_both(gate_in[:, at])
        for s in range(2):
            rows = slice(s * SEQ, (s + 1) * SEQ)
            merged[rows, at] = (st_out[s, 8:, at] * act[rows]).astype(BF16)

    @pl.loop(0, 4)
    def _(c):
        at = pl.ds(pl.multiple_of(c * 256, 256), 256)
        part[:, at] = nn(merged[...], wog[:, :, at].reshape(RC, 256))


def mlp(
    places, tok, cot, part, other, gains, y0, y1, y2, y3, z0, z1, z2, z3, x0, x1, x2, x3,
    residual, normed2, hidden, ggu, down, back,
    win, wdown, sems,
):
    for j, piece in enumerate((y0, y1, y2, y3)):
        y_copy(piece, places, j, win, sems.at[0], YB, YIN, 0)
    for j, piece in enumerate((z0, z1, z2, z3)):
        z_copy(piece, places, j, win, sems.at[0], YIN)
    for j, piece in enumerate((x0, x1, x2, x3)):
        x_copy(piece, places, j, wdown, sems.at[1], True)
    for s in range(2):
        rows, theirs = slice(s * SEQ, (s + 1) * SEQ), slice((1 - s) * SEQ, (2 - s) * SEQ)
        v = tok[rows].astype(F32) + (part[rows] + other[theirs])
        residual[rows] = v
        normed2[rows] = (v * inv_rms(v) * gains[1:2]).astype(BF16)
    landed(win, sems.at[0])
    landed(wdown, sems.at[1])
    down[...] = jnp.zeros_like(down)
    back[...] = jnp.zeros_like(back)

    @pl.loop(0, 6)
    def _(c):
        at = pl.ds(pl.multiple_of(c * 256, 256), 256)
        up = pl.ds(pl.multiple_of(FC + c * 256, 256), 256)
        wa, wu = win[:, :, at].reshape(D, 256), win[:, :, up].reshape(D, 256)
        a = nn(normed2[...], wa)
        b = nn(normed2[...], wu)
        ga, da = gelu_both(a)
        h = (ga * b).astype(BF16)
        hidden[:, at] = h
        wd = wdown[at]
        gh = nt(cot[...], wd)
        gg_a = (gh * b * da).astype(BF16)
        gg_b = (gh * ga).astype(BF16)
        ggu[:, at] = gg_a
        ggu[:, up] = gg_b
        down[...] += nn(h, wd)
        back[...] += nt(gg_a, wa) + nt(gg_b, wu)


def emit(block, places, axis, outs, sems):
    copies = []
    for j, out in enumerate(outs):
        at = places[axis, (0, 2, 3, 1)[j]]
        copies.append(pltpu.make_async_copy(block.at[at], out, sems.at[j]))
        copies[-1].start()
    return copies


BLOCKS = [
    (xh, yl, z, xl, yh) for xh in range(2) for yl in range(2) for z in range(4) for xl in range(2) for yh in range(2)
]


def put_y(block, value, at):
    for k, (xh, yl, z, xl, yh) in enumerate(BLOCKS):
        block[2 * yh + yl, 2 * xh + xl, z, :, at] = value[16 * k : 16 * k + 16]


def put_z(block, value, at):
    for k, (xh, yl, z, xl, yh) in enumerate(BLOCKS):
        block[z, 2 * yh + yl, 2 * xh + xl, :, at] = value[16 * k : 16 * k + 16]


def mlp_grads(
    places, cot, normed2, hidden, ggu,
    y0, y1, y2, y3, z0, z1, z2, z3, x0, x1, x2, x3,
    by, bz, bx, sems,
):
    @pl.loop(0, 2)
    def _(xh):
        at = pl.ds(pl.multiple_of(xh * 768, 256), 768)
        v = tn(hidden[:, at], cot[...]).astype(BF16)
        for z in range(4):
            for xl in range(2):
                r = 96 * (2 * z + xl)
                bx[2 * xh + xl, z] = v[r : r + 96]

    copies = emit(bx, places, 0, (x0, x1, x2, x3), sems.at[0])

    @pl.loop(0, 6)
    def _(c):
        at = pl.ds(pl.multiple_of(c * 256, 256), 256)
        put_y(by, tn(normed2[...], ggu[:, at]).astype(BF16), at)

    copies += emit(by, places, 1, (y0, y1, y2, y3), sems.at[1])

    @pl.loop(0, 6)
    def _(c):
        at = pl.ds(pl.multiple_of(c * 256, 256), 256)
        up = pl.ds(pl.multiple_of(FC + c * 256, 256), 256)
        put_z(bz, tn(normed2[...], ggu[:, up]).astype(BF16), at)

    copies += emit(bz, places, 2, (z0, z1, z2, z3), sems.at[2])
    for copy in copies:
        copy.wait()


def rec_backward(
    places, tok, cot, residual, part, other, normed, merged, u_in, gate_in, conv_low, rate, inp, st_in, coeff,
    gains, chans, tables, masks, wy0, wy1, wy2, wy3, wx0, wx1, wx2, wx3,
    own_residual, mixed_part, y0, y1, y2, y3, z0, z1, z2, z3, x0, x1, x2, x3,
    wb, wog, grad_branch, gs, lam, rate_low, inp_low, direct, gmix, rolled, sums, by, bz, bx, sems, out_sems,
):
    for j, piece in enumerate((wx0, wx1, wx2, wx3)):
        x_copy(piece, places, j, wog, sems.at[1], False)
    for j, piece in enumerate((wy0, wy1, wy2, wy3)):
        y_copy(piece, places, j, wb, sems.at[0], 0, BRANCH, 0)
    sums[...] = jnp.zeros_like(sums)
    for s in range(2):
        rows, theirs = slice(s * SEQ, (s + 1) * SEQ), slice((1 - s) * SEQ, (2 - s) * SEQ)
        grad, term = rms_back(part[rows] + other[theirs], residual[rows], gains[1:2])
        grad = cot[rows].astype(F32) + grad
        grad_branch[rows] = grad.astype(BF16)
        if s == 0:
            own_residual[...] = grad
            sums[9:10] = jnp.sum(term, axis=0, keepdims=True)
    v = tn(merged[...], grad_branch[...]).astype(BF16)
    for b in range(16):
        bx[(b // 8) * 2 + b % 2, (b // 2) % 4, :, 0:D] = v[48 * b : 48 * b + 48]
    landed(wog, sems.at[1])

    gs[...] = nt(grad_branch[...], wog[:, :, 0:D].reshape(RC, D))

    @pl.loop(0, 6)
    def _(c):
        at = cols(c)
        act, act_grad = gelu_both(gate_in[:, at])
        g = gs[:, at]
        for s in range(2):
            rows = slice(s * SEQ, (s + 1) * SEQ)
            gmix[rows, pl.ds(pl.multiple_of(RC + c * LANES, LANES), LANES)] = (
                g[rows] * st_in[s, 8:, at] * act_grad[rows]
            ).astype(BF16)
        gs[:, at] = g * act

    row = lax.broadcasted_iota(jnp.int32, (8, RC), 0)

    def backward(n, carry):
        i = SEQ // 8 - 1 - n
        new = []
        for s in range(2):
            at = pl.ds(pl.multiple_of(s * SEQ + i * 8, 8), 8)
            own = coeff[at]
            later_a, later_lam = carry[s]
            a = jnp.where(row == 7, later_a, pltpu.roll(own, 7, 0))
            b = gs[at]
            for k in (1, 2, 4):
                here = row < 8 - k
                b = jnp.where(here, b + a * pltpu.roll(b, 8 - k, 0), b)
                a = jnp.where(here, a * pltpu.roll(a, 8 - k, 0), a)
            h = b + a * later_lam
            lam[at] = h
            new.append((own[0:1], h[0:1]))
        return tuple(new)

    zero = jnp.zeros((1, RC), F32)
    lax.fori_loop(0, SEQ // 8, backward, ((zero, zero), (zero, zero)))

    @pl.loop(0, 6)
    def _(c):
        at = cols(c)
        decay = chans[7:8, at]
        for s in range(2):
            rows = slice(s * SEQ, (s + 1) * SEQ)
            keep, starts = masks[0, rows], masks[1, rows]
            rg, ig, sd, q, root, scale = gates(
                rate[rows, at], inp[rows, at], chans[5:6, at], chans[6:7, at], decay, keep, starts
            )
            conv = conv_low[rows, at].astype(F32)
            l = lam[rows, at]
            common = l * keep
            grad_coeff = l * st_in[s, 7 : PAD - 1, at]
            direct[rows, at] = common * scale * ig
            d_ig = common * scale * conv
            d_scale = common * ig * conv
            d_sd = (1.0 - starts) * (grad_coeff * keep - d_scale * jnp.where(q > 0.001, sd / root, 0.0))
            d_log = d_sd * sd * -8.0
            d_rate = d_log * decay * rg * (1.0 - rg)
            d_inp = d_ig * ig * (1.0 - ig)
            rate_low[rows, at] = d_rate.astype(BF16)
            inp_low[rows, at] = d_inp.astype(BF16)
            for n, term in ((5, d_rate), (6, d_inp), (7, d_log * rg)):
                sums[n : n + 1, at] += jnp.sum(term, axis=0, keepdims=True)

    turn = turn_matrix()
    top, left = quarter_masks()
    for p in range(2):
        at = slice(2 * HS * p, 2 * HS * (p + 1))
        direct[:, at] += nt(rate_low[:, at], tables[2 * p]) + nt(inp_low[:, at], tables[2 * p + 1])
        dr = tn(conv_low[:, at], rate_low[:, at]).astype(BF16)
        di = tn(conv_low[:, at], inp_low[:, at]).astype(BF16)
        none = jnp.zeros_like(dr)
        straight = jnp.where(top, jnp.where(left, dr, none), jnp.where(left, none, di))
        crossed = jnp.where(top, jnp.where(left, di, none), jnp.where(left, none, dr))
        g = (straight.astype(F32) + nn(crossed, turn)).astype(BF16)
        for b in range(8):
            m = 8 * p + b
            bx[(m // 8) * 2 + m % 2, (m // 2) % 4, :, D : D + 384] = g[48 * b : 48 * b + 48]

    rolled[:, SEQ:] = jnp.zeros((2, 8, LANES), F32)

    @pl.loop(0, 6)
    def _(c):
        at = cols(c)
        for s in range(2):
            rows = slice(s * SEQ, (s + 1) * SEQ)
            g = direct[rows, at]
            gu = chans[0:1, at] * g
            sums[4:5, at] += jnp.sum(g, axis=0, keepdims=True)
            sums[0:1, at] += jnp.sum(g * u_in[s, 8:, at], axis=0, keepdims=True)
            for k in range(1, 4):
                w = g * masks[1 + k, rows]
                sums[k : k + 1, at] += jnp.sum(w * u_in[s, 8 - k : PAD - k, at], axis=0, keepdims=True)
                rolled[s, 0:SEQ] = w
                gu = gu + chans[k : k + 1, at] * rolled[s, k : SEQ + k]
            gmix[rows, at] = (gu * masks[0, rows]).astype(BF16)

    v = jnp.concatenate([sums[0:8, 0:RC], jnp.zeros((LANES - 8, RC), F32)], axis=0).T.astype(BF16)
    for b in range(16):
        bx[(b // 8) * 2 + b % 2, (b // 2) % 4, :, 1408:] = v[48 * b : 48 * b + 48]
    copies = emit(bx, places, 0, (x0, x1, x2, x3), out_sems.at[0])
    landed(wb, sems.at[0])
    mixed_part[...] = nt(gmix[...], wb[...].reshape(D, BRANCH))
    t = tok[...].astype(F32)
    sums[8:9] = jnp.sum(mixed_part[...] * (t * inv_rms(t)), axis=0, keepdims=True)
    v = jnp.concatenate([sums[8:16], jnp.zeros((LANES - 8, D), F32)], axis=0).T.astype(BF16)
    put_y(by, v, pl.ds(768, LANES))

    @pl.loop(0, 3)
    def _(c):
        at = pl.ds(pl.multiple_of(c * 256, 256), 256)
        put_y(by, tn(normed[...], gmix[:, at]).astype(BF16), at)

    copies += emit(by, places, 1, (y0, y1, y2, y3), out_sems.at[1])

    @pl.loop(0, 3)
    def _(c):
        at = pl.ds(pl.multiple_of(c * 256, 256), 256)
        put_z(bz, tn(normed[...], gmix[:, pl.ds(pl.multiple_of(RC + c * 256, 256), 256)]).astype(BF16), at)

    copies += emit(bz, places, 2, (z0, z1, z2, z3), out_sems.at[2])
    for copy in copies:
        copy.wait()


VM, ANY, SM = pltpu.VMEM, pl.ANY, pltpu.SMEM


def kernel(body, ins, spaces, outs, scratch, mib, flops):
    moved = sum(v.size * v.dtype.itemsize for v in ins)
    return pl.pallas_call(
        body,
        out_shape=[jax.ShapeDtypeStruct(s, d) for s, d, _ in outs],
        in_specs=[pl.BlockSpec(memory_space=s) for s in spaces],
        out_specs=[pl.BlockSpec(memory_space=s) for _, _, s in outs],
        scratch_shapes=scratch,
        compiler_params=pltpu.CompilerParams(vmem_limit_bytes=mib * 2**20),
        cost_estimate=pl.CostEstimate(flops=flops, bytes_accessed=moved, transcendentals=0),
    )(*ins)


def shards(
    tokens, cotangent, segment, keep_mask, conv_state, lru_state, norm1_gain, conv_weight, lru_bias, decay_rate,
    gate_weight, branch_weight, out_weight, norm2_gain, mlp_in_weight, mlp_out_weight,
):
    here = my_place()
    core = here["core"]
    odd = here["y"] % 2 == 1
    places = jnp.stack([jnp.stack(ring_places(axis, here)) for axis in "xyz"]).astype(jnp.int32)

    small = jnp.pad(jnp.stack([norm1_gain, norm2_gain], axis=1), ((0, 0), (0, 126)))
    branch = branch_weight.reshape(8, 4, 2, 384)
    inner = mlp_in_weight.reshape(8, 4, 2, 768)
    halves = [
        jnp.concatenate([branch[:, :, c].reshape(8, BRANCH), small, inner[:, :, c].reshape(8, INNER)], axis=1)
        for c in range(2)
    ]
    first = send(jnp.where(odd, halves[1], halves[0]), spread(0))
    second = send(jnp.where(odd, halves[0], halves[1]), spread(1))
    low = jnp.where(core == 0, first, second)
    high = jnp.where(core == 0, second, first)
    block = jnp.concatenate([low, high], axis=0)
    y_block, z_block = block[:, :YN], block[:, YN:]
    perchan = jnp.concatenate([conv_weight, lru_bias, decay_rate[None]], axis=0).T
    og = jnp.concatenate([out_weight, gate_weight, jnp.pad(perchan, ((0, 0), (0, 120)))], axis=1)
    x_block = jnp.concatenate([mlp_out_weight, og.reshape(12, 2, 768).transpose(1, 0, 2).reshape(24, 768)], axis=1)

    x_block = gather_ring(x_block, "y", here)
    x_block = jnp.concatenate(
        [
            x_block[..., :D].reshape(96, D),
            x_block[..., D:].reshape(4, 2, 12, 768).transpose(1, 0, 2, 3).reshape(96, 768),
        ],
        axis=1,
    )
    y_block = gather_ring(y_block, "z", here)
    z_block = gather_ring(z_block, "x", here).reshape(2, 2, 16, ZIN)
    x_block = gather_ring(x_block, "z", here)
    y_block = gather_ring(y_block, "x", here, (2, 4, 2, 16, YN), lambda i: (i // 2, 0, i % 2, 0, 0))
    z_block = gather_ring(z_block, "y", here, (2, 2, 2, 2, 16, ZIN), lambda i: (0, i % 2, 0, i // 2, 0, 0))
    z_block = z_block.reshape(2, 2, 4, 16, ZIN)
    xs, ys, zs = ring_pieces(x_block, "x"), ring_pieces(y_block, "y"), ring_pieces(z_block, "z")

    def both(v):
        return jnp.concatenate([v, swap(v)], axis=0)

    tok = both(tokens).reshape(TOK, D)
    cot = both(cotangent).reshape(TOK, D)
    marks = both(jnp.concatenate([segment, keep_mask], axis=1).astype(F32))
    seg, keep = marks[:, :SEQ], marks[:, SEQ:]
    states = jnp.concatenate([conv_state, lru_state[:, None]], axis=1)
    states = jnp.concatenate([core_half(states, core, 2), swap(core_half(states, 1 - core, 2))], axis=0)
    earlier = [jnp.concatenate([jnp.repeat(seg[:, :1], k, axis=1), seg[:, : SEQ - k]], axis=1) for k in range(1, 4)]
    masks = jnp.stack([keep, (earlier[0] != seg).astype(F32)] + [(e == seg).astype(F32) for e in earlier])
    masks = jnp.broadcast_to(masks.reshape(5, TOK, 1), (5, TOK, LANES))

    wide, act, low_act = ((TOK, D), F32, VM), ((TOK, RC), F32, VM), ((TOK, RC), BF16, VM)
    (part, merged, normed, u, gate_in, conv_low, rate, inp, st, coeff, gains, chans, tables, finals) = kernel(
        rec_forward,
        (places, tok, masks, states[:, :3], states[:, 3:], *ys, *xs),
        [SM] + [VM] * 4 + [ANY] * 8,
        [
            wide, low_act, ((TOK, D), BF16, VM), ((2, PAD, RC), F32, VM), act, low_act, act, act,
            ((2, PAD, RC), F32, VM), act, ((8, D), F32, VM), ((8, RC), F32, VM), ((4, 2 * HS, 2 * HS), BF16, VM),
            ((2, 4, RC), F32, VM),
        ],
        [
            pltpu.VMEM((64, 16, YB), BF16),
            pltpu.VMEM((16, 48, 1536), BF16),
            pltpu.VMEM((TOK, RC), F32),
            pltpu.SemaphoreType.DMA((2,)),
        ],
        32,
        2 * TOK * (D * BRANCH + RC * (D + 768)),
    )
    residual, normed2, hidden, ggu, down, back = kernel(
        mlp,
        (places, tok, cot, part, swap(part), gains, *ys, *zs, *xs),
        [SM] + [VM] * 5 + [ANY] * 12,
        [wide, ((TOK, D), BF16, VM), ((TOK, FC), BF16, VM), ((TOK, INNER), BF16, VM), wide, wide],
        [
            pltpu.VMEM((64, 16, INNER), BF16),
            pltpu.VMEM((FC, D), BF16),
            pltpu.SemaphoreType.DMA((2,)),
        ],
        40,
        2 * TOK * D * (2 * INNER + 2 * FC),
    )
    back_other = swap(back)
    y_shape, z_shape, x_shape = (4, 4, 16, FC), (4, 4, 16, FC), (4, 96, D)
    outs = kernel(
        mlp_grads,
        (places, cot, normed2, hidden, ggu),
        [SM] + [VM] * 4,
        [(s, BF16, ANY) for s in (y_shape, z_shape, x_shape) for _ in range(4)],
        [
            pltpu.VMEM((4,) + y_shape, BF16),
            pltpu.VMEM((4,) + z_shape, BF16),
            pltpu.VMEM((4,) + x_shape, BF16),
            pltpu.SemaphoreType.DMA((3, 4)),
        ],
        32,
        2 * TOK * D * (INNER + FC),
    )
    in_y, in_z, down_x = outs[:4], outs[4:8], outs[8:]
    y_shape, z_shape, x_shape = (4, 4, 16, 768 + LANES), (4, 4, 16, 768), (4, 48, 1536)
    outs = kernel(
        rec_backward,
        (places, tok, cot, residual, back, back_other, normed, merged, u, gate_in, conv_low, rate, inp, st, coeff,
         gains, chans, tables, masks, *ys, *xs),
        [SM] + [VM] * 18 + [ANY] * 8,
        [((SEQ, D), F32, VM), wide] + [(s, BF16, ANY) for s in (y_shape, z_shape, x_shape) for _ in range(4)],
        [
            pltpu.VMEM((64, 16, BRANCH), BF16),
            pltpu.VMEM((16, 48, 1536), BF16),
            pltpu.VMEM((TOK, D), BF16),
            pltpu.VMEM((TOK, RC), F32),
            pltpu.VMEM((TOK, RC), F32),
            pltpu.VMEM((TOK, RC), BF16),
            pltpu.VMEM((TOK, RC), BF16),
            pltpu.VMEM((TOK, RC), F32),
            pltpu.VMEM((TOK, BRANCH), BF16),
            pltpu.VMEM((2, PAD, LANES), F32),
            pltpu.VMEM((16, D), F32),
            pltpu.VMEM((4,) + y_shape, BF16),
            pltpu.VMEM((4,) + z_shape, BF16),
            pltpu.VMEM((4,) + x_shape, BF16),
            pltpu.SemaphoreType.DMA((2,)),
            pltpu.SemaphoreType.DMA((3, 4)),
        ],
        44,
        2 * TOK * D * (2 * BRANCH + 2 * RC),
    )
    grad_residual, part = outs[:2]
    branch_y, branch_z, og_x = outs[2:6], outs[6:10], outs[10:]

    output = (residual[:SEQ] + (down[:SEQ] + swap(down[SEQ:]))).astype(BF16)
    grad, _ = rms_back(part[:SEQ] + swap(part[SEQ:]), tok[:SEQ].astype(F32), gains[0])
    input_grad = (grad_residual + grad).astype(BF16)

    g_in_y, g_in_z = sum_rings(in_y, "yxz", here), sum_rings(in_z, "zyx", here)
    g_branch_y, g_branch_z = sum_rings(branch_y, "yxz", here), sum_rings(branch_z, "zyx", here)

    def x_sum(terms, rows):
        total = sum_ring(*terms, "x")
        total = sum_ring(*ring_terms(total.astype(BF16), "z", here), "z").astype(BF16)
        return sum_ring(*ring_terms(total.reshape(4, rows, -1), "y", here), "y")

    g_down, g_og = x_sum(down_x, 24), x_sum(og_x, 12)
    block = jnp.concatenate([g_branch_y[:, :768], g_branch_z, g_in_y, g_in_z, g_branch_y[:, 768:]], axis=1)
    low, high = block[:8], block[8:]
    first = send(jnp.where(core == 0, low, high), collect(0))
    second = send(jnp.where(core == 0, high, low), collect(1))
    halves = [jnp.where(odd, second, first), jnp.where(odd, first, second)]
    branch_grad = jnp.stack([v[:, :BRANCH].reshape(8, 4, 384) for v in halves], axis=2).reshape(8, 2 * R)
    in_grad = jnp.stack([v[:, BRANCH : BRANCH + INNER].reshape(8, 4, 768) for v in halves], axis=2).reshape(8, 2 * F)
    small = halves[0][:, BRANCH + INNER :] + halves[1][:, BRANCH + INNER :]
    perchan = g_og[:, 1408:1416].T
    mine, theirs = finals[:1], swap(finals[1:])
    finals = jnp.stack(
        [v.reshape(1, 4, 2, 384) for v in (jnp.where(core == 0, mine, theirs), jnp.where(core == 0, theirs, mine))],
        axis=3,
    ).reshape(1, 4, R)
    return (
        output[None],
        input_grad[None],
        finals[:, :3],
        finals[:, 3],
        small[:, 0],
        perchan[:4],
        perchan[4:7],
        perchan[7],
        g_og[:, D : D + 384],
        branch_grad,
        g_og[:, :D],
        small[:, 1],
        in_grad,
        g_down,
    )


def solution(mesh):
    rows, last = P(AXES), P(None, AXES)
    specs = [rows] * 6 + [rows, last, last] + [rows] * 7
    outs = [rows] * 4 + [rows, last, last] + [rows] * 7
    return jax.shard_map(
        shards, mesh=mesh, in_specs=tuple(specs), out_specs=tuple(outs), check_vma=False
    )
```

```python
import jax
import jax.numpy as jnp
from jax import lax
from jax.experimental import pallas as pl
from jax.experimental.pallas import tpu as pltpu
from jax.sharding import PartitionSpec as P

AXES = ("dp", "fsdp")
D, R, F, SEQ = 1024, 1536, 3072, 128
RC, FC = R // 2, F // 2
HS = 192
F32, BF16 = jnp.float32, jnp.bfloat16
BRANCH, INNER = 2 * RC, 2 * FC
TOK, PAD, LANES = 2 * SEQ, SEQ + 8, 128

EARLY, LATE = 1408, 2304
UNIT = EARLY + LATE
OG, PB, PI, QB = 1152, 256, 768, 1280
DC = PB + PI + UNIT
OGC = 1536
DOWN = DC + OGC
OWN = DOWN + D + D // 2


def place_of(device):
    outer, inner = divmod(device, 32)
    x_hi, core = divmod(outer, 2)
    z, rest = divmod(inner, 8)
    x_lo, y = divmod(rest, 4)
    return dict(x=x_hi * 2 + x_lo, y=y, z=z, core=core)


def device_at(x, y, z, core):
    return ((x // 2) * 2 + core) * 32 + z * 8 + (x % 2) * 4 + y


def pairs(move):
    return [(d, device_at(**move(place_of(d)))) for d in range(128)]


def along(axis, steps):
    def move(p):
        sign = 1 if p["core"] == 0 else -1
        return {**p, axis: (p[axis] + sign * steps) % 4}

    return pairs(move)


def other_core(p):
    return {**p, "core": 1 - p["core"]}


def opposite(axis):
    return pairs(lambda p: {**p, axis: (p[axis] + 2) % 4})


def send(value, route):
    return lax.ppermute(value, AXES, route)


def swap(value):
    return send(value, pairs(other_core))


def my_place():
    device = lax.axis_index(AXES)
    outer, inner = device // 32, device % 32
    return dict(x=(outer // 2) * 2 + (inner // 4) % 2, y=inner % 4, z=inner // 8, core=outer % 2)


def ring_places(axis, here):
    sign, at = 1 - 2 * here["core"], here[axis]
    return [at, (at - sign) % 4, (at + sign) % 4, (at + 2) % 4]


def ring(block, axis):
    one = send(block, along(axis, 1))
    two = send(one, along(axis, 1))
    return block, one, send(two, along(axis, 1)), two


def ring_direct(block, axis):
    return block, send(block, along(axis, 1)), send(block, along(axis, -1)), send(block, opposite(axis))


def terms_direct(terms, axis):
    own, ahead, far, behind = terms
    return own, send(ahead, along(axis, 1)), send(far, opposite(axis)), send(behind, along(axis, -1))


def total(*terms):
    out = terms[0].astype(F32)
    for term in terms[1:]:
        out = out + term.astype(F32)
    return out.astype(BF16)


def core_half(array, core, blocks):
    v = array.reshape(array.shape[:-1] + (blocks, 2, array.shape[-1] // (2 * blocks)))
    v = lax.dynamic_index_in_dim(v, core, v.ndim - 2, keepdims=False)
    return v.reshape(array.shape[:-1] + (array.shape[-1] // 2,))


def dot(a, b, dims):
    return lax.dot_general(a, b, (dims, ((), ())), preferred_element_type=F32)


def nn(a, b):
    return dot(a, b, ((1,), (0,)))


def nt(a, b):
    return dot(a, b, ((1,), (1,)))


def tn(a, b):
    return dot(a, b, ((0,), (0,)))


def inv_rms(v):
    return lax.rsqrt(jnp.mean(v * v, axis=-1, keepdims=True) + 1e-6)


def rms_back(grad, v, gain):
    s = inv_rms(v)
    n = v * s
    g2 = grad * gain
    return s * (g2 - n * jnp.mean(g2 * n, axis=-1, keepdims=True)), grad * n


C0, C1 = 0.7978845608028654, 0.044715


def gelu_both(a):
    t = jnp.tanh(C0 * (a + C1 * (a * a * a)))
    half = 0.5 * (1.0 + t)
    return a * half, half + 0.5 * a * (1.0 - t * t) * (C0 * (1.0 + 3.0 * C1 * (a * a)))


def gates(rate, inp, bias1, bias2, decay, keep, starts):
    rg = jax.nn.sigmoid(rate + bias1)
    ig = jax.nn.sigmoid(inp + bias2)
    sd = jnp.exp(-8.0 * rg * decay)
    q = 1.0 - sd * sd
    root = jnp.sqrt(jnp.maximum(q, 0.001))
    scale = starts + (1.0 - starts) * root
    return rg, ig, sd, q, root, scale


def cols(c):
    return pl.ds(pl.multiple_of(c * LANES, LANES), LANES)


class Saves:
    def __init__(self, sem):
        self.sem, self.copies = sem, []

    def start(self, source, target):
        self.copies.append(pltpu.make_async_copy(source, target, self.sem.at[len(self.copies)]))
        self.copies[-1].start()

    def wait(self):
        for copy in self.copies:
            copy.wait()


def pick(rows, where):
    return jnp.where(lax.broadcasted_iota(jnp.int32, (rows, where.shape[1]), 0) == where, 1.0, 0.0).astype(BF16)


def stand(values, rows):
    v = values.astype(F32)
    i = lax.broadcasted_iota(jnp.int32, (rows, v.shape[1]), 0)
    j = lax.broadcasted_iota(jnp.int32, (rows, v.shape[1]), 1)
    lane = lax.broadcasted_iota(jnp.int32, (rows, LANES), 1)
    out = jnp.zeros((rows, LANES), F32)
    for n in range(v.shape[0]):
        column = jnp.sum(jnp.where(i == j, v[n : n + 1], 0.0), axis=1, keepdims=True)
        out = out + jnp.where(lane == n, column, 0.0)
    return out


def pack(places, branch, inner, gain, out, gate, perchan, down, mine, theirs, own):
    gains = stand(gain[...], 8).astype(BF16)

    def halves(outs):
        for c, to_core in enumerate(outs):
            for q in range(4):
                v = branch[:, 768 * q + 384 * c : 768 * q + 384 * c + 384]
                if q == 0:
                    to_core[:, 0:PB] = v[:, 0:PB]
                    to_core[:, PB + PI : PB + PI + 128] = v[:, PB:]
                else:
                    to_core[:, PI + 384 * q : PI + 384 * q + 384] = v
                v = inner[:, 1536 * q + 768 * c : 1536 * q + 768 * c + 768]
                to = PB if q == 0 else DC - LATE + 768 * (q - 1)
                to_core[:, to : to + 768] = v
            tile = DC - LATE - LANES
            to_core[:, tile : tile + LANES] = gains

    @pl.when(places[3, 0] == 0)
    def _():
        halves((mine, theirs))

    @pl.when(places[3, 0] == 1)
    def _():
        halves((theirs, mine))

    own[...] = jnp.zeros_like(own)
    own[0:12, 0:D] = out[...]
    own[0:12, D : D + 384] = gate[...]
    own[:, 1408:OGC] = stand(perchan[...], 16).astype(BF16)
    own[:, OGC : OGC + D] = down[0:16]
    own[:, OGC + D :] = jnp.concatenate(
        [down[16:24, 0:512].astype(F32), down[16:24, 512:].astype(F32)], axis=0
    ).astype(BF16)


def join(places, mine, theirs, own, block):
    def rows(low, high):
        block[:, 0:DC] = jnp.concatenate([low[...].astype(F32), high[...].astype(F32)], axis=0).astype(BF16)

    @pl.when(places[3, 0] == 0)
    def _():
        rows(mine, theirs)

    @pl.when(places[3, 0] == 1)
    def _():
        rows(theirs, mine)

    block[:, DC:] = own[...]


def unit(places, p0, p1, p2, p3, *rest):
    o_p, o_q, p, q, d, dn, sems = rest[-7:]
    ogs = []
    s = lax.broadcasted_iota(jnp.int32, (1, 64), 1)
    y = jnp.zeros((1, 64), jnp.int32)
    for j, piece in enumerate((p0, p1, p2, p3)):
        at = places[1, j]
        y = jnp.where(s // 16 == j, at, y)
        v = piece[:, 0:DC].astype(F32)
        for c in range(2):
            d[pl.ds(pl.multiple_of(c * 32 + at * 8, 8), 8)] = v[8 * c : 8 * c + 8]
        ogs.append(piece[:, DC:DOWN])
        v = piece[:, DOWN:].astype(F32)
        dn[pl.ds(pl.multiple_of(at * 24, 8), 16)] = v[:, 0:D]
        for h in range(2):
            dn[pl.ds(pl.multiple_of(at * 24 + 16, 8), 8), 512 * h : 512 * h + 512] = v[8 * h : 8 * h + 8, D:]
    saves = Saves(sems)
    q[...] = d[:, PB + PI :].astype(BF16)
    saves.start(q, o_q)
    p[:, OG:EARLY] = d[:, 0:PB].astype(BF16)
    p[:, UNIT - PI :] = d[:, PB : PB + PI].astype(BF16)
    i = s % 16
    og = nn(pick(48, jnp.where(i < 12, y * 12 + i, 64)), jnp.concatenate(ogs, axis=0)).astype(BF16)
    p[0:48, 0:OG] = og[:, 0:OG]
    for r in range(3):
        p[48:64, 384 * r : 384 * r + 384] = og[16 * r : 16 * r + 16, OG:]
    p[:, EARLY : EARLY + D] = dn[0:64].astype(BF16)
    p[0:32, EARLY + D : EARLY + FC] = dn[64:96, 0:512].astype(BF16)
    p[32:64, EARLY + D : EARLY + FC] = dn[64:96, 512:1024].astype(BF16)
    saves.start(p, o_p)
    saves.wait()


def planes(places, p0, p1, p2, p3, q0, q1, q2, q3, o_pe, o_qe, o_pl, o_ql, p, q, in_sems, out_sems):
    loads, saves = Saves(in_sems), Saves(out_sems)
    for pieces, axis, stack in (((p0, p1, p2, p3), 2, p), ((q0, q1, q2, q3), 0, q)):
        for j, piece in enumerate(pieces):
            loads.start(piece, stack.at[places[axis, j]])
    for n, (stack, out) in enumerate(((p, o_pe), (q, o_qe))):
        for copy in loads.copies[4 * n : 4 * n + 4]:
            copy.wait()
        saves.start(stack.at[:, :, pl.ds(0, EARLY)], out)
    for stack, out in ((p, o_pl), (q, o_ql)):
        saves.start(stack.at[:, :, pl.ds(EARLY, LATE)], out)
    saves.wait()


def ring_rows(x, z):
    return (x // 2) * 512 + z * 64 + (x % 2) * 32


def unit_copy(piece, x, z, first, count, block, to, sem):
    for c in range(2):
        rows = pl.ds(pl.multiple_of(ring_rows(x, z) + 256 * c, 32), 32)
        pltpu.make_async_copy(
            piece.at[pl.ds(32 * c, 32), pl.ds(first, count)], block.at[rows, pl.ds(to, count)], sem
        ).start()


def p_copy(piece, places, j, first, count, block, to, sem):
    for z in range(4):
        unit_copy(piece.at[z], places[0, j], z, first, count, block, to, sem)


def q_copy(piece, places, j, first, count, block, to, sem):
    for x in range(4):
        unit_copy(piece.at[x], x, places[2, j], first, count, block, to, sem)


def og_copy(piece, places, j, block, sem):
    x = places[0, j]
    for z in range(4):
        b = (x // 2) * 8 + z * 2 + x % 2
        pltpu.make_async_copy(
            piece.at[z, pl.ds(0, 48), pl.ds(0, OG)], block.at[b, :, pl.ds(0, OG)], sem
        ).start()
        for r in range(3):
            pltpu.make_async_copy(
                piece.at[z, pl.ds(48, 16), pl.ds(384 * r, 384)], block.at[b, pl.ds(16 * r, 16), pl.ds(OG, 384)], sem
            ).start()


def down_copy(piece, places, j, block, sem):
    x = places[0, j]
    for z in range(4):
        row = ((x // 2) * 8 + z * 2 + x % 2) * 96
        rows = pl.ds(pl.multiple_of(row, 32), 64)
        pltpu.make_async_copy(piece.at[z, :, pl.ds(0, D)], block.at[rows], sem).start()
        rows = pl.ds(pl.multiple_of(row + 64, 32), 32)
        for h in range(2):
            pltpu.make_async_copy(
                piece.at[z, pl.ds(32 * h, 32), pl.ds(D, 512)], block.at[rows, pl.ds(512 * h, 512)], sem
            ).start()


def landed(block, sem):
    pltpu.make_async_copy(block, block, sem).wait()


def turn_matrix():
    i = lax.broadcasted_iota(jnp.int32, (2 * HS, 2 * HS), 0)
    j = lax.broadcasted_iota(jnp.int32, (2 * HS, 2 * HS), 1)
    return jnp.where((i == j + HS) | (j == i + HS), 1.0, 0.0).astype(BF16)


def quarter_masks():
    i = lax.broadcasted_iota(jnp.int32, (2 * HS, 2 * HS), 0) < HS
    j = lax.broadcasted_iota(jnp.int32, (2 * HS, 2 * HS), 1) < HS
    return i, j


def rec_forward(
    places, tok, masks, conv_before, lru_before, p0, p1, p2, p3, q0, q1, q2, q3,
    part, finals, gains, chans, o_normed, o_merged, o_u, o_gate, o_conv, o_rate, o_inp, o_st, o_tables,
    wb, wog, normed, merged, u, gate_in, conv_low, rate, inp, st, tables, coeff, drive, sems, out_sems,
):
    for j, (p, q) in enumerate(((p0, q0), (p1, q1), (p2, q2), (p3, q3))):
        p_copy(p, places, j, OG, PB, wb, 0, sems.at[0])
        q_copy(q, places, j, 0, EARLY, wb, PB, sems.at[0])
    for j, p in enumerate((p0, p1, p2, p3)):
        og_copy(p, places, j, wog, sems.at[1])
    saves = Saves(out_sems)
    t = tok[...].astype(F32)
    scaled = t * inv_rms(t)
    landed(wb, sems.at[0])
    gains[...] = wb[:, BRANCH:].astype(F32).T[:8]
    normed[...] = (scaled * gains[0:1]).astype(BF16)
    saves.start(normed, o_normed)
    for s in range(2):
        u[s, 0:8] = jnp.zeros((8, RC), F32)
        u[s, 5:8] = conv_before[s]
        st[s, 0:8] = jnp.zeros((8, RC), F32)
        st[s, 7:8] = lru_before[s]

    v = nn(normed[...], wb[:, 0:RC])
    for s in range(2):
        rows = slice(s * SEQ, (s + 1) * SEQ)
        for c in range(6):
            u[s, 8:, LANES * c : LANES * c + LANES] = v[rows, LANES * c : LANES * c + LANES] * masks[0, rows]

    saves.start(u, o_u)

    gate_in[...] = nn(normed[...], wb[:, RC:BRANCH])

    saves.start(gate_in, o_gate)
    landed(wog, sems.at[1])
    chans[...] = wog[:, :, 1408:].reshape(RC, LANES).astype(F32).T[:8]

    @pl.loop(0, 6)
    def _(c):
        at = cols(c)
        for s in range(2):
            rows = slice(s * SEQ, (s + 1) * SEQ)
            v = chans[4:5, at] + chans[0:1, at] * u[s, 8:, at]
            for k in range(1, 4):
                v = v + chans[k : k + 1, at] * (u[s, 8 - k : PAD - k, at] * masks[1 + k, rows])
            conv_low[rows, at] = v.astype(BF16)

    saves.start(conv_low, o_conv)
    turn = turn_matrix()
    top, left = quarter_masks()
    for p in range(2):
        g = wog[8 * p : 8 * p + 8, :, D : D + 384].reshape(2 * HS, 2 * HS)
        turned = nn(g, turn).astype(BF16)
        zero = jnp.zeros_like(g)
        tables[2 * p] = jnp.where(left, jnp.where(top, g, zero), jnp.where(top, zero, turned))
        tables[2 * p + 1] = jnp.where(left, jnp.where(top, turned, zero), jnp.where(top, zero, g))
        at = slice(2 * HS * p, 2 * HS * (p + 1))
        rate[:, at] = nn(conv_low[:, at], tables[2 * p])
        inp[:, at] = nn(conv_low[:, at], tables[2 * p + 1])
    saves.start(tables, o_tables)
    saves.start(rate, o_rate)
    saves.start(inp, o_inp)

    @pl.loop(0, 6)
    def _(c):
        at = cols(c)
        keep, starts = masks[0], masks[1]
        _, ig, sd, _, _, scale = gates(
            rate[:, at], inp[:, at], chans[5:6, at], chans[6:7, at], chans[7:8, at], keep, starts
        )
        coeff[:, at] = (1.0 - starts) * (keep * sd + (1.0 - keep))
        drive[:, at] = keep * scale * ig * conv_low[:, at].astype(F32)

    row = lax.broadcasted_iota(jnp.int32, (8, RC), 0)

    def forward(i, carry):
        new = []
        for s in range(2):
            at = pl.ds(pl.multiple_of(s * SEQ + i * 8, 8), 8)
            a, b = coeff[at], drive[at]
            for k in (1, 2, 4):
                later = row >= k
                b = jnp.where(later, a * pltpu.roll(b, k, 0) + b, b)
                a = jnp.where(later, a * pltpu.roll(a, k, 0), a)
            h = a * carry[s] + b
            st[s, pl.ds(pl.multiple_of(8 + i * 8, 8), 8)] = h
            new.append(h[7:8])
        return tuple(new)

    last = lax.fori_loop(0, SEQ // 8, forward, (lru_before[0], lru_before[1]))
    saves.start(st, o_st)
    part[TOK:] = jnp.zeros((8, D), F32)
    part[TOK : TOK + 3, 0:RC] = u[1, PAD - 3 :]
    part[TOK + 3 : TOK + 4, 0:RC] = last[1]
    finals[0:3] = u[0, PAD - 3 :]
    finals[3:4] = last[0]

    @pl.loop(0, 6)
    def _(c):
        at = cols(c)
        act, _ = gelu_both(gate_in[:, at])
        for s in range(2):
            rows = slice(s * SEQ, (s + 1) * SEQ)
            merged[rows, at] = (st[s, 8:, at] * act[rows]).astype(BF16)

    saves.start(merged, o_merged)

    part[0:TOK] = nn(merged[...], wog[:, :, 0:D].reshape(RC, D))

    saves.wait()


def mlp(
    places, tok, cot, part, other, gains, p0, p1, p2, p3, q0, q1, q2, q3,
    normed2, hidden, ggu, o_residual, o_base, o_back,
    win, wdown, residual, down, back, base, sems, out_sems,
):
    for j, (p, q) in enumerate(((p0, q0), (p1, q1), (p2, q2), (p3, q3))):
        p_copy(p, places, j, FC, PI, win, 0, sems.at[0])
        q_copy(q, places, j, 0, LATE, win, PI, sems.at[0])
    for j, p in enumerate((p0, p1, p2, p3)):
        down_copy(p, places, j, wdown, sems.at[1])
    saves = Saves(out_sems)
    for s in range(2):
        rows, theirs = slice(s * SEQ, (s + 1) * SEQ), slice((1 - s) * SEQ, (2 - s) * SEQ)
        v = tok[rows].astype(F32) + (part[rows] + other[theirs])
        residual[rows] = v
        normed2[rows] = (v * inv_rms(v) * gains[1:2]).astype(BF16)
    saves.start(residual, o_residual)
    down[...] = jnp.zeros_like(down)
    back[...] = jnp.zeros_like(back)
    landed(win, sems.at[0])
    landed(wdown, sems.at[1])

    @pl.loop(0, 3)
    def _(c):
        at = pl.ds(pl.multiple_of(c * 512, 512), 512)
        up = pl.ds(pl.multiple_of(FC + c * 512, 512), 512)
        wa, wu = win[:, at], win[:, up]
        a = nn(normed2[...], wa)
        b = nn(normed2[...], wu)
        ga, da = gelu_both(a)
        h = (ga * b).astype(BF16)
        hidden[:, at] = h
        wd = wdown[at]
        gh = nt(cot[...], wd)
        gg_a = (gh * b * da).astype(BF16)
        gg_b = (gh * ga).astype(BF16)
        ggu[:, at] = gg_a
        ggu[:, up] = gg_b
        down[...] += nn(h, wd)
        back[...] += nt(gg_a, wa) + nt(gg_b, wu)

    saves.start(back, o_back.at[pl.ds(0, TOK)])
    saves.start(down.at[pl.ds(SEQ, SEQ)], o_back.at[pl.ds(TOK, SEQ)])
    base[...] = residual[0:SEQ] + down[0:SEQ]
    saves.start(base, o_base)
    saves.wait()


def emit(saves, block, places, axis, outs):
    for j, out in enumerate(outs):
        saves.start(block.at[places[axis, (0, 2, 3, 1)[j]]], out)


RINGS = [(x, z) for x in range(4) for z in range(4)]


def mlp_grads(
    places, cot, normed2, hidden, ggu, p0, p1, p2, p3, q0, q1, q2, q3,
    bp, bq, out_sems,
):
    saves = Saves(out_sems)

    @pl.loop(0, 2)
    def _(xh):
        at = pl.ds(pl.multiple_of(xh * 768, 256), 768)
        v = tn(hidden[:, at], cot[...]).astype(BF16)
        for z in range(4):
            for xl in range(2):
                r = 96 * (2 * z + xl)
                bp[2 * xh + xl, z, :, 0:D] = v[r : r + 64]
                bp[2 * xh + xl, z, 0:32, D:FC] = v[r + 64 : r + 96, 0:512]
                bp[2 * xh + xl, z, 32:64, D:FC] = v[r + 64 : r + 96, 512:1024]

    def put(block, order, first, to):
        v = tn(normed2[...], ggu[:, first : first + 768]).astype(BF16)
        for x, z in RINGS:
            for half in range(2):
                r = ring_rows(x, z) + 256 * half
                at = (x, z) if order else (z, x)
                block[(*at, slice(32 * half, 32 * half + 32), slice(to, to + 768))] = v[r : r + 32]

    put(bp, True, 0, FC)
    emit(saves, bp, places, 0, (p0, p1, p2, p3))
    for part in range(3):
        put(bq, False, 768 * (part + 1), 768 * part)
    emit(saves, bq, places, 2, (q0, q1, q2, q3))
    saves.wait()


def rec_backward(
    places, tok, cot, masks, gains, chans, i_back, i_other, i_residual, i_normed, i_merged, i_u, i_gate, i_conv, i_rate,
    i_inp, i_st, i_tables, wp0, wp1, wp2, wp3, wq0, wq1, wq2, wq3,
    o_residual, o_mine, o_theirs, p0, p1, p2, p3, q0, q1, q2, q3,
    wb, wog, part, other, residual, normed, merged, u_in, gate_in, conv_low, rate, inp, st_in, tables,
    coeff, grad_branch, gs, lam, rate_low, inp_low, direct, gmix, rolled, sums, mixed_part, own_residual, bp, bq,
    sems, in_sems, out_sems,
):
    ins = Saves(in_sems)
    for source, target in (
        (i_back.at[pl.ds(0, TOK)], part), (i_other.at[pl.ds(0, TOK)], other), (i_residual, residual), (i_merged, merged), (i_gate, gate_in), (i_st, st_in),
        (i_rate, rate), (i_inp, inp), (i_conv, conv_low), (i_tables, tables), (i_u, u_in), (i_normed, normed),
    ):
        ins.start(source, target)
    for j, p in enumerate((wp0, wp1, wp2, wp3)):
        og_copy(p, places, j, wog, sems.at[1])
    for j, (p, q) in enumerate(((wp0, wq0), (wp1, wq1), (wp2, wq2), (wp3, wq3))):
        p_copy(p, places, j, OG, PB, wb, 0, sems.at[0])
        q_copy(q, places, j, 0, QB, wb, PB, sems.at[0])
    saves = Saves(out_sems)
    sums[...] = jnp.zeros_like(sums)
    for copy in ins.copies[0:3]:
        copy.wait()
    for s in range(2):
        rows, theirs = slice(s * SEQ, (s + 1) * SEQ), slice((1 - s) * SEQ, (2 - s) * SEQ)
        grad, term = rms_back(part[rows] + other[theirs], residual[rows], gains[1:2])
        grad = cot[rows].astype(F32) + grad
        grad_branch[rows] = grad.astype(BF16)
        if s == 0:
            own_residual[...] = grad
            sums[9:10] = jnp.sum(term, axis=0, keepdims=True)
    saves.start(own_residual, o_residual)

    def put_og(b, first, v):
        x, z = (b // 8) * 2 + b % 2, (b // 2) % 4
        n = min(max(OG - first, 0), v.shape[1])
        if n:
            bp[x, z, 0:48, first : first + n] = v[:, :n]
        if n < v.shape[1]:
            to = first + n - OG
            for r in range(3):
                bp[x, z, 48:64, 384 * r + to : 384 * r + to + v.shape[1] - n] = v[16 * r : 16 * r + 16, n:]

    ins.copies[3].wait()
    v = tn(merged[...], grad_branch[...]).astype(BF16)
    for b in range(16):
        put_og(b, 0, v[48 * b : 48 * b + 48])
    landed(wog, sems.at[1])
    gs[...] = nt(grad_branch[...], wog[:, :, 0:D].reshape(RC, D))
    for copy in ins.copies[4:6]:
        copy.wait()

    @pl.loop(0, 6)
    def _(c):
        at = cols(c)
        act, act_grad = gelu_both(gate_in[:, at])
        g = gs[:, at]
        for s in range(2):
            rows = slice(s * SEQ, (s + 1) * SEQ)
            gmix[rows, pl.ds(pl.multiple_of(RC + c * LANES, LANES), LANES)] = (
                g[rows] * st_in[s, 8:, at] * act_grad[rows]
            ).astype(BF16)
        gs[:, at] = g * act

    for copy in ins.copies[6:9]:
        copy.wait()

    @pl.loop(0, 6)
    def _(c):
        at = cols(c)
        keep, starts = masks[0], masks[1]
        rg = jax.nn.sigmoid(rate[:, at] + chans[5:6, at])
        sd = jnp.exp(-8.0 * rg * chans[7:8, at])
        coeff[:, at] = (1.0 - starts) * (keep * sd + (1.0 - keep))

    row = lax.broadcasted_iota(jnp.int32, (8, RC), 0)

    def backward(n, carry):
        i = SEQ // 8 - 1 - n
        new = []
        for s in range(2):
            at = pl.ds(pl.multiple_of(s * SEQ + i * 8, 8), 8)
            own = coeff[at]
            later_a, later_lam = carry[s]
            a = jnp.where(row == 7, later_a, pltpu.roll(own, 7, 0))
            b = gs[at]
            for k in (1, 2, 4):
                here = row < 8 - k
                b = jnp.where(here, b + a * pltpu.roll(b, 8 - k, 0), b)
                a = jnp.where(here, a * pltpu.roll(a, 8 - k, 0), a)
            h = b + a * later_lam
            lam[at] = h
            new.append((own[0:1], h[0:1]))
        return tuple(new)

    zero = jnp.zeros((1, RC), F32)
    lax.fori_loop(0, SEQ // 8, backward, ((zero, zero), (zero, zero)))

    @pl.loop(0, 6)
    def _(c):
        at = cols(c)
        decay = chans[7:8, at]
        for s in range(2):
            rows = slice(s * SEQ, (s + 1) * SEQ)
            keep, starts = masks[0, rows], masks[1, rows]
            rg, ig, sd, q, root, scale = gates(
                rate[rows, at], inp[rows, at], chans[5:6, at], chans[6:7, at], decay, keep, starts
            )
            conv = conv_low[rows, at].astype(F32)
            l = lam[rows, at]
            common = l * keep
            grad_coeff = l * st_in[s, 7 : PAD - 1, at]
            direct[rows, at] = common * scale * ig
            d_ig = common * scale * conv
            d_scale = common * ig * conv
            d_sd = (1.0 - starts) * (grad_coeff * keep - d_scale * jnp.where(q > 0.001, sd / root, 0.0))
            d_log = d_sd * sd * -8.0
            d_rate = d_log * decay * rg * (1.0 - rg)
            d_inp = d_ig * ig * (1.0 - ig)
            rate_low[rows, at] = d_rate.astype(BF16)
            inp_low[rows, at] = d_inp.astype(BF16)
            for n, term in ((5, d_rate), (6, d_inp), (7, d_log * rg)):
                sums[n : n + 1, at] += jnp.sum(term, axis=0, keepdims=True)

    for copy in ins.copies[9:]:
        copy.wait()
    turn = turn_matrix()
    top, left = quarter_masks()
    for p in range(2):
        at = slice(2 * HS * p, 2 * HS * (p + 1))
        direct[:, at] += nt(rate_low[:, at], tables[2 * p]) + nt(inp_low[:, at], tables[2 * p + 1])
        dr = tn(conv_low[:, at], rate_low[:, at]).astype(BF16)
        di = tn(conv_low[:, at], inp_low[:, at]).astype(BF16)
        none = jnp.zeros_like(dr)
        straight = jnp.where(top, jnp.where(left, dr, none), jnp.where(left, none, di))
        crossed = jnp.where(top, jnp.where(left, di, none), jnp.where(left, none, dr))
        g = (straight.astype(F32) + nn(crossed, turn)).astype(BF16)
        for b in range(8):
            put_og(8 * p + b, D, g[48 * b : 48 * b + 48])

    rolled[:, SEQ:] = jnp.zeros((2, 8, LANES), F32)

    @pl.loop(0, 6)
    def _(c):
        at = cols(c)
        for s in range(2):
            rows = slice(s * SEQ, (s + 1) * SEQ)
            g = direct[rows, at]
            gu = chans[0:1, at] * g
            sums[4:5, at] += jnp.sum(g, axis=0, keepdims=True)
            sums[0:1, at] += jnp.sum(g * u_in[s, 8:, at], axis=0, keepdims=True)
            for k in range(1, 4):
                w = g * masks[1 + k, rows]
                sums[k : k + 1, at] += jnp.sum(w * u_in[s, 8 - k : PAD - k, at], axis=0, keepdims=True)
                rolled[s, 0:SEQ] = w
                gu = gu + chans[k : k + 1, at] * rolled[s, k : SEQ + k]
            gmix[rows, at] = (gu * masks[0, rows]).astype(BF16)

    v = jnp.concatenate([sums[0:8, 0:RC], jnp.zeros((LANES - 8, RC), F32)], axis=0).T.astype(BF16)
    for b in range(16):
        put_og(b, 1408, v[48 * b : 48 * b + 48])
    landed(wb, sems.at[0])

    v = tn(normed[...], gmix[:, 0:PB]).astype(BF16)
    for x, z in RINGS:
        for half in range(2):
            r = ring_rows(x, z) + 256 * half
            bp[x, z, 32 * half : 32 * half + 32, OG:EARLY] = v[r : r + 32]
    emit(saves, bp, places, 0, (p0, p1, p2, p3))
    mixed_part[...] = nt(gmix[...], wb[...])
    saves.start(mixed_part.at[pl.ds(0, SEQ)], o_mine)
    saves.start(mixed_part.at[pl.ds(SEQ, SEQ)], o_theirs)
    t = tok[...].astype(F32)
    sums[8:9] = jnp.sum(mixed_part[...] * (t * inv_rms(t)), axis=0, keepdims=True)
    v = jnp.concatenate([sums[8:16], jnp.zeros((LANES - 8, D), F32)], axis=0).T.astype(BF16)
    for x, z in RINGS:
        for half in range(2):
            r = ring_rows(x, z) + 256 * half
            bq[z, x, 32 * half : 32 * half + 32, QB:EARLY] = v[r : r + 32]

    v = tn(normed[...], gmix[:, PB:]).astype(BF16)
    for x, z in RINGS:
        for half in range(2):
            r = ring_rows(x, z) + 256 * half
            bq[z, x, 32 * half : 32 * half + 32, 0:QB] = v[r : r + 32]
    emit(saves, bq, places, 2, (q0, q1, q2, q3))
    saves.wait()


def load(sources, targets, sems):
    copies = Saves(sems)
    for source, target in zip(sources, targets):
        copies.start(source, target)
    copies.wait()


def join_sums(
    places, eo_p, eu_p, lo_p, lu_p, eo_q, eu_q, lo_q, lu_q,
    tp0, tp1, tp2, tp3, tq0, tq1, tq2, tq3,
    early, late, out, in_sems, out_sems,
):
    loads, saves = Saves(in_sems), Saves(out_sems)
    for n, (a, b, c, d) in enumerate(((eo_p, eu_p, lo_p, lu_p), (eo_q, eu_q, lo_q, lu_q))):
        for source, target in ((a, early.at[n, 0]), (b, early.at[n, 1]), (c, late.at[n, 0]), (d, late.at[n, 1])):
            loads.start(source, target)
    for n, (axis, outs) in enumerate(((2, (tp0, tp1, tp2, tp3)), (0, (tq0, tq1, tq2, tq3)))):
        for copy in loads.copies[4 * n : 4 * n + 4]:
            copy.wait()
        for j, target in enumerate(outs):
            at, to = places[axis, (0, 2, 3, 1)[j]], 4 * n + j
            out[to, :, 0:EARLY] = add(early[n, 0, at], early[n, 1, at])
            out[to, :, EARLY:] = add(late[n, 0, at], late[n, 1, at])
            saves.start(out.at[to], target)
    saves.wait()


def add(a, b):
    return (a.astype(F32) + b.astype(F32)).astype(BF16)


def half_sums(a_p, b_p, c_p, d_p, a_q, b_q, c_q, d_q, *rest):
    outs, (early, late, in_sems, out_sems) = rest[-8:-4], rest[-4:]
    loads, saves = Saves(in_sems), Saves(out_sems)
    for n, (a, b, c, d) in enumerate(((a_p, b_p, c_p, d_p), (a_q, b_q, c_q, d_q))):
        for source, target in ((a, early.at[n, 0]), (b, early.at[n, 1]), (c, late.at[n, 0]), (d, late.at[n, 1])):
            loads.start(source, target)
    for n in range(2):
        for i, v in enumerate((early, late)):
            loads.copies[4 * n + 2 * i].wait()
            loads.copies[4 * n + 2 * i + 1].wait()
            v[n, 0] = add(v[n, 0], v[n, 1])
            saves.start(v.at[n, 0], outs[2 * n + i])
    saves.wait()


def pass_on(a_p, f_p, a_q, f_q, *rest):
    o_p, o_q, v, in_sems, out_sems = rest[-5:]
    loads, saves = Saves(in_sems), Saves(out_sems)
    for i, source in enumerate((a_p, f_p, a_q, f_q)):
        loads.start(source, v.at[i])
    for n, out in enumerate((o_p, o_q)):
        loads.copies[2 * n].wait()
        loads.copies[2 * n + 1].wait()
        v[2 * n] = (v[2 * n].astype(F32) + v[2 * n + 1].astype(F32)).astype(BF16)
        saves.start(v.at[2 * n], out)
    saves.wait()


def cut(
    places, p0, p1, p2, q0, q1, q2,
    o0, o1, o2, o3,
    parts, sp, sq, sd, in_sems,
):
    load((p0, p1, p2, q0, q1, q2), [parts.at[i] for i in range(6)], in_sems)
    for n, out in enumerate((sp, sq)):
        out[...] = parts[3 * n].astype(F32) + parts[3 * n + 1].astype(F32) + parts[3 * n + 2].astype(F32)
    sd[0:64] = sp[:, EARLY : EARLY + D]
    sd[64:96, 0:512] = sp[0:32, EARLY + D : EARLY + FC]
    sd[64:96, 512:1024] = sp[32:64, EARLY + D : EARLY + FC]
    tail = jnp.concatenate([sp[48:64, 384 * r : 384 * r + 384] for r in range(3)], axis=0)
    og = jnp.concatenate([sp[0:48, 0:OG], tail], axis=1).astype(BF16)
    i = lax.broadcasted_iota(jnp.int32, (16, 48), 0)
    s = lax.broadcasted_iota(jnp.int32, (16, 48), 1)

    def two(rows):
        return jnp.concatenate(rows, axis=0).astype(BF16)

    for j, out in enumerate((o0, o1, o2, o3)):
        y = places[1, (0, 2, 3, 1)[j]]
        rows = [pl.ds(pl.multiple_of(32 * c + y * 8, 8), 8) for c in range(2)]
        out[:, 0:PB] = two([sp[r, OG:EARLY] for r in rows])
        out[:, PB : PB + PI] = two([sp[r, UNIT - PI :] for r in rows])
        out[:, PB + PI : DC] = two([sq[r] for r in rows])
        mine = jnp.where((s == i + y * 12) & (i < 12), 1.0, 0.0).astype(BF16)
        out[:, DC:DOWN] = nn(mine, og).astype(BF16)
        down = sd[pl.ds(pl.multiple_of(y * 24, 8), 24)]
        out[:, DOWN : DOWN + D] = down[0:16].astype(BF16)
        out[:, DOWN + D :] = two([down[16:24, 0:512], down[16:24, 512:]])


def finish(places, o0, o1, o2, o3, mine, theirs, out_grad, gate_grad, chan_grad, down_grad, v):
    v[...] = o0[...].astype(F32) + o1[...].astype(F32) + o2[...].astype(F32) + o3[...].astype(F32)
    core = places[3, 0]
    theirs[...] = v[pl.ds(pl.multiple_of((1 - core) * 8, 8), 8), 0:DC]
    mine[...] = v[pl.ds(pl.multiple_of(core * 8, 8), 8), 0:DC]
    out_grad[...] = v[0:12, DC : DC + D]
    gate_grad[...] = v[0:12, DC + D : DC + D + 384]
    chan_grad[...] = v[:, DC + D + 384 : DOWN].T[0:8]
    down_grad[0:16] = v[:, DOWN : DOWN + D]
    down_grad[16:24, 0:512] = v[0:8, DOWN + D :]
    down_grad[16:24, 512:] = v[8:16, DOWN + D :]


def unpack(places, mine, theirs, branch, inner, gains):
    def halves(ins):
        for c, v in enumerate(ins):
            for q in range(4):
                to = 768 * q + 384 * c
                if q == 0:
                    branch[:, to : to + PB] = v[:, 0:PB]
                    branch[:, to + PB : to + 384] = v[:, PB + PI : PB + PI + 128]
                else:
                    branch[:, to : to + 384] = v[:, PI + 384 * q : PI + 384 * q + 384]
                at = PB if q == 0 else DC - LATE + 768 * (q - 1)
                to = 1536 * q + 768 * c
                inner[:, to : to + 768] = v[:, at : at + 768]

    gains[...] = mine[:, DC - LATE - LANES : DC - LATE] + theirs[:, DC - LATE - LANES : DC - LATE]

    @pl.when(places[3, 0] == 0)
    def _():
        halves((mine, theirs))

    @pl.when(places[3, 0] == 1)
    def _():
        halves((theirs, mine))


VM, HB, SM = pltpu.VMEM, pltpu.HBM, pltpu.SMEM


def kernel(body, ins, spaces, outs, scratch, mib, flops=0):
    moved = sum(v.size * v.dtype.itemsize for v in ins)
    ins = [pltpu.with_memory_space_constraint(v, HB) if s is HB else v for v, s in zip(ins, spaces)]
    return pl.pallas_call(
        body,
        out_shape=[HB(s, d) if at is HB else jax.ShapeDtypeStruct(s, d) for s, d, at in outs],
        in_specs=[pl.BlockSpec(memory_space=s) for s in spaces],
        out_specs=[pl.BlockSpec(memory_space=s) for _, _, s in outs],
        scratch_shapes=scratch,
        compiler_params=pltpu.CompilerParams(vmem_limit_bytes=mib * 2**20),
        cost_estimate=pl.CostEstimate(flops=flops, bytes_accessed=moved, transcendentals=0),
    )(*ins)


def shards(
    tokens, cotangent, segment, keep_mask, conv_state, lru_state, norm1_gain, conv_weight, lru_bias, decay_rate,
    gate_weight, branch_weight, out_weight, norm2_gain, mlp_in_weight, mlp_out_weight,
):
    here = my_place()
    core = here["core"]
    zero = jnp.zeros_like(core)
    places = jnp.stack(
        [jnp.stack(ring_places(axis, here)) for axis in "xyz"] + [jnp.stack([core, zero, zero, zero])]
    ).astype(jnp.int32)
    vmem, dma = pltpu.VMEM, pltpu.SemaphoreType.DMA

    tc = jnp.concatenate([tokens[0], cotangent[0]], axis=0)
    tc_other = swap(tc)
    marks = jnp.concatenate([segment, keep_mask], axis=1).astype(F32)
    states = jnp.concatenate([conv_state[0], lru_state], axis=0)
    sent = jnp.concatenate([core_half(states, 1 - core, 2), jnp.pad(marks, ((0, 0), (0, RC - 2 * SEQ)))], axis=0)
    sent = swap(sent)

    mine, theirs, own = kernel(
        pack,
        (places, branch_weight, mlp_in_weight, jnp.stack([norm1_gain, norm2_gain]), out_weight, gate_weight,
         jnp.concatenate([conv_weight, lru_bias, decay_rate[None]], axis=0), mlp_out_weight),
        [SM] + [VM] * 7,
        [((8, DC), BF16, VM)] * 2 + [((16, OWN - DC), BF16, VM)],
        [],
        8,
    )
    (block,) = kernel(join, (places, mine, swap(theirs), own), [SM] + [VM] * 3, [((16, OWN), BF16, VM)], [], 8)

    row = ((64, UNIT), BF16)
    p, q = kernel(
        unit,
        (places, *ring_direct(block, "y"), tc_other, sent),
        [SM] + [VM] * 4 + [HB] * 2,
        [(*row, HB)] * 2,
        [vmem(*row), vmem(*row), vmem((64, DC), F32), vmem((96, D), F32), dma((2,))],
        16,
    )
    early, late = (4, 64, EARLY), (4, 64, LATE)
    stack = ((4, 64, UNIT), BF16)
    pe, qe, pl_, ql = kernel(
        planes,
        (places, *ring_direct(p, "z"), *ring_direct(q, "x")),
        [SM] + [HB] * 8,
        [(early, BF16, HB)] * 2 + [(late, BF16, HB)] * 2,
        [vmem(*stack), vmem(*stack), dma((8,)), dma((4,))],
        8,
    )
    pe, qe, pl_, ql = ring(pe, "x"), ring(qe, "z"), ring(pl_, "x"), ring(ql, "z")

    tok = jnp.concatenate([tc[:SEQ], tc_other[:SEQ]], axis=0)
    cot = jnp.concatenate([tc[SEQ:], tc_other[SEQ:]], axis=0)
    states = jnp.stack([core_half(states, core, 2), sent[:4]])
    marks = jnp.concatenate([marks, sent[4:, : 2 * SEQ]], axis=0)
    seg, keep = marks[:, :SEQ], marks[:, SEQ:]
    earlier = [jnp.concatenate([jnp.repeat(seg[:, :1], k, axis=1), seg[:, : SEQ - k]], axis=1) for k in range(1, 4)]
    masks = jnp.stack([keep, (earlier[0] != seg).astype(F32)] + [(e == seg).astype(F32) for e in earlier])
    masks = jnp.broadcast_to(masks.reshape(5, TOK, 1), (5, TOK, LANES))

    wide, wide_low = ((TOK, D), F32), ((TOK, D), BF16)
    act, act_low, padded = ((TOK, RC), F32), ((TOK, RC), BF16), ((2, PAD, RC), F32)
    tables = ((4, 2 * HS, 2 * HS), BF16)
    saved = [wide_low, act_low, padded, act, act_low, act, act, padded, tables]
    part, finals, gains, chans, normed, merged, u, gate_in, conv_low, rate, inp, st, table = kernel(
        rec_forward,
        (places, tok, masks, states[:, :3], states[:, 3:], *pe, *qe),
        [SM] + [VM] * 4 + [HB] * 8,
        [((TOK + 8, D), F32, VM), ((4, RC), F32, VM), ((8, D), F32, VM), ((8, RC), F32, VM)]
        + [(*v, HB) for v in saved],
        [vmem((D, PB + EARLY), BF16), vmem((16, 48, 1536), BF16)]
        + [vmem(*v) for v in saved + [act, act]]
        + [dma((2,)), dma((9,))],
        32,
        2 * TOK * (D * BRANCH + RC * (D + 768)),
    )
    half = ((SEQ, D), F32)
    other = swap(part)
    normed2, hidden, ggu, residual, base, back = kernel(
        mlp,
        (places, tok, cot, part, other, gains, *pl_, *ql),
        [SM] + [VM] * 5 + [HB] * 8,
        [(*wide_low, VM), ((TOK, FC), BF16, VM), ((TOK, INNER), BF16, VM)] + [(*v, HB) for v in (wide, half, ((TOK + SEQ, D), F32))],
        [vmem((D, INNER), BF16), vmem((FC, D), BF16)]
        + [vmem(*v) for v in (wide, wide, wide, half)]
        + [dma((2,)), dma((4,))],
        32,
        2 * TOK * D * (2 * INNER + 2 * FC),
    )
    back_other = swap(back)
    outs = kernel(
        mlp_grads,
        (places, cot, normed2, hidden, ggu),
        [SM] + [VM] * 4,
        [(late, BF16, HB)] * 8,
        [vmem((4,) + late, BF16), vmem((4,) + late, BF16), dma((8,))],
        32,
        2 * TOK * D * (INNER + FC),
    )
    lp, lq = outs[:4], outs[4:]
    far = send(lp[2], along("x", 1)), send(lq[2], along("z", 1))
    down = send(lp[3], along("x", -1)), send(lq[3], along("z", -1))
    outs = kernel(
        rec_backward,
        (places, tok, cot, masks, gains, chans, back, back_other, residual, normed, merged, u, gate_in, conv_low, rate,
         inp, st, table, *pe, *qe),
        [SM] + [VM] * 5 + [HB] * 20,
        [(*v, HB) for v in (half, half, half)] + [(early, BF16, HB)] * 8,
        [vmem((D, BRANCH), BF16), vmem((16, 48, 1536), BF16)]
        + [vmem(*v) for v in (wide, wide, wide, wide_low, act_low, padded, act, act_low, act, act, padded, tables)]
        + [vmem(*v) for v in (act, wide_low, act, act, act_low, act_low, act, ((TOK, BRANCH), BF16))]
        + [vmem((2, PAD, LANES), F32), vmem((16, D), F32), vmem(*wide), vmem(*half)]
        + [vmem((4,) + early, BF16), vmem((4,) + early, BF16), dma((2,)), dma((12,)), dma((11,))],
        48,
        2 * TOK * D * (2 * BRANCH + 2 * RC),
    )
    grad_residual, mixed_mine, mixed_theirs = outs[:3]
    ep, eq = outs[3:7], outs[7:]
    def passed(terms, far, routes, shape, until, scratch):
        (p, q), (a, b) = terms, routes
        up = kernel(
            pass_on,
            (p[1], far[0], q[1], far[1], *until),
            [HB] * (4 + len(until)),
            [(shape, BF16, HB)] * 2,
            [vmem((4,) + shape, BF16), dma((4,)), dma((2,))],
            scratch,
        )
        return send(up[0], along(a, 1)), send(up[1], along(b, 1))

    early_far = send(ep[2], along("x", 1)), send(eq[2], along("z", 1))
    early_down = send(ep[3], along("x", -1)), send(eq[3], along("z", -1))
    late_up = passed((lp, lq), far, "xz", late, (ep[0], *down), 16)
    early_up = passed((ep, eq), early_far, "xz", early, early_down, 16)

    summed = kernel(
        half_sums,
        (ep[0], early_down[0], lp[0], down[0], eq[0], early_down[1], lq[0], down[1]),
        [HB] * 8,
        [(early, BF16, HB), (late, BF16, HB)] * 2,
        [vmem((2, 2) + early, BF16), vmem((2, 2) + late, BF16), dma((8,)), dma((4,))],
        24,
    )
    outs = kernel(
        join_sums,
        (places, summed[0], early_up[0], summed[1], late_up[0], summed[2], early_up[1], summed[3], late_up[1]),
        [SM] + [HB] * 8,
        [(*row, HB)] * 8,
        [vmem((2, 2) + early, BF16), vmem((2, 2) + late, BF16), vmem((8, 64, UNIT), BF16), dma((8,)), dma((8,))],
        32,
    )
    tp, tq = outs[:4], outs[4:]
    far = send(tp[2], along("z", 1)), send(tq[2], along("x", 1))
    down = send(tp[3], along("z", -1)), send(tq[3], along("x", -1))
    up = kernel(
        pass_on,
        (tp[1], far[0], tq[1], far[1], *down),
        [HB] * 6,
        [(*row, HB)] * 2,
        [vmem((4, 64, UNIT), BF16), dma((4,)), dma((2,))],
        8,
    )
    up = send(up[0], along("z", 1)), send(up[1], along("x", 1))
    sums = kernel(
        cut,
        (places, tp[0], down[0], up[0], tq[0], down[1], up[1]),
        [SM] + [HB] * 6,
        [((16, OWN), BF16, VM)] * 4,
        [vmem((6, 64, UNIT), BF16), vmem((64, UNIT), F32), vmem((64, UNIT), F32), vmem((96, D), F32), dma((6,))],
        16,
    )
    mine, theirs, out_grad, gate_grad, chan_grad, down_grad = kernel(
        finish,
        (places, *terms_direct(sums, "y")),
        [SM] + [VM] * 4,
        [((8, DC), F32, VM)] * 2 + [(s, F32, VM) for s in ((12, D), (12, 384), (8, 16), (24, D))],
        [vmem((16, OWN), F32)],
        8,
    )
    branch_grad, in_grad, gain_grads = kernel(
        unpack,
        (places, mine, swap(theirs)),
        [SM] + [VM] * 2,
        [((8, 2 * R), F32, VM), ((8, 2 * F), F32, VM), ((8, LANES), F32, VM)],
        [],
        8,
    )

    output = (base + back_other[TOK:]).astype(BF16)
    grad, _ = rms_back(mixed_mine + swap(mixed_theirs), tok[:SEQ].astype(F32), gains[0])
    input_grad = (grad_residual + grad).astype(BF16)
    theirs = other[TOK : TOK + 4, :RC]
    finals = jnp.stack(
        [v.reshape(1, 4, 2, 384) for v in (jnp.where(core == 0, finals, theirs), jnp.where(core == 0, theirs, finals))],
        axis=3,
    ).reshape(1, 4, R)
    return (
        output[None],
        input_grad[None],
        finals[:, :3],
        finals[:, 3],
        gain_grads[:, 0],
        chan_grad[:4, :12],
        chan_grad[4:7, :12],
        chan_grad[7, :12],
        gate_grad,
        branch_grad,
        out_grad,
        gain_grads[:, 1],
        in_grad,
        down_grad,
    )


def solution(mesh):
    rows, last = P(AXES), P(None, AXES)
    specs = [rows] * 6 + [rows, last, last] + [rows] * 7
    outs = [rows] * 4 + [rows, last, last] + [rows] * 7
    return jax.shard_map(
        shards, mesh=mesh, in_specs=tuple(specs), out_specs=tuple(outs), check_vma=False
    )
```

```python
import jax
import jax.numpy as jnp
from jax import lax
from jax.experimental import pallas as pl
from jax.experimental.pallas import tpu as pltpu
from jax.sharding import PartitionSpec as P

AXES = ("dp", "fsdp")
D, R, F, SEQ = 1024, 1536, 3072, 128
RC, FC = R // 2, F // 2
HS = 192
F32, BF16 = jnp.float32, jnp.bfloat16
BRANCH, INNER = 2 * RC, 2 * FC
TOK, PAD, LANES = 2 * SEQ, SEQ + 8, 128

EARLY, LATE = 1408, 2304
UNIT = EARLY + LATE
OG, PB, PI, QB = 1152, 256, 768, 1280
DC = PB + PI + UNIT
OGC = 1536
DOWN = DC + OGC
OWN = DOWN + D + D // 2


def place_of(device):
    outer, inner = divmod(device, 32)
    x_hi, core = divmod(outer, 2)
    z, rest = divmod(inner, 8)
    x_lo, y = divmod(rest, 4)
    return dict(x=x_hi * 2 + x_lo, y=y, z=z, core=core)


def device_at(x, y, z, core):
    return ((x // 2) * 2 + core) * 32 + z * 8 + (x % 2) * 4 + y


def pairs(move):
    return [(d, device_at(**move(place_of(d)))) for d in range(128)]


def along(axis, steps):
    def move(p):
        sign = 1 if p["core"] == 0 else -1
        return {**p, axis: (p[axis] + sign * steps) % 4}

    return pairs(move)


def other_core(p):
    return {**p, "core": 1 - p["core"]}


def opposite(axis):
    return pairs(lambda p: {**p, axis: (p[axis] + 2) % 4})


def send(value, route):
    return lax.ppermute(value, AXES, route)


def swap(value):
    return send(value, pairs(other_core))


def my_place():
    device = lax.axis_index(AXES)
    outer, inner = device // 32, device % 32
    return dict(x=(outer // 2) * 2 + (inner // 4) % 2, y=inner % 4, z=inner // 8, core=outer % 2)


def ring_places(axis, here):
    sign, at = 1 - 2 * here["core"], here[axis]
    return [at, (at - sign) % 4, (at + sign) % 4, (at + 2) % 4]


def ring(block, axis):
    one = send(block, along(axis, 1))
    two = send(one, along(axis, 1))
    return block, one, send(two, along(axis, 1)), two


def ring_direct(block, axis):
    return block, send(block, along(axis, 1)), send(block, along(axis, -1)), send(block, opposite(axis))


def terms_direct(terms, axis):
    own, ahead, far, behind = terms
    return own, send(ahead, along(axis, 1)), send(far, opposite(axis)), send(behind, along(axis, -1))


def total(*terms):
    out = terms[0].astype(F32)
    for term in terms[1:]:
        out = out + term.astype(F32)
    return out.astype(BF16)


def core_half(array, core, blocks):
    v = array.reshape(array.shape[:-1] + (blocks, 2, array.shape[-1] // (2 * blocks)))
    v = lax.dynamic_index_in_dim(v, core, v.ndim - 2, keepdims=False)
    return v.reshape(array.shape[:-1] + (array.shape[-1] // 2,))


def dot(a, b, dims):
    return lax.dot_general(a, b, (dims, ((), ())), preferred_element_type=F32)


def nn(a, b):
    return dot(a, b, ((1,), (0,)))


def nt(a, b):
    return dot(a, b, ((1,), (1,)))


def tn(a, b):
    return dot(a, b, ((0,), (0,)))


def inv_rms(v):
    return lax.rsqrt(jnp.mean(v * v, axis=-1, keepdims=True) + 1e-6)


def rms_back(grad, v, gain):
    s = inv_rms(v)
    n = v * s
    g2 = grad * gain
    return s * (g2 - n * jnp.mean(g2 * n, axis=-1, keepdims=True)), grad * n


C0, C1 = 0.7978845608028654, 0.044715


def gelu_both(a):
    t = jnp.tanh(C0 * (a + C1 * (a * a * a)))
    half = 0.5 * (1.0 + t)
    return a * half, half + 0.5 * a * (1.0 - t * t) * (C0 * (1.0 + 3.0 * C1 * (a * a)))


def gates(rate, inp, bias1, bias2, decay, keep, starts):
    rg = jax.nn.sigmoid(rate + bias1)
    ig = jax.nn.sigmoid(inp + bias2)
    sd = jnp.exp(-8.0 * rg * decay)
    q = 1.0 - sd * sd
    root = jnp.sqrt(jnp.maximum(q, 0.001))
    scale = starts + (1.0 - starts) * root
    return rg, ig, sd, q, root, scale


def cols(c):
    return pl.ds(pl.multiple_of(c * LANES, LANES), LANES)


class Saves:
    def __init__(self, sem):
        self.sem, self.copies = sem, []

    def start(self, source, target):
        self.copies.append(pltpu.make_async_copy(source, target, self.sem.at[len(self.copies)]))
        self.copies[-1].start()

    def wait(self):
        for copy in self.copies:
            copy.wait()


def pick(rows, where):
    return jnp.where(lax.broadcasted_iota(jnp.int32, (rows, where.shape[1]), 0) == where, 1.0, 0.0).astype(BF16)


def stand(values, rows):
    v = values.astype(F32)
    i = lax.broadcasted_iota(jnp.int32, (rows, v.shape[1]), 0)
    j = lax.broadcasted_iota(jnp.int32, (rows, v.shape[1]), 1)
    lane = lax.broadcasted_iota(jnp.int32, (rows, LANES), 1)
    out = jnp.zeros((rows, LANES), F32)
    for n in range(v.shape[0]):
        column = jnp.sum(jnp.where(i == j, v[n : n + 1], 0.0), axis=1, keepdims=True)
        out = out + jnp.where(lane == n, column, 0.0)
    return out


def pack(places, branch, inner, gain, out, gate, perchan, down, mine, theirs, own):
    gains = stand(gain[...], 8).astype(BF16)

    def halves(outs):
        for c, to_core in enumerate(outs):
            for q in range(4):
                v = branch[:, 768 * q + 384 * c : 768 * q + 384 * c + 384]
                if q == 0:
                    to_core[:, 0:PB] = v[:, 0:PB]
                    to_core[:, PB + PI : PB + PI + 128] = v[:, PB:]
                else:
                    to_core[:, PI + 384 * q : PI + 384 * q + 384] = v
                v = inner[:, 1536 * q + 768 * c : 1536 * q + 768 * c + 768]
                to = PB if q == 0 else DC - LATE + 768 * (q - 1)
                to_core[:, to : to + 768] = v
            tile = DC - LATE - LANES
            to_core[:, tile : tile + LANES] = gains

    @pl.when(places[3, 0] == 0)
    def _():
        halves((mine, theirs))

    @pl.when(places[3, 0] == 1)
    def _():
        halves((theirs, mine))

    own[...] = jnp.zeros_like(own)
    own[0:12, 0:D] = out[...]
    own[0:12, D : D + 384] = gate[...]
    own[:, 1408:OGC] = stand(perchan[...], 16).astype(BF16)
    own[:, OGC : OGC + D] = down[0:16]
    own[:, OGC + D :] = jnp.concatenate(
        [down[16:24, 0:512].astype(F32), down[16:24, 512:].astype(F32)], axis=0
    ).astype(BF16)


def join(places, mine, theirs, own, block):
    def rows(low, high):
        block[:, 0:DC] = jnp.concatenate([low[...].astype(F32), high[...].astype(F32)], axis=0).astype(BF16)

    @pl.when(places[3, 0] == 0)
    def _():
        rows(mine, theirs)

    @pl.when(places[3, 0] == 1)
    def _():
        rows(theirs, mine)

    block[:, DC:] = own[...]


def unit(places, p0, p1, p2, p3, *rest):
    o_p, o_q, p, q, d, dn, sems = rest[-7:]
    ogs = []
    s = lax.broadcasted_iota(jnp.int32, (1, 64), 1)
    y = jnp.zeros((1, 64), jnp.int32)
    for j, piece in enumerate((p0, p1, p2, p3)):
        at = places[1, j]
        y = jnp.where(s // 16 == j, at, y)
        v = piece[:, 0:DC].astype(F32)
        for c in range(2):
            d[pl.ds(pl.multiple_of(c * 32 + at * 8, 8), 8)] = v[8 * c : 8 * c + 8]
        ogs.append(piece[:, DC:DOWN])
        v = piece[:, DOWN:].astype(F32)
        dn[pl.ds(pl.multiple_of(at * 24, 8), 16)] = v[:, 0:D]
        for h in range(2):
            dn[pl.ds(pl.multiple_of(at * 24 + 16, 8), 8), 512 * h : 512 * h + 512] = v[8 * h : 8 * h + 8, D:]
    saves = Saves(sems)
    q[...] = d[:, PB + PI :].astype(BF16)
    for c in range(2):
        saves.start(q.at[pl.ds(32 * c, 32)], o_q.at[c])
    p[:, OG:EARLY] = d[:, 0:PB].astype(BF16)
    p[:, UNIT - PI :] = d[:, PB : PB + PI].astype(BF16)
    i = s % 16
    og = nn(pick(48, jnp.where(i < 12, y * 12 + i, 64)), jnp.concatenate(ogs, axis=0)).astype(BF16)
    p[0:48, 0:OG] = og[:, 0:OG]
    for r in range(3):
        p[48:64, 384 * r : 384 * r + 384] = og[16 * r : 16 * r + 16, OG:]
    p[:, EARLY : EARLY + D] = dn[0:64].astype(BF16)
    p[0:32, EARLY + D : EARLY + FC] = dn[64:96, 0:512].astype(BF16)
    p[32:64, EARLY + D : EARLY + FC] = dn[64:96, 512:1024].astype(BF16)
    for c in range(2):
        saves.start(p.at[pl.ds(32 * c, 32)], o_p.at[c])
    saves.wait()


def planes(places, p0, p1, p2, p3, q0, q1, q2, q3, o_pe, o_qe, o_pl, o_ql, p, q, in_sems, out_sems):
    loads, saves = Saves(in_sems), Saves(out_sems)
    for j, piece in enumerate((p0, p1, p2, p3)):
        loads.start(piece, p.at[:, places[2, j]])
    for j, piece in enumerate((q0, q1, q2, q3)):
        x = places[0, j]
        loads.start(piece, q.at[x // 2, :, x % 2])
    for n, (stack, out) in enumerate(((p, o_pe), (q, o_qe))):
        for copy in loads.copies[4 * n : 4 * n + 4]:
            copy.wait()
        saves.start(stack.at[..., pl.ds(0, EARLY)], out)
    for stack, out in ((p, o_pl), (q, o_ql)):
        saves.start(stack.at[..., pl.ds(EARLY, LATE)], out)
    saves.wait()


ROWS = (2, 2, 4, 2, 32)
OG_ROWS, DOWN_ROWS = (2, 4, 2, 48), (2, 4, 2, 96)


def ring_rows(x, z):
    return (x // 2) * 512 + z * 64 + (x % 2) * 32


def p_copy(piece, places, j, first, count, block, to, sem):
    x = places[0, j]
    target = block.at[x // 2, :, :, x % 2, :, pl.ds(to, count)]
    pltpu.make_async_copy(piece.at[..., pl.ds(first, count)], target, sem).start()


def q_copy(piece, places, j, first, count, block, to, sem):
    target = block.at[:, :, places[2, j], :, :, pl.ds(to, count)]
    pltpu.make_async_copy(piece.at[..., pl.ds(first, count)], target, sem).start()


def og_copy(piece, places, j, block, sem):
    x = places[0, j]
    block = block.at[x // 2, :, x % 2]
    for source, target in (
        (piece.at[0, :, :, pl.ds(0, OG)], block.at[:, pl.ds(0, 32), pl.ds(0, OG)]),
        (piece.at[1, :, pl.ds(0, 16), pl.ds(0, OG)], block.at[:, pl.ds(32, 16), pl.ds(0, OG)]),
    ):
        pltpu.make_async_copy(source, target, sem).start()
    for r in range(3):
        pltpu.make_async_copy(
            piece.at[1, :, pl.ds(16, 16), pl.ds(384 * r, 384)], block.at[:, pl.ds(16 * r, 16), pl.ds(OG, 384)], sem
        ).start()


def down_copy(piece, places, j, block, sem):
    x = places[0, j]
    block = block.at[x // 2, :, x % 2]
    for h in range(2):
        pltpu.make_async_copy(piece.at[h, :, :, pl.ds(0, D)], block.at[:, pl.ds(32 * h, 32)], sem).start()
        pltpu.make_async_copy(
            piece.at[h, :, :, pl.ds(D, 512)], block.at[:, pl.ds(64, 32), pl.ds(512 * h, 512)], sem
        ).start()


def rows_of(block, first, count):
    return block[..., first : first + count].reshape(D, count)


def landed(block, sem):
    pltpu.make_async_copy(block, block, sem).wait()


def turn_matrix():
    i = lax.broadcasted_iota(jnp.int32, (2 * HS, 2 * HS), 0)
    j = lax.broadcasted_iota(jnp.int32, (2 * HS, 2 * HS), 1)
    return jnp.where((i == j + HS) | (j == i + HS), 1.0, 0.0).astype(BF16)


def quarter_masks():
    i = lax.broadcasted_iota(jnp.int32, (2 * HS, 2 * HS), 0) < HS
    j = lax.broadcasted_iota(jnp.int32, (2 * HS, 2 * HS), 1) < HS
    return i, j


def rec_forward(
    places, tok, masks, conv_before, lru_before, p0, p1, p2, p3, q0, q1, q2, q3,
    part, finals, gains, chans, o_normed, o_merged, o_u, o_gate, o_conv, o_rate, o_inp, o_st, o_tables,
    wb, wog, normed, merged, u, gate_in, conv_low, rate, inp, st, tables, coeff, drive, sems, out_sems,
):
    for j, (p, q) in enumerate(((p0, q0), (p1, q1), (p2, q2), (p3, q3))):
        p_copy(p, places, j, OG, PB, wb, 0, sems.at[0])
        q_copy(q, places, j, 0, EARLY, wb, PB, sems.at[0])
    for j, p in enumerate((p0, p1, p2, p3)):
        og_copy(p, places, j, wog, sems.at[1])
    saves = Saves(out_sems)
    t = tok[...].astype(F32)
    scaled = t * inv_rms(t)
    landed(wb, sems.at[0])
    gains[...] = rows_of(wb, BRANCH, LANES).astype(F32).T[:8]
    normed[...] = (scaled * gains[0:1]).astype(BF16)
    saves.start(normed, o_normed)
    for s in range(2):
        u[s, 0:8] = jnp.zeros((8, RC), F32)
        u[s, 5:8] = conv_before[s]
        st[s, 0:8] = jnp.zeros((8, RC), F32)
        st[s, 7:8] = lru_before[s]

    v = nn(normed[...], rows_of(wb, 0, RC))
    for s in range(2):
        rows = slice(s * SEQ, (s + 1) * SEQ)
        for c in range(6):
            u[s, 8:, LANES * c : LANES * c + LANES] = v[rows, LANES * c : LANES * c + LANES] * masks[0, rows]

    saves.start(u, o_u)

    gate_in[...] = nn(normed[...], rows_of(wb, RC, RC))

    saves.start(gate_in, o_gate)
    landed(wog, sems.at[1])
    chans[...] = wog[..., 1408:].reshape(RC, LANES).astype(F32).T[:8]

    @pl.loop(0, 6)
    def _(c):
        at = cols(c)
        for s in range(2):
            rows = slice(s * SEQ, (s + 1) * SEQ)
            v = chans[4:5, at] + chans[0:1, at] * u[s, 8:, at]
            for k in range(1, 4):
                v = v + chans[k : k + 1, at] * (u[s, 8 - k : PAD - k, at] * masks[1 + k, rows])
            conv_low[rows, at] = v.astype(BF16)

    saves.start(conv_low, o_conv)
    turn = turn_matrix()
    top, left = quarter_masks()
    for p in range(2):
        g = wog[p, :, :, :, D : D + 384].reshape(2 * HS, 2 * HS)
        turned = nn(g, turn).astype(BF16)
        zero = jnp.zeros_like(g)
        tables[2 * p] = jnp.where(left, jnp.where(top, g, zero), jnp.where(top, zero, turned))
        tables[2 * p + 1] = jnp.where(left, jnp.where(top, turned, zero), jnp.where(top, zero, g))
        at = slice(2 * HS * p, 2 * HS * (p + 1))
        rate[:, at] = nn(conv_low[:, at], tables[2 * p])
        inp[:, at] = nn(conv_low[:, at], tables[2 * p + 1])
    saves.start(tables, o_tables)
    saves.start(rate, o_rate)
    saves.start(inp, o_inp)

    @pl.loop(0, 6)
    def _(c):
        at = cols(c)
        keep, starts = masks[0], masks[1]
        _, ig, sd, _, _, scale = gates(
            rate[:, at], inp[:, at], chans[5:6, at], chans[6:7, at], chans[7:8, at], keep, starts
        )
        coeff[:, at] = (1.0 - starts) * (keep * sd + (1.0 - keep))
        drive[:, at] = keep * scale * ig * conv_low[:, at].astype(F32)

    row = lax.broadcasted_iota(jnp.int32, (8, RC), 0)

    def forward(i, carry):
        new = []
        for s in range(2):
            at = pl.ds(pl.multiple_of(s * SEQ + i * 8, 8), 8)
            a, b = coeff[at], drive[at]
            for k in (1, 2, 4):
                later = row >= k
                b = jnp.where(later, a * pltpu.roll(b, k, 0) + b, b)
                a = jnp.where(later, a * pltpu.roll(a, k, 0), a)
            h = a * carry[s] + b
            st[s, pl.ds(pl.multiple_of(8 + i * 8, 8), 8)] = h
            new.append(h[7:8])
        return tuple(new)

    last = lax.fori_loop(0, SEQ // 8, forward, (lru_before[0], lru_before[1]))
    saves.start(st, o_st)
    part[TOK:] = jnp.zeros((8, D), F32)
    part[TOK : TOK + 3, 0:RC] = u[1, PAD - 3 :]
    part[TOK + 3 : TOK + 4, 0:RC] = last[1]
    finals[0:3] = u[0, PAD - 3 :]
    finals[3:4] = last[0]

    @pl.loop(0, 6)
    def _(c):
        at = cols(c)
        act, _ = gelu_both(gate_in[:, at])
        for s in range(2):
            rows = slice(s * SEQ, (s + 1) * SEQ)
            merged[rows, at] = (st[s, 8:, at] * act[rows]).astype(BF16)

    saves.start(merged, o_merged)

    part[0:TOK] = nn(merged[...], wog[..., 0:D].reshape(RC, D))

    saves.wait()


def mlp(
    places, tok, cot, part, other, gains, p0, p1, p2, p3, q0, q1, q2, q3,
    normed2, hidden, ggu, o_residual, o_base, o_back,
    win, wdown, residual, down, back, base, sems, out_sems,
):
    for j, (p, q) in enumerate(((p0, q0), (p1, q1), (p2, q2), (p3, q3))):
        p_copy(p, places, j, FC, PI, win, 0, sems.at[0])
        q_copy(q, places, j, 0, LATE, win, PI, sems.at[0])
    for j, p in enumerate((p0, p1, p2, p3)):
        down_copy(p, places, j, wdown, sems.at[1])
    saves = Saves(out_sems)
    for s in range(2):
        rows, theirs = slice(s * SEQ, (s + 1) * SEQ), slice((1 - s) * SEQ, (2 - s) * SEQ)
        v = tok[rows].astype(F32) + (part[rows] + other[theirs])
        residual[rows] = v
        normed2[rows] = (v * inv_rms(v) * gains[1:2]).astype(BF16)
    saves.start(residual, o_residual)
    down[...] = jnp.zeros_like(down)
    back[...] = jnp.zeros_like(back)
    landed(win, sems.at[0])
    for c in range(2):
        at, up = slice(768 * c, 768 * c + 768), slice(FC + 768 * c, FC + 768 * c + 768)
        wa, wu = rows_of(win, 768 * c, 768), rows_of(win, FC + 768 * c, 768)
        a = nn(normed2[...], wa)
        b = nn(normed2[...], wu)
        ga, da = gelu_both(a)
        h = (ga * b).astype(BF16)
        hidden[:, at] = h
        if c == 0:
            landed(wdown, sems.at[1])
        wd = wdown[c].reshape(768, D)
        gh = nt(cot[...], wd)
        gg_a = (gh * b * da).astype(BF16)
        gg_b = (gh * ga).astype(BF16)
        ggu[:, at] = gg_a
        ggu[:, up] = gg_b
        down[...] += nn(h, wd)
        back[...] += nt(gg_a, wa) + nt(gg_b, wu)

    saves.start(back, o_back.at[pl.ds(0, TOK)])
    saves.start(down.at[pl.ds(SEQ, SEQ)], o_back.at[pl.ds(TOK, SEQ)])
    base[...] = residual[0:SEQ] + down[0:SEQ]
    saves.start(base, o_base)
    saves.wait()


def emit(saves, block, places, axis, outs):
    for j, out in enumerate(outs):
        saves.start(block.at[places[axis, (0, 2, 3, 1)[j]]], out)


RINGS = [(x, z) for x in range(4) for z in range(4)]


def mlp_grads(
    places, cot, normed2, hidden, ggu, p0, p1, p2, p3, q0, q1, q2, q3,
    bp, bq, out_sems,
):
    saves = Saves(out_sems)

    @pl.loop(0, 2)
    def _(xh):
        at = pl.ds(pl.multiple_of(xh * 768, 256), 768)
        v = tn(hidden[:, at], cot[...]).astype(BF16)
        for z in range(4):
            for xl in range(2):
                r = 96 * (2 * z + xl)
                bp[2 * xh + xl, z, :, 0:D] = v[r : r + 64]
                bp[2 * xh + xl, z, 0:32, D:FC] = v[r + 64 : r + 96, 0:512]
                bp[2 * xh + xl, z, 32:64, D:FC] = v[r + 64 : r + 96, 512:1024]

    def put(block, order, first, to):
        v = tn(normed2[...], ggu[:, first : first + 768]).astype(BF16)
        for x, z in RINGS:
            for half in range(2):
                r = ring_rows(x, z) + 256 * half
                at = (x, z) if order else (z, x)
                block[(*at, slice(32 * half, 32 * half + 32), slice(to, to + 768))] = v[r : r + 32]

    put(bp, True, 0, FC)
    emit(saves, bp, places, 0, (p0, p1, p2, p3))
    for part in range(3):
        put(bq, False, 768 * (part + 1), 768 * part)
    emit(saves, bq, places, 2, (q0, q1, q2, q3))
    saves.wait()


def rec_backward(
    places, tok, cot, masks, gains, chans, other, i_back, i_residual, i_normed, i_merged, i_u, i_gate, i_conv, i_rate,
    i_inp, i_st, i_tables, wp0, wp1, wp2, wp3, wq0, wq1, wq2, wq3,
    o_residual, o_mine, o_theirs, p0, p1, p2, p3, q0, q1, q2, q3,
    wb, wog, part, residual, normed, merged, u_in, gate_in, conv_low, rate, inp, st_in, tables,
    coeff, grad_branch, gs, lam, rate_low, inp_low, direct, gmix, rolled, sums, mixed_part, own_residual, bp, bq,
    sems, in_sems, out_sems,
):
    ins = Saves(in_sems)
    for source, target in (
        (i_back.at[pl.ds(0, TOK)], part), (i_residual, residual), (i_merged, merged), (i_gate, gate_in), (i_st, st_in),
        (i_rate, rate), (i_inp, inp), (i_conv, conv_low), (i_tables, tables), (i_u, u_in), (i_normed, normed),
    ):
        ins.start(source, target)
    for j, p in enumerate((wp0, wp1, wp2, wp3)):
        og_copy(p, places, j, wog, sems.at[1])
    for j, (p, q) in enumerate(((wp0, wq0), (wp1, wq1), (wp2, wq2), (wp3, wq3))):
        p_copy(p, places, j, OG, PB, wb, 0, sems.at[0])
        q_copy(q, places, j, 0, QB, wb, PB, sems.at[0])
    saves = Saves(out_sems)
    sums[...] = jnp.zeros_like(sums)
    for copy in ins.copies[0:2]:
        copy.wait()
    for s in range(2):
        rows, theirs = slice(s * SEQ, (s + 1) * SEQ), slice((1 - s) * SEQ, (2 - s) * SEQ)
        grad, term = rms_back(part[rows] + other[theirs], residual[rows], gains[1:2])
        grad = cot[rows].astype(F32) + grad
        grad_branch[rows] = grad.astype(BF16)
        if s == 0:
            own_residual[...] = grad
            sums[9:10] = jnp.sum(term, axis=0, keepdims=True)
    saves.start(own_residual, o_residual)

    def put_og(b, first, v):
        x, z = (b // 8) * 2 + b % 2, (b // 2) % 4
        n = min(max(OG - first, 0), v.shape[1])
        if n:
            bp[x, z, 0:48, first : first + n] = v[:, :n]
        if n < v.shape[1]:
            to = first + n - OG
            for r in range(3):
                bp[x, z, 48:64, 384 * r + to : 384 * r + to + v.shape[1] - n] = v[16 * r : 16 * r + 16, n:]

    ins.copies[2].wait()
    v = tn(merged[...], grad_branch[...]).astype(BF16)
    for b in range(16):
        put_og(b, 0, v[48 * b : 48 * b + 48])
    landed(wog, sems.at[1])
    gs[...] = nt(grad_branch[...], wog[..., 0:D].reshape(RC, D))
    for copy in ins.copies[3:5]:
        copy.wait()

    @pl.loop(0, 6)
    def _(c):
        at = cols(c)
        act, act_grad = gelu_both(gate_in[:, at])
        g = gs[:, at]
        for s in range(2):
            rows = slice(s * SEQ, (s + 1) * SEQ)
            gmix[rows, pl.ds(pl.multiple_of(RC + c * LANES, LANES), LANES)] = (
                g[rows] * st_in[s, 8:, at] * act_grad[rows]
            ).astype(BF16)
        gs[:, at] = g * act

    for copy in ins.copies[5:8]:
        copy.wait()

    @pl.loop(0, 6)
    def _(c):
        at = cols(c)
        keep, starts = masks[0], masks[1]
        rg = jax.nn.sigmoid(rate[:, at] + chans[5:6, at])
        sd = jnp.exp(-8.0 * rg * chans[7:8, at])
        coeff[:, at] = (1.0 - starts) * (keep * sd + (1.0 - keep))

    row = lax.broadcasted_iota(jnp.int32, (8, RC), 0)

    def backward(n, carry):
        i = SEQ // 8 - 1 - n
        new = []
        for s in range(2):
            at = pl.ds(pl.multiple_of(s * SEQ + i * 8, 8), 8)
            own = coeff[at]
            later_a, later_lam = carry[s]
            a = jnp.where(row == 7, later_a, pltpu.roll(own, 7, 0))
            b = gs[at]
            for k in (1, 2, 4):
                here = row < 8 - k
                b = jnp.where(here, b + a * pltpu.roll(b, 8 - k, 0), b)
                a = jnp.where(here, a * pltpu.roll(a, 8 - k, 0), a)
            h = b + a * later_lam
            lam[at] = h
            new.append((own[0:1], h[0:1]))
        return tuple(new)

    zero = jnp.zeros((1, RC), F32)
    lax.fori_loop(0, SEQ // 8, backward, ((zero, zero), (zero, zero)))

    @pl.loop(0, 6)
    def _(c):
        at = cols(c)
        decay = chans[7:8, at]
        for s in range(2):
            rows = slice(s * SEQ, (s + 1) * SEQ)
            keep, starts = masks[0, rows], masks[1, rows]
            rg, ig, sd, q, root, scale = gates(
                rate[rows, at], inp[rows, at], chans[5:6, at], chans[6:7, at], decay, keep, starts
            )
            conv = conv_low[rows, at].astype(F32)
            l = lam[rows, at]
            common = l * keep
            grad_coeff = l * st_in[s, 7 : PAD - 1, at]
            direct[rows, at] = common * scale * ig
            d_ig = common * scale * conv
            d_scale = common * ig * conv
            d_sd = (1.0 - starts) * (grad_coeff * keep - d_scale * jnp.where(q > 0.001, sd / root, 0.0))
            d_log = d_sd * sd * -8.0
            d_rate = d_log * decay * rg * (1.0 - rg)
            d_inp = d_ig * ig * (1.0 - ig)
            rate_low[rows, at] = d_rate.astype(BF16)
            inp_low[rows, at] = d_inp.astype(BF16)
            for n, term in ((5, d_rate), (6, d_inp), (7, d_log * rg)):
                sums[n : n + 1, at] += jnp.sum(term, axis=0, keepdims=True)

    for copy in ins.copies[8:]:
        copy.wait()
    turn = turn_matrix()
    top, left = quarter_masks()
    for p in range(2):
        at = slice(2 * HS * p, 2 * HS * (p + 1))
        direct[:, at] += nt(rate_low[:, at], tables[2 * p]) + nt(inp_low[:, at], tables[2 * p + 1])
        dr = tn(conv_low[:, at], rate_low[:, at]).astype(BF16)
        di = tn(conv_low[:, at], inp_low[:, at]).astype(BF16)
        none = jnp.zeros_like(dr)
        straight = jnp.where(top, jnp.where(left, dr, none), jnp.where(left, none, di))
        crossed = jnp.where(top, jnp.where(left, di, none), jnp.where(left, none, dr))
        g = (straight.astype(F32) + nn(crossed, turn)).astype(BF16)
        for b in range(8):
            put_og(8 * p + b, D, g[48 * b : 48 * b + 48])

    rolled[:, SEQ:] = jnp.zeros((2, 8, LANES), F32)

    @pl.loop(0, 6)
    def _(c):
        at = cols(c)
        for s in range(2):
            rows = slice(s * SEQ, (s + 1) * SEQ)
            g = direct[rows, at]
            gu = chans[0:1, at] * g
            sums[4:5, at] += jnp.sum(g, axis=0, keepdims=True)
            sums[0:1, at] += jnp.sum(g * u_in[s, 8:, at], axis=0, keepdims=True)
            for k in range(1, 4):
                w = g * masks[1 + k, rows]
                sums[k : k + 1, at] += jnp.sum(w * u_in[s, 8 - k : PAD - k, at], axis=0, keepdims=True)
                rolled[s, 0:SEQ] = w
                gu = gu + chans[k : k + 1, at] * rolled[s, k : SEQ + k]
            gmix[rows, at] = (gu * masks[0, rows]).astype(BF16)

    v = jnp.concatenate([sums[0:8, 0:RC], jnp.zeros((LANES - 8, RC), F32)], axis=0).T.astype(BF16)
    for b in range(16):
        put_og(b, 1408, v[48 * b : 48 * b + 48])
    landed(wb, sems.at[0])

    v = tn(normed[...], gmix[:, 0:PB]).astype(BF16)
    for x, z in RINGS:
        for half in range(2):
            r = ring_rows(x, z) + 256 * half
            bp[x, z, 32 * half : 32 * half + 32, OG:EARLY] = v[r : r + 32]
    emit(saves, bp, places, 0, (p0, p1, p2, p3))
    mixed_part[...] = nt(gmix[...], rows_of(wb, 0, BRANCH))
    saves.start(mixed_part.at[pl.ds(0, SEQ)], o_mine)
    saves.start(mixed_part.at[pl.ds(SEQ, SEQ)], o_theirs)
    t = tok[...].astype(F32)
    sums[8:9] = jnp.sum(mixed_part[...] * (t * inv_rms(t)), axis=0, keepdims=True)
    v = jnp.concatenate([sums[8:16], jnp.zeros((LANES - 8, D), F32)], axis=0).T.astype(BF16)
    for x, z in RINGS:
        for half in range(2):
            r = ring_rows(x, z) + 256 * half
            bq[z, x, 32 * half : 32 * half + 32, QB:EARLY] = v[r : r + 32]

    v = tn(normed[...], gmix[:, PB:]).astype(BF16)
    for x, z in RINGS:
        for half in range(2):
            r = ring_rows(x, z) + 256 * half
            bq[z, x, 32 * half : 32 * half + 32, 0:QB] = v[r : r + 32]
    emit(saves, bq, places, 2, (q0, q1, q2, q3))
    saves.wait()


def load(sources, targets, sems):
    copies = Saves(sems)
    for source, target in zip(sources, targets):
        copies.start(source, target)
    copies.wait()


def join_sums(
    places, eo_p, eu_p, lo_p, lu_p, eo_q, eu_q, lo_q, lu_q,
    tp0, tp1, tp2, tp3, tq0, tq1, tq2, tq3,
    early, late, out, in_sems, out_sems,
):
    loads, saves = Saves(in_sems), Saves(out_sems)
    for n, (a, b, c, d) in enumerate(((eo_p, eu_p, lo_p, lu_p), (eo_q, eu_q, lo_q, lu_q))):
        for source, target in ((a, early.at[n, 0]), (b, early.at[n, 1]), (c, late.at[n, 0]), (d, late.at[n, 1])):
            loads.start(source, target)
    for n, (axis, outs) in enumerate(((2, (tp0, tp1, tp2, tp3)), (0, (tq0, tq1, tq2, tq3)))):
        for copy in loads.copies[4 * n : 4 * n + 4]:
            copy.wait()
        for j, target in enumerate(outs):
            at, to = places[axis, (0, 2, 3, 1)[j]], 4 * n + j
            out[to, :, 0:EARLY] = add(early[n, 0, at], early[n, 1, at])
            out[to, :, EARLY:] = add(late[n, 0, at], late[n, 1, at])
            saves.start(out.at[to], target)
    saves.wait()


def add(a, b):
    return (a.astype(F32) + b.astype(F32)).astype(BF16)


def half_sums(a_p, b_p, c_p, d_p, a_q, b_q, c_q, d_q, *rest):
    outs, (early, late, in_sems, out_sems) = rest[-8:-4], rest[-4:]
    loads, saves = Saves(in_sems), Saves(out_sems)
    for n, (a, b, c, d) in enumerate(((a_p, b_p, c_p, d_p), (a_q, b_q, c_q, d_q))):
        for source, target in ((a, early.at[n, 0]), (b, early.at[n, 1]), (c, late.at[n, 0]), (d, late.at[n, 1])):
            loads.start(source, target)
    for n in range(2):
        for i, v in enumerate((early, late)):
            loads.copies[4 * n + 2 * i].wait()
            loads.copies[4 * n + 2 * i + 1].wait()
            v[n, 0] = add(v[n, 0], v[n, 1])
            saves.start(v.at[n, 0], outs[2 * n + i])
    saves.wait()


def pass_on(a_p, f_p, a_q, f_q, *rest):
    o_p, o_q, v, in_sems, out_sems = rest[-5:]
    loads, saves = Saves(in_sems), Saves(out_sems)
    for i, source in enumerate((a_p, f_p, a_q, f_q)):
        loads.start(source, v.at[i])
    for n, out in enumerate((o_p, o_q)):
        loads.copies[2 * n].wait()
        loads.copies[2 * n + 1].wait()
        v[2 * n] = (v[2 * n].astype(F32) + v[2 * n + 1].astype(F32)).astype(BF16)
        saves.start(v.at[2 * n], out)
    saves.wait()


def cut(
    places, p0, p1, p2, q0, q1, q2,
    o0, o1, o2, o3,
    parts, sp, sq, sd, in_sems,
):
    load((p0, p1, p2, q0, q1, q2), [parts.at[i] for i in range(6)], in_sems)
    for n, out in enumerate((sp, sq)):
        out[...] = parts[3 * n].astype(F32) + parts[3 * n + 1].astype(F32) + parts[3 * n + 2].astype(F32)
    sd[0:64] = sp[:, EARLY : EARLY + D]
    sd[64:96, 0:512] = sp[0:32, EARLY + D : EARLY + FC]
    sd[64:96, 512:1024] = sp[32:64, EARLY + D : EARLY + FC]
    tail = jnp.concatenate([sp[48:64, 384 * r : 384 * r + 384] for r in range(3)], axis=0)
    og = jnp.concatenate([sp[0:48, 0:OG], tail], axis=1).astype(BF16)
    i = lax.broadcasted_iota(jnp.int32, (16, 48), 0)
    s = lax.broadcasted_iota(jnp.int32, (16, 48), 1)

    def two(rows):
        return jnp.concatenate(rows, axis=0).astype(BF16)

    for j, out in enumerate((o0, o1, o2, o3)):
        y = places[1, (0, 2, 3, 1)[j]]
        rows = [pl.ds(pl.multiple_of(32 * c + y * 8, 8), 8) for c in range(2)]
        out[:, 0:PB] = two([sp[r, OG:EARLY] for r in rows])
        out[:, PB : PB + PI] = two([sp[r, UNIT - PI :] for r in rows])
        out[:, PB + PI : DC] = two([sq[r] for r in rows])
        mine = jnp.where((s == i + y * 12) & (i < 12), 1.0, 0.0).astype(BF16)
        out[:, DC:DOWN] = nn(mine, og).astype(BF16)
        down = sd[pl.ds(pl.multiple_of(y * 24, 8), 24)]
        out[:, DOWN : DOWN + D] = down[0:16].astype(BF16)
        out[:, DOWN + D :] = two([down[16:24, 0:512], down[16:24, 512:]])


def finish(places, o0, o1, o2, o3, mine, theirs, out_grad, gate_grad, chan_grad, down_grad, v):
    v[...] = o0[...].astype(F32) + o1[...].astype(F32) + o2[...].astype(F32) + o3[...].astype(F32)
    core = places[3, 0]
    theirs[...] = v[pl.ds(pl.multiple_of((1 - core) * 8, 8), 8), 0:DC]
    mine[...] = v[pl.ds(pl.multiple_of(core * 8, 8), 8), 0:DC]
    out_grad[...] = v[0:12, DC : DC + D]
    gate_grad[...] = v[0:12, DC + D : DC + D + 384]
    chan_grad[...] = v[:, DC + D + 384 : DOWN].T[0:8]
    down_grad[0:16] = v[:, DOWN : DOWN + D]
    down_grad[16:24, 0:512] = v[0:8, DOWN + D :]
    down_grad[16:24, 512:] = v[8:16, DOWN + D :]


def unpack(places, mine, theirs, branch, inner, gains):
    def halves(ins):
        for c, v in enumerate(ins):
            for q in range(4):
                to = 768 * q + 384 * c
                if q == 0:
                    branch[:, to : to + PB] = v[:, 0:PB]
                    branch[:, to + PB : to + 384] = v[:, PB + PI : PB + PI + 128]
                else:
                    branch[:, to : to + 384] = v[:, PI + 384 * q : PI + 384 * q + 384]
                at = PB if q == 0 else DC - LATE + 768 * (q - 1)
                to = 1536 * q + 768 * c
                inner[:, to : to + 768] = v[:, at : at + 768]

    gains[...] = mine[:, DC - LATE - LANES : DC - LATE] + theirs[:, DC - LATE - LANES : DC - LATE]

    @pl.when(places[3, 0] == 0)
    def _():
        halves((mine, theirs))

    @pl.when(places[3, 0] == 1)
    def _():
        halves((theirs, mine))


VM, HB, SM, ANY = pltpu.VMEM, pltpu.HBM, pltpu.SMEM, pl.ANY


def kernel(body, ins, spaces, outs, scratch, mib, flops=0):
    moved = sum(v.size * v.dtype.itemsize for v in ins)
    ins = [pltpu.with_memory_space_constraint(v, HB) if s is HB else v for v, s in zip(ins, spaces)]
    return pl.pallas_call(
        body,
        out_shape=[HB(s, d) if at is HB else jax.ShapeDtypeStruct(s, d) for s, d, at in outs],
        in_specs=[pl.BlockSpec(memory_space=s) for s in spaces],
        out_specs=[pl.BlockSpec(memory_space=s) for _, _, s in outs],
        scratch_shapes=scratch,
        compiler_params=pltpu.CompilerParams(vmem_limit_bytes=mib * 2**20),
        cost_estimate=pl.CostEstimate(flops=flops, bytes_accessed=moved, transcendentals=0),
    )(*ins)


def shards(
    tokens, cotangent, segment, keep_mask, conv_state, lru_state, norm1_gain, conv_weight, lru_bias, decay_rate,
    gate_weight, branch_weight, out_weight, norm2_gain, mlp_in_weight, mlp_out_weight,
):
    here = my_place()
    core = here["core"]
    zero = jnp.zeros_like(core)
    places = jnp.stack(
        [jnp.stack(ring_places(axis, here)) for axis in "xyz"] + [jnp.stack([core, zero, zero, zero])]
    ).astype(jnp.int32)
    vmem, dma = pltpu.VMEM, pltpu.SemaphoreType.DMA

    tc = jnp.concatenate([tokens[0], cotangent[0]], axis=0)
    tc_other = swap(tc)
    marks = jnp.concatenate([segment, keep_mask], axis=1).astype(F32)
    states = jnp.concatenate([conv_state[0], lru_state], axis=0)
    sent = jnp.concatenate([core_half(states, 1 - core, 2), jnp.pad(marks, ((0, 0), (0, RC - 2 * SEQ)))], axis=0)
    sent = swap(sent)

    mine, theirs, own = kernel(
        pack,
        (places, branch_weight, mlp_in_weight, jnp.stack([norm1_gain, norm2_gain]), out_weight, gate_weight,
         jnp.concatenate([conv_weight, lru_bias, decay_rate[None]], axis=0), mlp_out_weight),
        [SM] + [VM] * 7,
        [((8, DC), BF16, VM)] * 2 + [((16, OWN - DC), BF16, VM)],
        [],
        8,
    )
    (block,) = kernel(join, (places, mine, swap(theirs), own), [SM] + [VM] * 3, [((16, OWN), BF16, VM)], [], 8)

    row = ((64, UNIT), BF16)
    unit_of = ((2, 32, UNIT), BF16)
    p, q = kernel(
        unit,
        (places, *ring_direct(block, "y"), tc_other, sent),
        [SM] + [VM] * 4 + [ANY] * 2,
        [(*unit_of, HB)] * 2,
        [vmem(*row), vmem(*row), vmem((64, DC), F32), vmem((96, D), F32), dma((4,))],
        16,
    )
    early, late = (4, 64, EARLY), (4, 64, LATE)
    stack = ((4, 64, UNIT), BF16)
    pe, qe, pl_, ql = kernel(
        planes,
        (places, *ring_direct(p, "z"), *ring_direct(q, "x")),
        [SM] + [HB, HB, HB, ANY, HB, ANY, HB, ANY],
        [(v, BF16, HB) for n in (EARLY, LATE) for v in ((2, 4, 32, n), (2, 2, 2, 32, n))],
        [vmem((2, 4, 32, UNIT), BF16), vmem((2, 2, 2, 32, UNIT), BF16), dma((8,)), dma((4,))],
        8,
    )
    pe, qe, pl_, ql = ring(pe, "x"), ring(qe, "z"), ring(pl_, "x"), ring(ql, "z")

    tok = jnp.concatenate([tc[:SEQ], tc_other[:SEQ]], axis=0)
    cot = jnp.concatenate([tc[SEQ:], tc_other[SEQ:]], axis=0)
    states = jnp.stack([core_half(states, core, 2), sent[:4]])
    marks = jnp.concatenate([marks, sent[4:, : 2 * SEQ]], axis=0)
    seg, keep = marks[:, :SEQ], marks[:, SEQ:]
    earlier = [jnp.concatenate([jnp.repeat(seg[:, :1], k, axis=1), seg[:, : SEQ - k]], axis=1) for k in range(1, 4)]
    masks = jnp.stack([keep, (earlier[0] != seg).astype(F32)] + [(e == seg).astype(F32) for e in earlier])
    masks = jnp.broadcast_to(masks.reshape(5, TOK, 1), (5, TOK, LANES))

    wide, wide_low = ((TOK, D), F32), ((TOK, D), BF16)
    act, act_low, padded = ((TOK, RC), F32), ((TOK, RC), BF16), ((2, PAD, RC), F32)
    tables = ((4, 2 * HS, 2 * HS), BF16)
    saved = [wide_low, act_low, padded, act, act_low, act, act, padded, tables]
    part, finals, gains, chans, normed, merged, u, gate_in, conv_low, rate, inp, st, table = kernel(
        rec_forward,
        (places, tok, masks, states[:, :3], states[:, 3:], *pe, *qe),
        [SM] + [VM] * 4 + [HB] * 8,
        [((TOK + 8, D), F32, VM), ((4, RC), F32, VM), ((8, D), F32, VM), ((8, RC), F32, VM)]
        + [(*v, HB) for v in saved],
        [vmem((*ROWS, PB + EARLY), BF16), vmem((*OG_ROWS, OGC), BF16)]
        + [vmem(*v) for v in saved + [act, act]]
        + [dma((2,)), dma((9,))],
        32,
        2 * TOK * (D * BRANCH + RC * (D + 768)),
    )
    half = ((SEQ, D), F32)
    other = swap(part)
    normed2, hidden, ggu, residual, base, back = kernel(
        mlp,
        (places, tok, cot, part, other, gains, *pl_, *ql),
        [SM] + [VM] * 5 + [ANY] * 8,
        [(*wide_low, VM), ((TOK, FC), BF16, VM), ((TOK, INNER), BF16, VM)] + [(*v, HB) for v in (wide, half, ((TOK + SEQ, D), F32))],
        [vmem((*ROWS, INNER), BF16), vmem((*DOWN_ROWS, D), BF16)]
        + [vmem(*v) for v in (wide, wide, wide, half)]
        + [dma((2,)), dma((4,))],
        32,
        2 * TOK * D * (2 * INNER + 2 * FC),
    )
    back_other = swap(back)
    outs = kernel(
        mlp_grads,
        (places, cot, normed2, hidden, ggu),
        [SM] + [VM] * 4,
        [(late, BF16, HB)] * 8,
        [vmem((4,) + late, BF16), vmem((4,) + late, BF16), dma((8,))],
        32,
        2 * TOK * D * (INNER + FC),
    )
    lp, lq = outs[:4], outs[4:]
    far = send(lp[2], along("x", 1)), send(lq[2], along("z", 1))
    down = send(lp[3], along("x", -1)), send(lq[3], along("z", -1))
    outs = kernel(
        rec_backward,
        (places, tok, cot, masks, gains, chans, back_other, back, residual, normed, merged, u, gate_in, conv_low, rate,
         inp, st, table, *pe, *qe),
        [SM] + [VM] * 6 + [HB] * 19,
        [(*v, HB) for v in (half, half, half)] + [(early, BF16, HB)] * 8,
        [vmem((*ROWS, BRANCH), BF16), vmem((*OG_ROWS, OGC), BF16)]
        + [vmem(*v) for v in (wide, wide, wide_low, act_low, padded, act, act_low, act, act, padded, tables)]
        + [vmem(*v) for v in (act, wide_low, act, act, act_low, act_low, act, ((TOK, BRANCH), BF16))]
        + [vmem((2, PAD, LANES), F32), vmem((16, D), F32), vmem(*wide), vmem(*half)]
        + [vmem((4,) + early, BF16), vmem((4,) + early, BF16), dma((2,)), dma((11,)), dma((11,))],
        48,
        2 * TOK * D * (2 * BRANCH + 2 * RC),
    )
    grad_residual, mixed_mine, mixed_theirs = outs[:3]
    ep, eq = outs[3:7], outs[7:]
    def passed(terms, far, routes, shape, until, spaces):
        (p, q), (a, b) = terms, routes
        up = kernel(
            pass_on,
            (p[1], far[0], q[1], far[1], *until),
            [HB] * 4 + spaces,
            [(shape, BF16, HB)] * 2,
            [vmem((4,) + shape, BF16), dma((4,)), dma((2,))],
            16,
        )
        return send(up[0], along(a, 1)), send(up[1], along(b, 1))

    early_far = send(ep[2], along("x", 1)), send(eq[2], along("z", 1))
    early_down = send(ep[3], along("x", -1)), send(eq[3], along("z", -1))
    late_up = passed((lp, lq), far, "xz", late, (ep[0], *down), [HB] * 3)
    early_up = passed((ep, eq), early_far, "xz", early, early_down, [ANY] * 2)

    summed = kernel(
        half_sums,
        (ep[0], early_down[0], lp[0], down[0], eq[0], early_down[1], lq[0], down[1]),
        [HB] * 8,
        [(early, BF16, HB), (late, BF16, HB)] * 2,
        [vmem((2, 2) + early, BF16), vmem((2, 2) + late, BF16), dma((8,)), dma((4,))],
        24,
    )
    outs = kernel(
        join_sums,
        (places, summed[0], early_up[0], summed[1], late_up[0], summed[2], early_up[1], summed[3], late_up[1]),
        [SM] + [HB] * 8,
        [(*row, HB)] * 8,
        [vmem((2, 2) + early, BF16), vmem((2, 2) + late, BF16), vmem((8, 64, UNIT), BF16), dma((8,)), dma((8,))],
        32,
    )
    tp, tq = outs[:4], outs[4:]
    far = send(tp[2], along("z", 1)), send(tq[2], along("x", 1))
    down = send(tp[3], along("z", -1)), send(tq[3], along("x", -1))
    up = kernel(
        pass_on,
        (tp[1], far[0], tq[1], far[1], *down),
        [HB] * 3 + [ANY] * 3,
        [(*row, HB)] * 2,
        [vmem((4, 64, UNIT), BF16), dma((4,)), dma((2,))],
        8,
    )
    up = send(up[0], along("z", 1)), send(up[1], along("x", 1))
    sums = kernel(
        cut,
        (places, tp[0], down[0], up[0], tq[0], down[1], up[1]),
        [SM] + [HB, HB, ANY] * 2,
        [((16, OWN), BF16, VM)] * 4,
        [vmem((6, 64, UNIT), BF16), vmem((64, UNIT), F32), vmem((64, UNIT), F32), vmem((96, D), F32), dma((6,))],
        16,
    )
    mine, theirs, out_grad, gate_grad, chan_grad, down_grad = kernel(
        finish,
        (places, *terms_direct(sums, "y")),
        [SM] + [VM] * 4,
        [((8, DC), F32, VM)] * 2 + [(s, F32, VM) for s in ((12, D), (12, 384), (8, 16), (24, D))],
        [vmem((16, OWN), F32)],
        8,
    )
    branch_grad, in_grad, gain_grads = kernel(
        unpack,
        (places, mine, swap(theirs)),
        [SM] + [VM] * 2,
        [((8, 2 * R), F32, VM), ((8, 2 * F), F32, VM), ((8, LANES), F32, VM)],
        [],
        8,
    )

    output = (base + back_other[TOK:]).astype(BF16)
    grad, _ = rms_back(mixed_mine + swap(mixed_theirs), tok[:SEQ].astype(F32), gains[0])
    input_grad = (grad_residual + grad).astype(BF16)
    theirs = other[TOK : TOK + 4, :RC]
    finals = jnp.stack(
        [v.reshape(1, 4, 2, 384) for v in (jnp.where(core == 0, finals, theirs), jnp.where(core == 0, theirs, finals))],
        axis=3,
    ).reshape(1, 4, R)
    return (
        output[None],
        input_grad[None],
        finals[:, :3],
        finals[:, 3],
        gain_grads[:, 0],
        chan_grad[:4, :12],
        chan_grad[4:7, :12],
        chan_grad[7, :12],
        gate_grad,
        branch_grad,
        out_grad,
        gain_grads[:, 1],
        in_grad,
        down_grad,
    )


def solution(mesh):
    rows, last = P(AXES), P(None, AXES)
    specs = [rows] * 6 + [rows, last, last] + [rows] * 7
    outs = [rows] * 4 + [rows, last, last] + [rows] * 7
    return jax.shard_map(
        shards, mesh=mesh, in_specs=tuple(specs), out_specs=tuple(outs), check_vma=False
    )
```

```python
import jax
import jax.numpy as jnp
from jax import lax
from jax.experimental import pallas as pl
from jax.experimental.pallas import tpu as pltpu
from jax.sharding import PartitionSpec as P

AXES = ("dp", "fsdp")
D, R, F, SEQ = 1024, 1536, 3072, 128
RC, FC = R // 2, F // 2
HS = 192
F32, BF16 = jnp.float32, jnp.bfloat16
BRANCH, INNER = 2 * RC, 2 * FC
TOK, PAD, LANES = 2 * SEQ, SEQ + 8, 128

EARLY, LATE = 1408, 2304
UNIT = EARLY + LATE
OG, PB, PI, QB = 1152, 256, 768, 1280
DC = PB + PI + UNIT
OGC = 1536
DOWN = DC + OGC
OWN = DOWN + D + D // 2


def place_of(device):
    outer, inner = divmod(device, 32)
    x_hi, core = divmod(outer, 2)
    z, rest = divmod(inner, 8)
    x_lo, y = divmod(rest, 4)
    return dict(x=x_hi * 2 + x_lo, y=y, z=z, core=core)


def device_at(x, y, z, core):
    return ((x // 2) * 2 + core) * 32 + z * 8 + (x % 2) * 4 + y


def pairs(move):
    return [(d, device_at(**move(place_of(d)))) for d in range(128)]


def along(axis, steps):
    def move(p):
        sign = 1 if p["core"] == 0 else -1
        return {**p, axis: (p[axis] + sign * steps) % 4}

    return pairs(move)


def other_core(p):
    return {**p, "core": 1 - p["core"]}


def opposite(axis):
    return pairs(lambda p: {**p, axis: (p[axis] + 2) % 4})


def send(value, route):
    return lax.ppermute(value, AXES, route)


def swap(value):
    return send(value, pairs(other_core))


def my_place():
    device = lax.axis_index(AXES)
    outer, inner = device // 32, device % 32
    return dict(x=(outer // 2) * 2 + (inner // 4) % 2, y=inner % 4, z=inner // 8, core=outer % 2)


def ring_places(axis, here):
    sign, at = 1 - 2 * here["core"], here[axis]
    return [at, (at - sign) % 4, (at + sign) % 4, (at + 2) % 4]


def ring(block, axis):
    one = send(block, along(axis, 1))
    two = send(one, along(axis, 1))
    return block, one, send(two, along(axis, 1)), two


def ring_both(block, axis):
    up, down = send(block, along(axis, 1)), send(block, along(axis, -1))
    return block, up, down, send(up, along(axis, 1))


def ring_direct(block, axis):
    return block, send(block, along(axis, 1)), send(block, along(axis, -1)), send(block, opposite(axis))


def terms_direct(terms, axis):
    own, ahead, far, behind = terms
    return own, send(ahead, along(axis, 1)), send(far, opposite(axis)), send(behind, along(axis, -1))


def total(*terms):
    out = terms[0].astype(F32)
    for term in terms[1:]:
        out = out + term.astype(F32)
    return out.astype(BF16)


def core_half(array, core, blocks):
    v = array.reshape(array.shape[:-1] + (blocks, 2, array.shape[-1] // (2 * blocks)))
    v = lax.dynamic_index_in_dim(v, core, v.ndim - 2, keepdims=False)
    return v.reshape(array.shape[:-1] + (array.shape[-1] // 2,))


def dot(a, b, dims):
    return lax.dot_general(a, b, (dims, ((), ())), preferred_element_type=F32)


def nn(a, b):
    return dot(a, b, ((1,), (0,)))


def nt(a, b):
    return dot(a, b, ((1,), (1,)))


def tn(a, b):
    return dot(a, b, ((0,), (0,)))


def inv_rms(v):
    return lax.rsqrt(jnp.mean(v * v, axis=-1, keepdims=True) + 1e-6)


def rms_back(grad, v, gain):
    s = inv_rms(v)
    n = v * s
    g2 = grad * gain
    return s * (g2 - n * jnp.mean(g2 * n, axis=-1, keepdims=True)), grad * n


C0, C1 = 0.7978845608028654, 0.044715


def gelu_both(a):
    t = jnp.tanh(C0 * (a + C1 * (a * a * a)))
    half = 0.5 * (1.0 + t)
    return a * half, half + 0.5 * a * (1.0 - t * t) * (C0 * (1.0 + 3.0 * C1 * (a * a)))


def gates(rate, inp, bias1, bias2, decay, keep, starts):
    rg = jax.nn.sigmoid(rate + bias1)
    ig = jax.nn.sigmoid(inp + bias2)
    sd = jnp.exp(-8.0 * rg * decay)
    q = 1.0 - sd * sd
    root = jnp.sqrt(jnp.maximum(q, 0.001))
    scale = starts + (1.0 - starts) * root
    return rg, ig, sd, q, root, scale


def cols(c):
    return pl.ds(pl.multiple_of(c * LANES, LANES), LANES)


class Saves:
    def __init__(self, sem):
        self.sem, self.copies = sem, []

    def start(self, source, target):
        self.copies.append(pltpu.make_async_copy(source, target, self.sem.at[len(self.copies)]))
        self.copies[-1].start()

    def wait(self):
        for copy in self.copies:
            copy.wait()


def pick(rows, where):
    return jnp.where(lax.broadcasted_iota(jnp.int32, (rows, where.shape[1]), 0) == where, 1.0, 0.0).astype(BF16)


def stand(values, rows):
    v = values.astype(F32)
    i = lax.broadcasted_iota(jnp.int32, (rows, v.shape[1]), 0)
    j = lax.broadcasted_iota(jnp.int32, (rows, v.shape[1]), 1)
    lane = lax.broadcasted_iota(jnp.int32, (rows, LANES), 1)
    out = jnp.zeros((rows, LANES), F32)
    for n in range(v.shape[0]):
        column = jnp.sum(jnp.where(i == j, v[n : n + 1], 0.0), axis=1, keepdims=True)
        out = out + jnp.where(lane == n, column, 0.0)
    return out


def pack(places, branch, inner, gain, out, gate, perchan, down, mine, theirs, own):
    gains = stand(gain[...], 8).astype(BF16)

    def halves(outs):
        for c, to_core in enumerate(outs):
            for q in range(4):
                v = branch[:, 768 * q + 384 * c : 768 * q + 384 * c + 384]
                if q == 0:
                    to_core[:, 0:PB] = v[:, 0:PB]
                    to_core[:, PB + PI : PB + PI + 128] = v[:, PB:]
                else:
                    to_core[:, PI + 384 * q : PI + 384 * q + 384] = v
                v = inner[:, 1536 * q + 768 * c : 1536 * q + 768 * c + 768]
                to = PB if q == 0 else DC - LATE + 768 * (q - 1)
                to_core[:, to : to + 768] = v
            tile = DC - LATE - LANES
            to_core[:, tile : tile + LANES] = gains

    @pl.when(places[3, 0] == 0)
    def _():
        halves((mine, theirs))

    @pl.when(places[3, 0] == 1)
    def _():
        halves((theirs, mine))

    own[...] = jnp.zeros_like(own)
    own[0:12, 0:D] = out[...]
    own[0:12, D : D + 384] = gate[...]
    own[:, 1408:OGC] = stand(perchan[...], 16).astype(BF16)
    own[:, OGC : OGC + D] = down[0:16]
    own[:, OGC + D :] = jnp.concatenate(
        [down[16:24, 0:512].astype(F32), down[16:24, 512:].astype(F32)], axis=0
    ).astype(BF16)


def join(places, mine, theirs, own, block):
    def rows(low, high):
        block[:, 0:DC] = jnp.concatenate([low[...].astype(F32), high[...].astype(F32)], axis=0).astype(BF16)

    @pl.when(places[3, 0] == 0)
    def _():
        rows(mine, theirs)

    @pl.when(places[3, 0] == 1)
    def _():
        rows(theirs, mine)

    block[:, DC:] = own[...]


def unit(places, p0, p1, p2, p3, *rest):
    o_p, o_q, p, q, d, dn, sems = rest[-7:]
    ogs = []
    s = lax.broadcasted_iota(jnp.int32, (1, 64), 1)
    y = jnp.zeros((1, 64), jnp.int32)
    for j, piece in enumerate((p0, p1, p2, p3)):
        at = places[1, j]
        y = jnp.where(s // 16 == j, at, y)
        v = piece[:, 0:DC].astype(F32)
        for c in range(2):
            d[pl.ds(pl.multiple_of(c * 32 + at * 8, 8), 8)] = v[8 * c : 8 * c + 8]
        ogs.append(piece[:, DC:DOWN])
        v = piece[:, DOWN:].astype(F32)
        dn[pl.ds(pl.multiple_of(at * 24, 8), 16)] = v[:, 0:D]
        for h in range(2):
            dn[pl.ds(pl.multiple_of(at * 24 + 16, 8), 8), 512 * h : 512 * h + 512] = v[8 * h : 8 * h + 8, D:]
    saves = Saves(sems)
    q[...] = d[:, PB + PI :].astype(BF16)
    for c in range(2):
        saves.start(q.at[pl.ds(32 * c, 32)], o_q.at[c])
    p[:, OG:EARLY] = d[:, 0:PB].astype(BF16)
    p[:, UNIT - PI :] = d[:, PB : PB + PI].astype(BF16)
    i = s % 16
    og = nn(pick(48, jnp.where(i < 12, y * 12 + i, 64)), jnp.concatenate(ogs, axis=0)).astype(BF16)
    p[0:48, 0:OG] = og[:, 0:OG]
    for r in range(3):
        p[48:64, 384 * r : 384 * r + 384] = og[16 * r : 16 * r + 16, OG:]
    p[:, EARLY : EARLY + D] = dn[0:64].astype(BF16)
    p[0:32, EARLY + D : EARLY + FC] = dn[64:96, 0:512].astype(BF16)
    p[32:64, EARLY + D : EARLY + FC] = dn[64:96, 512:1024].astype(BF16)
    for c in range(2):
        saves.start(p.at[pl.ds(32 * c, 32)], o_p.at[c])
    saves.wait()


def planes(places, p0, p1, p2, p3, q0, q1, q2, q3, o_pe, o_qe, o_pl, o_ql, p, q, in_sems, out_sems):
    loads, saves = Saves(in_sems), Saves(out_sems)
    for j, piece in enumerate((p0, p1, p2, p3)):
        loads.start(piece, p.at[:, places[2, j]])
    for j, piece in enumerate((q0, q1, q2, q3)):
        x = places[0, j]
        loads.start(piece, q.at[x // 2, :, x % 2])
    for n, (stack, out) in enumerate(((p, o_pe), (q, o_qe))):
        for copy in loads.copies[4 * n : 4 * n + 4]:
            copy.wait()
        saves.start(stack.at[..., pl.ds(0, EARLY)], out)
    for stack, out in ((p, o_pl), (q, o_ql)):
        saves.start(stack.at[..., pl.ds(EARLY, LATE)], out)
    saves.wait()


ROWS = (2, 2, 4, 2, 32)
OG_ROWS, DOWN_ROWS = (2, 4, 2, 48), (2, 4, 2, 96)


def ring_rows(x, z):
    return (x // 2) * 512 + z * 64 + (x % 2) * 32


def p_copy(piece, places, j, first, count, block, to, sem):
    x = places[0, j]
    target = block.at[x // 2, :, :, x % 2, :, pl.ds(to, count)]
    pltpu.make_async_copy(piece.at[..., pl.ds(first, count)], target, sem).start()


def q_copy(piece, places, j, first, count, block, to, sem):
    target = block.at[:, :, places[2, j], :, :, pl.ds(to, count)]
    pltpu.make_async_copy(piece.at[..., pl.ds(first, count)], target, sem).start()


def og_copy(piece, places, j, block, sem):
    x = places[0, j]
    block = block.at[x // 2, :, x % 2]
    for source, target in (
        (piece.at[0, :, :, pl.ds(0, OG)], block.at[:, pl.ds(0, 32), pl.ds(0, OG)]),
        (piece.at[1, :, pl.ds(0, 16), pl.ds(0, OG)], block.at[:, pl.ds(32, 16), pl.ds(0, OG)]),
    ):
        pltpu.make_async_copy(source, target, sem).start()
    for r in range(3):
        pltpu.make_async_copy(
            piece.at[1, :, pl.ds(16, 16), pl.ds(384 * r, 384)], block.at[:, pl.ds(16 * r, 16), pl.ds(OG, 384)], sem
        ).start()


def down_copy(piece, places, j, block, sem):
    x = places[0, j]
    block = block.at[x // 2, :, x % 2]
    for h in range(2):
        pltpu.make_async_copy(piece.at[h, :, :, pl.ds(0, D)], block.at[:, pl.ds(32 * h, 32)], sem).start()
        pltpu.make_async_copy(
            piece.at[h, :, :, pl.ds(D, 512)], block.at[:, pl.ds(64, 32), pl.ds(512 * h, 512)], sem
        ).start()


def rows_of(block, first, count):
    return block[..., first : first + count].reshape(D, count)


def landed(block, sem):
    pltpu.make_async_copy(block, block, sem).wait()


def turn_matrix():
    i = lax.broadcasted_iota(jnp.int32, (2 * HS, 2 * HS), 0)
    j = lax.broadcasted_iota(jnp.int32, (2 * HS, 2 * HS), 1)
    return jnp.where((i == j + HS) | (j == i + HS), 1.0, 0.0).astype(BF16)


def quarter_masks():
    i = lax.broadcasted_iota(jnp.int32, (2 * HS, 2 * HS), 0) < HS
    j = lax.broadcasted_iota(jnp.int32, (2 * HS, 2 * HS), 1) < HS
    return i, j


def rec_forward(
    places, tok, masks, conv_before, lru_before, p0, p1, p2, p3, q0, q1, q2, q3,
    part, finals, gains, chans, o_normed, o_merged, o_u, o_gate, o_conv, o_rate, o_inp, o_st, o_tables,
    wb, wog, normed, merged, u, gate_in, conv_low, rate, inp, st, tables, coeff, drive, sems, out_sems,
):
    for j, (p, q) in enumerate(((p0, q0), (p1, q1), (p2, q2), (p3, q3))):
        p_copy(p, places, j, OG, PB, wb, 0, sems.at[0])
        q_copy(q, places, j, 0, EARLY, wb, PB, sems.at[0])
    for j, p in enumerate((p0, p1, p2, p3)):
        og_copy(p, places, j, wog, sems.at[1])
    saves = Saves(out_sems)
    t = tok[...].astype(F32)
    scaled = t * inv_rms(t)
    landed(wb, sems.at[0])
    gains[...] = rows_of(wb, BRANCH, LANES).astype(F32).T[:8]
    normed[...] = (scaled * gains[0:1]).astype(BF16)
    saves.start(normed, o_normed)
    for s in range(2):
        u[s, 0:8] = jnp.zeros((8, RC), F32)
        u[s, 5:8] = conv_before[s]
        st[s, 0:8] = jnp.zeros((8, RC), F32)
        st[s, 7:8] = lru_before[s]

    v = nn(normed[...], rows_of(wb, 0, RC))
    for s in range(2):
        rows = slice(s * SEQ, (s + 1) * SEQ)
        for c in range(6):
            u[s, 8:, LANES * c : LANES * c + LANES] = v[rows, LANES * c : LANES * c + LANES] * masks[0, rows]

    saves.start(u, o_u)

    gate_in[...] = nn(normed[...], rows_of(wb, RC, RC))

    saves.start(gate_in, o_gate)
    landed(wog, sems.at[1])
    chans[...] = wog[..., 1408:].reshape(RC, LANES).astype(F32).T[:8]

    @pl.loop(0, 6)
    def _(c):
        at = cols(c)
        for s in range(2):
            rows = slice(s * SEQ, (s + 1) * SEQ)
            v = chans[4:5, at] + chans[0:1, at] * u[s, 8:, at]
            for k in range(1, 4):
                v = v + chans[k : k + 1, at] * (u[s, 8 - k : PAD - k, at] * masks[1 + k, rows])
            conv_low[rows, at] = v.astype(BF16)

    saves.start(conv_low, o_conv)
    turn = turn_matrix()
    top, left = quarter_masks()
    for p in range(2):
        g = wog[p, :, :, :, D : D + 384].reshape(2 * HS, 2 * HS)
        turned = nn(g, turn).astype(BF16)
        zero = jnp.zeros_like(g)
        tables[2 * p] = jnp.where(left, jnp.where(top, g, zero), jnp.where(top, zero, turned))
        tables[2 * p + 1] = jnp.where(left, jnp.where(top, turned, zero), jnp.where(top, zero, g))
        at = slice(2 * HS * p, 2 * HS * (p + 1))
        rate[:, at] = nn(conv_low[:, at], tables[2 * p])
        inp[:, at] = nn(conv_low[:, at], tables[2 * p + 1])
    saves.start(tables, o_tables)
    saves.start(rate, o_rate)
    saves.start(inp, o_inp)

    @pl.loop(0, 6)
    def _(c):
        at = cols(c)
        keep, starts = masks[0], masks[1]
        _, ig, sd, _, _, scale = gates(
            rate[:, at], inp[:, at], chans[5:6, at], chans[6:7, at], chans[7:8, at], keep, starts
        )
        coeff[:, at] = (1.0 - starts) * (keep * sd + (1.0 - keep))
        drive[:, at] = keep * scale * ig * conv_low[:, at].astype(F32)

    row = lax.broadcasted_iota(jnp.int32, (8, RC), 0)

    def forward(i, carry):
        new = []
        for s in range(2):
            at = pl.ds(pl.multiple_of(s * SEQ + i * 8, 8), 8)
            a, b = coeff[at], drive[at]
            for k in (1, 2, 4):
                later = row >= k
                b = jnp.where(later, a * pltpu.roll(b, k, 0) + b, b)
                a = jnp.where(later, a * pltpu.roll(a, k, 0), a)
            h = a * carry[s] + b
            st[s, pl.ds(pl.multiple_of(8 + i * 8, 8), 8)] = h
            new.append(h[7:8])
        return tuple(new)

    last = lax.fori_loop(0, SEQ // 8, forward, (lru_before[0], lru_before[1]))
    saves.start(st, o_st)
    part[TOK:] = jnp.zeros((8, D), F32)
    part[TOK : TOK + 3, 0:RC] = u[1, PAD - 3 :]
    part[TOK + 3 : TOK + 4, 0:RC] = last[1]
    finals[0:3] = u[0, PAD - 3 :]
    finals[3:4] = last[0]

    @pl.loop(0, 6)
    def _(c):
        at = cols(c)
        act, _ = gelu_both(gate_in[:, at])
        for s in range(2):
            rows = slice(s * SEQ, (s + 1) * SEQ)
            merged[rows, at] = (st[s, 8:, at] * act[rows]).astype(BF16)

    saves.start(merged, o_merged)

    part[0:TOK] = nn(merged[...], wog[..., 0:D].reshape(RC, D))

    saves.wait()


def mlp(
    places, tok, cot, part, other, gains, p0, p1, p2, p3, q0, q1, q2, q3,
    normed2, hidden, ggu, o_residual, o_base, o_back,
    win, wdown, residual, down, back, base, sems, out_sems,
):
    for j, (p, q) in enumerate(((p0, q0), (p1, q1), (p2, q2), (p3, q3))):
        p_copy(p, places, j, FC, PI, win, 0, sems.at[0])
        q_copy(q, places, j, 0, LATE, win, PI, sems.at[0])
    for j, p in enumerate((p0, p1, p2, p3)):
        down_copy(p, places, j, wdown, sems.at[1])
    saves = Saves(out_sems)
    for s in range(2):
        rows, theirs = slice(s * SEQ, (s + 1) * SEQ), slice((1 - s) * SEQ, (2 - s) * SEQ)
        v = tok[rows].astype(F32) + (part[rows] + other[theirs])
        residual[rows] = v
        normed2[rows] = (v * inv_rms(v) * gains[1:2]).astype(BF16)
    saves.start(residual, o_residual)
    down[...] = jnp.zeros_like(down)
    back[...] = jnp.zeros_like(back)
    landed(win, sems.at[0])
    for c in range(2):
        at, up = slice(768 * c, 768 * c + 768), slice(FC + 768 * c, FC + 768 * c + 768)
        wa, wu = rows_of(win, 768 * c, 768), rows_of(win, FC + 768 * c, 768)
        a = nn(normed2[...], wa)
        b = nn(normed2[...], wu)
        ga, da = gelu_both(a)
        h = (ga * b).astype(BF16)
        hidden[:, at] = h
        if c == 0:
            landed(wdown, sems.at[1])
        wd = wdown[c].reshape(768, D)
        gh = nt(cot[...], wd)
        gg_a = (gh * b * da).astype(BF16)
        gg_b = (gh * ga).astype(BF16)
        ggu[:, at] = gg_a
        ggu[:, up] = gg_b
        down[...] += nn(h, wd)
        back[...] += nt(gg_a, wa) + nt(gg_b, wu)

    saves.start(back, o_back.at[pl.ds(0, TOK)])
    saves.start(down.at[pl.ds(SEQ, SEQ)], o_back.at[pl.ds(TOK, SEQ)])
    base[...] = residual[0:SEQ] + down[0:SEQ]
    saves.start(base, o_base)
    saves.wait()


def emit(saves, block, places, axis, outs):
    for j, out in enumerate(outs):
        saves.start(block.at[places[axis, (0, 2, 3, 1)[j]]], out)


RINGS = [(x, z) for x in range(4) for z in range(4)]


def mlp_grads(
    places, cot, normed2, hidden, ggu, p0, p1, p2, p3, q0, q1, q2, q3,
    bp, bq, out_sems,
):
    saves = Saves(out_sems)

    @pl.loop(0, 2)
    def _(xh):
        at = pl.ds(pl.multiple_of(xh * 768, 256), 768)
        v = tn(hidden[:, at], cot[...]).astype(BF16)
        for z in range(4):
            for xl in range(2):
                r = 96 * (2 * z + xl)
                bp[2 * xh + xl, z, :, 0:D] = v[r : r + 64]
                bp[2 * xh + xl, z, 0:32, D:FC] = v[r + 64 : r + 96, 0:512]
                bp[2 * xh + xl, z, 32:64, D:FC] = v[r + 64 : r + 96, 512:1024]

    def put(block, order, first, to):
        v = tn(normed2[...], ggu[:, first : first + 768]).astype(BF16)
        for x, z in RINGS:
            for half in range(2):
                r = ring_rows(x, z) + 256 * half
                at = (x, z) if order else (z, x)
                block[(*at, slice(32 * half, 32 * half + 32), slice(to, to + 768))] = v[r : r + 32]

    put(bp, True, 0, FC)
    emit(saves, bp, places, 0, (p0, p1, p2, p3))
    for part in range(3):
        put(bq, False, 768 * (part + 1), 768 * part)
    emit(saves, bq, places, 2, (q0, q1, q2, q3))
    saves.wait()


def rec_backward(
    places, tok, cot, masks, gains, chans, other, i_back, i_residual, i_normed, i_merged, i_u, i_gate, i_conv, i_rate,
    i_inp, i_st, i_tables, wp0, wp1, wp2, wp3, wq0, wq1, wq2, wq3,
    o_residual, o_mine, o_theirs, p0, p1, p2, p3, q0, q1, q2, q3,
    wb, wog, part, residual, normed, merged, u_in, gate_in, conv_low, rate, inp, st_in, tables,
    coeff, grad_branch, gs, lam, rate_low, inp_low, direct, gmix, rolled, sums, mixed_part, own_residual, bp, bq,
    sems, in_sems, out_sems,
):
    ins = Saves(in_sems)
    for source, target in (
        (i_back.at[pl.ds(0, TOK)], part), (i_residual, residual), (i_merged, merged), (i_gate, gate_in), (i_st, st_in),
        (i_rate, rate), (i_inp, inp), (i_conv, conv_low), (i_tables, tables), (i_u, u_in), (i_normed, normed),
    ):
        ins.start(source, target)
    for j, p in enumerate((wp0, wp1, wp2, wp3)):
        og_copy(p, places, j, wog, sems.at[1])
    for j, (p, q) in enumerate(((wp0, wq0), (wp1, wq1), (wp2, wq2), (wp3, wq3))):
        p_copy(p, places, j, OG, PB, wb, 0, sems.at[0])
        q_copy(q, places, j, 0, QB, wb, PB, sems.at[0])
    saves = Saves(out_sems)
    sums[...] = jnp.zeros_like(sums)
    for copy in ins.copies[0:2]:
        copy.wait()
    for s in range(2):
        rows, theirs = slice(s * SEQ, (s + 1) * SEQ), slice((1 - s) * SEQ, (2 - s) * SEQ)
        grad, term = rms_back(part[rows] + other[theirs], residual[rows], gains[1:2])
        grad = cot[rows].astype(F32) + grad
        grad_branch[rows] = grad.astype(BF16)
        if s == 0:
            own_residual[...] = grad
            sums[9:10] = jnp.sum(term, axis=0, keepdims=True)
    saves.start(own_residual, o_residual)

    def put_og(b, first, v):
        x, z = (b // 8) * 2 + b % 2, (b // 2) % 4
        n = min(max(OG - first, 0), v.shape[1])
        if n:
            bp[x, z, 0:48, first : first + n] = v[:, :n]
        if n < v.shape[1]:
            to = first + n - OG
            for r in range(3):
                bp[x, z, 48:64, 384 * r + to : 384 * r + to + v.shape[1] - n] = v[16 * r : 16 * r + 16, n:]

    ins.copies[2].wait()
    v = tn(merged[...], grad_branch[...]).astype(BF16)
    for b in range(16):
        put_og(b, 0, v[48 * b : 48 * b + 48])
    landed(wog, sems.at[1])
    gs[...] = nt(grad_branch[...], wog[..., 0:D].reshape(RC, D))
    for copy in ins.copies[3:5]:
        copy.wait()

    @pl.loop(0, 6)
    def _(c):
        at = cols(c)
        act, act_grad = gelu_both(gate_in[:, at])
        g = gs[:, at]
        for s in range(2):
            rows = slice(s * SEQ, (s + 1) * SEQ)
            gmix[rows, pl.ds(pl.multiple_of(RC + c * LANES, LANES), LANES)] = (
                g[rows] * st_in[s, 8:, at] * act_grad[rows]
            ).astype(BF16)
        gs[:, at] = g * act

    for copy in ins.copies[5:8]:
        copy.wait()

    @pl.loop(0, 6)
    def _(c):
        at = cols(c)
        keep, starts = masks[0], masks[1]
        rg = jax.nn.sigmoid(rate[:, at] + chans[5:6, at])
        sd = jnp.exp(-8.0 * rg * chans[7:8, at])
        coeff[:, at] = (1.0 - starts) * (keep * sd + (1.0 - keep))

    row = lax.broadcasted_iota(jnp.int32, (8, RC), 0)

    def backward(n, carry):
        i = SEQ // 8 - 1 - n
        new = []
        for s in range(2):
            at = pl.ds(pl.multiple_of(s * SEQ + i * 8, 8), 8)
            own = coeff[at]
            later_a, later_lam = carry[s]
            a = jnp.where(row == 7, later_a, pltpu.roll(own, 7, 0))
            b = gs[at]
            for k in (1, 2, 4):
                here = row < 8 - k
                b = jnp.where(here, b + a * pltpu.roll(b, 8 - k, 0), b)
                a = jnp.where(here, a * pltpu.roll(a, 8 - k, 0), a)
            h = b + a * later_lam
            lam[at] = h
            new.append((own[0:1], h[0:1]))
        return tuple(new)

    zero = jnp.zeros((1, RC), F32)
    lax.fori_loop(0, SEQ // 8, backward, ((zero, zero), (zero, zero)))

    @pl.loop(0, 6)
    def _(c):
        at = cols(c)
        decay = chans[7:8, at]
        for s in range(2):
            rows = slice(s * SEQ, (s + 1) * SEQ)
            keep, starts = masks[0, rows], masks[1, rows]
            rg, ig, sd, q, root, scale = gates(
                rate[rows, at], inp[rows, at], chans[5:6, at], chans[6:7, at], decay, keep, starts
            )
            conv = conv_low[rows, at].astype(F32)
            l = lam[rows, at]
            common = l * keep
            grad_coeff = l * st_in[s, 7 : PAD - 1, at]
            direct[rows, at] = common * scale * ig
            d_ig = common * scale * conv
            d_scale = common * ig * conv
            d_sd = (1.0 - starts) * (grad_coeff * keep - d_scale * jnp.where(q > 0.001, sd / root, 0.0))
            d_log = d_sd * sd * -8.0
            d_rate = d_log * decay * rg * (1.0 - rg)
            d_inp = d_ig * ig * (1.0 - ig)
            rate_low[rows, at] = d_rate.astype(BF16)
            inp_low[rows, at] = d_inp.astype(BF16)
            for n, term in ((5, d_rate), (6, d_inp), (7, d_log * rg)):
                sums[n : n + 1, at] += jnp.sum(term, axis=0, keepdims=True)

    for copy in ins.copies[8:]:
        copy.wait()
    turn = turn_matrix()
    top, left = quarter_masks()
    for p in range(2):
        at = slice(2 * HS * p, 2 * HS * (p + 1))
        direct[:, at] += nt(rate_low[:, at], tables[2 * p]) + nt(inp_low[:, at], tables[2 * p + 1])
        dr = tn(conv_low[:, at], rate_low[:, at]).astype(BF16)
        di = tn(conv_low[:, at], inp_low[:, at]).astype(BF16)
        none = jnp.zeros_like(dr)
        straight = jnp.where(top, jnp.where(left, dr, none), jnp.where(left, none, di))
        crossed = jnp.where(top, jnp.where(left, di, none), jnp.where(left, none, dr))
        g = (straight.astype(F32) + nn(crossed, turn)).astype(BF16)
        for b in range(8):
            put_og(8 * p + b, D, g[48 * b : 48 * b + 48])

    rolled[:, SEQ:] = jnp.zeros((2, 8, LANES), F32)

    @pl.loop(0, 6)
    def _(c):
        at = cols(c)
        for s in range(2):
            rows = slice(s * SEQ, (s + 1) * SEQ)
            g = direct[rows, at]
            gu = chans[0:1, at] * g
            sums[4:5, at] += jnp.sum(g, axis=0, keepdims=True)
            sums[0:1, at] += jnp.sum(g * u_in[s, 8:, at], axis=0, keepdims=True)
            for k in range(1, 4):
                w = g * masks[1 + k, rows]
                sums[k : k + 1, at] += jnp.sum(w * u_in[s, 8 - k : PAD - k, at], axis=0, keepdims=True)
                rolled[s, 0:SEQ] = w
                gu = gu + chans[k : k + 1, at] * rolled[s, k : SEQ + k]
            gmix[rows, at] = (gu * masks[0, rows]).astype(BF16)

    v = jnp.concatenate([sums[0:8, 0:RC], jnp.zeros((LANES - 8, RC), F32)], axis=0).T.astype(BF16)
    for b in range(16):
        put_og(b, 1408, v[48 * b : 48 * b + 48])
    landed(wb, sems.at[0])

    v = tn(normed[...], gmix[:, 0:PB]).astype(BF16)
    for x, z in RINGS:
        for half in range(2):
            r = ring_rows(x, z) + 256 * half
            bp[x, z, 32 * half : 32 * half + 32, OG:EARLY] = v[r : r + 32]
    emit(saves, bp, places, 0, (p0, p1, p2, p3))
    mixed_part[...] = nt(gmix[...], rows_of(wb, 0, BRANCH))
    saves.start(mixed_part.at[pl.ds(0, SEQ)], o_mine)
    saves.start(mixed_part.at[pl.ds(SEQ, SEQ)], o_theirs)
    t = tok[...].astype(F32)
    sums[8:9] = jnp.sum(mixed_part[...] * (t * inv_rms(t)), axis=0, keepdims=True)
    v = jnp.concatenate([sums[8:16], jnp.zeros((LANES - 8, D), F32)], axis=0).T.astype(BF16)
    for x, z in RINGS:
        for half in range(2):
            r = ring_rows(x, z) + 256 * half
            bq[z, x, 32 * half : 32 * half + 32, QB:EARLY] = v[r : r + 32]

    v = tn(normed[...], gmix[:, PB:]).astype(BF16)
    for x, z in RINGS:
        for half in range(2):
            r = ring_rows(x, z) + 256 * half
            bq[z, x, 32 * half : 32 * half + 32, 0:QB] = v[r : r + 32]
    emit(saves, bq, places, 2, (q0, q1, q2, q3))
    saves.wait()


def load(sources, targets, sems):
    copies = Saves(sems)
    for source, target in zip(sources, targets):
        copies.start(source, target)
    copies.wait()


def join_sums(
    places, eo_p, eu_p, lo_p, lu_p, eo_q, eu_q, lo_q, lu_q,
    tp0, tp1, tp2, tp3, tq0, tq1, tq2, tq3,
    early, late, out, in_sems, out_sems,
):
    loads, saves = Saves(in_sems), Saves(out_sems)
    for n, (a, b, c, d) in enumerate(((eo_p, eu_p, lo_p, lu_p), (eo_q, eu_q, lo_q, lu_q))):
        for source, target in ((a, early.at[n, 0]), (b, early.at[n, 1]), (c, late.at[n, 0]), (d, late.at[n, 1])):
            loads.start(source, target)
    for n, (axis, outs) in enumerate(((2, (tp0, tp1, tp2, tp3)), (0, (tq0, tq1, tq2, tq3)))):
        for copy in loads.copies[4 * n : 4 * n + 4]:
            copy.wait()
        for j, target in enumerate(outs):
            at, to = places[axis, (0, 2, 3, 1)[j]], 4 * n + j
            out[to, :, 0:EARLY] = add(early[n, 0, at], early[n, 1, at])
            out[to, :, EARLY:] = add(late[n, 0, at], late[n, 1, at])
            saves.start(out.at[to], target)
    saves.wait()


def add(a, b):
    return (a.astype(F32) + b.astype(F32)).astype(BF16)


def half_sums(a_p, b_p, c_p, d_p, a_q, b_q, c_q, d_q, *rest):
    outs, (early, late, in_sems, out_sems) = rest[-8:-4], rest[-4:]
    loads, saves = Saves(in_sems), Saves(out_sems)
    for n, (a, b, c, d) in enumerate(((a_p, b_p, c_p, d_p), (a_q, b_q, c_q, d_q))):
        for source, target in ((a, early.at[n, 0]), (b, early.at[n, 1]), (c, late.at[n, 0]), (d, late.at[n, 1])):
            loads.start(source, target)
    for n in range(2):
        for i, v in enumerate((early, late)):
            loads.copies[4 * n + 2 * i].wait()
            loads.copies[4 * n + 2 * i + 1].wait()
            v[n, 0] = add(v[n, 0], v[n, 1])
            saves.start(v.at[n, 0], outs[2 * n + i])
    saves.wait()


def pass_on(a_p, f_p, a_q, f_q, *rest):
    o_p, o_q, v, in_sems, out_sems = rest[-5:]
    loads, saves = Saves(in_sems), Saves(out_sems)
    for i, source in enumerate((a_p, f_p, a_q, f_q)):
        loads.start(source, v.at[i])
    for n, out in enumerate((o_p, o_q)):
        loads.copies[2 * n].wait()
        loads.copies[2 * n + 1].wait()
        v[2 * n] = (v[2 * n].astype(F32) + v[2 * n + 1].astype(F32)).astype(BF16)
        saves.start(v.at[2 * n], out)
    saves.wait()


def cut(
    places, p0, p1, p2, q0, q1, q2,
    o0, o1, o2, o3,
    parts, sp, sq, sd, in_sems,
):
    load((p0, p1, p2, q0, q1, q2), [parts.at[i] for i in range(6)], in_sems)
    for n, out in enumerate((sp, sq)):
        out[...] = parts[3 * n].astype(F32) + parts[3 * n + 1].astype(F32) + parts[3 * n + 2].astype(F32)
    sd[0:64] = sp[:, EARLY : EARLY + D]
    sd[64:96, 0:512] = sp[0:32, EARLY + D : EARLY + FC]
    sd[64:96, 512:1024] = sp[32:64, EARLY + D : EARLY + FC]
    tail = jnp.concatenate([sp[48:64, 384 * r : 384 * r + 384] for r in range(3)], axis=0)
    og = jnp.concatenate([sp[0:48, 0:OG], tail], axis=1).astype(BF16)
    i = lax.broadcasted_iota(jnp.int32, (16, 48), 0)
    s = lax.broadcasted_iota(jnp.int32, (16, 48), 1)

    def two(rows):
        return jnp.concatenate(rows, axis=0).astype(BF16)

    for j, out in enumerate((o0, o1, o2, o3)):
        y = places[1, (0, 2, 3, 1)[j]]
        rows = [pl.ds(pl.multiple_of(32 * c + y * 8, 8), 8) for c in range(2)]
        out[:, 0:PB] = two([sp[r, OG:EARLY] for r in rows])
        out[:, PB : PB + PI] = two([sp[r, UNIT - PI :] for r in rows])
        out[:, PB + PI : DC] = two([sq[r] for r in rows])
        mine = jnp.where((s == i + y * 12) & (i < 12), 1.0, 0.0).astype(BF16)
        out[:, DC:DOWN] = nn(mine, og).astype(BF16)
        down = sd[pl.ds(pl.multiple_of(y * 24, 8), 24)]
        out[:, DOWN : DOWN + D] = down[0:16].astype(BF16)
        out[:, DOWN + D :] = two([down[16:24, 0:512], down[16:24, 512:]])


def finish(places, o0, o1, o2, o3, mine, theirs, out_grad, gate_grad, chan_grad, down_grad, v):
    v[...] = o0[...].astype(F32) + o1[...].astype(F32) + o2[...].astype(F32) + o3[...].astype(F32)
    core = places[3, 0]
    theirs[...] = v[pl.ds(pl.multiple_of((1 - core) * 8, 8), 8), 0:DC]
    mine[...] = v[pl.ds(pl.multiple_of(core * 8, 8), 8), 0:DC]
    out_grad[...] = v[0:12, DC : DC + D]
    gate_grad[...] = v[0:12, DC + D : DC + D + 384]
    chan_grad[...] = v[:, DC + D + 384 : DOWN].T[0:8]
    down_grad[0:16] = v[:, DOWN : DOWN + D]
    down_grad[16:24, 0:512] = v[0:8, DOWN + D :]
    down_grad[16:24, 512:] = v[8:16, DOWN + D :]


def unpack(places, mine, theirs, branch, inner, gains):
    def halves(ins):
        for c, v in enumerate(ins):
            for q in range(4):
                to = 768 * q + 384 * c
                if q == 0:
                    branch[:, to : to + PB] = v[:, 0:PB]
                    branch[:, to + PB : to + 384] = v[:, PB + PI : PB + PI + 128]
                else:
                    branch[:, to : to + 384] = v[:, PI + 384 * q : PI + 384 * q + 384]
                at = PB if q == 0 else DC - LATE + 768 * (q - 1)
                to = 1536 * q + 768 * c
                inner[:, to : to + 768] = v[:, at : at + 768]

    gains[...] = mine[:, DC - LATE - LANES : DC - LATE] + theirs[:, DC - LATE - LANES : DC - LATE]

    @pl.when(places[3, 0] == 0)
    def _():
        halves((mine, theirs))

    @pl.when(places[3, 0] == 1)
    def _():
        halves((theirs, mine))


VM, HB, SM, ANY = pltpu.VMEM, pltpu.HBM, pltpu.SMEM, pl.ANY


def kernel(body, ins, spaces, outs, scratch, mib, flops=0):
    moved = sum(v.size * v.dtype.itemsize for v in ins)
    ins = [pltpu.with_memory_space_constraint(v, HB) if s is HB else v for v, s in zip(ins, spaces)]
    return pl.pallas_call(
        body,
        out_shape=[HB(s, d) if at is HB else jax.ShapeDtypeStruct(s, d) for s, d, at in outs],
        in_specs=[pl.BlockSpec(memory_space=s) for s in spaces],
        out_specs=[pl.BlockSpec(memory_space=s) for _, _, s in outs],
        scratch_shapes=scratch,
        compiler_params=pltpu.CompilerParams(vmem_limit_bytes=mib * 2**20),
        cost_estimate=pl.CostEstimate(flops=flops, bytes_accessed=moved, transcendentals=0),
    )(*ins)


def shards(
    tokens, cotangent, segment, keep_mask, conv_state, lru_state, norm1_gain, conv_weight, lru_bias, decay_rate,
    gate_weight, branch_weight, out_weight, norm2_gain, mlp_in_weight, mlp_out_weight,
):
    here = my_place()
    core = here["core"]
    zero = jnp.zeros_like(core)
    places = jnp.stack(
        [jnp.stack(ring_places(axis, here)) for axis in "xyz"] + [jnp.stack([core, zero, zero, zero])]
    ).astype(jnp.int32)
    vmem, dma = pltpu.VMEM, pltpu.SemaphoreType.DMA

    tc = jnp.concatenate([tokens[0], cotangent[0]], axis=0)
    tc_other = swap(tc)
    marks = jnp.concatenate([segment, keep_mask], axis=1).astype(F32)
    states = jnp.concatenate([conv_state[0], lru_state], axis=0)
    sent = jnp.concatenate([core_half(states, 1 - core, 2), jnp.pad(marks, ((0, 0), (0, RC - 2 * SEQ)))], axis=0)
    sent = swap(sent)

    mine, theirs, own = kernel(
        pack,
        (places, branch_weight, mlp_in_weight, jnp.stack([norm1_gain, norm2_gain]), out_weight, gate_weight,
         jnp.concatenate([conv_weight, lru_bias, decay_rate[None]], axis=0), mlp_out_weight),
        [SM] + [VM] * 7,
        [((8, DC), BF16, VM)] * 2 + [((16, OWN - DC), BF16, VM)],
        [],
        8,
    )
    (block,) = kernel(join, (places, mine, swap(theirs), own), [SM] + [VM] * 3, [((16, OWN), BF16, VM)], [], 8)

    row = ((64, UNIT), BF16)
    unit_of = ((2, 32, UNIT), BF16)
    p, q = kernel(
        unit,
        (places, *ring_direct(block, "y"), tc_other, sent),
        [SM] + [VM] * 4 + [ANY] * 2,
        [(*unit_of, HB)] * 2,
        [vmem(*row), vmem(*row), vmem((64, DC), F32), vmem((96, D), F32), dma((4,))],
        16,
    )
    early, late = (4, 64, EARLY), (4, 64, LATE)
    stack = ((4, 64, UNIT), BF16)
    pe, qe, pl_, ql = kernel(
        planes,
        (places, *ring_both(p, "z"), *ring_both(q, "x")),
        [SM] + [HB, HB, HB, ANY, HB, ANY, HB, ANY],
        [(v, BF16, HB) for n in (EARLY, LATE) for v in ((2, 4, 32, n), (2, 2, 2, 32, n))],
        [vmem((2, 4, 32, UNIT), BF16), vmem((2, 2, 2, 32, UNIT), BF16), dma((8,)), dma((4,))],
        8,
    )
    pe, qe, pl_, ql = ring_both(pe, "x"), ring_both(qe, "z"), ring_both(pl_, "x"), ring_both(ql, "z")

    tok = jnp.concatenate([tc[:SEQ], tc_other[:SEQ]], axis=0)
    cot = jnp.concatenate([tc[SEQ:], tc_other[SEQ:]], axis=0)
    states = jnp.stack([core_half(states, core, 2), sent[:4]])
    marks = jnp.concatenate([marks, sent[4:, : 2 * SEQ]], axis=0)
    seg, keep = marks[:, :SEQ], marks[:, SEQ:]
    earlier = [jnp.concatenate([jnp.repeat(seg[:, :1], k, axis=1), seg[:, : SEQ - k]], axis=1) for k in range(1, 4)]
    masks = jnp.stack([keep, (earlier[0] != seg).astype(F32)] + [(e == seg).astype(F32) for e in earlier])
    masks = jnp.broadcast_to(masks.reshape(5, TOK, 1), (5, TOK, LANES))

    wide, wide_low = ((TOK, D), F32), ((TOK, D), BF16)
    act, act_low, padded = ((TOK, RC), F32), ((TOK, RC), BF16), ((2, PAD, RC), F32)
    tables = ((4, 2 * HS, 2 * HS), BF16)
    saved = [wide_low, act_low, padded, act, act_low, act, act, padded, tables]
    part, finals, gains, chans, normed, merged, u, gate_in, conv_low, rate, inp, st, table = kernel(
        rec_forward,
        (places, tok, masks, states[:, :3], states[:, 3:], *pe, *qe),
        [SM] + [VM] * 4 + [HB] * 8,
        [((TOK + 8, D), F32, VM), ((4, RC), F32, VM), ((8, D), F32, VM), ((8, RC), F32, VM)]
        + [(*v, HB) for v in saved],
        [vmem((*ROWS, PB + EARLY), BF16), vmem((*OG_ROWS, OGC), BF16)]
        + [vmem(*v) for v in saved + [act, act]]
        + [dma((2,)), dma((9,))],
        32,
        2 * TOK * (D * BRANCH + RC * (D + 768)),
    )
    half = ((SEQ, D), F32)
    other = swap(part)
    normed2, hidden, ggu, residual, base, back = kernel(
        mlp,
        (places, tok, cot, part, other, gains, *pl_, *ql),
        [SM] + [VM] * 5 + [ANY] * 8,
        [(*wide_low, VM), ((TOK, FC), BF16, VM), ((TOK, INNER), BF16, VM)] + [(*v, HB) for v in (wide, half, ((TOK + SEQ, D), F32))],
        [vmem((*ROWS, INNER), BF16), vmem((*DOWN_ROWS, D), BF16)]
        + [vmem(*v) for v in (wide, wide, wide, half)]
        + [dma((2,)), dma((4,))],
        32,
        2 * TOK * D * (2 * INNER + 2 * FC),
    )
    back_other = swap(back)
    outs = kernel(
        mlp_grads,
        (places, cot, normed2, hidden, ggu),
        [SM] + [VM] * 4,
        [(late, BF16, HB)] * 8,
        [vmem((4,) + late, BF16), vmem((4,) + late, BF16), dma((8,))],
        32,
        2 * TOK * D * (INNER + FC),
    )
    lp, lq = outs[:4], outs[4:]
    far = send(lp[2], along("x", 1)), send(lq[2], along("z", 1))
    down = send(lp[3], along("x", -1)), send(lq[3], along("z", -1))
    outs = kernel(
        rec_backward,
        (places, tok, cot, masks, gains, chans, back_other, back, residual, normed, merged, u, gate_in, conv_low, rate,
         inp, st, table, *pe, *qe),
        [SM] + [VM] * 6 + [HB] * 19,
        [(*v, HB) for v in (half, half, half)] + [(early, BF16, HB)] * 8,
        [vmem((*ROWS, BRANCH), BF16), vmem((*OG_ROWS, OGC), BF16)]
        + [vmem(*v) for v in (wide, wide, wide_low, act_low, padded, act, act_low, act, act, padded, tables)]
        + [vmem(*v) for v in (act, wide_low, act, act, act_low, act_low, act, ((TOK, BRANCH), BF16))]
        + [vmem((2, PAD, LANES), F32), vmem((16, D), F32), vmem(*wide), vmem(*half)]
        + [vmem((4,) + early, BF16), vmem((4,) + early, BF16), dma((2,)), dma((11,)), dma((11,))],
        48,
        2 * TOK * D * (2 * BRANCH + 2 * RC),
    )
    grad_residual, mixed_mine, mixed_theirs = outs[:3]
    ep, eq = outs[3:7], outs[7:]
    def passed(terms, far, routes, shape, until, spaces):
        (p, q), (a, b) = terms, routes
        up = kernel(
            pass_on,
            (p[1], far[0], q[1], far[1], *until),
            [HB] * 4 + spaces,
            [(shape, BF16, HB)] * 2,
            [vmem((4,) + shape, BF16), dma((4,)), dma((2,))],
            16,
        )
        return send(up[0], along(a, 1)), send(up[1], along(b, 1))

    early_far = send(ep[2], along("x", 1)), send(eq[2], along("z", 1))
    early_down = send(ep[3], along("x", -1)), send(eq[3], along("z", -1))
    late_up = passed((lp, lq), far, "xz", late, (ep[0], *down), [HB] * 3)
    early_up = passed((ep, eq), early_far, "xz", early, early_down, [ANY] * 2)

    summed = kernel(
        half_sums,
        (ep[0], early_down[0], lp[0], down[0], eq[0], early_down[1], lq[0], down[1]),
        [HB] * 8,
        [(early, BF16, HB), (late, BF16, HB)] * 2,
        [vmem((2, 2) + early, BF16), vmem((2, 2) + late, BF16), dma((8,)), dma((4,))],
        24,
    )
    outs = kernel(
        join_sums,
        (places, summed[0], early_up[0], summed[1], late_up[0], summed[2], early_up[1], summed[3], late_up[1]),
        [SM] + [HB] * 8,
        [(*row, HB)] * 8,
        [vmem((2, 2) + early, BF16), vmem((2, 2) + late, BF16), vmem((8, 64, UNIT), BF16), dma((8,)), dma((8,))],
        32,
    )
    tp, tq = outs[:4], outs[4:]
    far = send(tp[2], along("z", 1)), send(tq[2], along("x", 1))
    down = send(tp[3], along("z", -1)), send(tq[3], along("x", -1))
    up = kernel(
        pass_on,
        (tp[1], far[0], tq[1], far[1], *down),
        [HB] * 3 + [ANY] * 3,
        [(*row, HB)] * 2,
        [vmem((4, 64, UNIT), BF16), dma((4,)), dma((2,))],
        8,
    )
    up = send(up[0], along("z", 1)), send(up[1], along("x", 1))
    sums = kernel(
        cut,
        (places, tp[0], down[0], up[0], tq[0], down[1], up[1]),
        [SM] + [HB, HB, ANY] * 2,
        [((16, OWN), BF16, VM)] * 4,
        [vmem((6, 64, UNIT), BF16), vmem((64, UNIT), F32), vmem((64, UNIT), F32), vmem((96, D), F32), dma((6,))],
        16,
    )
    mine, theirs, out_grad, gate_grad, chan_grad, down_grad = kernel(
        finish,
        (places, *terms_direct(sums, "y")),
        [SM] + [VM] * 4,
        [((8, DC), F32, VM)] * 2 + [(s, F32, VM) for s in ((12, D), (12, 384), (8, 16), (24, D))],
        [vmem((16, OWN), F32)],
        8,
    )
    branch_grad, in_grad, gain_grads = kernel(
        unpack,
        (places, mine, swap(theirs)),
        [SM] + [VM] * 2,
        [((8, 2 * R), F32, VM), ((8, 2 * F), F32, VM), ((8, LANES), F32, VM)],
        [],
        8,
    )

    output = (base + back_other[TOK:]).astype(BF16)
    grad, _ = rms_back(mixed_mine + swap(mixed_theirs), tok[:SEQ].astype(F32), gains[0])
    input_grad = (grad_residual + grad).astype(BF16)
    theirs = other[TOK : TOK + 4, :RC]
    finals = jnp.stack(
        [v.reshape(1, 4, 2, 384) for v in (jnp.where(core == 0, finals, theirs), jnp.where(core == 0, theirs, finals))],
        axis=3,
    ).reshape(1, 4, R)
    return (
        output[None],
        input_grad[None],
        finals[:, :3],
        finals[:, 3],
        gain_grads[:, 0],
        chan_grad[:4, :12],
        chan_grad[4:7, :12],
        chan_grad[7, :12],
        gate_grad,
        branch_grad,
        out_grad,
        gain_grads[:, 1],
        in_grad,
        down_grad,
    )


def solution(mesh):
    rows, last = P(AXES), P(None, AXES)
    specs = [rows] * 6 + [rows, last, last] + [rows] * 7
    outs = [rows] * 4 + [rows, last, last] + [rows] * 7
    return jax.shard_map(
        shards, mesh=mesh, in_specs=tuple(specs), out_specs=tuple(outs), check_vma=False
    )
```

```python
import jax
import jax.numpy as jnp
from jax import lax
from jax.experimental import pallas as pl
from jax.experimental.pallas import tpu as pltpu
from jax.sharding import PartitionSpec as P

AXES = ("dp", "fsdp")
D, R, F, SEQ = 1024, 1536, 3072, 128
RC, FC = R // 2, F // 2
HS = 192
F32, BF16 = jnp.float32, jnp.bfloat16
BRANCH, INNER = 2 * RC, 2 * FC
TOK, PAD, LANES = 2 * SEQ, SEQ + 8, 128

EARLY, LATE = 1408, 2304
UNIT = EARLY + LATE
OG, PB, PI, QB = 1152, 256, 768, 1280
DC = PB + PI + UNIT
OGC = 1536
DOWN = DC + OGC
OWN = DOWN + D + D // 2


def place_of(device):
    outer, inner = divmod(device, 32)
    x_hi, core = divmod(outer, 2)
    z, rest = divmod(inner, 8)
    x_lo, y = divmod(rest, 4)
    return dict(x=x_hi * 2 + x_lo, y=y, z=z, core=core)


def device_at(x, y, z, core):
    return ((x // 2) * 2 + core) * 32 + z * 8 + (x % 2) * 4 + y


def pairs(move):
    return [(d, device_at(**move(place_of(d)))) for d in range(128)]


def along(axis, steps):
    def move(p):
        sign = 1 if p["core"] == 0 else -1
        return {**p, axis: (p[axis] + sign * steps) % 4}

    return pairs(move)


def other_core(p):
    return {**p, "core": 1 - p["core"]}


def partner(axis, turn):
    def move(p):
        i = p[axis]
        return {**p, axis: i ^ 1 if (p["core"] + turn) % 2 == 0 else 3 - i}

    return pairs(move)


def opposite(axis):
    return pairs(lambda p: {**p, axis: (p[axis] + 2) % 4})


def send(value, route):
    return lax.ppermute(value, AXES, route)


def swap(value):
    return send(value, pairs(other_core))


def my_place():
    device = lax.axis_index(AXES)
    outer, inner = device // 32, device % 32
    return dict(x=(outer // 2) * 2 + (inner // 4) % 2, y=inner % 4, z=inner // 8, core=outer % 2)


def ring_places(axis, here):
    sign, at = 1 - 2 * here["core"], here[axis]
    return [at, (at - sign) % 4, (at + sign) % 4, (at + 2) % 4]


def ring(block, axis):
    one = send(block, along(axis, 1))
    two = send(one, along(axis, 1))
    return block, one, send(two, along(axis, 1)), two


def ring_both(block, axis):
    up, down = send(block, along(axis, 1)), send(block, along(axis, -1))
    return block, up, down, send(up, along(axis, 1))


def pair_places(axis, here):
    i, odd = here[axis], here["core"] == 1
    by_one, by_ends = i + 1 - 2 * (i % 2), 3 - i
    return [i, jnp.where(odd, by_one, by_ends), jnp.where(odd, by_ends, by_one), (i + 2) % 4]


def ring_direct(block, axis):
    return block, send(block, along(axis, 1)), send(block, along(axis, -1)), send(block, opposite(axis))


def terms_direct(terms, axis):
    own, ahead, far, behind = terms
    return own, send(ahead, along(axis, 1)), send(far, opposite(axis)), send(behind, along(axis, -1))


def total(*terms):
    out = terms[0].astype(F32)
    for term in terms[1:]:
        out = out + term.astype(F32)
    return out.astype(BF16)


def core_half(array, core, blocks):
    v = array.reshape(array.shape[:-1] + (blocks, 2, array.shape[-1] // (2 * blocks)))
    v = lax.dynamic_index_in_dim(v, core, v.ndim - 2, keepdims=False)
    return v.reshape(array.shape[:-1] + (array.shape[-1] // 2,))


def dot(a, b, dims):
    return lax.dot_general(a, b, (dims, ((), ())), preferred_element_type=F32)


def nn(a, b):
    return dot(a, b, ((1,), (0,)))


def nt(a, b):
    return dot(a, b, ((1,), (1,)))


def tn(a, b):
    return dot(a, b, ((0,), (0,)))


def inv_rms(v):
    return lax.rsqrt(jnp.mean(v * v, axis=-1, keepdims=True) + 1e-6)


def rms_back(grad, v, gain):
    s = inv_rms(v)
    n = v * s
    g2 = grad * gain
    return s * (g2 - n * jnp.mean(g2 * n, axis=-1, keepdims=True)), grad * n


C0, C1 = 0.7978845608028654, 0.044715


def gelu_both(a):
    t = jnp.tanh(C0 * (a + C1 * (a * a * a)))
    half = 0.5 * (1.0 + t)
    return a * half, half + 0.5 * a * (1.0 - t * t) * (C0 * (1.0 + 3.0 * C1 * (a * a)))


def gates(rate, inp, bias1, bias2, decay, keep, starts):
    rg = jax.nn.sigmoid(rate + bias1)
    ig = jax.nn.sigmoid(inp + bias2)
    sd = jnp.exp(-8.0 * rg * decay)
    q = 1.0 - sd * sd
    root = jnp.sqrt(jnp.maximum(q, 0.001))
    scale = starts + (1.0 - starts) * root
    return rg, ig, sd, q, root, scale


def cols(c):
    return pl.ds(pl.multiple_of(c * LANES, LANES), LANES)


class Saves:
    def __init__(self, sem):
        self.sem, self.copies = sem, []

    def start(self, source, target):
        self.copies.append(pltpu.make_async_copy(source, target, self.sem.at[len(self.copies)]))
        self.copies[-1].start()

    def wait(self):
        for copy in self.copies:
            copy.wait()


def pick(rows, where):
    return jnp.where(lax.broadcasted_iota(jnp.int32, (rows, where.shape[1]), 0) == where, 1.0, 0.0).astype(BF16)


def stand(values, rows):
    v = values.astype(F32)
    i = lax.broadcasted_iota(jnp.int32, (rows, v.shape[1]), 0)
    j = lax.broadcasted_iota(jnp.int32, (rows, v.shape[1]), 1)
    lane = lax.broadcasted_iota(jnp.int32, (rows, LANES), 1)
    out = jnp.zeros((rows, LANES), F32)
    for n in range(v.shape[0]):
        column = jnp.sum(jnp.where(i == j, v[n : n + 1], 0.0), axis=1, keepdims=True)
        out = out + jnp.where(lane == n, column, 0.0)
    return out


def load(sources, targets, sems):
    copies = Saves(sems)
    for source, target in zip(sources, targets):
        copies.start(source, target)
    copies.wait()


def pack(
    places, i_branch, i_inner, gain, i_out, i_gate, perchan, i_down, mine, theirs, own,
    branch, inner, out, gate, down, sems,
):
    load((i_branch, i_inner, i_out, i_gate, i_down), (branch, inner, out, gate, down), sems)

    gains = stand(gain[...], 8).astype(BF16)

    def halves(outs):
        for c, to_core in enumerate(outs):
            for q in range(4):
                v = branch[:, 768 * q + 384 * c : 768 * q + 384 * c + 384]
                if q == 0:
                    to_core[:, 0:PB] = v[:, 0:PB]
                    to_core[:, PB + PI : PB + PI + 128] = v[:, PB:]
                else:
                    to_core[:, PI + 384 * q : PI + 384 * q + 384] = v
                v = inner[:, 1536 * q + 768 * c : 1536 * q + 768 * c + 768]
                to = PB if q == 0 else DC - LATE + 768 * (q - 1)
                to_core[:, to : to + 768] = v
            tile = DC - LATE - LANES
            to_core[:, tile : tile + LANES] = gains

    @pl.when(places[3, 0] == 0)
    def _():
        halves((mine, theirs))

    @pl.when(places[3, 0] == 1)
    def _():
        halves((theirs, mine))

    own[...] = jnp.zeros_like(own)
    own[0:12, 0:D] = out[...]
    own[0:12, D : D + 384] = gate[...]
    own[:, 1408:OGC] = stand(perchan[...], 16).astype(BF16)
    own[:, OGC : OGC + D] = down[0:16]
    own[:, OGC + D :] = jnp.concatenate(
        [down[16:24, 0:512].astype(F32), down[16:24, 512:].astype(F32)], axis=0
    ).astype(BF16)


def join(places, mine, theirs, own, block):
    def rows(low, high):
        block[:, 0:DC] = jnp.concatenate([low[...].astype(F32), high[...].astype(F32)], axis=0).astype(BF16)

    @pl.when(places[3, 0] == 0)
    def _():
        rows(mine, theirs)

    @pl.when(places[3, 0] == 1)
    def _():
        rows(theirs, mine)

    block[:, DC:] = own[...]


def unit(places, p0, p1, p2, p3, *rest):
    o_p, o_q, p, q, d, dn, sems = rest[-7:]
    ogs = []
    s = lax.broadcasted_iota(jnp.int32, (1, 64), 1)
    y = jnp.zeros((1, 64), jnp.int32)
    for j, piece in enumerate((p0, p1, p2, p3)):
        at = places[1, j]
        y = jnp.where(s // 16 == j, at, y)
        v = piece[:, 0:DC].astype(F32)
        for c in range(2):
            d[pl.ds(pl.multiple_of(c * 32 + at * 8, 8), 8)] = v[8 * c : 8 * c + 8]
        ogs.append(piece[:, DC:DOWN])
        v = piece[:, DOWN:].astype(F32)
        dn[pl.ds(pl.multiple_of(at * 24, 8), 16)] = v[:, 0:D]
        for h in range(2):
            dn[pl.ds(pl.multiple_of(at * 24 + 16, 8), 8), 512 * h : 512 * h + 512] = v[8 * h : 8 * h + 8, D:]
    saves = Saves(sems)
    q[...] = d[:, PB + PI :].astype(BF16)
    for c in range(2):
        saves.start(q.at[pl.ds(32 * c, 32)], o_q.at[c])
    p[:, OG:EARLY] = d[:, 0:PB].astype(BF16)
    p[:, UNIT - PI :] = d[:, PB : PB + PI].astype(BF16)
    i = s % 16
    og = nn(pick(48, jnp.where(i < 12, y * 12 + i, 64)), jnp.concatenate(ogs, axis=0)).astype(BF16)
    p[0:48, 0:OG] = og[:, 0:OG]
    for r in range(3):
        p[48:64, 384 * r : 384 * r + 384] = og[16 * r : 16 * r + 16, OG:]
    p[:, EARLY : EARLY + D] = dn[0:64].astype(BF16)
    p[0:32, EARLY + D : EARLY + FC] = dn[64:96, 0:512].astype(BF16)
    p[32:64, EARLY + D : EARLY + FC] = dn[64:96, 512:1024].astype(BF16)
    for c in range(2):
        saves.start(p.at[pl.ds(32 * c, 32)], o_p.at[c])
    saves.wait()


def planes(which):
    def body(places, *refs):
        n = len(which)
        (o_pe, o_qe, o_pl, o_ql), v, in_sems, out_sems = refs[-7:-3], *refs[-3:]
        loads, saves = Saves(in_sems), Saves(out_sems)
        for i, piece in enumerate(refs[: 2 * n]):
            loads.start(piece, v.at[i])
        for i in range(2 * n):
            loads.copies[i].wait()
            j = which[i % n]
            x = places[0, j]
            for first, count, p, q in ((0, EARLY, o_pe, o_qe), (EARLY, LATE, o_pl, o_ql)):
                target = p.at[:, places[2, j]] if i < n else q.at[x // 2, :, x % 2]
                saves.start(v.at[i, :, :, pl.ds(first, count)], target)
        saves.wait()

    return body


ROWS = (2, 2, 4, 2, 32)
OG_ROWS, DOWN_ROWS = (2, 4, 2, 48), (2, 4, 2, 96)


def ring_rows(x, z):
    return (x // 2) * 512 + z * 64 + (x % 2) * 32


def p_copy(piece, places, j, first, count, block, to, sem):
    x = places[0, j]
    target = block.at[x // 2, :, :, x % 2, :, pl.ds(to, count)]
    pltpu.make_async_copy(piece.at[..., pl.ds(first, count)], target, sem).start()


def q_copy(piece, places, j, first, count, block, to, sem):
    target = block.at[:, :, places[2, j], :, :, pl.ds(to, count)]
    pltpu.make_async_copy(piece.at[..., pl.ds(first, count)], target, sem).start()


def og_copy(piece, places, j, block, sem):
    x = places[0, j]
    block = block.at[x // 2, :, x % 2]
    for source, target in (
        (piece.at[0, :, :, pl.ds(0, OG)], block.at[:, pl.ds(0, 32), pl.ds(0, OG)]),
        (piece.at[1, :, pl.ds(0, 16), pl.ds(0, OG)], block.at[:, pl.ds(32, 16), pl.ds(0, OG)]),
    ):
        pltpu.make_async_copy(source, target, sem).start()
    for r in range(3):
        pltpu.make_async_copy(
            piece.at[1, :, pl.ds(16, 16), pl.ds(384 * r, 384)], block.at[:, pl.ds(16 * r, 16), pl.ds(OG, 384)], sem
        ).start()


def down_copy(piece, places, j, block, sem):
    x = places[0, j]
    block = block.at[x // 2, :, x % 2]
    for h in range(2):
        pltpu.make_async_copy(piece.at[h, :, :, pl.ds(0, D)], block.at[:, pl.ds(32 * h, 32)], sem).start()
        pltpu.make_async_copy(
            piece.at[h, :, :, pl.ds(D, 512)], block.at[:, pl.ds(64, 32), pl.ds(512 * h, 512)], sem
        ).start()


def rows_of(block, first, count):
    return block[..., first : first + count].reshape(D, count)


def landed(block, sem):
    pltpu.make_async_copy(block, block, sem).wait()


def turn_matrix():
    i = lax.broadcasted_iota(jnp.int32, (2 * HS, 2 * HS), 0)
    j = lax.broadcasted_iota(jnp.int32, (2 * HS, 2 * HS), 1)
    return jnp.where((i == j + HS) | (j == i + HS), 1.0, 0.0).astype(BF16)


def quarter_masks():
    i = lax.broadcasted_iota(jnp.int32, (2 * HS, 2 * HS), 0) < HS
    j = lax.broadcasted_iota(jnp.int32, (2 * HS, 2 * HS), 1) < HS
    return i, j


def rec_forward(
    places, tok, masks, conv_before, lru_before, p0, p1, p2, p3, q0, q1, q2, q3,
    part, finals, gains, chans, o_normed, o_merged, o_u, o_gate, o_conv, o_rate, o_inp, o_st, o_tables,
    wb, wog, normed, merged, u, gate_in, conv_low, rate, inp, st, tables, coeff, drive, sems, out_sems,
):
    for j, (p, q) in enumerate(((p0, q0), (p1, q1), (p2, q2), (p3, q3))):
        p_copy(p, places, j, OG, PB, wb, 0, sems.at[0])
        q_copy(q, places, j, 0, EARLY, wb, PB, sems.at[0])
    for j, p in enumerate((p0, p1, p2, p3)):
        og_copy(p, places, j, wog, sems.at[1])
    saves = Saves(out_sems)
    t = tok[...].astype(F32)
    scaled = t * inv_rms(t)
    landed(wb, sems.at[0])
    gains[...] = rows_of(wb, BRANCH, LANES).astype(F32).T[:8]
    normed[...] = (scaled * gains[0:1]).astype(BF16)
    saves.start(normed, o_normed)
    for s in range(2):
        u[s, 0:8] = jnp.zeros((8, RC), F32)
        u[s, 5:8] = conv_before[s]
        st[s, 0:8] = jnp.zeros((8, RC), F32)
        st[s, 7:8] = lru_before[s]

    v = nn(normed[...], rows_of(wb, 0, RC))
    for s in range(2):
        rows = slice(s * SEQ, (s + 1) * SEQ)
        for c in range(6):
            u[s, 8:, LANES * c : LANES * c + LANES] = v[rows, LANES * c : LANES * c + LANES] * masks[0, rows]

    saves.start(u, o_u)

    gate_in[...] = nn(normed[...], rows_of(wb, RC, RC))

    saves.start(gate_in, o_gate)
    landed(wog, sems.at[1])
    chans[...] = wog[..., 1408:].reshape(RC, LANES).astype(F32).T[:8]

    @pl.loop(0, 6)
    def _(c):
        at = cols(c)
        for s in range(2):
            rows = slice(s * SEQ, (s + 1) * SEQ)
            v = chans[4:5, at] + chans[0:1, at] * u[s, 8:, at]
            for k in range(1, 4):
                v = v + chans[k : k + 1, at] * (u[s, 8 - k : PAD - k, at] * masks[1 + k, rows])
            conv_low[rows, at] = v.astype(BF16)

    saves.start(conv_low, o_conv)
    turn = turn_matrix()
    top, left = quarter_masks()
    for p in range(2):
        g = wog[p, :, :, :, D : D + 384].reshape(2 * HS, 2 * HS)
        turned = nn(g, turn).astype(BF16)
        zero = jnp.zeros_like(g)
        tables[2 * p] = jnp.where(left, jnp.where(top, g, zero), jnp.where(top, zero, turned))
        tables[2 * p + 1] = jnp.where(left, jnp.where(top, turned, zero), jnp.where(top, zero, g))
        at = slice(2 * HS * p, 2 * HS * (p + 1))
        rate[:, at] = nn(conv_low[:, at], tables[2 * p])
        inp[:, at] = nn(conv_low[:, at], tables[2 * p + 1])
    saves.start(tables, o_tables)
    saves.start(rate, o_rate)
    saves.start(inp, o_inp)

    @pl.loop(0, 6)
    def _(c):
        at = cols(c)
        keep, starts = masks[0], masks[1]
        _, ig, sd, _, _, scale = gates(
            rate[:, at], inp[:, at], chans[5:6, at], chans[6:7, at], chans[7:8, at], keep, starts
        )
        coeff[:, at] = (1.0 - starts) * (keep * sd + (1.0 - keep))
        drive[:, at] = keep * scale * ig * conv_low[:, at].astype(F32)

    row = lax.broadcasted_iota(jnp.int32, (8, RC), 0)

    def forward(i, carry):
        new = []
        for s in range(2):
            at = pl.ds(pl.multiple_of(s * SEQ + i * 8, 8), 8)
            a, b = coeff[at], drive[at]
            for k in (1, 2, 4):
                later = row >= k
                b = jnp.where(later, a * pltpu.roll(b, k, 0) + b, b)
                a = jnp.where(later, a * pltpu.roll(a, k, 0), a)
            h = a * carry[s] + b
            st[s, pl.ds(pl.multiple_of(8 + i * 8, 8), 8)] = h
            new.append(h[7:8])
        return tuple(new)

    last = lax.fori_loop(0, SEQ // 8, forward, (lru_before[0], lru_before[1]))
    saves.start(st, o_st)
    part[TOK:] = jnp.zeros((8, D), F32)
    part[TOK : TOK + 3, 0:RC] = u[1, PAD - 3 :]
    part[TOK + 3 : TOK + 4, 0:RC] = last[1]
    finals[0:3] = u[0, PAD - 3 :]
    finals[3:4] = last[0]

    @pl.loop(0, 6)
    def _(c):
        at = cols(c)
        act, _ = gelu_both(gate_in[:, at])
        for s in range(2):
            rows = slice(s * SEQ, (s + 1) * SEQ)
            merged[rows, at] = (st[s, 8:, at] * act[rows]).astype(BF16)

    saves.start(merged, o_merged)

    part[0:TOK] = nn(merged[...], wog[..., 0:D].reshape(RC, D))

    saves.wait()


def mlp_norm(tok, part, other, gains, normed2, own, o_residual, residual, sem):
    for s in range(2):
        rows, theirs = slice(s * SEQ, (s + 1) * SEQ), slice((1 - s) * SEQ, (2 - s) * SEQ)
        v = tok[rows].astype(F32) + (part[rows] + other[theirs])
        residual[rows] = v
        normed2[rows] = (v * inv_rms(v) * gains[1:2]).astype(BF16)
    copy = pltpu.make_async_copy(residual, o_residual, sem)
    copy.start()
    own[...] = residual[0:SEQ]
    copy.wait()


def mlp(
    places, cot, normed2, own, p0, p1, p2, p3, q0, q1, q2, q3,
    hidden, ggu, o_base, o_back,
    win, wdown, down, back, base, sems, out_sems,
):
    for j, (p, q) in enumerate(((p0, q0), (p1, q1), (p2, q2), (p3, q3))):
        p_copy(p, places, j, FC, PI, win, 0, sems.at[0])
        q_copy(q, places, j, 0, LATE, win, PI, sems.at[0])
    for j, p in enumerate((p0, p1, p2, p3)):
        down_copy(p, places, j, wdown, sems.at[1])
    saves = Saves(out_sems)
    down[...] = jnp.zeros_like(down)
    back[...] = jnp.zeros_like(back)
    landed(win, sems.at[0])
    for c in range(2):
        at, up = slice(768 * c, 768 * c + 768), slice(FC + 768 * c, FC + 768 * c + 768)
        wa, wu = rows_of(win, 768 * c, 768), rows_of(win, FC + 768 * c, 768)
        a = nn(normed2[...], wa)
        b = nn(normed2[...], wu)
        ga, da = gelu_both(a)
        h = (ga * b).astype(BF16)
        hidden[:, at] = h
        if c == 0:
            landed(wdown, sems.at[1])
        wd = wdown[c].reshape(768, D)
        gh = nt(cot[...], wd)
        gg_a = (gh * b * da).astype(BF16)
        gg_b = (gh * ga).astype(BF16)
        ggu[:, at] = gg_a
        ggu[:, up] = gg_b
        down[...] += nn(h, wd)
        back[...] += nt(gg_a, wa) + nt(gg_b, wu)

    saves.start(back, o_back.at[pl.ds(0, TOK)])
    saves.start(down.at[pl.ds(SEQ, SEQ)], o_back.at[pl.ds(TOK, SEQ)])
    base[...] = own[...] + down[0:SEQ]
    saves.start(base, o_base)
    saves.wait()


def emit(saves, block, places, axis, outs):
    for j in range(4):
        saves.start(block.at[places[4 + axis, j]], outs[j // 2].at[j % 2])


RINGS = [(x, z) for x in range(4) for z in range(4)]


def emit_columns(saves, block, places, axis, outs, first, count):
    for j in range(4):
        columns = pl.ds(first, count)
        saves.start(block.at[places[4 + axis, j], :, :, columns], outs[j // 2].at[j % 2, :, :, columns])


def mlp_grads(
    places, cot, normed2, hidden, ggu, p0, p1, q0, q1,
    bp, bq, out_sems,
):
    saves = Saves(out_sems)
    for xh in range(2):
        v = tn(hidden[:, 768 * xh : 768 * xh + 768], cot[...]).astype(BF16)
        for z in range(4):
            for xl in range(2):
                r = 96 * (2 * z + xl)
                bp[2 * xh + xl, z, :, 0:D] = v[r : r + 64]
                bp[2 * xh + xl, z, 0:32, D:FC] = v[r + 64 : r + 96, 0:512]
                bp[2 * xh + xl, z, 32:64, D:FC] = v[r + 64 : r + 96, 512:1024]
    emit_columns(saves, bp, places, 0, (p0, p1), 0, FC)

    def put(block, order, first, to):
        v = tn(normed2[...], ggu[:, first : first + 768]).astype(BF16)
        for x, z in RINGS:
            for half in range(2):
                r = ring_rows(x, z) + 256 * half
                at = (x, z) if order else (z, x)
                block[(*at, slice(32 * half, 32 * half + 32), slice(to, to + 768))] = v[r : r + 32]

    put(bp, True, 0, FC)
    emit_columns(saves, bp, places, 0, (p0, p1), FC, PI)
    for part in range(3):
        put(bq, False, 768 * (part + 1), 768 * part)
        emit_columns(saves, bq, places, 2, (q0, q1), 768 * part, 768)
    saves.wait()


def rec_backward(
    places, tok, cot, masks, gains, chans, other, i_back, i_residual, i_normed, i_merged, i_u, i_gate, i_conv, i_rate,
    i_inp, i_st, i_tables, wp0, wp1, wp2, wp3, wq0, wq1, wq2, wq3,
    o_residual, o_mine, o_theirs, p0, p1, q0, q1,
    wb, wog, part, residual, normed, merged, u_in, gate_in, conv_low, rate, inp, st_in, tables,
    coeff, grad_branch, gs, lam, rate_low, inp_low, direct, gmix, rolled, sums, mixed_part, own_residual, bp, bq,
    sems, in_sems, out_sems,
):
    ins = Saves(in_sems)
    for source, target in (
        (i_back.at[pl.ds(0, TOK)], part), (i_residual, residual), (i_merged, merged), (i_gate, gate_in), (i_st, st_in),
        (i_rate, rate), (i_inp, inp), (i_conv, conv_low), (i_tables, tables), (i_u, u_in), (i_normed, normed),
    ):
        ins.start(source, target)
    for j, p in enumerate((wp0, wp1, wp2, wp3)):
        og_copy(p, places, j, wog, sems.at[1])
    for j, (p, q) in enumerate(((wp0, wq0), (wp1, wq1), (wp2, wq2), (wp3, wq3))):
        p_copy(p, places, j, OG, PB, wb, 0, sems.at[0])
        q_copy(q, places, j, 0, QB, wb, PB, sems.at[0])
    saves = Saves(out_sems)
    sums[...] = jnp.zeros_like(sums)
    for copy in ins.copies[0:2]:
        copy.wait()
    for s in range(2):
        rows, theirs = slice(s * SEQ, (s + 1) * SEQ), slice((1 - s) * SEQ, (2 - s) * SEQ)
        grad, term = rms_back(part[rows] + other[theirs], residual[rows], gains[1:2])
        grad = cot[rows].astype(F32) + grad
        grad_branch[rows] = grad.astype(BF16)
        if s == 0:
            own_residual[...] = grad
            sums[9:10] = jnp.sum(term, axis=0, keepdims=True)
    saves.start(own_residual, o_residual)

    def put_og(b, first, v):
        x, z = (b // 8) * 2 + b % 2, (b // 2) % 4
        n = min(max(OG - first, 0), v.shape[1])
        if n:
            bp[x, z, 0:48, first : first + n] = v[:, :n]
        if n < v.shape[1]:
            to = first + n - OG
            for r in range(3):
                bp[x, z, 48:64, 384 * r + to : 384 * r + to + v.shape[1] - n] = v[16 * r : 16 * r + 16, n:]

    ins.copies[2].wait()
    v = tn(merged[...], grad_branch[...]).astype(BF16)
    for b in range(16):
        put_og(b, 0, v[48 * b : 48 * b + 48])
    landed(wog, sems.at[1])
    gs[...] = nt(grad_branch[...], wog[..., 0:D].reshape(RC, D))
    for copy in ins.copies[3:5]:
        copy.wait()

    @pl.loop(0, 6)
    def _(c):
        at = cols(c)
        act, act_grad = gelu_both(gate_in[:, at])
        g = gs[:, at]
        for s in range(2):
            rows = slice(s * SEQ, (s + 1) * SEQ)
            gmix[rows, pl.ds(pl.multiple_of(RC + c * LANES, LANES), LANES)] = (
                g[rows] * st_in[s, 8:, at] * act_grad[rows]
            ).astype(BF16)
        gs[:, at] = g * act

    for copy in ins.copies[5:8]:
        copy.wait()

    @pl.loop(0, 6)
    def _(c):
        at = cols(c)
        keep, starts = masks[0], masks[1]
        rg = jax.nn.sigmoid(rate[:, at] + chans[5:6, at])
        sd = jnp.exp(-8.0 * rg * chans[7:8, at])
        coeff[:, at] = (1.0 - starts) * (keep * sd + (1.0 - keep))

    row = lax.broadcasted_iota(jnp.int32, (8, RC), 0)

    def backward(n, carry):
        i = SEQ // 8 - 1 - n
        new = []
        for s in range(2):
            at = pl.ds(pl.multiple_of(s * SEQ + i * 8, 8), 8)
            own = coeff[at]
            later_a, later_lam = carry[s]
            a = jnp.where(row == 7, later_a, pltpu.roll(own, 7, 0))
            b = gs[at]
            for k in (1, 2, 4):
                here = row < 8 - k
                b = jnp.where(here, b + a * pltpu.roll(b, 8 - k, 0), b)
                a = jnp.where(here, a * pltpu.roll(a, 8 - k, 0), a)
            h = b + a * later_lam
            lam[at] = h
            new.append((own[0:1], h[0:1]))
        return tuple(new)

    zero = jnp.zeros((1, RC), F32)
    lax.fori_loop(0, SEQ // 8, backward, ((zero, zero), (zero, zero)))

    @pl.loop(0, 6)
    def _(c):
        at = cols(c)
        decay = chans[7:8, at]
        for s in range(2):
            rows = slice(s * SEQ, (s + 1) * SEQ)
            keep, starts = masks[0, rows], masks[1, rows]
            rg, ig, sd, q, root, scale = gates(
                rate[rows, at], inp[rows, at], chans[5:6, at], chans[6:7, at], decay, keep, starts
            )
            conv = conv_low[rows, at].astype(F32)
            l = lam[rows, at]
            common = l * keep
            grad_coeff = l * st_in[s, 7 : PAD - 1, at]
            direct[rows, at] = common * scale * ig
            d_ig = common * scale * conv
            d_scale = common * ig * conv
            d_sd = (1.0 - starts) * (grad_coeff * keep - d_scale * jnp.where(q > 0.001, sd / root, 0.0))
            d_log = d_sd * sd * -8.0
            d_rate = d_log * decay * rg * (1.0 - rg)
            d_inp = d_ig * ig * (1.0 - ig)
            rate_low[rows, at] = d_rate.astype(BF16)
            inp_low[rows, at] = d_inp.astype(BF16)
            for n, term in ((5, d_rate), (6, d_inp), (7, d_log * rg)):
                sums[n : n + 1, at] += jnp.sum(term, axis=0, keepdims=True)

    for copy in ins.copies[8:]:
        copy.wait()
    turn = turn_matrix()
    top, left = quarter_masks()
    for p in range(2):
        at = slice(2 * HS * p, 2 * HS * (p + 1))
        direct[:, at] += nt(rate_low[:, at], tables[2 * p]) + nt(inp_low[:, at], tables[2 * p + 1])
        dr = tn(conv_low[:, at], rate_low[:, at]).astype(BF16)
        di = tn(conv_low[:, at], inp_low[:, at]).astype(BF16)
        none = jnp.zeros_like(dr)
        straight = jnp.where(top, jnp.where(left, dr, none), jnp.where(left, none, di))
        crossed = jnp.where(top, jnp.where(left, di, none), jnp.where(left, none, dr))
        g = (straight.astype(F32) + nn(crossed, turn)).astype(BF16)
        for b in range(8):
            put_og(8 * p + b, D, g[48 * b : 48 * b + 48])

    rolled[:, SEQ:] = jnp.zeros((2, 8, LANES), F32)

    @pl.loop(0, 6)
    def _(c):
        at = cols(c)
        for s in range(2):
            rows = slice(s * SEQ, (s + 1) * SEQ)
            g = direct[rows, at]
            gu = chans[0:1, at] * g
            sums[4:5, at] += jnp.sum(g, axis=0, keepdims=True)
            sums[0:1, at] += jnp.sum(g * u_in[s, 8:, at], axis=0, keepdims=True)
            for k in range(1, 4):
                w = g * masks[1 + k, rows]
                sums[k : k + 1, at] += jnp.sum(w * u_in[s, 8 - k : PAD - k, at], axis=0, keepdims=True)
                rolled[s, 0:SEQ] = w
                gu = gu + chans[k : k + 1, at] * rolled[s, k : SEQ + k]
            gmix[rows, at] = (gu * masks[0, rows]).astype(BF16)

    v = jnp.concatenate([sums[0:8, 0:RC], jnp.zeros((LANES - 8, RC), F32)], axis=0).T.astype(BF16)
    for b in range(16):
        put_og(b, 1408, v[48 * b : 48 * b + 48])
    landed(wb, sems.at[0])

    v = tn(normed[...], gmix[:, 0:PB]).astype(BF16)
    for x, z in RINGS:
        for half in range(2):
            r = ring_rows(x, z) + 256 * half
            bp[x, z, 32 * half : 32 * half + 32, OG:EARLY] = v[r : r + 32]
    emit(saves, bp, places, 0, (p0, p1))
    mixed_part[...] = nt(gmix[...], rows_of(wb, 0, BRANCH))
    saves.start(mixed_part.at[pl.ds(0, SEQ)], o_mine)
    saves.start(mixed_part.at[pl.ds(SEQ, SEQ)], o_theirs)
    t = tok[...].astype(F32)
    sums[8:9] = jnp.sum(mixed_part[...] * (t * inv_rms(t)), axis=0, keepdims=True)
    v = jnp.concatenate([sums[8:16], jnp.zeros((LANES - 8, D), F32)], axis=0).T.astype(BF16)
    for x, z in RINGS:
        for half in range(2):
            r = ring_rows(x, z) + 256 * half
            bq[z, x, 32 * half : 32 * half + 32, QB:EARLY] = v[r : r + 32]

    v = tn(normed[...], gmix[:, PB:]).astype(BF16)
    for x, z in RINGS:
        for half in range(2):
            r = ring_rows(x, z) + 256 * half
            bq[z, x, 32 * half : 32 * half + 32, 0:QB] = v[r : r + 32]
    emit(saves, bq, places, 2, (q0, q1))
    saves.wait()


def join_sums(
    places, eo_p, eu_p, lo_p, lu_p, eo_q, eu_q, lo_q, lu_q,
    p0, p1, q0, q1,
    early, late, out, in_sems, out_sems,
):
    loads, saves = Saves(in_sems), Saves(out_sems)
    for n, (a, b, c, d) in enumerate(((eo_p, eu_p, lo_p, lu_p), (eo_q, eu_q, lo_q, lu_q))):
        for source, target in ((a, early.at[n, 0]), (b, early.at[n, 1]), (c, late.at[n, 0]), (d, late.at[n, 1])):
            loads.start(source, target)
    for n, (axis, outs) in enumerate(((2, (p0, p1)), (0, (q0, q1)))):
        for copy in loads.copies[4 * n : 4 * n + 4]:
            copy.wait()
        for j in range(4):
            at, to = places[4 + axis, j], 4 * n + j
            out[to, :, 0:EARLY] = add(early[n, 0, at], early[n, 1, at])
            out[to, :, EARLY:] = add(late[n, 0, at], late[n, 1, at])
            saves.start(out.at[to], outs[j // 2].at[j % 2])
    saves.wait()


def add(a, b):
    return (a.astype(F32) + b.astype(F32)).astype(BF16)


def half_sums(a_p, b_p, c_p, d_p, a_q, b_q, c_q, d_q, *rest):
    outs, (early, late, in_sems, out_sems) = rest[-8:-4], rest[-4:]
    loads, saves = Saves(in_sems), Saves(out_sems)
    for n, (a, b, c, d) in enumerate(((a_p, b_p, c_p, d_p), (a_q, b_q, c_q, d_q))):
        for source, target in ((a, early.at[n, 0]), (b, early.at[n, 1]), (c, late.at[n, 0]), (d, late.at[n, 1])):
            loads.start(source.at[0], target)
    for n in range(2):
        for i, v in enumerate((early, late)):
            loads.copies[4 * n + 2 * i].wait()
            loads.copies[4 * n + 2 * i + 1].wait()
            v[n, 0] = add(v[n, 0], v[n, 1])
            saves.start(v.at[n, 0], outs[2 * n + i])
    saves.wait()


def pass_on(a_p, f_p, a_q, f_q, *rest):
    o_p, o_q, v, in_sems, out_sems = rest[-5:]
    loads, saves = Saves(in_sems), Saves(out_sems)
    for i, source in enumerate((a_p, f_p, a_q, f_q)):
        loads.start(source.at[1], v.at[i])
    for n, out in enumerate((o_p, o_q)):
        loads.copies[2 * n].wait()
        loads.copies[2 * n + 1].wait()
        v[2 * n] = add(v[2 * n], v[2 * n + 1])
        saves.start(v.at[2 * n], out)
    saves.wait()


def cut(
    places, p0, p1, p2, q0, q1, q2,
    o0, o1, o2, o3,
    parts, sp, sq, sd, in_sems,
):
    load((p0.at[0], p1.at[0], p2, q0.at[0], q1.at[0], q2), [parts.at[i] for i in range(6)], in_sems)
    for n, out in enumerate((sp, sq)):
        out[...] = parts[3 * n].astype(F32) + parts[3 * n + 1].astype(F32) + parts[3 * n + 2].astype(F32)
    sd[0:64] = sp[:, EARLY : EARLY + D]
    sd[64:96, 0:512] = sp[0:32, EARLY + D : EARLY + FC]
    sd[64:96, 512:1024] = sp[32:64, EARLY + D : EARLY + FC]
    tail = jnp.concatenate([sp[48:64, 384 * r : 384 * r + 384] for r in range(3)], axis=0)
    og = jnp.concatenate([sp[0:48, 0:OG], tail], axis=1).astype(BF16)
    i = lax.broadcasted_iota(jnp.int32, (16, 48), 0)
    s = lax.broadcasted_iota(jnp.int32, (16, 48), 1)

    def two(rows):
        return jnp.concatenate(rows, axis=0).astype(BF16)

    for j, out in enumerate((o0, o1, o2, o3)):
        y = places[1, (0, 2, 3, 1)[j]]
        rows = [pl.ds(pl.multiple_of(32 * c + y * 8, 8), 8) for c in range(2)]
        out[:, 0:PB] = two([sp[r, OG:EARLY] for r in rows])
        out[:, PB : PB + PI] = two([sp[r, UNIT - PI :] for r in rows])
        out[:, PB + PI : DC] = two([sq[r] for r in rows])
        mine = jnp.where((s == i + y * 12) & (i < 12), 1.0, 0.0).astype(BF16)
        out[:, DC:DOWN] = nn(mine, og).astype(BF16)
        down = sd[pl.ds(pl.multiple_of(y * 24, 8), 24)]
        out[:, DOWN : DOWN + D] = down[0:16].astype(BF16)
        out[:, DOWN + D :] = two([down[16:24, 0:512], down[16:24, 512:]])


def finish(places, o0, o1, o2, o3, mine, theirs, out_grad, gate_grad, chan_grad, down_grad, v):
    v[...] = o0[...].astype(F32) + o1[...].astype(F32) + o2[...].astype(F32) + o3[...].astype(F32)
    core = places[3, 0]
    theirs[...] = v[pl.ds(pl.multiple_of((1 - core) * 8, 8), 8), 0:DC]
    mine[...] = v[pl.ds(pl.multiple_of(core * 8, 8), 8), 0:DC]
    out_grad[...] = v[0:12, DC : DC + D]
    gate_grad[...] = v[0:12, DC + D : DC + D + 384]
    chan_grad[...] = v[:, DC + D + 384 : DOWN].T[0:8]
    down_grad[0:16] = v[:, DOWN : DOWN + D]
    down_grad[16:24, 0:512] = v[0:8, DOWN + D :]
    down_grad[16:24, 512:] = v[8:16, DOWN + D :]


def unpack(places, mine, theirs, branch, inner, gains):
    def halves(ins):
        for c, v in enumerate(ins):
            for q in range(4):
                to = 768 * q + 384 * c
                if q == 0:
                    branch[:, to : to + PB] = v[:, 0:PB]
                    branch[:, to + PB : to + 384] = v[:, PB + PI : PB + PI + 128]
                else:
                    branch[:, to : to + 384] = v[:, PI + 384 * q : PI + 384 * q + 384]
                at = PB if q == 0 else DC - LATE + 768 * (q - 1)
                to = 1536 * q + 768 * c
                inner[:, to : to + 768] = v[:, at : at + 768]

    gains[...] = mine[:, DC - LATE - LANES : DC - LATE] + theirs[:, DC - LATE - LANES : DC - LATE]

    @pl.when(places[3, 0] == 0)
    def _():
        halves((mine, theirs))

    @pl.when(places[3, 0] == 1)
    def _():
        halves((theirs, mine))


VM, HB, SM, ANY = pltpu.VMEM, pltpu.HBM, pltpu.SMEM, pl.ANY


def kernel(body, ins, spaces, outs, scratch, mib, flops=0, aliases={}):
    moved = sum(v.size * v.dtype.itemsize for v in ins)
    ins = [pltpu.with_memory_space_constraint(v, HB) if s is HB else v for v, s in zip(ins, spaces)]
    return pl.pallas_call(
        body,
        out_shape=[HB(s, d) if at is HB else jax.ShapeDtypeStruct(s, d) for s, d, at in outs],
        in_specs=[pl.BlockSpec(memory_space=s) for s in spaces],
        out_specs=[pl.BlockSpec(memory_space=s) for _, _, s in outs],
        scratch_shapes=scratch,
        input_output_aliases=aliases,
        compiler_params=pltpu.CompilerParams(vmem_limit_bytes=mib * 2**20),
        cost_estimate=pl.CostEstimate(flops=flops, bytes_accessed=moved, transcendentals=0),
    )(*ins)


def shards(
    tokens, cotangent, segment, keep_mask, conv_state, lru_state, norm1_gain, conv_weight, lru_bias, decay_rate,
    gate_weight, branch_weight, out_weight, norm2_gain, mlp_in_weight, mlp_out_weight,
):
    here = my_place()
    core = here["core"]
    zero = jnp.zeros_like(core)
    places = jnp.stack(
        [jnp.stack(ring_places(axis, here)) for axis in "xyz"]
        + [jnp.stack([core, zero, zero, zero])]
        + [jnp.stack(pair_places(axis, here)) for axis in "xyz"]
    ).astype(jnp.int32)
    vmem, dma = pltpu.VMEM, pltpu.SemaphoreType.DMA

    tc = jnp.concatenate([tokens[0], cotangent[0]], axis=0)
    tc_other = swap(tc)
    marks = jnp.concatenate([segment, keep_mask], axis=1).astype(F32)
    states = jnp.concatenate([conv_state[0], lru_state], axis=0)
    sent = jnp.concatenate([core_half(states, 1 - core, 2), jnp.pad(marks, ((0, 0), (0, RC - 2 * SEQ)))], axis=0)
    sent = swap(sent)

    mine, theirs, own = kernel(
        pack,
        (places, branch_weight, mlp_in_weight, jnp.stack([norm1_gain, norm2_gain]), out_weight, gate_weight,
         jnp.concatenate([conv_weight, lru_bias, decay_rate[None]], axis=0), mlp_out_weight),
        [SM, HB, HB, VM, HB, HB, VM, HB],
        [((8, DC), BF16, VM)] * 2 + [((16, OWN - DC), BF16, VM)],
        [vmem(v.shape, BF16) for v in (branch_weight, mlp_in_weight, out_weight, gate_weight, mlp_out_weight)]
        + [dma((5,))],
        8,
    )
    (block,) = kernel(join, (places, mine, swap(theirs), own), [SM] + [VM] * 3, [((16, OWN), BF16, VM)], [], 8)

    row = ((64, UNIT), BF16)
    unit_of = ((2, 32, UNIT), BF16)
    p, q = kernel(
        unit,
        (places, *ring_direct(block, "y"), tc_other, sent),
        [SM] + [VM] * 4 + [ANY] * 2,
        [(*unit_of, HB)] * 2,
        [vmem(*row), vmem(*row), vmem((64, DC), F32), vmem((96, D), F32), dma((4,))],
        16,
    )
    early, late = (4, 64, EARLY), (4, 64, LATE)
    stack = ((4, 64, UNIT), BF16)
    p, q = ring_both(p, "z"), ring_both(q, "x")
    stacks = [((*v, n), BF16, HB) for n in (EARLY, LATE) for v in ((2, 4, 32), (2, 2, 2, 32))]
    unit_of = (2, 32, UNIT)
    partial = kernel(
        planes((0, 1, 2)),
        (places, *p[:3], *q[:3]),
        [SM] + [HB] * 6,
        stacks,
        [vmem((6, *unit_of), BF16), dma((6,)), dma((12,))],
        8,
    )
    pe, qe, pl_, ql = kernel(
        planes((3,)),
        (places, p[3], q[3], *partial),
        [SM, ANY, ANY] + [HB] * 4,
        stacks,
        [vmem((2, *unit_of), BF16), dma((2,)), dma((4,))],
        8,
        aliases={3 + i: i for i in range(4)},
    )
    pe, qe, pl_, ql = ring_both(pe, "x"), ring_both(qe, "z"), ring_both(pl_, "x"), ring_both(ql, "z")

    tok = jnp.concatenate([tc[:SEQ], tc_other[:SEQ]], axis=0)
    cot = jnp.concatenate([tc[SEQ:], tc_other[SEQ:]], axis=0)
    states = jnp.stack([core_half(states, core, 2), sent[:4]])
    marks = jnp.concatenate([marks, sent[4:, : 2 * SEQ]], axis=0)
    seg, keep = marks[:, :SEQ], marks[:, SEQ:]
    earlier = [jnp.concatenate([jnp.repeat(seg[:, :1], k, axis=1), seg[:, : SEQ - k]], axis=1) for k in range(1, 4)]
    masks = jnp.stack([keep, (earlier[0] != seg).astype(F32)] + [(e == seg).astype(F32) for e in earlier])
    masks = jnp.broadcast_to(masks.reshape(5, TOK, 1), (5, TOK, LANES))

    wide, wide_low = ((TOK, D), F32), ((TOK, D), BF16)
    act, act_low, padded = ((TOK, RC), F32), ((TOK, RC), BF16), ((2, PAD, RC), F32)
    tables = ((4, 2 * HS, 2 * HS), BF16)
    saved = [wide_low, act_low, padded, act, act_low, act, act, padded, tables]
    part, finals, gains, chans, normed, merged, u, gate_in, conv_low, rate, inp, st, table = kernel(
        rec_forward,
        (places, tok, masks, states[:, :3], states[:, 3:], *pe, *qe),
        [SM] + [VM] * 4 + [HB] * 8,
        [((TOK + 8, D), F32, VM), ((4, RC), F32, VM), ((8, D), F32, VM), ((8, RC), F32, VM)]
        + [(*v, HB) for v in saved],
        [vmem((*ROWS, PB + EARLY), BF16), vmem((*OG_ROWS, OGC), BF16)]
        + [vmem(*v) for v in saved + [act, act]]
        + [dma((2,)), dma((9,))],
        32,
        2 * TOK * (D * BRANCH + RC * (D + 768)),
    )
    half = ((SEQ, D), F32)
    other = swap(part)
    normed2, own, residual = kernel(
        mlp_norm,
        (tok, part, other, gains),
        [VM] * 4,
        [(*wide_low, VM), (*half, VM), (*wide, HB)],
        [vmem(*wide), dma],
        16,
    )
    hidden, ggu, base, back = kernel(
        mlp,
        (places, cot, normed2, own, *pl_, *ql),
        [SM] + [VM] * 3 + [ANY] * 8,
        [((TOK, FC), BF16, VM), ((TOK, INNER), BF16, VM), (*half, HB), ((TOK + SEQ, D), F32, HB)],
        [vmem((*ROWS, INNER), BF16), vmem((*DOWN_ROWS, D), BF16)]
        + [vmem(*v) for v in (wide, wide, half)]
        + [dma((2,)), dma((3,))],
        32,
        2 * TOK * D * (2 * INNER + 2 * FC),
    )
    back_other = swap(back)
    outs = kernel(
        mlp_grads,
        (places, cot, normed2, hidden, ggu),
        [SM] + [VM] * 4,
        [((2, *late), BF16, HB)] * 4,
        [vmem((4,) + late, BF16), vmem((4,) + late, BF16), dma((20,))],
        32,
        2 * TOK * D * (INNER + FC),
    )
    lp, lq = outs[:2], outs[2:]

    def first_half(p, q, routes):
        return send(p[1], partner(routes[0], 0)), send(q[1], partner(routes[1], 0))

    def second_half(p, q, came, routes, shape, until=()):
        up = kernel(
            pass_on,
            (p[0], came[0], q[0], came[1], *until),
            [HB] * (4 + len(until)),
            [(shape, BF16, HB)] * 2,
            [vmem((4,) + shape, BF16), dma((4,)), dma((2,))],
            16,
        )
        return send(up[0], partner(routes[0], 1)), send(up[1], partner(routes[1], 1))

    late_came = first_half(lp, lq, "xz")
    outs = kernel(
        rec_backward,
        (places, tok, cot, masks, gains, chans, back_other, back, residual, normed, merged, u, gate_in, conv_low, rate,
         inp, st, table, *pe, *qe),
        [SM] + [VM] * 6 + [HB] * 19,
        [(*v, HB) for v in (half, half, half)] + [((2, *early), BF16, HB)] * 4,
        [vmem((*ROWS, BRANCH), BF16), vmem((*OG_ROWS, OGC), BF16)]
        + [vmem(*v) for v in (wide, wide, wide_low, act_low, padded, act, act_low, act, act, padded, tables)]
        + [vmem(*v) for v in (act, wide_low, act, act, act_low, act_low, act, ((TOK, BRANCH), BF16))]
        + [vmem((2, PAD, LANES), F32), vmem((16, D), F32), vmem(*wide), vmem(*half)]
        + [vmem((4,) + early, BF16), vmem((4,) + early, BF16), dma((2,)), dma((11,)), dma((11,))],
        48,
        2 * TOK * D * (2 * BRANCH + 2 * RC),
    )
    grad_residual, mixed_mine, mixed_theirs = outs[:3]
    ep, eq = outs[3:5], outs[5:]
    early_came = first_half(ep, eq, "xz")
    late_up = second_half(lp, lq, late_came, "xz", late, (ep[0],))
    early_up = second_half(ep, eq, early_came, "xz", early)

    summed = kernel(
        half_sums,
        (ep[0], early_came[0], lp[0], late_came[0], eq[0], early_came[1], lq[0], late_came[1]),
        [HB] * 8,
        [(early, BF16, HB), (late, BF16, HB)] * 2,
        [vmem((2, 2) + early, BF16), vmem((2, 2) + late, BF16), dma((8,)), dma((4,))],
        24,
    )
    outs = kernel(
        join_sums,
        (places, summed[0], early_up[0], summed[1], late_up[0], summed[2], early_up[1], summed[3], late_up[1]),
        [SM] + [HB] * 8,
        [((2, 64, UNIT), BF16, HB)] * 4,
        [vmem((2, 2) + early, BF16), vmem((2, 2) + late, BF16), vmem((8, 64, UNIT), BF16), dma((8,)), dma((8,))],
        32,
    )
    tp, tq = outs[:2], outs[2:]
    came = first_half(tp, tq, "zx")
    up = second_half(tp, tq, came, "zx", (64, UNIT))
    sums = kernel(
        cut,
        (places, tp[0], came[0], up[0], tq[0], came[1], up[1]),
        [SM] + [HB, HB, ANY] * 2,
        [((16, OWN), BF16, VM)] * 4,
        [vmem((6, 64, UNIT), BF16), vmem((64, UNIT), F32), vmem((64, UNIT), F32), vmem((96, D), F32), dma((6,))],
        16,
    )
    mine, theirs, out_grad, gate_grad, chan_grad, down_grad = kernel(
        finish,
        (places, *terms_direct(sums, "y")),
        [SM] + [VM] * 4,
        [((8, DC), F32, VM)] * 2 + [(s, F32, VM) for s in ((12, D), (12, 384), (8, 16), (24, D))],
        [vmem((16, OWN), F32)],
        8,
    )
    branch_grad, in_grad, gain_grads = kernel(
        unpack,
        (places, mine, swap(theirs)),
        [SM] + [VM] * 2,
        [((8, 2 * R), F32, VM), ((8, 2 * F), F32, VM), ((8, LANES), F32, VM)],
        [],
        8,
    )

    output = (base + back_other[TOK:]).astype(BF16)
    grad, _ = rms_back(mixed_mine + swap(mixed_theirs), tok[:SEQ].astype(F32), gains[0])
    input_grad = (grad_residual + grad).astype(BF16)
    theirs = other[TOK : TOK + 4, :RC]
    finals = jnp.stack(
        [v.reshape(1, 4, 2, 384) for v in (jnp.where(core == 0, finals, theirs), jnp.where(core == 0, theirs, finals))],
        axis=3,
    ).reshape(1, 4, R)
    return (
        output[None],
        input_grad[None],
        finals[:, :3],
        finals[:, 3],
        gain_grads[:, 0],
        chan_grad[:4, :12],
        chan_grad[4:7, :12],
        chan_grad[7, :12],
        gate_grad,
        branch_grad,
        out_grad,
        gain_grads[:, 1],
        in_grad,
        down_grad,
    )


def solution(mesh):
    rows, last = P(AXES), P(None, AXES)
    specs = [rows] * 6 + [rows, last, last] + [rows] * 7
    outs = [rows] * 4 + [rows, last, last] + [rows] * 7
    return jax.shard_map(
        shards, mesh=mesh, in_specs=tuple(specs), out_specs=tuple(outs), check_vma=False
    )
```

```python
import jax
import jax.numpy as jnp
from jax import lax
from jax.experimental import pallas as pl
from jax.experimental.pallas import tpu as pltpu
from jax.sharding import PartitionSpec as P

AXES = ("dp", "fsdp")
D, R, F, SEQ = 1024, 1536, 3072, 128
RC, FC = R // 2, F // 2
HS = 192
F32, BF16 = jnp.float32, jnp.bfloat16
BRANCH, INNER = 2 * RC, 2 * FC
TOK, PAD, LANES = 2 * SEQ, SEQ + 8, 128

EARLY, LATE = 1408, 2304
UNIT = EARLY + LATE
OG, PB, PI, QB = 1152, 256, 768, 1280
DC = PB + PI + UNIT
OGC = 1536
DOWN = DC + OGC
OWN = DOWN + D + D // 2


def place_of(device):
    outer, inner = divmod(device, 32)
    x_hi, core = divmod(outer, 2)
    z, rest = divmod(inner, 8)
    x_lo, y = divmod(rest, 4)
    return dict(x=x_hi * 2 + x_lo, y=y, z=z, core=core)


def device_at(x, y, z, core):
    return ((x // 2) * 2 + core) * 32 + z * 8 + (x % 2) * 4 + y


def pairs(move):
    return [(d, device_at(**move(place_of(d)))) for d in range(128)]


def along(axis, steps):
    def move(p):
        sign = 1 if p["core"] == 0 else -1
        return {**p, axis: (p[axis] + sign * steps) % 4}

    return pairs(move)


def other_core(p):
    return {**p, "core": 1 - p["core"]}


def partner(axis, turn):
    def move(p):
        i = p[axis]
        return {**p, axis: i ^ 1 if (p["core"] + turn) % 2 == 0 else 3 - i}

    return pairs(move)


def opposite(axis):
    return pairs(lambda p: {**p, axis: (p[axis] + 2) % 4})


def send(value, route):
    return lax.ppermute(value, AXES, route)


def swap(value):
    return send(value, pairs(other_core))


def my_place():
    device = lax.axis_index(AXES)
    outer, inner = device // 32, device % 32
    return dict(x=(outer // 2) * 2 + (inner // 4) % 2, y=inner % 4, z=inner // 8, core=outer % 2)


def ring_places(axis, here):
    sign, at = 1 - 2 * here["core"], here[axis]
    return [at, (at - sign) % 4, (at + sign) % 4, (at + 2) % 4]


def ring(block, axis):
    one = send(block, along(axis, 1))
    two = send(one, along(axis, 1))
    return block, one, send(two, along(axis, 1)), two


def ring_both(block, axis):
    up, down = send(block, along(axis, 1)), send(block, along(axis, -1))
    return block, up, down, send(up, along(axis, 1))


def pair_places(axis, here):
    i, odd = here[axis], here["core"] == 1
    by_one, by_ends = i + 1 - 2 * (i % 2), 3 - i
    return [i, jnp.where(odd, by_one, by_ends), jnp.where(odd, by_ends, by_one), (i + 2) % 4]


def ring_direct(block, axis):
    return block, send(block, along(axis, 1)), send(block, along(axis, -1)), send(block, opposite(axis))


def terms_direct(terms, axis):
    own, ahead, far, behind = terms
    return own, send(ahead, along(axis, 1)), send(far, opposite(axis)), send(behind, along(axis, -1))


def total(*terms):
    out = terms[0].astype(F32)
    for term in terms[1:]:
        out = out + term.astype(F32)
    return out.astype(BF16)


def core_half(array, core, blocks):
    v = array.reshape(array.shape[:-1] + (blocks, 2, array.shape[-1] // (2 * blocks)))
    v = lax.dynamic_index_in_dim(v, core, v.ndim - 2, keepdims=False)
    return v.reshape(array.shape[:-1] + (array.shape[-1] // 2,))


def dot(a, b, dims):
    return lax.dot_general(a, b, (dims, ((), ())), preferred_element_type=F32)


def nn(a, b):
    return dot(a, b, ((1,), (0,)))


def nt(a, b):
    return dot(a, b, ((1,), (1,)))


def tn(a, b):
    return dot(a, b, ((0,), (0,)))


def inv_rms(v):
    return lax.rsqrt(jnp.mean(v * v, axis=-1, keepdims=True) + 1e-6)


def rms_back(grad, v, gain):
    s = inv_rms(v)
    n = v * s
    g2 = grad * gain
    return s * (g2 - n * jnp.mean(g2 * n, axis=-1, keepdims=True)), grad * n


C0, C1 = 0.7978845608028654, 0.044715


def gelu_both(a):
    t = jnp.tanh(C0 * (a + C1 * (a * a * a)))
    half = 0.5 * (1.0 + t)
    return a * half, half + 0.5 * a * (1.0 - t * t) * (C0 * (1.0 + 3.0 * C1 * (a * a)))


def gates(rate, inp, bias1, bias2, decay, keep, starts):
    rg = jax.nn.sigmoid(rate + bias1)
    ig = jax.nn.sigmoid(inp + bias2)
    sd = jnp.exp(-8.0 * rg * decay)
    q = 1.0 - sd * sd
    root = jnp.sqrt(jnp.maximum(q, 0.001))
    scale = starts + (1.0 - starts) * root
    return rg, ig, sd, q, root, scale


def cols(c):
    return pl.ds(pl.multiple_of(c * LANES, LANES), LANES)


class Saves:
    def __init__(self, sem):
        self.sem, self.copies = sem, []

    def start(self, source, target):
        self.copies.append(pltpu.make_async_copy(source, target, self.sem.at[len(self.copies)]))
        self.copies[-1].start()

    def wait(self):
        for copy in self.copies:
            copy.wait()


def pick(rows, where):
    return jnp.where(lax.broadcasted_iota(jnp.int32, (rows, where.shape[1]), 0) == where, 1.0, 0.0).astype(BF16)


def stand(values, rows):
    v = values.astype(F32)
    i = lax.broadcasted_iota(jnp.int32, (rows, v.shape[1]), 0)
    j = lax.broadcasted_iota(jnp.int32, (rows, v.shape[1]), 1)
    lane = lax.broadcasted_iota(jnp.int32, (rows, LANES), 1)
    out = jnp.zeros((rows, LANES), F32)
    for n in range(v.shape[0]):
        column = jnp.sum(jnp.where(i == j, v[n : n + 1], 0.0), axis=1, keepdims=True)
        out = out + jnp.where(lane == n, column, 0.0)
    return out


def load(sources, targets, sems):
    copies = Saves(sems)
    for source, target in zip(sources, targets):
        copies.start(source, target)
    copies.wait()


def pack(
    places, i_branch, i_inner, gain, i_out, i_gate, perchan, i_down, mine, theirs, own,
    branch, inner, out, gate, down, sems,
):
    load((i_branch, i_inner, i_out, i_gate, i_down), (branch, inner, out, gate, down), sems)

    gains = stand(gain[...], 8).astype(BF16)

    def halves(outs):
        for c, to_core in enumerate(outs):
            for q in range(4):
                v = branch[:, 768 * q + 384 * c : 768 * q + 384 * c + 384]
                if q == 0:
                    to_core[:, 0:PB] = v[:, 0:PB]
                    to_core[:, PB + PI : PB + PI + 128] = v[:, PB:]
                else:
                    to_core[:, PI + 384 * q : PI + 384 * q + 384] = v
                v = inner[:, 1536 * q + 768 * c : 1536 * q + 768 * c + 768]
                to = PB if q == 0 else DC - LATE + 768 * (q - 1)
                to_core[:, to : to + 768] = v
            tile = DC - LATE - LANES
            to_core[:, tile : tile + LANES] = gains

    @pl.when(places[3, 0] == 0)
    def _():
        halves((mine, theirs))

    @pl.when(places[3, 0] == 1)
    def _():
        halves((theirs, mine))

    own[...] = jnp.zeros_like(own)
    own[0:12, 0:D] = out[...]
    own[0:12, D : D + 384] = gate[...]
    own[:, 1408:OGC] = stand(perchan[...], 16).astype(BF16)
    own[:, OGC : OGC + D] = down[0:16]
    own[:, OGC + D :] = jnp.concatenate(
        [down[16:24, 0:512].astype(F32), down[16:24, 512:].astype(F32)], axis=0
    ).astype(BF16)


def join(places, mine, theirs, own, block):
    def rows(low, high):
        block[:, 0:DC] = jnp.concatenate([low[...].astype(F32), high[...].astype(F32)], axis=0).astype(BF16)

    @pl.when(places[3, 0] == 0)
    def _():
        rows(mine, theirs)

    @pl.when(places[3, 0] == 1)
    def _():
        rows(theirs, mine)

    block[:, DC:] = own[...]


def unit(places, p0, p1, p2, p3, *rest):
    o_p, o_q, p, q, d, dn, sems = rest[-7:]
    ogs = []
    s = lax.broadcasted_iota(jnp.int32, (1, 64), 1)
    y = jnp.zeros((1, 64), jnp.int32)
    for j, piece in enumerate((p0, p1, p2, p3)):
        at = places[1, j]
        y = jnp.where(s // 16 == j, at, y)
        v = piece[:, 0:DC].astype(F32)
        for c in range(2):
            d[pl.ds(pl.multiple_of(c * 32 + at * 8, 8), 8)] = v[8 * c : 8 * c + 8]
        ogs.append(piece[:, DC:DOWN])
        v = piece[:, DOWN:].astype(F32)
        dn[pl.ds(pl.multiple_of(at * 24, 8), 16)] = v[:, 0:D]
        for h in range(2):
            dn[pl.ds(pl.multiple_of(at * 24 + 16, 8), 8), 512 * h : 512 * h + 512] = v[8 * h : 8 * h + 8, D:]
    saves = Saves(sems)
    q[...] = d[:, PB + PI :].astype(BF16)
    for c in range(2):
        saves.start(q.at[pl.ds(32 * c, 32)], o_q.at[c])
    p[:, OG:EARLY] = d[:, 0:PB].astype(BF16)
    p[:, UNIT - PI :] = d[:, PB : PB + PI].astype(BF16)
    i = s % 16
    og = nn(pick(48, jnp.where(i < 12, y * 12 + i, 64)), jnp.concatenate(ogs, axis=0)).astype(BF16)
    p[0:48, 0:OG] = og[:, 0:OG]
    for r in range(3):
        p[48:64, 384 * r : 384 * r + 384] = og[16 * r : 16 * r + 16, OG:]
    p[:, EARLY : EARLY + D] = dn[0:64].astype(BF16)
    p[0:32, EARLY + D : EARLY + FC] = dn[64:96, 0:512].astype(BF16)
    p[32:64, EARLY + D : EARLY + FC] = dn[64:96, 512:1024].astype(BF16)
    for c in range(2):
        saves.start(p.at[pl.ds(32 * c, 32)], o_p.at[c])
    saves.wait()


def planes(which):
    def body(places, *refs):
        n = len(which)
        (o_pe, o_qe, o_pl, o_ql), v, in_sems, out_sems = refs[-7:-3], *refs[-3:]
        loads, saves = Saves(in_sems), Saves(out_sems)
        for i, piece in enumerate(refs[: 2 * n]):
            loads.start(piece, v.at[i])
        for i in range(2 * n):
            loads.copies[i].wait()
            j = which[i % n]
            x = places[0, j]
            for first, count, p, q in ((0, EARLY, o_pe, o_qe), (EARLY, LATE, o_pl, o_ql)):
                target = p.at[:, places[2, j]] if i < n else q.at[x // 2, :, x % 2]
                saves.start(v.at[i, :, :, pl.ds(first, count)], target)
        saves.wait()

    return body


ROWS = (2, 2, 4, 2, 32)
OG_ROWS, DOWN_ROWS = (2, 4, 2, 48), (2, 4, 2, 96)


def ring_rows(x, z):
    return (x // 2) * 512 + z * 64 + (x % 2) * 32


def p_copy(piece, places, j, first, count, block, to, sem):
    x = places[0, j]
    target = block.at[x // 2, :, :, x % 2, :, pl.ds(to, count)]
    pltpu.make_async_copy(piece.at[..., pl.ds(first, count)], target, sem).start()


def q_copy(piece, places, j, first, count, block, to, sem):
    target = block.at[:, :, places[2, j], :, :, pl.ds(to, count)]
    pltpu.make_async_copy(piece.at[..., pl.ds(first, count)], target, sem).start()


def og_copy(piece, places, j, block, sem):
    x = places[0, j]
    block = block.at[x // 2, :, x % 2]
    for source, target in (
        (piece.at[0, :, :, pl.ds(0, OG)], block.at[:, pl.ds(0, 32), pl.ds(0, OG)]),
        (piece.at[1, :, pl.ds(0, 16), pl.ds(0, OG)], block.at[:, pl.ds(32, 16), pl.ds(0, OG)]),
    ):
        pltpu.make_async_copy(source, target, sem).start()
    for r in range(3):
        pltpu.make_async_copy(
            piece.at[1, :, pl.ds(16, 16), pl.ds(384 * r, 384)], block.at[:, pl.ds(16 * r, 16), pl.ds(OG, 384)], sem
        ).start()


def down_copy(piece, places, j, block, sem):
    x = places[0, j]
    block = block.at[x // 2, :, x % 2]
    for h in range(2):
        pltpu.make_async_copy(piece.at[h, :, :, pl.ds(0, D)], block.at[:, pl.ds(32 * h, 32)], sem).start()
        pltpu.make_async_copy(
            piece.at[h, :, :, pl.ds(D, 512)], block.at[:, pl.ds(64, 32), pl.ds(512 * h, 512)], sem
        ).start()


def rows_of(block, first, count):
    return block[..., first : first + count].reshape(D, count)


def landed(block, sem):
    pltpu.make_async_copy(block, block, sem).wait()


def turn_matrix():
    i = lax.broadcasted_iota(jnp.int32, (2 * HS, 2 * HS), 0)
    j = lax.broadcasted_iota(jnp.int32, (2 * HS, 2 * HS), 1)
    return jnp.where((i == j + HS) | (j == i + HS), 1.0, 0.0).astype(BF16)


def quarter_masks():
    i = lax.broadcasted_iota(jnp.int32, (2 * HS, 2 * HS), 0) < HS
    j = lax.broadcasted_iota(jnp.int32, (2 * HS, 2 * HS), 1) < HS
    return i, j


def rec_forward(
    places, tok, masks, conv_before, lru_before, p0, p1, p2, p3, q0, q1, q2, q3,
    part, finals, gains, chans, o_normed, o_merged, o_u, o_gate, o_conv, o_rate, o_inp, o_st, o_tables,
    wb, wog, normed, merged, u, gate_in, conv_low, rate, inp, st, tables, coeff, drive, sems, out_sems,
):
    for j, (p, q) in enumerate(((p0, q0), (p1, q1), (p2, q2), (p3, q3))):
        p_copy(p, places, j, OG, PB, wb, 0, sems.at[0])
        q_copy(q, places, j, 0, EARLY, wb, PB, sems.at[0])
    for j, p in enumerate((p0, p1, p2, p3)):
        og_copy(p, places, j, wog, sems.at[1])
    saves = Saves(out_sems)
    t = tok[...].astype(F32)
    scaled = t * inv_rms(t)
    landed(wb, sems.at[0])
    gains[...] = rows_of(wb, BRANCH, LANES).astype(F32).T[:8]
    normed[...] = (scaled * gains[0:1]).astype(BF16)
    saves.start(normed, o_normed)
    for s in range(2):
        u[s, 0:8] = jnp.zeros((8, RC), F32)
        u[s, 5:8] = conv_before[s]
        st[s, 0:8] = jnp.zeros((8, RC), F32)
        st[s, 7:8] = lru_before[s]

    v = nn(normed[...], rows_of(wb, 0, RC))
    for s in range(2):
        rows = slice(s * SEQ, (s + 1) * SEQ)
        for c in range(6):
            u[s, 8:, LANES * c : LANES * c + LANES] = v[rows, LANES * c : LANES * c + LANES] * masks[0, rows]

    saves.start(u, o_u)

    gate_in[...] = nn(normed[...], rows_of(wb, RC, RC))

    saves.start(gate_in, o_gate)
    landed(wog, sems.at[1])
    chans[...] = wog[..., 1408:].reshape(RC, LANES).astype(F32).T[:8]

    @pl.loop(0, 6)
    def _(c):
        at = cols(c)
        for s in range(2):
            rows = slice(s * SEQ, (s + 1) * SEQ)
            v = chans[4:5, at] + chans[0:1, at] * u[s, 8:, at]
            for k in range(1, 4):
                v = v + chans[k : k + 1, at] * (u[s, 8 - k : PAD - k, at] * masks[1 + k, rows])
            conv_low[rows, at] = v.astype(BF16)

    saves.start(conv_low, o_conv)
    turn = turn_matrix()
    top, left = quarter_masks()
    for p in range(2):
        g = wog[p, :, :, :, D : D + 384].reshape(2 * HS, 2 * HS)
        turned = nn(g, turn).astype(BF16)
        zero = jnp.zeros_like(g)
        tables[2 * p] = jnp.where(left, jnp.where(top, g, zero), jnp.where(top, zero, turned))
        tables[2 * p + 1] = jnp.where(left, jnp.where(top, turned, zero), jnp.where(top, zero, g))
        at = slice(2 * HS * p, 2 * HS * (p + 1))
        rate[:, at] = nn(conv_low[:, at], tables[2 * p])
        inp[:, at] = nn(conv_low[:, at], tables[2 * p + 1])
    saves.start(tables, o_tables)
    saves.start(rate, o_rate)
    saves.start(inp, o_inp)

    @pl.loop(0, 6)
    def _(c):
        at = cols(c)
        keep, starts = masks[0], masks[1]
        _, ig, sd, _, _, scale = gates(
            rate[:, at], inp[:, at], chans[5:6, at], chans[6:7, at], chans[7:8, at], keep, starts
        )
        coeff[:, at] = (1.0 - starts) * (keep * sd + (1.0 - keep))
        drive[:, at] = keep * scale * ig * conv_low[:, at].astype(F32)

    row = lax.broadcasted_iota(jnp.int32, (8, RC), 0)

    def forward(i, carry):
        new = []
        for s in range(2):
            at = pl.ds(pl.multiple_of(s * SEQ + i * 8, 8), 8)
            a, b = coeff[at], drive[at]
            for k in (1, 2, 4):
                later = row >= k
                b = jnp.where(later, a * pltpu.roll(b, k, 0) + b, b)
                a = jnp.where(later, a * pltpu.roll(a, k, 0), a)
            h = a * carry[s] + b
            st[s, pl.ds(pl.multiple_of(8 + i * 8, 8), 8)] = h
            new.append(h[7:8])
        return tuple(new)

    last = lax.fori_loop(0, SEQ // 8, forward, (lru_before[0], lru_before[1]))
    saves.start(st, o_st)
    part[TOK:] = jnp.zeros((8, D), F32)
    part[TOK : TOK + 3, 0:RC] = u[1, PAD - 3 :]
    part[TOK + 3 : TOK + 4, 0:RC] = last[1]
    finals[0:3] = u[0, PAD - 3 :]
    finals[3:4] = last[0]

    @pl.loop(0, 6)
    def _(c):
        at = cols(c)
        act, _ = gelu_both(gate_in[:, at])
        for s in range(2):
            rows = slice(s * SEQ, (s + 1) * SEQ)
            merged[rows, at] = (st[s, 8:, at] * act[rows]).astype(BF16)

    saves.start(merged, o_merged)

    part[0:TOK] = nn(merged[...], wog[..., 0:D].reshape(RC, D))

    saves.wait()


def mlp_norm(tok, part, other, gains, normed2, own, o_residual, residual, sem):
    for s in range(2):
        rows, theirs = slice(s * SEQ, (s + 1) * SEQ), slice((1 - s) * SEQ, (2 - s) * SEQ)
        v = tok[rows].astype(F32) + (part[rows] + other[theirs])
        residual[rows] = v
        normed2[rows] = (v * inv_rms(v) * gains[1:2]).astype(BF16)
    copy = pltpu.make_async_copy(residual, o_residual, sem)
    copy.start()
    own[...] = residual[0:SEQ]
    copy.wait()


def mlp(
    places, cot, normed2, own, p0, p1, p2, p3, q0, q1, q2, q3,
    hidden, ggu, o_base, o_back,
    win, wdown, down, back, base, sems, out_sems,
):
    for j, (p, q) in enumerate(((p0, q0), (p1, q1), (p2, q2), (p3, q3))):
        p_copy(p, places, j, FC, PI, win, 0, sems.at[0])
        q_copy(q, places, j, 0, LATE, win, PI, sems.at[0])
    for j, p in enumerate((p0, p1, p2, p3)):
        down_copy(p, places, j, wdown, sems.at[1])
    saves = Saves(out_sems)
    down[...] = jnp.zeros_like(down)
    back[...] = jnp.zeros_like(back)
    landed(win, sems.at[0])
    for c in range(2):
        at, up = slice(768 * c, 768 * c + 768), slice(FC + 768 * c, FC + 768 * c + 768)
        wa, wu = rows_of(win, 768 * c, 768), rows_of(win, FC + 768 * c, 768)
        a = nn(normed2[...], wa)
        b = nn(normed2[...], wu)
        ga, da = gelu_both(a)
        h = (ga * b).astype(BF16)
        hidden[:, at] = h
        if c == 0:
            landed(wdown, sems.at[1])
        wd = wdown[c].reshape(768, D)
        gh = nt(cot[...], wd)
        gg_a = (gh * b * da).astype(BF16)
        gg_b = (gh * ga).astype(BF16)
        ggu[:, at] = gg_a
        ggu[:, up] = gg_b
        down[...] += nn(h, wd)
        back[...] += nt(gg_a, wa) + nt(gg_b, wu)

    saves.start(back, o_back.at[pl.ds(0, TOK)])
    saves.start(down.at[pl.ds(SEQ, SEQ)], o_back.at[pl.ds(TOK, SEQ)])
    base[...] = own[...] + down[0:SEQ]
    saves.start(base, o_base)
    saves.wait()


def emit(saves, block, places, axis, outs):
    for j in range(4):
        saves.start(block.at[places[4 + axis, j]], outs[j // 2].at[j % 2])


RINGS = [(x, z) for x in range(4) for z in range(4)]


def emit_columns(saves, block, places, axis, outs, first, count):
    for j in range(4):
        columns = pl.ds(first, count)
        saves.start(block.at[places[4 + axis, j], :, :, columns], outs[j // 2].at[j % 2, :, :, columns])


def mlp_grads(
    places, cot, normed2, hidden, ggu, p0, p1, q0, q1,
    bp, bq, out_sems,
):
    saves = Saves(out_sems)
    for xh in range(2):
        v = tn(hidden[:, 768 * xh : 768 * xh + 768], cot[...]).astype(BF16)
        for z in range(4):
            for xl in range(2):
                r = 96 * (2 * z + xl)
                bp[2 * xh + xl, z, :, 0:D] = v[r : r + 64]
                bp[2 * xh + xl, z, 0:32, D:FC] = v[r + 64 : r + 96, 0:512]
                bp[2 * xh + xl, z, 32:64, D:FC] = v[r + 64 : r + 96, 512:1024]
    emit_columns(saves, bp, places, 0, (p0, p1), 0, FC)

    def put(block, order, first, to):
        v = tn(normed2[...], ggu[:, first : first + 768]).astype(BF16)
        for x, z in RINGS:
            for half in range(2):
                r = ring_rows(x, z) + 256 * half
                at = (x, z) if order else (z, x)
                block[(*at, slice(32 * half, 32 * half + 32), slice(to, to + 768))] = v[r : r + 32]

    put(bp, True, 0, FC)
    emit_columns(saves, bp, places, 0, (p0, p1), FC, PI)
    for part in range(3):
        put(bq, False, 768 * (part + 1), 768 * part)
        emit_columns(saves, bq, places, 2, (q0, q1), 768 * part, 768)
    saves.wait()


def rec_backward(
    places, tok, cot, masks, gains, chans, other, i_back, i_residual, i_normed, i_merged, i_u, i_gate, i_conv, i_rate,
    i_inp, i_st, i_tables, wp0, wp1, wp2, wp3, wq0, wq1, wq2, wq3,
    o_residual, o_mine, o_theirs, p0, p1, q0, q1,
    wb, wog, part, residual, normed, merged, u_in, gate_in, conv_low, rate, inp, st_in, tables,
    coeff, grad_branch, gs, lam, rate_low, inp_low, direct, gmix, rolled, sums, mixed_part, own_residual, bp, bq,
    sems, in_sems, out_sems,
):
    ins = Saves(in_sems)
    for source, target in (
        (i_back.at[pl.ds(0, TOK)], part), (i_residual, residual), (i_merged, merged), (i_gate, gate_in), (i_st, st_in),
        (i_rate, rate), (i_inp, inp), (i_conv, conv_low), (i_tables, tables), (i_u, u_in), (i_normed, normed),
    ):
        ins.start(source, target)
    for j, p in enumerate((wp0, wp1, wp2, wp3)):
        og_copy(p, places, j, wog, sems.at[1])
    for j, (p, q) in enumerate(((wp0, wq0), (wp1, wq1), (wp2, wq2), (wp3, wq3))):
        p_copy(p, places, j, OG, PB, wb, 0, sems.at[0])
        q_copy(q, places, j, 0, QB, wb, PB, sems.at[0])
    saves = Saves(out_sems)
    sums[...] = jnp.zeros_like(sums)
    for copy in ins.copies[0:2]:
        copy.wait()
    for s in range(2):
        rows, theirs = slice(s * SEQ, (s + 1) * SEQ), slice((1 - s) * SEQ, (2 - s) * SEQ)
        grad, term = rms_back(part[rows] + other[theirs], residual[rows], gains[1:2])
        grad = cot[rows].astype(F32) + grad
        grad_branch[rows] = grad.astype(BF16)
        if s == 0:
            own_residual[...] = grad
            sums[9:10] = jnp.sum(term, axis=0, keepdims=True)
    saves.start(own_residual, o_residual)

    def put_og(b, first, v):
        x, z = (b // 8) * 2 + b % 2, (b // 2) % 4
        n = min(max(OG - first, 0), v.shape[1])
        if n:
            bp[x, z, 0:48, first : first + n] = v[:, :n]
        if n < v.shape[1]:
            to = first + n - OG
            for r in range(3):
                bp[x, z, 48:64, 384 * r + to : 384 * r + to + v.shape[1] - n] = v[16 * r : 16 * r + 16, n:]

    ins.copies[2].wait()
    v = tn(merged[...], grad_branch[...]).astype(BF16)
    for b in range(16):
        put_og(b, 0, v[48 * b : 48 * b + 48])
    landed(wog, sems.at[1])
    gs[...] = nt(grad_branch[...], wog[..., 0:D].reshape(RC, D))
    for copy in ins.copies[3:5]:
        copy.wait()

    @pl.loop(0, 6)
    def _(c):
        at = cols(c)
        act, act_grad = gelu_both(gate_in[:, at])
        g = gs[:, at]
        for s in range(2):
            rows = slice(s * SEQ, (s + 1) * SEQ)
            gmix[rows, pl.ds(pl.multiple_of(RC + c * LANES, LANES), LANES)] = (
                g[rows] * st_in[s, 8:, at] * act_grad[rows]
            ).astype(BF16)
        gs[:, at] = g * act

    for copy in ins.copies[5:8]:
        copy.wait()

    @pl.loop(0, 6)
    def _(c):
        at = cols(c)
        keep, starts = masks[0], masks[1]
        rg = jax.nn.sigmoid(rate[:, at] + chans[5:6, at])
        sd = jnp.exp(-8.0 * rg * chans[7:8, at])
        coeff[:, at] = (1.0 - starts) * (keep * sd + (1.0 - keep))

    row = lax.broadcasted_iota(jnp.int32, (8, RC), 0)

    def backward(n, carry):
        i = SEQ // 8 - 1 - n
        new = []
        for s in range(2):
            at = pl.ds(pl.multiple_of(s * SEQ + i * 8, 8), 8)
            own = coeff[at]
            later_a, later_lam = carry[s]
            a = jnp.where(row == 7, later_a, pltpu.roll(own, 7, 0))
            b = gs[at]
            for k in (1, 2, 4):
                here = row < 8 - k
                b = jnp.where(here, b + a * pltpu.roll(b, 8 - k, 0), b)
                a = jnp.where(here, a * pltpu.roll(a, 8 - k, 0), a)
            h = b + a * later_lam
            lam[at] = h
            new.append((own[0:1], h[0:1]))
        return tuple(new)

    zero = jnp.zeros((1, RC), F32)
    lax.fori_loop(0, SEQ // 8, backward, ((zero, zero), (zero, zero)))

    @pl.loop(0, 6)
    def _(c):
        at = cols(c)
        decay = chans[7:8, at]
        for s in range(2):
            rows = slice(s * SEQ, (s + 1) * SEQ)
            keep, starts = masks[0, rows], masks[1, rows]
            rg, ig, sd, q, root, scale = gates(
                rate[rows, at], inp[rows, at], chans[5:6, at], chans[6:7, at], decay, keep, starts
            )
            conv = conv_low[rows, at].astype(F32)
            l = lam[rows, at]
            common = l * keep
            grad_coeff = l * st_in[s, 7 : PAD - 1, at]
            direct[rows, at] = common * scale * ig
            d_ig = common * scale * conv
            d_scale = common * ig * conv
            d_sd = (1.0 - starts) * (grad_coeff * keep - d_scale * jnp.where(q > 0.001, sd / root, 0.0))
            d_log = d_sd * sd * -8.0
            d_rate = d_log * decay * rg * (1.0 - rg)
            d_inp = d_ig * ig * (1.0 - ig)
            rate_low[rows, at] = d_rate.astype(BF16)
            inp_low[rows, at] = d_inp.astype(BF16)
            for n, term in ((5, d_rate), (6, d_inp), (7, d_log * rg)):
                sums[n : n + 1, at] += jnp.sum(term, axis=0, keepdims=True)

    for copy in ins.copies[8:]:
        copy.wait()
    turn = turn_matrix()
    top, left = quarter_masks()
    for p in range(2):
        at = slice(2 * HS * p, 2 * HS * (p + 1))
        direct[:, at] += nt(rate_low[:, at], tables[2 * p]) + nt(inp_low[:, at], tables[2 * p + 1])
        dr = tn(conv_low[:, at], rate_low[:, at]).astype(BF16)
        di = tn(conv_low[:, at], inp_low[:, at]).astype(BF16)
        none = jnp.zeros_like(dr)
        straight = jnp.where(top, jnp.where(left, dr, none), jnp.where(left, none, di))
        crossed = jnp.where(top, jnp.where(left, di, none), jnp.where(left, none, dr))
        g = (straight.astype(F32) + nn(crossed, turn)).astype(BF16)
        for b in range(8):
            put_og(8 * p + b, D, g[48 * b : 48 * b + 48])

    rolled[:, SEQ:] = jnp.zeros((2, 8, LANES), F32)

    @pl.loop(0, 6)
    def _(c):
        at = cols(c)
        for s in range(2):
            rows = slice(s * SEQ, (s + 1) * SEQ)
            g = direct[rows, at]
            gu = chans[0:1, at] * g
            sums[4:5, at] += jnp.sum(g, axis=0, keepdims=True)
            sums[0:1, at] += jnp.sum(g * u_in[s, 8:, at], axis=0, keepdims=True)
            for k in range(1, 4):
                w = g * masks[1 + k, rows]
                sums[k : k + 1, at] += jnp.sum(w * u_in[s, 8 - k : PAD - k, at], axis=0, keepdims=True)
                rolled[s, 0:SEQ] = w
                gu = gu + chans[k : k + 1, at] * rolled[s, k : SEQ + k]
            gmix[rows, at] = (gu * masks[0, rows]).astype(BF16)

    v = jnp.concatenate([sums[0:8, 0:RC], jnp.zeros((LANES - 8, RC), F32)], axis=0).T.astype(BF16)
    for b in range(16):
        put_og(b, 1408, v[48 * b : 48 * b + 48])
    landed(wb, sems.at[0])

    v = tn(normed[...], gmix[:, 0:PB]).astype(BF16)
    for x, z in RINGS:
        for half in range(2):
            r = ring_rows(x, z) + 256 * half
            bp[x, z, 32 * half : 32 * half + 32, OG:EARLY] = v[r : r + 32]
    emit(saves, bp, places, 0, (p0, p1))
    mixed_part[...] = nt(gmix[...], rows_of(wb, 0, BRANCH))
    saves.start(mixed_part.at[pl.ds(0, SEQ)], o_mine)
    saves.start(mixed_part.at[pl.ds(SEQ, SEQ)], o_theirs)
    t = tok[...].astype(F32)
    sums[8:9] = jnp.sum(mixed_part[...] * (t * inv_rms(t)), axis=0, keepdims=True)
    v = jnp.concatenate([sums[8:16], jnp.zeros((LANES - 8, D), F32)], axis=0).T.astype(BF16)
    for x, z in RINGS:
        for half in range(2):
            r = ring_rows(x, z) + 256 * half
            bq[z, x, 32 * half : 32 * half + 32, QB:EARLY] = v[r : r + 32]

    v = tn(normed[...], gmix[:, PB:]).astype(BF16)
    for x, z in RINGS:
        for half in range(2):
            r = ring_rows(x, z) + 256 * half
            bq[z, x, 32 * half : 32 * half + 32, 0:QB] = v[r : r + 32]
    emit(saves, bq, places, 2, (q0, q1))
    saves.wait()


def join_sums(
    places, eo_p, eu_p, lo_p, lu_p, eo_q, eu_q, lo_q, lu_q,
    p0, p1, q0, q1,
    out, out_sems,
):
    saves = Saves(out_sems)
    for n, (axis, outs, a, b, c, d) in enumerate(
        ((2, (p0, p1), eo_p, eu_p, lo_p, lu_p), (0, (q0, q1), eo_q, eu_q, lo_q, lu_q))
    ):
        for j in range(4):
            at, to = places[4 + axis, j], 4 * n + j
            out[to, :, 0:EARLY] = add(a[at], b[at])
            out[to, :, EARLY:] = add(c[at], d[at])
            saves.start(out.at[to], outs[j // 2].at[j % 2])
    saves.wait()


def add(a, b):
    return (a.astype(F32) + b.astype(F32)).astype(BF16)


def half_sums(a_p, b_p, c_p, d_p, a_q, b_q, c_q, d_q, *rest):
    outs, (early, late, in_sems) = rest[-7:-3], rest[-3:]
    loads = Saves(in_sems)
    for n, (a, b, c, d) in enumerate(((a_p, b_p, c_p, d_p), (a_q, b_q, c_q, d_q))):
        for source, target in ((a, early.at[n, 0]), (b, early.at[n, 1]), (c, late.at[n, 0]), (d, late.at[n, 1])):
            loads.start(source.at[0], target)
    for n in range(2):
        for i, v in enumerate((early, late)):
            loads.copies[4 * n + 2 * i].wait()
            loads.copies[4 * n + 2 * i + 1].wait()
            outs[2 * n + i][...] = add(v[n, 0], v[n, 1])


def pass_on(a_p, f_p, a_q, f_q, *rest):
    o_p, o_q, v, in_sems, out_sems = rest[-5:]
    loads, saves = Saves(in_sems), Saves(out_sems)
    for i, source in enumerate((a_p, f_p, a_q, f_q)):
        loads.start(source.at[1], v.at[i])
    for n, out in enumerate((o_p, o_q)):
        loads.copies[2 * n].wait()
        loads.copies[2 * n + 1].wait()
        v[2 * n] = add(v[2 * n], v[2 * n + 1])
        saves.start(v.at[2 * n], out)
    saves.wait()


def cut(
    places, p0, p1, p2, q0, q1, q2,
    o0, o1, o2, o3,
    parts, sp, sq, sd, in_sems,
):
    load((p0.at[0], p1.at[0], p2, q0.at[0], q1.at[0], q2), [parts.at[i] for i in range(6)], in_sems)
    for n, out in enumerate((sp, sq)):
        out[...] = parts[3 * n].astype(F32) + parts[3 * n + 1].astype(F32) + parts[3 * n + 2].astype(F32)
    sd[0:64] = sp[:, EARLY : EARLY + D]
    sd[64:96, 0:512] = sp[0:32, EARLY + D : EARLY + FC]
    sd[64:96, 512:1024] = sp[32:64, EARLY + D : EARLY + FC]
    tail = jnp.concatenate([sp[48:64, 384 * r : 384 * r + 384] for r in range(3)], axis=0)
    og = jnp.concatenate([sp[0:48, 0:OG], tail], axis=1).astype(BF16)
    i = lax.broadcasted_iota(jnp.int32, (16, 48), 0)
    s = lax.broadcasted_iota(jnp.int32, (16, 48), 1)

    def two(rows):
        return jnp.concatenate(rows, axis=0).astype(BF16)

    for j, out in enumerate((o0, o1, o2, o3)):
        y = places[1, (0, 2, 3, 1)[j]]
        rows = [pl.ds(pl.multiple_of(32 * c + y * 8, 8), 8) for c in range(2)]
        out[:, 0:PB] = two([sp[r, OG:EARLY] for r in rows])
        out[:, PB : PB + PI] = two([sp[r, UNIT - PI :] for r in rows])
        out[:, PB + PI : DC] = two([sq[r] for r in rows])
        mine = jnp.where((s == i + y * 12) & (i < 12), 1.0, 0.0).astype(BF16)
        out[:, DC:DOWN] = nn(mine, og).astype(BF16)
        down = sd[pl.ds(pl.multiple_of(y * 24, 8), 24)]
        out[:, DOWN : DOWN + D] = down[0:16].astype(BF16)
        out[:, DOWN + D :] = two([down[16:24, 0:512], down[16:24, 512:]])


def finish(places, o0, o1, o2, o3, mine, theirs, out_grad, gate_grad, chan_grad, down_grad, v):
    v[...] = o0[...].astype(F32) + o1[...].astype(F32) + o2[...].astype(F32) + o3[...].astype(F32)
    core = places[3, 0]
    theirs[...] = v[pl.ds(pl.multiple_of((1 - core) * 8, 8), 8), 0:DC]
    mine[...] = v[pl.ds(pl.multiple_of(core * 8, 8), 8), 0:DC]
    out_grad[...] = v[0:12, DC : DC + D]
    gate_grad[...] = v[0:12, DC + D : DC + D + 384]
    chan_grad[...] = v[:, DC + D + 384 : DOWN].T[0:8]
    down_grad[0:16] = v[:, DOWN : DOWN + D]
    down_grad[16:24, 0:512] = v[0:8, DOWN + D :]
    down_grad[16:24, 512:] = v[8:16, DOWN + D :]


def unpack(places, mine, theirs, branch, inner, gains):
    def halves(ins):
        for c, v in enumerate(ins):
            for q in range(4):
                to = 768 * q + 384 * c
                if q == 0:
                    branch[:, to : to + PB] = v[:, 0:PB]
                    branch[:, to + PB : to + 384] = v[:, PB + PI : PB + PI + 128]
                else:
                    branch[:, to : to + 384] = v[:, PI + 384 * q : PI + 384 * q + 384]
                at = PB if q == 0 else DC - LATE + 768 * (q - 1)
                to = 1536 * q + 768 * c
                inner[:, to : to + 768] = v[:, at : at + 768]

    gains[...] = mine[:, DC - LATE - LANES : DC - LATE] + theirs[:, DC - LATE - LANES : DC - LATE]

    @pl.when(places[3, 0] == 0)
    def _():
        halves((mine, theirs))

    @pl.when(places[3, 0] == 1)
    def _():
        halves((theirs, mine))


VM, HB, SM, ANY = pltpu.VMEM, pltpu.HBM, pltpu.SMEM, pl.ANY


def kernel(body, ins, spaces, outs, scratch, mib, flops=0, aliases={}):
    moved = sum(v.size * v.dtype.itemsize for v in ins)
    ins = [pltpu.with_memory_space_constraint(v, HB) if s is HB else v for v, s in zip(ins, spaces)]
    return pl.pallas_call(
        body,
        out_shape=[HB(s, d) if at is HB else jax.ShapeDtypeStruct(s, d) for s, d, at in outs],
        in_specs=[pl.BlockSpec(memory_space=s) for s in spaces],
        out_specs=[pl.BlockSpec(memory_space=s) for _, _, s in outs],
        scratch_shapes=scratch,
        input_output_aliases=aliases,
        compiler_params=pltpu.CompilerParams(vmem_limit_bytes=mib * 2**20),
        cost_estimate=pl.CostEstimate(flops=flops, bytes_accessed=moved, transcendentals=0),
    )(*ins)


def shards(
    tokens, cotangent, segment, keep_mask, conv_state, lru_state, norm1_gain, conv_weight, lru_bias, decay_rate,
    gate_weight, branch_weight, out_weight, norm2_gain, mlp_in_weight, mlp_out_weight,
):
    here = my_place()
    core = here["core"]
    zero = jnp.zeros_like(core)
    places = jnp.stack(
        [jnp.stack(ring_places(axis, here)) for axis in "xyz"]
        + [jnp.stack([core, zero, zero, zero])]
        + [jnp.stack(pair_places(axis, here)) for axis in "xyz"]
    ).astype(jnp.int32)
    vmem, dma = pltpu.VMEM, pltpu.SemaphoreType.DMA

    tc = jnp.concatenate([tokens[0], cotangent[0]], axis=0)
    tc_other = swap(tc)
    marks = jnp.concatenate([segment, keep_mask], axis=1).astype(F32)
    states = jnp.concatenate([conv_state[0], lru_state], axis=0)
    sent = jnp.concatenate([core_half(states, 1 - core, 2), jnp.pad(marks, ((0, 0), (0, RC - 2 * SEQ)))], axis=0)
    sent = swap(sent)

    mine, theirs, own = kernel(
        pack,
        (places, branch_weight, mlp_in_weight, jnp.stack([norm1_gain, norm2_gain]), out_weight, gate_weight,
         jnp.concatenate([conv_weight, lru_bias, decay_rate[None]], axis=0), mlp_out_weight),
        [SM, HB, HB, VM, HB, HB, VM, HB],
        [((8, DC), BF16, VM)] * 2 + [((16, OWN - DC), BF16, VM)],
        [vmem(v.shape, BF16) for v in (branch_weight, mlp_in_weight, out_weight, gate_weight, mlp_out_weight)]
        + [dma((5,))],
        8,
    )
    (block,) = kernel(join, (places, mine, swap(theirs), own), [SM] + [VM] * 3, [((16, OWN), BF16, VM)], [], 8)

    row = ((64, UNIT), BF16)
    unit_of = ((2, 32, UNIT), BF16)
    p, q = kernel(
        unit,
        (places, *ring_direct(block, "y"), tc_other, sent),
        [SM] + [VM] * 4 + [ANY] * 2,
        [(*unit_of, HB)] * 2,
        [vmem(*row), vmem(*row), vmem((64, DC), F32), vmem((96, D), F32), dma((4,))],
        16,
    )
    early, late = (4, 64, EARLY), (4, 64, LATE)
    stack = ((4, 64, UNIT), BF16)
    p, q = ring_both(p, "z"), ring_both(q, "x")
    stacks = [((*v, n), BF16, HB) for n in (EARLY, LATE) for v in ((2, 4, 32), (2, 2, 2, 32))]
    unit_of = (2, 32, UNIT)
    partial = kernel(
        planes((0, 1, 2)),
        (places, *p[:3], *q[:3]),
        [SM] + [HB] * 6,
        stacks,
        [vmem((6, *unit_of), BF16), dma((6,)), dma((12,))],
        8,
    )
    pe, qe, pl_, ql = kernel(
        planes((3,)),
        (places, p[3], q[3], *partial),
        [SM, ANY, ANY] + [HB] * 4,
        stacks,
        [vmem((2, *unit_of), BF16), dma((2,)), dma((4,))],
        8,
        aliases={3 + i: i for i in range(4)},
    )
    pe, qe, pl_, ql = ring_both(pe, "x"), ring_both(qe, "z"), ring_both(pl_, "x"), ring_both(ql, "z")

    tok = jnp.concatenate([tc[:SEQ], tc_other[:SEQ]], axis=0)
    cot = jnp.concatenate([tc[SEQ:], tc_other[SEQ:]], axis=0)
    states = jnp.stack([core_half(states, core, 2), sent[:4]])
    marks = jnp.concatenate([marks, sent[4:, : 2 * SEQ]], axis=0)
    seg, keep = marks[:, :SEQ], marks[:, SEQ:]
    earlier = [jnp.concatenate([jnp.repeat(seg[:, :1], k, axis=1), seg[:, : SEQ - k]], axis=1) for k in range(1, 4)]
    masks = jnp.stack([keep, (earlier[0] != seg).astype(F32)] + [(e == seg).astype(F32) for e in earlier])
    masks = jnp.broadcast_to(masks.reshape(5, TOK, 1), (5, TOK, LANES))

    wide, wide_low = ((TOK, D), F32), ((TOK, D), BF16)
    act, act_low, padded = ((TOK, RC), F32), ((TOK, RC), BF16), ((2, PAD, RC), F32)
    tables = ((4, 2 * HS, 2 * HS), BF16)
    saved = [wide_low, act_low, padded, act, act_low, act, act, padded, tables]
    part, finals, gains, chans, normed, merged, u, gate_in, conv_low, rate, inp, st, table = kernel(
        rec_forward,
        (places, tok, masks, states[:, :3], states[:, 3:], *pe, *qe),
        [SM] + [VM] * 4 + [HB] * 8,
        [((TOK + 8, D), F32, VM), ((4, RC), F32, VM), ((8, D), F32, VM), ((8, RC), F32, VM)]
        + [(*v, HB) for v in saved],
        [vmem((*ROWS, PB + EARLY), BF16), vmem((*OG_ROWS, OGC), BF16)]
        + [vmem(*v) for v in saved + [act, act]]
        + [dma((2,)), dma((9,))],
        32,
        2 * TOK * (D * BRANCH + RC * (D + 768)),
    )
    half = ((SEQ, D), F32)
    other = swap(part)
    normed2, own, residual = kernel(
        mlp_norm,
        (tok, part, other, gains),
        [VM] * 4,
        [(*wide_low, VM), (*half, VM), (*wide, HB)],
        [vmem(*wide), dma],
        16,
    )
    hidden, ggu, base, back = kernel(
        mlp,
        (places, cot, normed2, own, *pl_, *ql),
        [SM] + [VM] * 3 + [ANY] * 8,
        [((TOK, FC), BF16, VM), ((TOK, INNER), BF16, VM), (*half, HB), ((TOK + SEQ, D), F32, HB)],
        [vmem((*ROWS, INNER), BF16), vmem((*DOWN_ROWS, D), BF16)]
        + [vmem(*v) for v in (wide, wide, half)]
        + [dma((2,)), dma((3,))],
        32,
        2 * TOK * D * (2 * INNER + 2 * FC),
    )
    back_other = swap(back)
    outs = kernel(
        mlp_grads,
        (places, cot, normed2, hidden, ggu),
        [SM] + [VM] * 4,
        [((2, *late), BF16, HB)] * 4,
        [vmem((4,) + late, BF16), vmem((4,) + late, BF16), dma((20,))],
        32,
        2 * TOK * D * (INNER + FC),
    )
    lp, lq = outs[:2], outs[2:]

    def first_half(p, q, routes):
        return send(p[1], partner(routes[0], 0)), send(q[1], partner(routes[1], 0))

    def second_half(p, q, came, routes, shape, until=(), lands=HB):
        up = kernel(
            pass_on,
            (p[0], came[0], q[0], came[1], *until),
            [HB, lands, HB, lands] + [HB] * len(until),
            [(shape, BF16, HB)] * 2,
            [vmem((4,) + shape, BF16), dma((4,)), dma((2,))],
            16,
        )
        return send(up[0], partner(routes[0], 1)), send(up[1], partner(routes[1], 1))

    late_came = first_half(lp, lq, "xz")
    outs = kernel(
        rec_backward,
        (places, tok, cot, masks, gains, chans, back_other, back, residual, normed, merged, u, gate_in, conv_low, rate,
         inp, st, table, *pe, *qe),
        [SM] + [VM] * 6 + [HB] * 19,
        [(*v, HB) for v in (half, half, half)] + [((2, *early), BF16, HB)] * 4,
        [vmem((*ROWS, BRANCH), BF16), vmem((*OG_ROWS, OGC), BF16)]
        + [vmem(*v) for v in (wide, wide, wide_low, act_low, padded, act, act_low, act, act, padded, tables)]
        + [vmem(*v) for v in (act, wide_low, act, act, act_low, act_low, act, ((TOK, BRANCH), BF16))]
        + [vmem((2, PAD, LANES), F32), vmem((16, D), F32), vmem(*wide), vmem(*half)]
        + [vmem((4,) + early, BF16), vmem((4,) + early, BF16), dma((2,)), dma((11,)), dma((11,))],
        48,
        2 * TOK * D * (2 * BRANCH + 2 * RC),
    )
    grad_residual, mixed_mine, mixed_theirs = outs[:3]
    ep, eq = outs[3:5], outs[5:]
    early_came = first_half(ep, eq, "xz")
    late_up = second_half(lp, lq, late_came, "xz", late, (ep[0],))
    early_up = second_half(ep, eq, early_came, "xz", early)

    summed = kernel(
        half_sums,
        (ep[0], early_came[0], lp[0], late_came[0], eq[0], early_came[1], lq[0], late_came[1]),
        [HB] * 8,
        [(early, BF16, VM), (late, BF16, VM)] * 2,
        [vmem((2, 2) + early, BF16), vmem((2, 2) + late, BF16), dma((8,))],
        16,
    )
    outs = kernel(
        join_sums,
        (places, summed[0], early_up[0], summed[1], late_up[0], summed[2], early_up[1], summed[3], late_up[1]),
        [SM] + [VM] * 8,
        [((2, 64, UNIT), BF16, HB)] * 4,
        [vmem((8, 64, UNIT), BF16), dma((8,))],
        8,
    )
    tp, tq = outs[:2], outs[2:]
    came = first_half(tp, tq, "zx")
    up = second_half(tp, tq, came, "zx", (64, UNIT), lands=ANY)
    sums = kernel(
        cut,
        (places, tp[0], came[0], up[0], tq[0], came[1], up[1]),
        [SM] + [HB, ANY, ANY] * 2,
        [((16, OWN), BF16, VM)] * 4,
        [vmem((6, 64, UNIT), BF16), vmem((64, UNIT), F32), vmem((64, UNIT), F32), vmem((96, D), F32), dma((6,))],
        16,
    )
    mine, theirs, out_grad, gate_grad, chan_grad, down_grad = kernel(
        finish,
        (places, *terms_direct(sums, "y")),
        [SM] + [VM] * 4,
        [((8, DC), F32, VM)] * 2 + [(s, F32, VM) for s in ((12, D), (12, 384), (8, 16), (24, D))],
        [vmem((16, OWN), F32)],
        8,
    )
    branch_grad, in_grad, gain_grads = kernel(
        unpack,
        (places, mine, swap(theirs)),
        [SM] + [VM] * 2,
        [((8, 2 * R), F32, VM), ((8, 2 * F), F32, VM), ((8, LANES), F32, VM)],
        [],
        8,
    )

    output = (base + back_other[TOK:]).astype(BF16)
    grad, _ = rms_back(mixed_mine + swap(mixed_theirs), tok[:SEQ].astype(F32), gains[0])
    input_grad = (grad_residual + grad).astype(BF16)
    theirs = other[TOK : TOK + 4, :RC]
    finals = jnp.stack(
        [v.reshape(1, 4, 2, 384) for v in (jnp.where(core == 0, finals, theirs), jnp.where(core == 0, theirs, finals))],
        axis=3,
    ).reshape(1, 4, R)
    return (
        output[None],
        input_grad[None],
        finals[:, :3],
        finals[:, 3],
        gain_grads[:, 0],
        chan_grad[:4, :12],
        chan_grad[4:7, :12],
        chan_grad[7, :12],
        gate_grad,
        branch_grad,
        out_grad,
        gain_grads[:, 1],
        in_grad,
        down_grad,
    )


def solution(mesh):
    rows, last = P(AXES), P(None, AXES)
    specs = [rows] * 6 + [rows, last, last] + [rows] * 7
    outs = [rows] * 4 + [rows, last, last] + [rows] * 7
    return jax.shard_map(
        shards, mesh=mesh, in_specs=tuple(specs), out_specs=tuple(outs), check_vma=False
    )
```

```python
import jax
import jax.numpy as jnp
from jax import lax
from jax.experimental import pallas as pl
from jax.experimental.pallas import tpu as pltpu
from jax.sharding import PartitionSpec as P

AXES = ("dp", "fsdp")
D, R, F, SEQ = 1024, 1536, 3072, 128
RC, FC = R // 2, F // 2
HS = 192
F32, BF16 = jnp.float32, jnp.bfloat16
BRANCH, INNER = 2 * RC, 2 * FC
TOK, PAD, LANES = 2 * SEQ, SEQ + 8, 128

EARLY, LATE = 1408, 2304
UNIT = EARLY + LATE
OG, PB, PI, QB = 1152, 256, 768, 1280
DC = PB + PI + UNIT
OGC = 1536
DOWN = DC + OGC
OWN = DOWN + D + D // 2


def place_of(device):
    outer, inner = divmod(device, 32)
    x_hi, core = divmod(outer, 2)
    z, rest = divmod(inner, 8)
    x_lo, y = divmod(rest, 4)
    return dict(x=x_hi * 2 + x_lo, y=y, z=z, core=core)


def device_at(x, y, z, core):
    return ((x // 2) * 2 + core) * 32 + z * 8 + (x % 2) * 4 + y


def pairs(move):
    return [(d, device_at(**move(place_of(d)))) for d in range(128)]


def along(axis, steps):
    def move(p):
        sign = 1 if p["core"] == 0 else -1
        return {**p, axis: (p[axis] + sign * steps) % 4}

    return pairs(move)


def other_core(p):
    return {**p, "core": 1 - p["core"]}


def partner(axis, turn):
    def move(p):
        i = p[axis]
        return {**p, axis: i ^ 1 if (p["core"] + turn) % 2 == 0 else 3 - i}

    return pairs(move)


def opposite(axis):
    return pairs(lambda p: {**p, axis: (p[axis] + 2) % 4})


def send(value, route):
    return lax.ppermute(value, AXES, route)


def swap(value):
    return send(value, pairs(other_core))


def my_place():
    device = lax.axis_index(AXES)
    outer, inner = device // 32, device % 32
    return dict(x=(outer // 2) * 2 + (inner // 4) % 2, y=inner % 4, z=inner // 8, core=outer % 2)


def ring_places(axis, here):
    sign, at = 1 - 2 * here["core"], here[axis]
    return [at, (at - sign) % 4, (at + sign) % 4, (at + 2) % 4]


def ring(block, axis):
    one = send(block, along(axis, 1))
    two = send(one, along(axis, 1))
    return block, one, send(two, along(axis, 1)), two


def ring_both(block, axis):
    up, down = send(block, along(axis, 1)), send(block, along(axis, -1))
    return block, up, down, send(up, along(axis, 1))


def pair_places(axis, here):
    i, odd = here[axis], here["core"] == 1
    by_one, by_ends = i + 1 - 2 * (i % 2), 3 - i
    return [i, jnp.where(odd, by_one, by_ends), jnp.where(odd, by_ends, by_one), (i + 2) % 4]


def ring_direct(block, axis):
    return block, send(block, along(axis, 1)), send(block, along(axis, -1)), send(block, opposite(axis))


def terms_direct(terms, axis):
    own, ahead, far, behind = terms
    return own, send(ahead, along(axis, 1)), send(far, opposite(axis)), send(behind, along(axis, -1))


def total(*terms):
    out = terms[0].astype(F32)
    for term in terms[1:]:
        out = out + term.astype(F32)
    return out.astype(BF16)


def core_half(array, core, blocks):
    v = array.reshape(array.shape[:-1] + (blocks, 2, array.shape[-1] // (2 * blocks)))
    v = lax.dynamic_index_in_dim(v, core, v.ndim - 2, keepdims=False)
    return v.reshape(array.shape[:-1] + (array.shape[-1] // 2,))


def dot(a, b, dims):
    return lax.dot_general(a, b, (dims, ((), ())), preferred_element_type=F32)


def nn(a, b):
    return dot(a, b, ((1,), (0,)))


def nt(a, b):
    return dot(a, b, ((1,), (1,)))


def tn(a, b):
    return dot(a, b, ((0,), (0,)))


def inv_rms(v):
    return lax.rsqrt(jnp.mean(v * v, axis=-1, keepdims=True) + 1e-6)


def rms_back(grad, v, gain):
    s = inv_rms(v)
    n = v * s
    g2 = grad * gain
    return s * (g2 - n * jnp.mean(g2 * n, axis=-1, keepdims=True)), grad * n


C0, C1 = 0.7978845608028654, 0.044715


def gelu_both(a):
    t = jnp.tanh(C0 * (a + C1 * (a * a * a)))
    half = 0.5 * (1.0 + t)
    return a * half, half + 0.5 * a * (1.0 - t * t) * (C0 * (1.0 + 3.0 * C1 * (a * a)))


def gates(rate, inp, bias1, bias2, decay, keep, starts):
    rg = jax.nn.sigmoid(rate + bias1)
    ig = jax.nn.sigmoid(inp + bias2)
    sd = jnp.exp(-8.0 * rg * decay)
    q = 1.0 - sd * sd
    root = jnp.sqrt(jnp.maximum(q, 0.001))
    scale = starts + (1.0 - starts) * root
    return rg, ig, sd, q, root, scale


def cols(c):
    return pl.ds(pl.multiple_of(c * LANES, LANES), LANES)


class Saves:
    def __init__(self, sem):
        self.sem, self.copies = sem, []

    def start(self, source, target):
        self.copies.append(pltpu.make_async_copy(source, target, self.sem.at[len(self.copies)]))
        self.copies[-1].start()

    def wait(self):
        for copy in self.copies:
            copy.wait()


def pick(rows, where):
    return jnp.where(lax.broadcasted_iota(jnp.int32, (rows, where.shape[1]), 0) == where, 1.0, 0.0).astype(BF16)


def stand(values, rows):
    v = values.astype(F32)
    i = lax.broadcasted_iota(jnp.int32, (rows, v.shape[1]), 0)
    j = lax.broadcasted_iota(jnp.int32, (rows, v.shape[1]), 1)
    lane = lax.broadcasted_iota(jnp.int32, (rows, LANES), 1)
    out = jnp.zeros((rows, LANES), F32)
    for n in range(v.shape[0]):
        column = jnp.sum(jnp.where(i == j, v[n : n + 1], 0.0), axis=1, keepdims=True)
        out = out + jnp.where(lane == n, column, 0.0)
    return out


def load(sources, targets, sems):
    copies = Saves(sems)
    for source, target in zip(sources, targets):
        copies.start(source, target)
    copies.wait()


def pack(
    places, i_branch, i_inner, gain, i_out, i_gate, perchan, i_down, mine, theirs, own,
    branch, inner, out, gate, down, sems,
):
    load((i_branch, i_inner, i_out, i_gate, i_down), (branch, inner, out, gate, down), sems)

    gains = stand(gain[...], 8).astype(BF16)

    def halves(outs):
        for c, to_core in enumerate(outs):
            for q in range(4):
                v = branch[:, 768 * q + 384 * c : 768 * q + 384 * c + 384]
                if q == 0:
                    to_core[:, 0:PB] = v[:, 0:PB]
                    to_core[:, PB + PI : PB + PI + 128] = v[:, PB:]
                else:
                    to_core[:, PI + 384 * q : PI + 384 * q + 384] = v
                v = inner[:, 1536 * q + 768 * c : 1536 * q + 768 * c + 768]
                to = PB if q == 0 else DC - LATE + 768 * (q - 1)
                to_core[:, to : to + 768] = v
            tile = DC - LATE - LANES
            to_core[:, tile : tile + LANES] = gains

    @pl.when(places[3, 0] == 0)
    def _():
        halves((mine, theirs))

    @pl.when(places[3, 0] == 1)
    def _():
        halves((theirs, mine))

    own[...] = jnp.zeros_like(own)
    own[0:12, 0:D] = out[...]
    own[0:12, D : D + 384] = gate[...]
    own[:, 1408:OGC] = stand(perchan[...], 16).astype(BF16)
    own[:, OGC : OGC + D] = down[0:16]
    own[:, OGC + D :] = jnp.concatenate(
        [down[16:24, 0:512].astype(F32), down[16:24, 512:].astype(F32)], axis=0
    ).astype(BF16)


def join(places, mine, theirs, own, block):
    def rows(low, high):
        block[:, 0:DC] = jnp.concatenate([low[...].astype(F32), high[...].astype(F32)], axis=0).astype(BF16)

    @pl.when(places[3, 0] == 0)
    def _():
        rows(mine, theirs)

    @pl.when(places[3, 0] == 1)
    def _():
        rows(theirs, mine)

    block[:, DC:] = own[...]


def unit(places, p0, p1, p2, p3, *rest):
    o_p, o_q, p, q, d, dn, sems = rest[-7:]
    ogs = []
    s = lax.broadcasted_iota(jnp.int32, (1, 64), 1)
    y = jnp.zeros((1, 64), jnp.int32)
    for j, piece in enumerate((p0, p1, p2, p3)):
        at = places[1, j]
        y = jnp.where(s // 16 == j, at, y)
        v = piece[:, 0:DC].astype(F32)
        for c in range(2):
            d[pl.ds(pl.multiple_of(c * 32 + at * 8, 8), 8)] = v[8 * c : 8 * c + 8]
        ogs.append(piece[:, DC:DOWN])
        v = piece[:, DOWN:].astype(F32)
        dn[pl.ds(pl.multiple_of(at * 24, 8), 16)] = v[:, 0:D]
        for h in range(2):
            dn[pl.ds(pl.multiple_of(at * 24 + 16, 8), 8), 512 * h : 512 * h + 512] = v[8 * h : 8 * h + 8, D:]
    saves = Saves(sems)
    q[...] = d[:, PB + PI :].astype(BF16)
    for c in range(2):
        saves.start(q.at[pl.ds(32 * c, 32)], o_q.at[c])
    p[:, OG:EARLY] = d[:, 0:PB].astype(BF16)
    p[:, UNIT - PI :] = d[:, PB : PB + PI].astype(BF16)
    i = s % 16
    og = nn(pick(48, jnp.where(i < 12, y * 12 + i, 64)), jnp.concatenate(ogs, axis=0)).astype(BF16)
    p[0:48, 0:OG] = og[:, 0:OG]
    for r in range(3):
        p[48:64, 384 * r : 384 * r + 384] = og[16 * r : 16 * r + 16, OG:]
    p[:, EARLY : EARLY + D] = dn[0:64].astype(BF16)
    p[0:32, EARLY + D : EARLY + FC] = dn[64:96, 0:512].astype(BF16)
    p[32:64, EARLY + D : EARLY + FC] = dn[64:96, 512:1024].astype(BF16)
    for c in range(2):
        saves.start(p.at[pl.ds(32 * c, 32)], o_p.at[c])
    saves.wait()


def planes(which):
    def body(places, *refs):
        n = len(which)
        (o_pe, o_qe, o_pl, o_ql), v, in_sems, out_sems = refs[-7:-3], *refs[-3:]
        loads, saves = Saves(in_sems), Saves(out_sems)
        for i, piece in enumerate(refs[: 2 * n]):
            loads.start(piece, v.at[i])
        for i in range(2 * n):
            loads.copies[i].wait()
            j = which[i % n]
            x = places[0, j]
            for first, count, p, q in ((0, EARLY, o_pe, o_qe), (EARLY, LATE, o_pl, o_ql)):
                target = p.at[:, places[2, j]] if i < n else q.at[x // 2, :, x % 2]
                saves.start(v.at[i, :, :, pl.ds(first, count)], target)
        saves.wait()

    return body


ROWS = (2, 2, 4, 2, 32)
OG_ROWS, DOWN_ROWS = (2, 4, 2, 48), (2, 4, 2, 96)


def ring_rows(x, z):
    return (x // 2) * 512 + z * 64 + (x % 2) * 32


def p_copy(piece, places, j, first, count, block, to, sem):
    x = places[0, j]
    target = block.at[x // 2, :, :, x % 2, :, pl.ds(to, count)]
    pltpu.make_async_copy(piece.at[..., pl.ds(first, count)], target, sem).start()


def q_copy(piece, places, j, first, count, block, to, sem):
    target = block.at[:, :, places[2, j], :, :, pl.ds(to, count)]
    pltpu.make_async_copy(piece.at[..., pl.ds(first, count)], target, sem).start()


def og_copy(piece, places, j, block, sem):
    x = places[0, j]
    block = block.at[x // 2, :, x % 2]
    for source, target in (
        (piece.at[0, :, :, pl.ds(0, OG)], block.at[:, pl.ds(0, 32), pl.ds(0, OG)]),
        (piece.at[1, :, pl.ds(0, 16), pl.ds(0, OG)], block.at[:, pl.ds(32, 16), pl.ds(0, OG)]),
    ):
        pltpu.make_async_copy(source, target, sem).start()
    for r in range(3):
        pltpu.make_async_copy(
            piece.at[1, :, pl.ds(16, 16), pl.ds(384 * r, 384)], block.at[:, pl.ds(16 * r, 16), pl.ds(OG, 384)], sem
        ).start()


def down_copy(piece, places, j, block, sem):
    x = places[0, j]
    block = block.at[x // 2, :, x % 2]
    for h in range(2):
        pltpu.make_async_copy(piece.at[h, :, :, pl.ds(0, D)], block.at[:, pl.ds(32 * h, 32)], sem).start()
        pltpu.make_async_copy(
            piece.at[h, :, :, pl.ds(D, 512)], block.at[:, pl.ds(64, 32), pl.ds(512 * h, 512)], sem
        ).start()


def rows_of(block, first, count):
    return block[..., first : first + count].reshape(D, count)


def landed(block, sem):
    pltpu.make_async_copy(block, block, sem).wait()


def turn_matrix():
    i = lax.broadcasted_iota(jnp.int32, (2 * HS, 2 * HS), 0)
    j = lax.broadcasted_iota(jnp.int32, (2 * HS, 2 * HS), 1)
    return jnp.where((i == j + HS) | (j == i + HS), 1.0, 0.0).astype(BF16)


def quarter_masks():
    i = lax.broadcasted_iota(jnp.int32, (2 * HS, 2 * HS), 0) < HS
    j = lax.broadcasted_iota(jnp.int32, (2 * HS, 2 * HS), 1) < HS
    return i, j


def rec_forward(
    places, tok, masks, conv_before, lru_before, p0, p1, p2, p3, q0, q1, q2, q3,
    part, finals, gains, chans, o_normed, o_merged, o_u, o_gate, o_conv, o_rate, o_inp, o_st, o_tables,
    wb, wog, normed, merged, u, gate_in, conv_low, rate, inp, st, tables, coeff, drive, sems, out_sems,
):
    for j, (p, q) in enumerate(((p0, q0), (p1, q1), (p2, q2), (p3, q3))):
        p_copy(p, places, j, OG, PB, wb, 0, sems.at[0])
        q_copy(q, places, j, 0, EARLY, wb, PB, sems.at[0])
    for j, p in enumerate((p0, p1, p2, p3)):
        og_copy(p, places, j, wog, sems.at[1])
    saves = Saves(out_sems)
    t = tok[...].astype(F32)
    scaled = t * inv_rms(t)
    landed(wb, sems.at[0])
    gains[...] = rows_of(wb, BRANCH, LANES).astype(F32).T[:8]
    normed[...] = (scaled * gains[0:1]).astype(BF16)
    saves.start(normed, o_normed)
    for s in range(2):
        u[s, 0:8] = jnp.zeros((8, RC), F32)
        u[s, 5:8] = conv_before[s]
        st[s, 0:8] = jnp.zeros((8, RC), F32)
        st[s, 7:8] = lru_before[s]

    v = nn(normed[...], rows_of(wb, 0, RC))
    for s in range(2):
        rows = slice(s * SEQ, (s + 1) * SEQ)
        for c in range(6):
            u[s, 8:, LANES * c : LANES * c + LANES] = v[rows, LANES * c : LANES * c + LANES] * masks[0, rows]

    saves.start(u, o_u)

    gate_in[...] = nn(normed[...], rows_of(wb, RC, RC))

    saves.start(gate_in, o_gate)
    landed(wog, sems.at[1])
    chans[...] = wog[..., 1408:].reshape(RC, LANES).astype(F32).T[:8]

    @pl.loop(0, 6)
    def _(c):
        at = cols(c)
        for s in range(2):
            rows = slice(s * SEQ, (s + 1) * SEQ)
            v = chans[4:5, at] + chans[0:1, at] * u[s, 8:, at]
            for k in range(1, 4):
                v = v + chans[k : k + 1, at] * (u[s, 8 - k : PAD - k, at] * masks[1 + k, rows])
            conv_low[rows, at] = v.astype(BF16)

    saves.start(conv_low, o_conv)
    turn = turn_matrix()
    top, left = quarter_masks()
    for p in range(2):
        g = wog[p, :, :, :, D : D + 384].reshape(2 * HS, 2 * HS)
        turned = nn(g, turn).astype(BF16)
        zero = jnp.zeros_like(g)
        tables[2 * p] = jnp.where(left, jnp.where(top, g, zero), jnp.where(top, zero, turned))
        tables[2 * p + 1] = jnp.where(left, jnp.where(top, turned, zero), jnp.where(top, zero, g))
        at = slice(2 * HS * p, 2 * HS * (p + 1))
        rate[:, at] = nn(conv_low[:, at], tables[2 * p])
        inp[:, at] = nn(conv_low[:, at], tables[2 * p + 1])
    saves.start(tables, o_tables)
    saves.start(rate, o_rate)
    saves.start(inp, o_inp)

    @pl.loop(0, 6)
    def _(c):
        at = cols(c)
        keep, starts = masks[0], masks[1]
        _, ig, sd, _, _, scale = gates(
            rate[:, at], inp[:, at], chans[5:6, at], chans[6:7, at], chans[7:8, at], keep, starts
        )
        coeff[:, at] = (1.0 - starts) * (keep * sd + (1.0 - keep))
        drive[:, at] = keep * scale * ig * conv_low[:, at].astype(F32)

    row = lax.broadcasted_iota(jnp.int32, (8, RC), 0)

    def forward(i, carry):
        new = []
        for s in range(2):
            at = pl.ds(pl.multiple_of(s * SEQ + i * 8, 8), 8)
            a, b = coeff[at], drive[at]
            for k in (1, 2, 4):
                later = row >= k
                b = jnp.where(later, a * pltpu.roll(b, k, 0) + b, b)
                a = jnp.where(later, a * pltpu.roll(a, k, 0), a)
            h = a * carry[s] + b
            st[s, pl.ds(pl.multiple_of(8 + i * 8, 8), 8)] = h
            new.append(h[7:8])
        return tuple(new)

    last = lax.fori_loop(0, SEQ // 8, forward, (lru_before[0], lru_before[1]))
    saves.start(st, o_st)
    part[TOK:] = jnp.zeros((8, D), F32)
    part[TOK : TOK + 3, 0:RC] = u[1, PAD - 3 :]
    part[TOK + 3 : TOK + 4, 0:RC] = last[1]
    finals[0:3] = u[0, PAD - 3 :]
    finals[3:4] = last[0]

    @pl.loop(0, 6)
    def _(c):
        at = cols(c)
        act, _ = gelu_both(gate_in[:, at])
        for s in range(2):
            rows = slice(s * SEQ, (s + 1) * SEQ)
            merged[rows, at] = (st[s, 8:, at] * act[rows]).astype(BF16)

    saves.start(merged, o_merged)

    part[0:TOK] = nn(merged[...], wog[..., 0:D].reshape(RC, D))

    saves.wait()


def mlp_norm(tok, part, other, gains, normed2, own, o_residual, residual, sem):
    for s in range(2):
        rows, theirs = slice(s * SEQ, (s + 1) * SEQ), slice((1 - s) * SEQ, (2 - s) * SEQ)
        v = tok[rows].astype(F32) + (part[rows] + other[theirs])
        residual[rows] = v
        normed2[rows] = (v * inv_rms(v) * gains[1:2]).astype(BF16)
    copy = pltpu.make_async_copy(residual, o_residual, sem)
    copy.start()
    own[...] = residual[0:SEQ]
    copy.wait()


def mlp(
    places, cot, normed2, own, p0, p1, p2, p3, q0, q1, q2, q3,
    hidden, ggu, o_base, o_back,
    win, wdown, grad_hidden, down, back, base, sems, out_sems,
):
    for j, p in enumerate((p0, p1, p2, p3)):
        down_copy(p, places, j, wdown, sems.at[1])
    for j, (p, q) in enumerate(((p0, q0), (p1, q1), (p2, q2), (p3, q3))):
        p_copy(p, places, j, FC, PI, win, 0, sems.at[0])
        q_copy(q, places, j, 0, LATE, win, PI, sems.at[0])
    saves = Saves(out_sems)
    landed(wdown, sems.at[1])
    for c in range(2):
        grad_hidden[c] = nt(cot[...], wdown[c].reshape(768, D))
    landed(win, sems.at[0])
    for c in range(2):
        at, up = slice(768 * c, 768 * c + 768), slice(FC + 768 * c, FC + 768 * c + 768)
        wa, wu = rows_of(win, 768 * c, 768), rows_of(win, FC + 768 * c, 768)
        a = nn(normed2[...], wa)
        b = nn(normed2[...], wu)
        ga, da = gelu_both(a)
        h = (ga * b).astype(BF16)
        hidden[:, at] = h
        gh = grad_hidden[c]
        gg_a = (gh * b * da).astype(BF16)
        gg_b = (gh * ga).astype(BF16)
        ggu[:, at] = gg_a
        ggu[:, up] = gg_b
        if c == 0:
            down[...] = nn(h, wdown[c].reshape(768, D))
            back[...] = nt(gg_a, wa) + nt(gg_b, wu)
        else:
            down[...] += nn(h, wdown[c].reshape(768, D))
            back[...] += nt(gg_a, wa) + nt(gg_b, wu)

    saves.start(back, o_back.at[pl.ds(0, TOK)])
    saves.start(down.at[pl.ds(SEQ, SEQ)], o_back.at[pl.ds(TOK, SEQ)])
    base[...] = own[...] + down[0:SEQ]
    saves.start(base, o_base)
    saves.wait()


def emit(saves, block, places, axis, outs):
    for j in range(4):
        saves.start(block.at[places[4 + axis, j]], outs[j // 2].at[j % 2])


RINGS = [(x, z) for x in range(4) for z in range(4)]


def emit_columns(saves, block, places, axis, outs, first, count):
    for j in range(4):
        columns = pl.ds(first, count)
        saves.start(block.at[places[4 + axis, j], :, :, columns], outs[j // 2].at[j % 2, :, :, columns])


def mlp_grads(
    places, cot, normed2, hidden, ggu, p0, p1, q0, q1,
    bp, bq, out_sems,
):
    saves = Saves(out_sems)
    for xh in range(2):
        v = tn(hidden[:, 768 * xh : 768 * xh + 768], cot[...]).astype(BF16)
        for z in range(4):
            for xl in range(2):
                r = 96 * (2 * z + xl)
                bp[2 * xh + xl, z, :, 0:D] = v[r : r + 64]
                bp[2 * xh + xl, z, 0:32, D:FC] = v[r + 64 : r + 96, 0:512]
                bp[2 * xh + xl, z, 32:64, D:FC] = v[r + 64 : r + 96, 512:1024]
    emit_columns(saves, bp, places, 0, (p0, p1), 0, FC)

    def put(block, order, first, to):
        v = tn(normed2[...], ggu[:, first : first + 768]).astype(BF16)
        for x, z in RINGS:
            for half in range(2):
                r = ring_rows(x, z) + 256 * half
                at = (x, z) if order else (z, x)
                block[(*at, slice(32 * half, 32 * half + 32), slice(to, to + 768))] = v[r : r + 32]

    put(bp, True, 0, FC)
    emit_columns(saves, bp, places, 0, (p0, p1), FC, PI)
    for part in range(3):
        put(bq, False, 768 * (part + 1), 768 * part)
        emit_columns(saves, bq, places, 2, (q0, q1), 768 * part, 768)
    saves.wait()


def rec_backward(
    places, tok, cot, masks, gains, chans, other, i_back, i_residual, i_normed, i_merged, i_u, i_gate, i_conv, i_rate,
    i_inp, i_st, i_tables, wp0, wp1, wp2, wp3, wq0, wq1, wq2, wq3,
    o_residual, o_mine, o_theirs, p0, p1, q0, q1,
    wb, wog, part, residual, normed, merged, u_in, gate_in, conv_low, rate, inp, st_in, tables,
    coeff, grad_branch, gs, lam, rate_low, inp_low, direct, gmix, rolled, sums, mixed_part, own_residual, bp, bq,
    sems, in_sems, out_sems,
):
    ins = Saves(in_sems)
    for source, target in (
        (i_back.at[pl.ds(0, TOK)], part), (i_residual, residual), (i_merged, merged), (i_gate, gate_in), (i_st, st_in),
        (i_rate, rate), (i_inp, inp), (i_conv, conv_low), (i_tables, tables), (i_u, u_in), (i_normed, normed),
    ):
        ins.start(source, target)
    for j, p in enumerate((wp0, wp1, wp2, wp3)):
        og_copy(p, places, j, wog, sems.at[1])
    for j, (p, q) in enumerate(((wp0, wq0), (wp1, wq1), (wp2, wq2), (wp3, wq3))):
        p_copy(p, places, j, OG, PB, wb, 0, sems.at[0])
        q_copy(q, places, j, 0, QB, wb, PB, sems.at[0])
    saves = Saves(out_sems)
    sums[...] = jnp.zeros_like(sums)
    for copy in ins.copies[0:2]:
        copy.wait()
    for s in range(2):
        rows, theirs = slice(s * SEQ, (s + 1) * SEQ), slice((1 - s) * SEQ, (2 - s) * SEQ)
        grad, term = rms_back(part[rows] + other[theirs], residual[rows], gains[1:2])
        grad = cot[rows].astype(F32) + grad
        grad_branch[rows] = grad.astype(BF16)
        if s == 0:
            own_residual[...] = grad
            sums[9:10] = jnp.sum(term, axis=0, keepdims=True)
    saves.start(own_residual, o_residual)

    def put_og(b, first, v):
        x, z = (b // 8) * 2 + b % 2, (b // 2) % 4
        n = min(max(OG - first, 0), v.shape[1])
        if n:
            bp[x, z, 0:48, first : first + n] = v[:, :n]
        if n < v.shape[1]:
            to = first + n - OG
            for r in range(3):
                bp[x, z, 48:64, 384 * r + to : 384 * r + to + v.shape[1] - n] = v[16 * r : 16 * r + 16, n:]

    ins.copies[2].wait()
    v = tn(merged[...], grad_branch[...]).astype(BF16)
    for b in range(16):
        put_og(b, 0, v[48 * b : 48 * b + 48])
    landed(wog, sems.at[1])
    gs[...] = nt(grad_branch[...], wog[..., 0:D].reshape(RC, D))
    for copy in ins.copies[3:5]:
        copy.wait()

    @pl.loop(0, 6)
    def _(c):
        at = cols(c)
        act, act_grad = gelu_both(gate_in[:, at])
        g = gs[:, at]
        for s in range(2):
            rows = slice(s * SEQ, (s + 1) * SEQ)
            gmix[rows, pl.ds(pl.multiple_of(RC + c * LANES, LANES), LANES)] = (
                g[rows] * st_in[s, 8:, at] * act_grad[rows]
            ).astype(BF16)
        gs[:, at] = g * act

    for copy in ins.copies[5:8]:
        copy.wait()

    @pl.loop(0, 6)
    def _(c):
        at = cols(c)
        keep, starts = masks[0], masks[1]
        rg = jax.nn.sigmoid(rate[:, at] + chans[5:6, at])
        sd = jnp.exp(-8.0 * rg * chans[7:8, at])
        coeff[:, at] = (1.0 - starts) * (keep * sd + (1.0 - keep))

    row = lax.broadcasted_iota(jnp.int32, (8, RC), 0)

    def backward(n, carry):
        i = SEQ // 8 - 1 - n
        new = []
        for s in range(2):
            at = pl.ds(pl.multiple_of(s * SEQ + i * 8, 8), 8)
            own = coeff[at]
            later_a, later_lam = carry[s]
            a = jnp.where(row == 7, later_a, pltpu.roll(own, 7, 0))
            b = gs[at]
            for k in (1, 2, 4):
                here = row < 8 - k
                b = jnp.where(here, b + a * pltpu.roll(b, 8 - k, 0), b)
                a = jnp.where(here, a * pltpu.roll(a, 8 - k, 0), a)
            h = b + a * later_lam
            lam[at] = h
            new.append((own[0:1], h[0:1]))
        return tuple(new)

    zero = jnp.zeros((1, RC), F32)
    lax.fori_loop(0, SEQ // 8, backward, ((zero, zero), (zero, zero)))

    @pl.loop(0, 6)
    def _(c):
        at = cols(c)
        decay = chans[7:8, at]
        for s in range(2):
            rows = slice(s * SEQ, (s + 1) * SEQ)
            keep, starts = masks[0, rows], masks[1, rows]
            rg, ig, sd, q, root, scale = gates(
                rate[rows, at], inp[rows, at], chans[5:6, at], chans[6:7, at], decay, keep, starts
            )
            conv = conv_low[rows, at].astype(F32)
            l = lam[rows, at]
            common = l * keep
            grad_coeff = l * st_in[s, 7 : PAD - 1, at]
            direct[rows, at] = common * scale * ig
            d_ig = common * scale * conv
            d_scale = common * ig * conv
            d_sd = (1.0 - starts) * (grad_coeff * keep - d_scale * jnp.where(q > 0.001, sd / root, 0.0))
            d_log = d_sd * sd * -8.0
            d_rate = d_log * decay * rg * (1.0 - rg)
            d_inp = d_ig * ig * (1.0 - ig)
            rate_low[rows, at] = d_rate.astype(BF16)
            inp_low[rows, at] = d_inp.astype(BF16)
            for n, term in ((5, d_rate), (6, d_inp), (7, d_log * rg)):
                sums[n : n + 1, at] += jnp.sum(term, axis=0, keepdims=True)

    for copy in ins.copies[8:]:
        copy.wait()
    turn = turn_matrix()
    top, left = quarter_masks()
    for p in range(2):
        at = slice(2 * HS * p, 2 * HS * (p + 1))
        direct[:, at] += nt(rate_low[:, at], tables[2 * p]) + nt(inp_low[:, at], tables[2 * p + 1])
        dr = tn(conv_low[:, at], rate_low[:, at]).astype(BF16)
        di = tn(conv_low[:, at], inp_low[:, at]).astype(BF16)
        none = jnp.zeros_like(dr)
        straight = jnp.where(top, jnp.where(left, dr, none), jnp.where(left, none, di))
        crossed = jnp.where(top, jnp.where(left, di, none), jnp.where(left, none, dr))
        g = (straight.astype(F32) + nn(crossed, turn)).astype(BF16)
        for b in range(8):
            put_og(8 * p + b, D, g[48 * b : 48 * b + 48])

    rolled[:, SEQ:] = jnp.zeros((2, 8, LANES), F32)

    @pl.loop(0, 6)
    def _(c):
        at = cols(c)
        for s in range(2):
            rows = slice(s * SEQ, (s + 1) * SEQ)
            g = direct[rows, at]
            gu = chans[0:1, at] * g
            sums[4:5, at] += jnp.sum(g, axis=0, keepdims=True)
            sums[0:1, at] += jnp.sum(g * u_in[s, 8:, at], axis=0, keepdims=True)
            for k in range(1, 4):
                w = g * masks[1 + k, rows]
                sums[k : k + 1, at] += jnp.sum(w * u_in[s, 8 - k : PAD - k, at], axis=0, keepdims=True)
                rolled[s, 0:SEQ] = w
                gu = gu + chans[k : k + 1, at] * rolled[s, k : SEQ + k]
            gmix[rows, at] = (gu * masks[0, rows]).astype(BF16)

    v = jnp.concatenate([sums[0:8, 0:RC], jnp.zeros((LANES - 8, RC), F32)], axis=0).T.astype(BF16)
    for b in range(16):
        put_og(b, 1408, v[48 * b : 48 * b + 48])
    landed(wb, sems.at[0])

    v = tn(normed[...], gmix[:, 0:PB]).astype(BF16)
    for x, z in RINGS:
        for half in range(2):
            r = ring_rows(x, z) + 256 * half
            bp[x, z, 32 * half : 32 * half + 32, OG:EARLY] = v[r : r + 32]
    emit(saves, bp, places, 0, (p0, p1))
    mixed_part[...] = nt(gmix[...], rows_of(wb, 0, BRANCH))
    saves.start(mixed_part.at[pl.ds(0, SEQ)], o_mine)
    saves.start(mixed_part.at[pl.ds(SEQ, SEQ)], o_theirs)
    t = tok[...].astype(F32)
    sums[8:9] = jnp.sum(mixed_part[...] * (t * inv_rms(t)), axis=0, keepdims=True)
    v = jnp.concatenate([sums[8:16], jnp.zeros((LANES - 8, D), F32)], axis=0).T.astype(BF16)
    for x, z in RINGS:
        for half in range(2):
            r = ring_rows(x, z) + 256 * half
            bq[z, x, 32 * half : 32 * half + 32, QB:EARLY] = v[r : r + 32]

    v = tn(normed[...], gmix[:, PB:]).astype(BF16)
    for x, z in RINGS:
        for half in range(2):
            r = ring_rows(x, z) + 256 * half
            bq[z, x, 32 * half : 32 * half + 32, 0:QB] = v[r : r + 32]
    emit(saves, bq, places, 2, (q0, q1))
    saves.wait()


def join_sums(
    places, eo_p, eu_p, lo_p, lu_p, eo_q, eu_q, lo_q, lu_q,
    p0, p1, q0, q1,
    out, out_sems,
):
    saves = Saves(out_sems)
    for n, (axis, outs, a, b, c, d) in enumerate(
        ((2, (p0, p1), eo_p, eu_p, lo_p, lu_p), (0, (q0, q1), eo_q, eu_q, lo_q, lu_q))
    ):
        for j in range(4):
            at, to = places[4 + axis, j], 4 * n + j
            out[to, :, 0:EARLY] = add(a[at], b[at])
            out[to, :, EARLY:] = add(c[at], d[at])
            saves.start(out.at[to], outs[j // 2].at[j % 2])
    saves.wait()


def add(a, b):
    return (a.astype(F32) + b.astype(F32)).astype(BF16)


def half_sums(a_p, b_p, c_p, d_p, a_q, b_q, c_q, d_q, *rest):
    outs, (early, late, in_sems) = rest[-7:-3], rest[-3:]
    loads = Saves(in_sems)
    for n, (a, b, c, d) in enumerate(((a_p, b_p, c_p, d_p), (a_q, b_q, c_q, d_q))):
        for source, target in ((a, early.at[n, 0]), (b, early.at[n, 1]), (c, late.at[n, 0]), (d, late.at[n, 1])):
            loads.start(source.at[0], target)
    for n in range(2):
        for i, v in enumerate((early, late)):
            loads.copies[4 * n + 2 * i].wait()
            loads.copies[4 * n + 2 * i + 1].wait()
            outs[2 * n + i][...] = add(v[n, 0], v[n, 1])


def pass_on(a_p, f_p, a_q, f_q, *rest):
    o_p, o_q, v, in_sems, out_sems = rest[-5:]
    loads, saves = Saves(in_sems), Saves(out_sems)
    for i, source in enumerate((a_p, f_p, a_q, f_q)):
        loads.start(source.at[1], v.at[i])
    for n, out in enumerate((o_p, o_q)):
        loads.copies[2 * n].wait()
        loads.copies[2 * n + 1].wait()
        v[2 * n] = add(v[2 * n], v[2 * n + 1])
        saves.start(v.at[2 * n], out)
    saves.wait()


def cut(
    places, p0, p1, p2, q0, q1, q2,
    o0, o1, o2, o3,
    parts, sp, sq, sd, in_sems,
):
    load((p0.at[0], p1.at[0], p2, q0.at[0], q1.at[0], q2), [parts.at[i] for i in range(6)], in_sems)
    for n, out in enumerate((sp, sq)):
        out[...] = parts[3 * n].astype(F32) + parts[3 * n + 1].astype(F32) + parts[3 * n + 2].astype(F32)
    sd[0:64] = sp[:, EARLY : EARLY + D]
    sd[64:96, 0:512] = sp[0:32, EARLY + D : EARLY + FC]
    sd[64:96, 512:1024] = sp[32:64, EARLY + D : EARLY + FC]
    tail = jnp.concatenate([sp[48:64, 384 * r : 384 * r + 384] for r in range(3)], axis=0)
    og = jnp.concatenate([sp[0:48, 0:OG], tail], axis=1).astype(BF16)
    i = lax.broadcasted_iota(jnp.int32, (16, 48), 0)
    s = lax.broadcasted_iota(jnp.int32, (16, 48), 1)

    def two(rows):
        return jnp.concatenate(rows, axis=0).astype(BF16)

    for j, out in enumerate((o0, o1, o2, o3)):
        y = places[1, (0, 2, 3, 1)[j]]
        rows = [pl.ds(pl.multiple_of(32 * c + y * 8, 8), 8) for c in range(2)]
        out[:, 0:PB] = two([sp[r, OG:EARLY] for r in rows])
        out[:, PB : PB + PI] = two([sp[r, UNIT - PI :] for r in rows])
        out[:, PB + PI : DC] = two([sq[r] for r in rows])
        mine = jnp.where((s == i + y * 12) & (i < 12), 1.0, 0.0).astype(BF16)
        out[:, DC:DOWN] = nn(mine, og).astype(BF16)
        down = sd[pl.ds(pl.multiple_of(y * 24, 8), 24)]
        out[:, DOWN : DOWN + D] = down[0:16].astype(BF16)
        out[:, DOWN + D :] = two([down[16:24, 0:512], down[16:24, 512:]])


def finish(places, o0, o1, o2, o3, mine, theirs, out_grad, gate_grad, chan_grad, down_grad, v):
    v[...] = o0[...].astype(F32) + o1[...].astype(F32) + o2[...].astype(F32) + o3[...].astype(F32)
    core = places[3, 0]
    theirs[...] = v[pl.ds(pl.multiple_of((1 - core) * 8, 8), 8), 0:DC]
    mine[...] = v[pl.ds(pl.multiple_of(core * 8, 8), 8), 0:DC]
    out_grad[...] = v[0:12, DC : DC + D]
    gate_grad[...] = v[0:12, DC + D : DC + D + 384]
    chan_grad[...] = v[:, DC + D + 384 : DOWN].T[0:8]
    down_grad[0:16] = v[:, DOWN : DOWN + D]
    down_grad[16:24, 0:512] = v[0:8, DOWN + D :]
    down_grad[16:24, 512:] = v[8:16, DOWN + D :]


def unpack(places, mine, theirs, branch, inner, gains):
    def halves(ins):
        for c, v in enumerate(ins):
            for q in range(4):
                to = 768 * q + 384 * c
                if q == 0:
                    branch[:, to : to + PB] = v[:, 0:PB]
                    branch[:, to + PB : to + 384] = v[:, PB + PI : PB + PI + 128]
                else:
                    branch[:, to : to + 384] = v[:, PI + 384 * q : PI + 384 * q + 384]
                at = PB if q == 0 else DC - LATE + 768 * (q - 1)
                to = 1536 * q + 768 * c
                inner[:, to : to + 768] = v[:, at : at + 768]

    gains[...] = mine[:, DC - LATE - LANES : DC - LATE] + theirs[:, DC - LATE - LANES : DC - LATE]

    @pl.when(places[3, 0] == 0)
    def _():
        halves((mine, theirs))

    @pl.when(places[3, 0] == 1)
    def _():
        halves((theirs, mine))


VM, HB, SM, ANY = pltpu.VMEM, pltpu.HBM, pltpu.SMEM, pl.ANY


def kernel(body, ins, spaces, outs, scratch, mib, flops=0, aliases={}):
    moved = sum(v.size * v.dtype.itemsize for v in ins)
    ins = [pltpu.with_memory_space_constraint(v, HB) if s is HB else v for v, s in zip(ins, spaces)]
    return pl.pallas_call(
        body,
        out_shape=[HB(s, d) if at is HB else jax.ShapeDtypeStruct(s, d) for s, d, at in outs],
        in_specs=[pl.BlockSpec(memory_space=s) for s in spaces],
        out_specs=[pl.BlockSpec(memory_space=s) for _, _, s in outs],
        scratch_shapes=scratch,
        input_output_aliases=aliases,
        compiler_params=pltpu.CompilerParams(vmem_limit_bytes=mib * 2**20),
        cost_estimate=pl.CostEstimate(flops=flops, bytes_accessed=moved, transcendentals=0),
    )(*ins)


def shards(
    tokens, cotangent, segment, keep_mask, conv_state, lru_state, norm1_gain, conv_weight, lru_bias, decay_rate,
    gate_weight, branch_weight, out_weight, norm2_gain, mlp_in_weight, mlp_out_weight,
):
    here = my_place()
    core = here["core"]
    zero = jnp.zeros_like(core)
    places = jnp.stack(
        [jnp.stack(ring_places(axis, here)) for axis in "xyz"]
        + [jnp.stack([core, zero, zero, zero])]
        + [jnp.stack(pair_places(axis, here)) for axis in "xyz"]
    ).astype(jnp.int32)
    vmem, dma = pltpu.VMEM, pltpu.SemaphoreType.DMA

    tc = jnp.concatenate([tokens[0], cotangent[0]], axis=0)
    tc_other = swap(tc)
    marks = jnp.concatenate([segment, keep_mask], axis=1).astype(F32)
    states = jnp.concatenate([conv_state[0], lru_state], axis=0)
    sent = jnp.concatenate([core_half(states, 1 - core, 2), jnp.pad(marks, ((0, 0), (0, RC - 2 * SEQ)))], axis=0)
    sent = swap(sent)

    mine, theirs, own = kernel(
        pack,
        (places, branch_weight, mlp_in_weight, jnp.stack([norm1_gain, norm2_gain]), out_weight, gate_weight,
         jnp.concatenate([conv_weight, lru_bias, decay_rate[None]], axis=0), mlp_out_weight),
        [SM, HB, HB, VM, HB, HB, VM, HB],
        [((8, DC), BF16, VM)] * 2 + [((16, OWN - DC), BF16, VM)],
        [vmem(v.shape, BF16) for v in (branch_weight, mlp_in_weight, out_weight, gate_weight, mlp_out_weight)]
        + [dma((5,))],
        8,
    )
    (block,) = kernel(join, (places, mine, swap(theirs), own), [SM] + [VM] * 3, [((16, OWN), BF16, VM)], [], 8)

    row = ((64, UNIT), BF16)
    unit_of = ((2, 32, UNIT), BF16)
    p, q = kernel(
        unit,
        (places, *ring_direct(block, "y"), tc_other, sent),
        [SM] + [VM] * 4 + [ANY] * 2,
        [(*unit_of, HB)] * 2,
        [vmem(*row), vmem(*row), vmem((64, DC), F32), vmem((96, D), F32), dma((4,))],
        16,
    )
    early, late = (4, 64, EARLY), (4, 64, LATE)
    stack = ((4, 64, UNIT), BF16)
    p, q = ring_both(p, "z"), ring_both(q, "x")
    stacks = [((*v, n), BF16, HB) for n in (EARLY, LATE) for v in ((2, 4, 32), (2, 2, 2, 32))]
    unit_of = (2, 32, UNIT)
    partial = kernel(
        planes((0, 1, 2)),
        (places, *p[:3], *q[:3]),
        [SM] + [HB] * 6,
        stacks,
        [vmem((6, *unit_of), BF16), dma((6,)), dma((12,))],
        8,
    )
    pe, qe, pl_, ql = kernel(
        planes((3,)),
        (places, p[3], q[3], *partial),
        [SM, ANY, ANY] + [HB] * 4,
        stacks,
        [vmem((2, *unit_of), BF16), dma((2,)), dma((4,))],
        8,
        aliases={3 + i: i for i in range(4)},
    )
    pe, qe, pl_, ql = ring_both(pe, "x"), ring_both(qe, "z"), ring_both(pl_, "x"), ring_both(ql, "z")

    tok = jnp.concatenate([tc[:SEQ], tc_other[:SEQ]], axis=0)
    cot = jnp.concatenate([tc[SEQ:], tc_other[SEQ:]], axis=0)
    states = jnp.stack([core_half(states, core, 2), sent[:4]])
    marks = jnp.concatenate([marks, sent[4:, : 2 * SEQ]], axis=0)
    seg, keep = marks[:, :SEQ], marks[:, SEQ:]
    earlier = [jnp.concatenate([jnp.repeat(seg[:, :1], k, axis=1), seg[:, : SEQ - k]], axis=1) for k in range(1, 4)]
    masks = jnp.stack([keep, (earlier[0] != seg).astype(F32)] + [(e == seg).astype(F32) for e in earlier])
    masks = jnp.broadcast_to(masks.reshape(5, TOK, 1), (5, TOK, LANES))

    wide, wide_low = ((TOK, D), F32), ((TOK, D), BF16)
    act, act_low, padded = ((TOK, RC), F32), ((TOK, RC), BF16), ((2, PAD, RC), F32)
    tables = ((4, 2 * HS, 2 * HS), BF16)
    saved = [wide_low, act_low, padded, act, act_low, act, act, padded, tables]
    part, finals, gains, chans, normed, merged, u, gate_in, conv_low, rate, inp, st, table = kernel(
        rec_forward,
        (places, tok, masks, states[:, :3], states[:, 3:], *pe, *qe),
        [SM] + [VM] * 4 + [HB] * 8,
        [((TOK + 8, D), F32, VM), ((4, RC), F32, VM), ((8, D), F32, VM), ((8, RC), F32, VM)]
        + [(*v, HB) for v in saved],
        [vmem((*ROWS, PB + EARLY), BF16), vmem((*OG_ROWS, OGC), BF16)]
        + [vmem(*v) for v in saved + [act, act]]
        + [dma((2,)), dma((9,))],
        32,
        2 * TOK * (D * BRANCH + RC * (D + 768)),
    )
    half = ((SEQ, D), F32)
    other = swap(part)
    normed2, own, residual = kernel(
        mlp_norm,
        (tok, part, other, gains),
        [VM] * 4,
        [(*wide_low, VM), (*half, VM), (*wide, HB)],
        [vmem(*wide), dma],
        16,
    )
    hidden, ggu, base, back = kernel(
        mlp,
        (places, cot, normed2, own, *pl_, *ql),
        [SM] + [VM] * 3 + [ANY] * 8,
        [((TOK, FC), BF16, VM), ((TOK, INNER), BF16, VM), (*half, HB), ((TOK + SEQ, D), F32, HB)],
        [vmem((*ROWS, INNER), BF16), vmem((*DOWN_ROWS, D), BF16), vmem((2, TOK, 768), F32)]
        + [vmem(*v) for v in (wide, wide, half)]
        + [dma((2,)), dma((3,))],
        32,
        2 * TOK * D * (2 * INNER + 2 * FC),
    )
    back_other = swap(back)
    outs = kernel(
        mlp_grads,
        (places, cot, normed2, hidden, ggu),
        [SM] + [VM] * 4,
        [((2, *late), BF16, HB)] * 4,
        [vmem((4,) + late, BF16), vmem((4,) + late, BF16), dma((20,))],
        32,
        2 * TOK * D * (INNER + FC),
    )
    lp, lq = outs[:2], outs[2:]

    def first_half(p, q, routes):
        return send(p[1], partner(routes[0], 0)), send(q[1], partner(routes[1], 0))

    def second_half(p, q, came, routes, shape, until=(), lands=HB):
        up = kernel(
            pass_on,
            (p[0], came[0], q[0], came[1], *until),
            [HB, lands, HB, lands] + [HB] * len(until),
            [(shape, BF16, HB)] * 2,
            [vmem((4,) + shape, BF16), dma((4,)), dma((2,))],
            16,
        )
        return send(up[0], partner(routes[0], 1)), send(up[1], partner(routes[1], 1))

    late_came = first_half(lp, lq, "xz")
    outs = kernel(
        rec_backward,
        (places, tok, cot, masks, gains, chans, back_other, back, residual, normed, merged, u, gate_in, conv_low, rate,
         inp, st, table, *pe, *qe),
        [SM] + [VM] * 6 + [HB] * 19,
        [(*v, HB) for v in (half, half, half)] + [((2, *early), BF16, HB)] * 4,
        [vmem((*ROWS, BRANCH), BF16), vmem((*OG_ROWS, OGC), BF16)]
        + [vmem(*v) for v in (wide, wide, wide_low, act_low, padded, act, act_low, act, act, padded, tables)]
        + [vmem(*v) for v in (act, wide_low, act, act, act_low, act_low, act, ((TOK, BRANCH), BF16))]
        + [vmem((2, PAD, LANES), F32), vmem((16, D), F32), vmem(*wide), vmem(*half)]
        + [vmem((4,) + early, BF16), vmem((4,) + early, BF16), dma((2,)), dma((11,)), dma((11,))],
        48,
        2 * TOK * D * (2 * BRANCH + 2 * RC),
    )
    grad_residual, mixed_mine, mixed_theirs = outs[:3]
    ep, eq = outs[3:5], outs[5:]
    early_came = first_half(ep, eq, "xz")
    late_up = second_half(lp, lq, late_came, "xz", late, (ep[0],))
    early_up = second_half(ep, eq, early_came, "xz", early)

    summed = kernel(
        half_sums,
        (ep[0], early_came[0], lp[0], late_came[0], eq[0], early_came[1], lq[0], late_came[1]),
        [HB] * 8,
        [(early, BF16, VM), (late, BF16, VM)] * 2,
        [vmem((2, 2) + early, BF16), vmem((2, 2) + late, BF16), dma((8,))],
        16,
    )
    outs = kernel(
        join_sums,
        (places, summed[0], early_up[0], summed[1], late_up[0], summed[2], early_up[1], summed[3], late_up[1]),
        [SM] + [VM] * 8,
        [((2, 64, UNIT), BF16, HB)] * 4,
        [vmem((8, 64, UNIT), BF16), dma((8,))],
        8,
    )
    tp, tq = outs[:2], outs[2:]
    came = first_half(tp, tq, "zx")
    up = second_half(tp, tq, came, "zx", (64, UNIT), lands=ANY)
    sums = kernel(
        cut,
        (places, tp[0], came[0], up[0], tq[0], came[1], up[1]),
        [SM] + [HB, ANY, ANY] * 2,
        [((16, OWN), BF16, VM)] * 4,
        [vmem((6, 64, UNIT), BF16), vmem((64, UNIT), F32), vmem((64, UNIT), F32), vmem((96, D), F32), dma((6,))],
        16,
    )
    mine, theirs, out_grad, gate_grad, chan_grad, down_grad = kernel(
        finish,
        (places, *terms_direct(sums, "y")),
        [SM] + [VM] * 4,
        [((8, DC), F32, VM)] * 2 + [(s, F32, VM) for s in ((12, D), (12, 384), (8, 16), (24, D))],
        [vmem((16, OWN), F32)],
        8,
    )
    branch_grad, in_grad, gain_grads = kernel(
        unpack,
        (places, mine, swap(theirs)),
        [SM] + [VM] * 2,
        [((8, 2 * R), F32, VM), ((8, 2 * F), F32, VM), ((8, LANES), F32, VM)],
        [],
        8,
    )

    output = (base + back_other[TOK:]).astype(BF16)
    grad, _ = rms_back(mixed_mine + swap(mixed_theirs), tok[:SEQ].astype(F32), gains[0])
    input_grad = (grad_residual + grad).astype(BF16)
    theirs = other[TOK : TOK + 4, :RC]
    finals = jnp.stack(
        [v.reshape(1, 4, 2, 384) for v in (jnp.where(core == 0, finals, theirs), jnp.where(core == 0, theirs, finals))],
        axis=3,
    ).reshape(1, 4, R)
    return (
        output[None],
        input_grad[None],
        finals[:, :3],
        finals[:, 3],
        gain_grads[:, 0],
        chan_grad[:4, :12],
        chan_grad[4:7, :12],
        chan_grad[7, :12],
        gate_grad,
        branch_grad,
        out_grad,
        gain_grads[:, 1],
        in_grad,
        down_grad,
    )


def solution(mesh):
    rows, last = P(AXES), P(None, AXES)
    specs = [rows] * 6 + [rows, last, last] + [rows] * 7
    outs = [rows] * 4 + [rows, last, last] + [rows] * 7
    return jax.shard_map(
        shards, mesh=mesh, in_specs=tuple(specs), out_specs=tuple(outs), check_vma=False
    )
```

```python
import jax
import jax.numpy as jnp
from jax import lax
from jax.experimental import pallas as pl
from jax.experimental.pallas import tpu as pltpu
from jax.sharding import PartitionSpec as P

AXES = ("dp", "fsdp")
D, R, F, SEQ = 1024, 1536, 3072, 128
RC, FC = R // 2, F // 2
HS = 192
F32, BF16 = jnp.float32, jnp.bfloat16
BRANCH, INNER = 2 * RC, 2 * FC
TOK, PAD, LANES = 2 * SEQ, SEQ + 8, 128

EARLY, LATE = 1408, 2304
UNIT = EARLY + LATE
OG, PB, PI, QB = 1152, 256, 768, 1280
DC = PB + PI + UNIT
OGC = 1536
DOWN = DC + OGC
OWN = DOWN + D + D // 2


def place_of(device):
    outer, inner = divmod(device, 32)
    x_hi, core = divmod(outer, 2)
    z, rest = divmod(inner, 8)
    x_lo, y = divmod(rest, 4)
    return dict(x=x_hi * 2 + x_lo, y=y, z=z, core=core)


def device_at(x, y, z, core):
    return ((x // 2) * 2 + core) * 32 + z * 8 + (x % 2) * 4 + y


def pairs(move):
    return [(d, device_at(**move(place_of(d)))) for d in range(128)]


def along(axis, steps):
    def move(p):
        sign = 1 if p["core"] == 0 else -1
        return {**p, axis: (p[axis] + sign * steps) % 4}

    return pairs(move)


def other_core(p):
    return {**p, "core": 1 - p["core"]}


def partner(axis, turn):
    def move(p):
        i = p[axis]
        return {**p, axis: i ^ 1 if (p["core"] + turn) % 2 == 0 else 3 - i}

    return pairs(move)


def opposite(axis):
    return pairs(lambda p: {**p, axis: (p[axis] + 2) % 4})


def send(value, route):
    return lax.ppermute(value, AXES, route)


def swap(value):
    return send(value, pairs(other_core))


def my_place():
    device = lax.axis_index(AXES)
    outer, inner = device // 32, device % 32
    return dict(x=(outer // 2) * 2 + (inner // 4) % 2, y=inner % 4, z=inner // 8, core=outer % 2)


def ring_places(axis, here):
    sign, at = 1 - 2 * here["core"], here[axis]
    return [at, (at - sign) % 4, (at + sign) % 4, (at + 2) % 4]


def ring(block, axis):
    one = send(block, along(axis, 1))
    two = send(one, along(axis, 1))
    return block, one, send(two, along(axis, 1)), two


def ring_both(block, axis):
    up, down = send(block, along(axis, 1)), send(block, along(axis, -1))
    return block, up, down, send(up, along(axis, 1))


def pair_places(axis, here):
    i, odd = here[axis], here["core"] == 1
    by_one, by_ends = i + 1 - 2 * (i % 2), 3 - i
    return [i, jnp.where(odd, by_one, by_ends), jnp.where(odd, by_ends, by_one), (i + 2) % 4]


def ring_direct(block, axis):
    return block, send(block, along(axis, 1)), send(block, along(axis, -1)), send(block, opposite(axis))


def terms_direct(terms, axis):
    own, ahead, far, behind = terms
    return own, send(ahead, along(axis, 1)), send(far, opposite(axis)), send(behind, along(axis, -1))


def total(*terms):
    out = terms[0].astype(F32)
    for term in terms[1:]:
        out = out + term.astype(F32)
    return out.astype(BF16)


def core_half(array, core, blocks):
    v = array.reshape(array.shape[:-1] + (blocks, 2, array.shape[-1] // (2 * blocks)))
    v = lax.dynamic_index_in_dim(v, core, v.ndim - 2, keepdims=False)
    return v.reshape(array.shape[:-1] + (array.shape[-1] // 2,))


def dot(a, b, dims):
    return lax.dot_general(a, b, (dims, ((), ())), preferred_element_type=F32)


def nn(a, b):
    return dot(a, b, ((1,), (0,)))


def nt(a, b):
    return dot(a, b, ((1,), (1,)))


def tn(a, b):
    return dot(a, b, ((0,), (0,)))


def inv_rms(v):
    return lax.rsqrt(jnp.mean(v * v, axis=-1, keepdims=True) + 1e-6)


def rms_back(grad, v, gain):
    s = inv_rms(v)
    n = v * s
    g2 = grad * gain
    return s * (g2 - n * jnp.mean(g2 * n, axis=-1, keepdims=True)), grad * n


C0, C1 = 0.7978845608028654, 0.044715


def gelu_both(a):
    t = jnp.tanh(C0 * (a + C1 * (a * a * a)))
    half = 0.5 * (1.0 + t)
    return a * half, half + 0.5 * a * (1.0 - t * t) * (C0 * (1.0 + 3.0 * C1 * (a * a)))


def gates(rate, inp, bias1, bias2, decay, keep, starts):
    rg = jax.nn.sigmoid(rate + bias1)
    ig = jax.nn.sigmoid(inp + bias2)
    sd = jnp.exp(-8.0 * rg * decay)
    q = 1.0 - sd * sd
    root = jnp.sqrt(jnp.maximum(q, 0.001))
    scale = starts + (1.0 - starts) * root
    return rg, ig, sd, q, root, scale


def cols(c):
    return pl.ds(pl.multiple_of(c * LANES, LANES), LANES)


class Saves:
    def __init__(self, sem):
        self.sem, self.copies = sem, []

    def start(self, source, target):
        self.copies.append(pltpu.make_async_copy(source, target, self.sem.at[len(self.copies)]))
        self.copies[-1].start()

    def wait(self):
        for copy in self.copies:
            copy.wait()


def pick(rows, where):
    return jnp.where(lax.broadcasted_iota(jnp.int32, (rows, where.shape[1]), 0) == where, 1.0, 0.0).astype(BF16)


def stand(values, rows):
    v = values.astype(F32)
    i = lax.broadcasted_iota(jnp.int32, (rows, v.shape[1]), 0)
    j = lax.broadcasted_iota(jnp.int32, (rows, v.shape[1]), 1)
    lane = lax.broadcasted_iota(jnp.int32, (rows, LANES), 1)
    out = jnp.zeros((rows, LANES), F32)
    for n in range(v.shape[0]):
        column = jnp.sum(jnp.where(i == j, v[n : n + 1], 0.0), axis=1, keepdims=True)
        out = out + jnp.where(lane == n, column, 0.0)
    return out


def load(sources, targets, sems):
    copies = Saves(sems)
    for source, target in zip(sources, targets):
        copies.start(source, target)
    copies.wait()


def pack(
    places, i_branch, i_inner, gain, i_out, i_gate, perchan, i_down, mine, theirs, own,
    branch, inner, out, gate, down, sems,
):
    load((i_branch, i_inner, i_out, i_gate, i_down), (branch, inner, out, gate, down), sems)

    gains = stand(gain[...], 8).astype(BF16)

    def halves(outs):
        for c, to_core in enumerate(outs):
            for q in range(4):
                v = branch[:, 768 * q + 384 * c : 768 * q + 384 * c + 384]
                if q == 0:
                    to_core[:, 0:PB] = v[:, 0:PB]
                    to_core[:, PB + PI : PB + PI + 128] = v[:, PB:]
                else:
                    to_core[:, PI + 384 * q : PI + 384 * q + 384] = v
                v = inner[:, 1536 * q + 768 * c : 1536 * q + 768 * c + 768]
                to = PB if q == 0 else DC - LATE + 768 * (q - 1)
                to_core[:, to : to + 768] = v
            tile = DC - LATE - LANES
            to_core[:, tile : tile + LANES] = gains

    @pl.when(places[3, 0] == 0)
    def _():
        halves((mine, theirs))

    @pl.when(places[3, 0] == 1)
    def _():
        halves((theirs, mine))

    own[...] = jnp.zeros_like(own)
    own[0:12, 0:D] = out[...]
    own[0:12, D : D + 384] = gate[...]
    own[:, 1408:OGC] = stand(perchan[...], 16).astype(BF16)
    own[:, OGC : OGC + D] = down[0:16]
    own[:, OGC + D :] = jnp.concatenate(
        [down[16:24, 0:512].astype(F32), down[16:24, 512:].astype(F32)], axis=0
    ).astype(BF16)


def join(places, mine, theirs, own, block):
    def rows(low, high):
        block[:, 0:DC] = jnp.concatenate([low[...].astype(F32), high[...].astype(F32)], axis=0).astype(BF16)

    @pl.when(places[3, 0] == 0)
    def _():
        rows(mine, theirs)

    @pl.when(places[3, 0] == 1)
    def _():
        rows(theirs, mine)

    block[:, DC:] = own[...]


def unit(places, p0, p1, p2, p3, *rest):
    o_p, o_q, p, q, d, dn, sems = rest[-7:]
    ogs = []
    s = lax.broadcasted_iota(jnp.int32, (1, 64), 1)
    y = jnp.zeros((1, 64), jnp.int32)
    for j, piece in enumerate((p0, p1, p2, p3)):
        at = places[1, j]
        y = jnp.where(s // 16 == j, at, y)
        v = piece[:, 0:DC].astype(F32)
        for c in range(2):
            d[pl.ds(pl.multiple_of(c * 32 + at * 8, 8), 8)] = v[8 * c : 8 * c + 8]
        ogs.append(piece[:, DC:DOWN])
        v = piece[:, DOWN:].astype(F32)
        dn[pl.ds(pl.multiple_of(at * 24, 8), 16)] = v[:, 0:D]
        for h in range(2):
            dn[pl.ds(pl.multiple_of(at * 24 + 16, 8), 8), 512 * h : 512 * h + 512] = v[8 * h : 8 * h + 8, D:]
    saves = Saves(sems)
    q[...] = d[:, PB + PI :].astype(BF16)
    for c in range(2):
        saves.start(q.at[pl.ds(32 * c, 32)], o_q.at[c])
    p[:, OG:EARLY] = d[:, 0:PB].astype(BF16)
    p[:, UNIT - PI :] = d[:, PB : PB + PI].astype(BF16)
    i = s % 16
    og = nn(pick(48, jnp.where(i < 12, y * 12 + i, 64)), jnp.concatenate(ogs, axis=0)).astype(BF16)
    p[0:48, 0:OG] = og[:, 0:OG]
    for r in range(3):
        p[48:64, 384 * r : 384 * r + 384] = og[16 * r : 16 * r + 16, OG:]
    p[:, EARLY : EARLY + D] = dn[0:64].astype(BF16)
    p[0:32, EARLY + D : EARLY + FC] = dn[64:96, 0:512].astype(BF16)
    p[32:64, EARLY + D : EARLY + FC] = dn[64:96, 512:1024].astype(BF16)
    for c in range(2):
        saves.start(p.at[pl.ds(32 * c, 32)], o_p.at[c])
    saves.wait()


def planes(which):
    def body(places, *refs):
        n = len(which)
        (o_pe, o_qe, o_pl, o_ql), v, in_sems, out_sems = refs[-7:-3], *refs[-3:]
        loads, saves = Saves(in_sems), Saves(out_sems)
        for i, piece in enumerate(refs[: 2 * n]):
            loads.start(piece, v.at[i])
        for i in range(2 * n):
            loads.copies[i].wait()
            j = which[i % n]
            x = places[0, j]
            for first, count, p, q in ((0, EARLY, o_pe, o_qe), (EARLY, LATE, o_pl, o_ql)):
                target = p.at[:, places[2, j]] if i < n else q.at[x // 2, :, x % 2]
                saves.start(v.at[i, :, :, pl.ds(first, count)], target)
        saves.wait()

    return body


ROWS = (2, 2, 4, 2, 32)
OG_ROWS, DOWN_ROWS = (2, 4, 2, 48), (2, 4, 2, 96)


def ring_rows(x, z):
    return (x // 2) * 512 + z * 64 + (x % 2) * 32


def p_copy(piece, places, j, first, count, block, to, sem):
    x = places[0, j]
    target = block.at[x // 2, :, :, x % 2, :, pl.ds(to, count)]
    pltpu.make_async_copy(piece.at[..., pl.ds(first, count)], target, sem).start()


def q_copy(piece, places, j, first, count, block, to, sem):
    target = block.at[:, :, places[2, j], :, :, pl.ds(to, count)]
    pltpu.make_async_copy(piece.at[..., pl.ds(first, count)], target, sem).start()


def og_copy(piece, places, j, block, sem):
    x = places[0, j]
    block = block.at[x // 2, :, x % 2]
    for source, target in (
        (piece.at[0, :, :, pl.ds(0, OG)], block.at[:, pl.ds(0, 32), pl.ds(0, OG)]),
        (piece.at[1, :, pl.ds(0, 16), pl.ds(0, OG)], block.at[:, pl.ds(32, 16), pl.ds(0, OG)]),
    ):
        pltpu.make_async_copy(source, target, sem).start()
    for r in range(3):
        pltpu.make_async_copy(
            piece.at[1, :, pl.ds(16, 16), pl.ds(384 * r, 384)], block.at[:, pl.ds(16 * r, 16), pl.ds(OG, 384)], sem
        ).start()


def down_copy(piece, places, j, block, sem):
    x = places[0, j]
    block = block.at[x // 2, :, x % 2]
    for h in range(2):
        pltpu.make_async_copy(piece.at[h, :, :, pl.ds(0, D)], block.at[:, pl.ds(32 * h, 32)], sem).start()
        pltpu.make_async_copy(
            piece.at[h, :, :, pl.ds(D, 512)], block.at[:, pl.ds(64, 32), pl.ds(512 * h, 512)], sem
        ).start()


def rows_of(block, first, count):
    return block[..., first : first + count].reshape(D, count)


def landed(block, sem):
    pltpu.make_async_copy(block, block, sem).wait()


def turn_matrix():
    i = lax.broadcasted_iota(jnp.int32, (2 * HS, 2 * HS), 0)
    j = lax.broadcasted_iota(jnp.int32, (2 * HS, 2 * HS), 1)
    return jnp.where((i == j + HS) | (j == i + HS), 1.0, 0.0).astype(BF16)


def quarter_masks():
    i = lax.broadcasted_iota(jnp.int32, (2 * HS, 2 * HS), 0) < HS
    j = lax.broadcasted_iota(jnp.int32, (2 * HS, 2 * HS), 1) < HS
    return i, j


def rec_forward(
    places, tok, masks, conv_before, lru_before, p0, p1, p2, p3, q0, q1, q2, q3,
    part, finals, gains, chans, o_normed, o_merged, o_u, o_gate, o_conv, o_rate, o_inp, o_st, o_tables,
    wb, wog, normed, merged, u, gate_in, conv_low, rate, inp, st, tables, coeff, drive, sems, out_sems,
):
    for j, (p, q) in enumerate(((p0, q0), (p1, q1), (p2, q2), (p3, q3))):
        p_copy(p, places, j, OG, PB, wb, 0, sems.at[0])
        q_copy(q, places, j, 0, EARLY, wb, PB, sems.at[0])
    for j, p in enumerate((p0, p1, p2, p3)):
        og_copy(p, places, j, wog, sems.at[1])
    saves = Saves(out_sems)
    t = tok[...].astype(F32)
    scaled = t * inv_rms(t)
    landed(wb, sems.at[0])
    gains[...] = rows_of(wb, BRANCH, LANES).astype(F32).T[:8]
    normed[...] = (scaled * gains[0:1]).astype(BF16)
    saves.start(normed, o_normed)
    for s in range(2):
        u[s, 0:8] = jnp.zeros((8, RC), F32)
        u[s, 5:8] = conv_before[s]
        st[s, 0:8] = jnp.zeros((8, RC), F32)
        st[s, 7:8] = lru_before[s]

    v = nn(normed[...], rows_of(wb, 0, RC))
    for s in range(2):
        rows = slice(s * SEQ, (s + 1) * SEQ)
        for c in range(6):
            u[s, 8:, LANES * c : LANES * c + LANES] = v[rows, LANES * c : LANES * c + LANES] * masks[0, rows]

    saves.start(u, o_u)

    gate_in[...] = nn(normed[...], rows_of(wb, RC, RC))

    saves.start(gate_in, o_gate)
    landed(wog, sems.at[1])
    chans[...] = wog[..., 1408:].reshape(RC, LANES).astype(F32).T[:8]

    @pl.loop(0, 6)
    def _(c):
        at = cols(c)
        for s in range(2):
            rows = slice(s * SEQ, (s + 1) * SEQ)
            v = chans[4:5, at] + chans[0:1, at] * u[s, 8:, at]
            for k in range(1, 4):
                v = v + chans[k : k + 1, at] * (u[s, 8 - k : PAD - k, at] * masks[1 + k, rows])
            conv_low[rows, at] = v.astype(BF16)

    saves.start(conv_low, o_conv)
    turn = turn_matrix()
    top, left = quarter_masks()
    for p in range(2):
        g = wog[p, :, :, :, D : D + 384].reshape(2 * HS, 2 * HS)
        turned = nn(g, turn).astype(BF16)
        zero = jnp.zeros_like(g)
        tables[2 * p] = jnp.where(left, jnp.where(top, g, zero), jnp.where(top, zero, turned))
        tables[2 * p + 1] = jnp.where(left, jnp.where(top, turned, zero), jnp.where(top, zero, g))
        at = slice(2 * HS * p, 2 * HS * (p + 1))
        rate[:, at] = nn(conv_low[:, at], tables[2 * p])
        inp[:, at] = nn(conv_low[:, at], tables[2 * p + 1])
    saves.start(tables, o_tables)
    saves.start(rate, o_rate)
    saves.start(inp, o_inp)

    @pl.loop(0, 6)
    def _(c):
        at = cols(c)
        keep, starts = masks[0], masks[1]
        _, ig, sd, _, _, scale = gates(
            rate[:, at], inp[:, at], chans[5:6, at], chans[6:7, at], chans[7:8, at], keep, starts
        )
        coeff[:, at] = (1.0 - starts) * (keep * sd + (1.0 - keep))
        drive[:, at] = keep * scale * ig * conv_low[:, at].astype(F32)

    row = lax.broadcasted_iota(jnp.int32, (8, RC), 0)

    def forward(i, carry):
        new = []
        for s in range(2):
            at = pl.ds(pl.multiple_of(s * SEQ + i * 8, 8), 8)
            a, b = coeff[at], drive[at]
            for k in (1, 2, 4):
                later = row >= k
                b = jnp.where(later, a * pltpu.roll(b, k, 0) + b, b)
                a = jnp.where(later, a * pltpu.roll(a, k, 0), a)
            h = a * carry[s] + b
            st[s, pl.ds(pl.multiple_of(8 + i * 8, 8), 8)] = h
            new.append(h[7:8])
        return tuple(new)

    last = lax.fori_loop(0, SEQ // 8, forward, (lru_before[0], lru_before[1]))
    saves.start(st, o_st)
    part[TOK:] = jnp.zeros((8, D), F32)
    part[TOK : TOK + 3, 0:RC] = u[1, PAD - 3 :]
    part[TOK + 3 : TOK + 4, 0:RC] = last[1]
    finals[0:3] = u[0, PAD - 3 :]
    finals[3:4] = last[0]

    @pl.loop(0, 6)
    def _(c):
        at = cols(c)
        act, _ = gelu_both(gate_in[:, at])
        for s in range(2):
            rows = slice(s * SEQ, (s + 1) * SEQ)
            merged[rows, at] = (st[s, 8:, at] * act[rows]).astype(BF16)

    saves.start(merged, o_merged)

    part[0:TOK] = nn(merged[...], wog[..., 0:D].reshape(RC, D))

    saves.wait()


def mlp_norm(tok, part, other, gains, normed2, own, o_residual, residual, sem):
    for s in range(2):
        rows, theirs = slice(s * SEQ, (s + 1) * SEQ), slice((1 - s) * SEQ, (2 - s) * SEQ)
        v = tok[rows].astype(F32) + (part[rows] + other[theirs])
        residual[rows] = v
        normed2[rows] = (v * inv_rms(v) * gains[1:2]).astype(BF16)
    copy = pltpu.make_async_copy(residual, o_residual, sem)
    copy.start()
    own[...] = residual[0:SEQ]
    copy.wait()


def mlp(
    places, cot, normed2, own, p0, p1, p2, p3, q0, q1, q2, q3,
    hidden, ggu, o_base, o_back,
    win, wdown, grad_hidden, down, back, base, sems, out_sems,
):
    for j, p in enumerate((p0, p1, p2, p3)):
        down_copy(p, places, j, wdown, sems.at[1])
    for j, (p, q) in enumerate(((p0, q0), (p1, q1), (p2, q2), (p3, q3))):
        p_copy(p, places, j, FC, PI, win, 0, sems.at[0])
        q_copy(q, places, j, 0, LATE, win, PI, sems.at[0])
    saves = Saves(out_sems)
    down[...] = jnp.zeros_like(down)
    back[...] = jnp.zeros_like(back)
    landed(wdown, sems.at[1])

    @pl.loop(0, 2)
    def _(c):
        grad_hidden[c] = nt(cot[...], wdown[c].reshape(768, D))

    landed(win, sems.at[0])

    @pl.loop(0, 2)
    def _(c):
        at = pl.ds(pl.multiple_of(768 * c, 256), 768)
        up = pl.ds(pl.multiple_of(FC + 768 * c, 256), 768)
        wa, wu = win[..., at].reshape(D, 768), win[..., up].reshape(D, 768)
        a = nn(normed2[...], wa)
        b = nn(normed2[...], wu)
        ga, da = gelu_both(a)
        h = (ga * b).astype(BF16)
        hidden[:, at] = h
        gh = grad_hidden[c]
        gg_a = (gh * b * da).astype(BF16)
        gg_b = (gh * ga).astype(BF16)
        ggu[:, at] = gg_a
        ggu[:, up] = gg_b
        down[...] += nn(h, wdown[c].reshape(768, D))
        back[...] += nt(gg_a, wa) + nt(gg_b, wu)

    saves.start(back, o_back.at[pl.ds(0, TOK)])
    saves.start(down.at[pl.ds(SEQ, SEQ)], o_back.at[pl.ds(TOK, SEQ)])
    base[...] = own[...] + down[0:SEQ]
    saves.start(base, o_base)
    saves.wait()


def emit(saves, block, places, axis, outs):
    for j in range(4):
        saves.start(block.at[places[4 + axis, j]], outs[j // 2].at[j % 2])


RINGS = [(x, z) for x in range(4) for z in range(4)]


def emit_columns(saves, block, places, axis, outs, first, count):
    for j in range(4):
        columns = pl.ds(first, count)
        saves.start(block.at[places[4 + axis, j], :, :, columns], outs[j // 2].at[j % 2, :, :, columns])


def mlp_grads(
    places, cot, normed2, hidden, ggu, p0, p1, q0, q1,
    bp, bq, out_sems,
):
    saves = Saves(out_sems)
    @pl.loop(0, 2)
    def _(xh):
        v = tn(hidden[:, pl.ds(pl.multiple_of(768 * xh, 256), 768)], cot[...]).astype(BF16)
        for z in range(4):
            for xl in range(2):
                r = 96 * (2 * z + xl)
                bp[2 * xh + xl, z, :, 0:D] = v[r : r + 64]
                bp[2 * xh + xl, z, 0:32, D:FC] = v[r + 64 : r + 96, 0:512]
                bp[2 * xh + xl, z, 32:64, D:FC] = v[r + 64 : r + 96, 512:1024]

    emit_columns(saves, bp, places, 0, (p0, p1), 0, FC)

    def put(block, order, first, to):
        v = tn(normed2[...], ggu[:, pl.ds(pl.multiple_of(first, 256), 768)]).astype(BF16)
        for x, z in RINGS:
            for half in range(2):
                r = ring_rows(x, z) + 256 * half
                at = (x, z) if order else (z, x)
                columns = pl.ds(pl.multiple_of(to, 256), 768)
                block[(*at, slice(32 * half, 32 * half + 32), columns)] = v[r : r + 32]

    put(bp, True, 0, FC)
    emit_columns(saves, bp, places, 0, (p0, p1), FC, PI)

    @pl.loop(0, 3)
    def _(part):
        put(bq, False, 768 * (part + 1), 768 * part)

    emit_columns(saves, bq, places, 2, (q0, q1), 0, LATE)
    saves.wait()


def rec_backward(
    places, tok, cot, masks, gains, chans, other, i_back, i_residual, i_normed, i_merged, i_u, i_gate, i_conv, i_rate,
    i_inp, i_st, i_tables, wp0, wp1, wp2, wp3, wq0, wq1, wq2, wq3,
    o_residual, o_mine, o_theirs, p0, p1, q0, q1,
    wb, wog, part, residual, normed, merged, u_in, gate_in, conv_low, rate, inp, st_in, tables,
    coeff, grad_branch, gs, lam, rate_low, inp_low, direct, gmix, rolled, sums, mixed_part, own_residual, bp, bq,
    sems, in_sems, out_sems,
):
    ins = Saves(in_sems)
    for source, target in (
        (i_back.at[pl.ds(0, TOK)], part), (i_residual, residual), (i_merged, merged), (i_gate, gate_in), (i_st, st_in),
        (i_rate, rate), (i_inp, inp), (i_conv, conv_low), (i_tables, tables), (i_u, u_in), (i_normed, normed),
    ):
        ins.start(source, target)
    for j, p in enumerate((wp0, wp1, wp2, wp3)):
        og_copy(p, places, j, wog, sems.at[1])
    for j, (p, q) in enumerate(((wp0, wq0), (wp1, wq1), (wp2, wq2), (wp3, wq3))):
        p_copy(p, places, j, OG, PB, wb, 0, sems.at[0])
        q_copy(q, places, j, 0, QB, wb, PB, sems.at[0])
    saves = Saves(out_sems)
    sums[...] = jnp.zeros_like(sums)
    for copy in ins.copies[0:2]:
        copy.wait()
    for s in range(2):
        rows, theirs = slice(s * SEQ, (s + 1) * SEQ), slice((1 - s) * SEQ, (2 - s) * SEQ)
        grad, term = rms_back(part[rows] + other[theirs], residual[rows], gains[1:2])
        grad = cot[rows].astype(F32) + grad
        grad_branch[rows] = grad.astype(BF16)
        if s == 0:
            own_residual[...] = grad
            sums[9:10] = jnp.sum(term, axis=0, keepdims=True)
    saves.start(own_residual, o_residual)

    def put_og(b, first, v):
        x, z = (b // 8) * 2 + b % 2, (b // 2) % 4
        n = min(max(OG - first, 0), v.shape[1])
        if n:
            bp[x, z, 0:48, first : first + n] = v[:, :n]
        if n < v.shape[1]:
            to = first + n - OG
            for r in range(3):
                bp[x, z, 48:64, 384 * r + to : 384 * r + to + v.shape[1] - n] = v[16 * r : 16 * r + 16, n:]

    ins.copies[2].wait()
    v = tn(merged[...], grad_branch[...]).astype(BF16)
    for b in range(16):
        put_og(b, 0, v[48 * b : 48 * b + 48])
    landed(wog, sems.at[1])
    gs[...] = nt(grad_branch[...], wog[..., 0:D].reshape(RC, D))
    for copy in ins.copies[3:5]:
        copy.wait()

    @pl.loop(0, 6)
    def _(c):
        at = cols(c)
        act, act_grad = gelu_both(gate_in[:, at])
        g = gs[:, at]
        for s in range(2):
            rows = slice(s * SEQ, (s + 1) * SEQ)
            gmix[rows, pl.ds(pl.multiple_of(RC + c * LANES, LANES), LANES)] = (
                g[rows] * st_in[s, 8:, at] * act_grad[rows]
            ).astype(BF16)
        gs[:, at] = g * act

    for copy in ins.copies[5:8]:
        copy.wait()

    @pl.loop(0, 6)
    def _(c):
        at = cols(c)
        keep, starts = masks[0], masks[1]
        rg = jax.nn.sigmoid(rate[:, at] + chans[5:6, at])
        sd = jnp.exp(-8.0 * rg * chans[7:8, at])
        coeff[:, at] = (1.0 - starts) * (keep * sd + (1.0 - keep))

    row = lax.broadcasted_iota(jnp.int32, (8, RC), 0)

    def backward(n, carry):
        i = SEQ // 8 - 1 - n
        new = []
        for s in range(2):
            at = pl.ds(pl.multiple_of(s * SEQ + i * 8, 8), 8)
            own = coeff[at]
            later_a, later_lam = carry[s]
            a = jnp.where(row == 7, later_a, pltpu.roll(own, 7, 0))
            b = gs[at]
            for k in (1, 2, 4):
                here = row < 8 - k
                b = jnp.where(here, b + a * pltpu.roll(b, 8 - k, 0), b)
                a = jnp.where(here, a * pltpu.roll(a, 8 - k, 0), a)
            h = b + a * later_lam
            lam[at] = h
            new.append((own[0:1], h[0:1]))
        return tuple(new)

    zero = jnp.zeros((1, RC), F32)
    lax.fori_loop(0, SEQ // 8, backward, ((zero, zero), (zero, zero)))

    @pl.loop(0, 6)
    def _(c):
        at = cols(c)
        decay = chans[7:8, at]
        for s in range(2):
            rows = slice(s * SEQ, (s + 1) * SEQ)
            keep, starts = masks[0, rows], masks[1, rows]
            rg, ig, sd, q, root, scale = gates(
                rate[rows, at], inp[rows, at], chans[5:6, at], chans[6:7, at], decay, keep, starts
            )
            conv = conv_low[rows, at].astype(F32)
            l = lam[rows, at]
            common = l * keep
            grad_coeff = l * st_in[s, 7 : PAD - 1, at]
            direct[rows, at] = common * scale * ig
            d_ig = common * scale * conv
            d_scale = common * ig * conv
            d_sd = (1.0 - starts) * (grad_coeff * keep - d_scale * jnp.where(q > 0.001, sd / root, 0.0))
            d_log = d_sd * sd * -8.0
            d_rate = d_log * decay * rg * (1.0 - rg)
            d_inp = d_ig * ig * (1.0 - ig)
            rate_low[rows, at] = d_rate.astype(BF16)
            inp_low[rows, at] = d_inp.astype(BF16)
            for n, term in ((5, d_rate), (6, d_inp), (7, d_log * rg)):
                sums[n : n + 1, at] += jnp.sum(term, axis=0, keepdims=True)

    for copy in ins.copies[8:]:
        copy.wait()
    turn = turn_matrix()
    top, left = quarter_masks()
    for p in range(2):
        at = slice(2 * HS * p, 2 * HS * (p + 1))
        direct[:, at] += nt(rate_low[:, at], tables[2 * p]) + nt(inp_low[:, at], tables[2 * p + 1])
        dr = tn(conv_low[:, at], rate_low[:, at]).astype(BF16)
        di = tn(conv_low[:, at], inp_low[:, at]).astype(BF16)
        none = jnp.zeros_like(dr)
        straight = jnp.where(top, jnp.where(left, dr, none), jnp.where(left, none, di))
        crossed = jnp.where(top, jnp.where(left, di, none), jnp.where(left, none, dr))
        g = (straight.astype(F32) + nn(crossed, turn)).astype(BF16)
        for b in range(8):
            put_og(8 * p + b, D, g[48 * b : 48 * b + 48])

    rolled[:, SEQ:] = jnp.zeros((2, 8, LANES), F32)

    @pl.loop(0, 6)
    def _(c):
        at = cols(c)
        for s in range(2):
            rows = slice(s * SEQ, (s + 1) * SEQ)
            g = direct[rows, at]
            gu = chans[0:1, at] * g
            sums[4:5, at] += jnp.sum(g, axis=0, keepdims=True)
            sums[0:1, at] += jnp.sum(g * u_in[s, 8:, at], axis=0, keepdims=True)
            for k in range(1, 4):
                w = g * masks[1 + k, rows]
                sums[k : k + 1, at] += jnp.sum(w * u_in[s, 8 - k : PAD - k, at], axis=0, keepdims=True)
                rolled[s, 0:SEQ] = w
                gu = gu + chans[k : k + 1, at] * rolled[s, k : SEQ + k]
            gmix[rows, at] = (gu * masks[0, rows]).astype(BF16)

    v = jnp.concatenate([sums[0:8, 0:RC], jnp.zeros((LANES - 8, RC), F32)], axis=0).T.astype(BF16)
    for b in range(16):
        put_og(b, 1408, v[48 * b : 48 * b + 48])
    landed(wb, sems.at[0])

    v = tn(normed[...], gmix[:, 0:PB]).astype(BF16)
    for x, z in RINGS:
        for half in range(2):
            r = ring_rows(x, z) + 256 * half
            bp[x, z, 32 * half : 32 * half + 32, OG:EARLY] = v[r : r + 32]
    emit(saves, bp, places, 0, (p0, p1))
    mixed_part[...] = nt(gmix[...], rows_of(wb, 0, BRANCH))
    saves.start(mixed_part.at[pl.ds(0, SEQ)], o_mine)
    saves.start(mixed_part.at[pl.ds(SEQ, SEQ)], o_theirs)
    t = tok[...].astype(F32)
    sums[8:9] = jnp.sum(mixed_part[...] * (t * inv_rms(t)), axis=0, keepdims=True)
    v = jnp.concatenate([sums[8:16], jnp.zeros((LANES - 8, D), F32)], axis=0).T.astype(BF16)
    for x, z in RINGS:
        for half in range(2):
            r = ring_rows(x, z) + 256 * half
            bq[z, x, 32 * half : 32 * half + 32, QB:EARLY] = v[r : r + 32]

    v = tn(normed[...], gmix[:, PB:]).astype(BF16)
    for x, z in RINGS:
        for half in range(2):
            r = ring_rows(x, z) + 256 * half
            bq[z, x, 32 * half : 32 * half + 32, 0:QB] = v[r : r + 32]
    emit(saves, bq, places, 2, (q0, q1))
    saves.wait()


def join_sums(
    places, eo_p, eu_p, lo_p, lu_p, eo_q, eu_q, lo_q, lu_q,
    p0, p1, q0, q1,
    out, out_sems,
):
    saves = Saves(out_sems)
    for n, (axis, outs, a, b, c, d) in enumerate(
        ((2, (p0, p1), eo_p, eu_p, lo_p, lu_p), (0, (q0, q1), eo_q, eu_q, lo_q, lu_q))
    ):
        for j in range(4):
            at, to = places[4 + axis, j], 4 * n + j
            out[to, :, 0:EARLY] = add(a[at], b[at])
            out[to, :, EARLY:] = add(c[at], d[at])
            saves.start(out.at[to], outs[j // 2].at[j % 2])
    saves.wait()


def add(a, b):
    return (a.astype(F32) + b.astype(F32)).astype(BF16)


def half_sums(a_p, b_p, c_p, d_p, a_q, b_q, c_q, d_q, *rest):
    outs, (early, late, in_sems) = rest[-7:-3], rest[-3:]
    loads = Saves(in_sems)
    for n, (a, b, c, d) in enumerate(((a_p, b_p, c_p, d_p), (a_q, b_q, c_q, d_q))):
        for source, target in ((a, early.at[n, 0]), (b, early.at[n, 1]), (c, late.at[n, 0]), (d, late.at[n, 1])):
            loads.start(source.at[0], target)
    for n in range(2):
        for i, v in enumerate((early, late)):
            loads.copies[4 * n + 2 * i].wait()
            loads.copies[4 * n + 2 * i + 1].wait()
            outs[2 * n + i][...] = add(v[n, 0], v[n, 1])


def pass_on(a_p, f_p, a_q, f_q, *rest):
    o_p, o_q, v, in_sems, out_sems = rest[-5:]
    loads, saves = Saves(in_sems), Saves(out_sems)
    for i, source in enumerate((a_p, f_p, a_q, f_q)):
        loads.start(source.at[1], v.at[i])
    for n, out in enumerate((o_p, o_q)):
        loads.copies[2 * n].wait()
        loads.copies[2 * n + 1].wait()
        v[2 * n] = add(v[2 * n], v[2 * n + 1])
        saves.start(v.at[2 * n], out)
    saves.wait()


def cut(
    places, p0, p1, p2, q0, q1, q2,
    o0, o1, o2, o3,
    parts, sp, sq, sd, in_sems,
):
    load((p0.at[0], p1.at[0], p2, q0.at[0], q1.at[0], q2), [parts.at[i] for i in range(6)], in_sems)
    for n, out in enumerate((sp, sq)):
        out[...] = parts[3 * n].astype(F32) + parts[3 * n + 1].astype(F32) + parts[3 * n + 2].astype(F32)
    sd[0:64] = sp[:, EARLY : EARLY + D]
    sd[64:96, 0:512] = sp[0:32, EARLY + D : EARLY + FC]
    sd[64:96, 512:1024] = sp[32:64, EARLY + D : EARLY + FC]
    tail = jnp.concatenate([sp[48:64, 384 * r : 384 * r + 384] for r in range(3)], axis=0)
    og = jnp.concatenate([sp[0:48, 0:OG], tail], axis=1).astype(BF16)
    i = lax.broadcasted_iota(jnp.int32, (16, 48), 0)
    s = lax.broadcasted_iota(jnp.int32, (16, 48), 1)

    def two(rows):
        return jnp.concatenate(rows, axis=0).astype(BF16)

    for j, out in enumerate((o0, o1, o2, o3)):
        y = places[1, (0, 2, 3, 1)[j]]
        rows = [pl.ds(pl.multiple_of(32 * c + y * 8, 8), 8) for c in range(2)]
        out[:, 0:PB] = two([sp[r, OG:EARLY] for r in rows])
        out[:, PB : PB + PI] = two([sp[r, UNIT - PI :] for r in rows])
        out[:, PB + PI : DC] = two([sq[r] for r in rows])
        mine = jnp.where((s == i + y * 12) & (i < 12), 1.0, 0.0).astype(BF16)
        out[:, DC:DOWN] = nn(mine, og).astype(BF16)
        down = sd[pl.ds(pl.multiple_of(y * 24, 8), 24)]
        out[:, DOWN : DOWN + D] = down[0:16].astype(BF16)
        out[:, DOWN + D :] = two([down[16:24, 0:512], down[16:24, 512:]])


def finish(places, o0, o1, o2, o3, mine, theirs, out_grad, gate_grad, chan_grad, down_grad, v):
    v[...] = o0[...].astype(F32) + o1[...].astype(F32) + o2[...].astype(F32) + o3[...].astype(F32)
    core = places[3, 0]
    theirs[...] = v[pl.ds(pl.multiple_of((1 - core) * 8, 8), 8), 0:DC]
    mine[...] = v[pl.ds(pl.multiple_of(core * 8, 8), 8), 0:DC]
    out_grad[...] = v[0:12, DC : DC + D]
    gate_grad[...] = v[0:12, DC + D : DC + D + 384]
    chan_grad[...] = v[:, DC + D + 384 : DOWN].T[0:8]
    down_grad[0:16] = v[:, DOWN : DOWN + D]
    down_grad[16:24, 0:512] = v[0:8, DOWN + D :]
    down_grad[16:24, 512:] = v[8:16, DOWN + D :]


def unpack(places, mine, theirs, branch, inner, gains):
    def halves(ins):
        for c, v in enumerate(ins):
            for q in range(4):
                to = 768 * q + 384 * c
                if q == 0:
                    branch[:, to : to + PB] = v[:, 0:PB]
                    branch[:, to + PB : to + 384] = v[:, PB + PI : PB + PI + 128]
                else:
                    branch[:, to : to + 384] = v[:, PI + 384 * q : PI + 384 * q + 384]
                at = PB if q == 0 else DC - LATE + 768 * (q - 1)
                to = 1536 * q + 768 * c
                inner[:, to : to + 768] = v[:, at : at + 768]

    gains[...] = mine[:, DC - LATE - LANES : DC - LATE] + theirs[:, DC - LATE - LANES : DC - LATE]

    @pl.when(places[3, 0] == 0)
    def _():
        halves((mine, theirs))

    @pl.when(places[3, 0] == 1)
    def _():
        halves((theirs, mine))


VM, HB, SM, ANY = pltpu.VMEM, pltpu.HBM, pltpu.SMEM, pl.ANY


def kernel(body, ins, spaces, outs, scratch, mib, flops=0, aliases={}):
    moved = sum(v.size * v.dtype.itemsize for v in ins)
    ins = [pltpu.with_memory_space_constraint(v, HB) if s is HB else v for v, s in zip(ins, spaces)]
    return pl.pallas_call(
        body,
        out_shape=[HB(s, d) if at is HB else jax.ShapeDtypeStruct(s, d) for s, d, at in outs],
        in_specs=[pl.BlockSpec(memory_space=s) for s in spaces],
        out_specs=[pl.BlockSpec(memory_space=s) for _, _, s in outs],
        scratch_shapes=scratch,
        input_output_aliases=aliases,
        compiler_params=pltpu.CompilerParams(vmem_limit_bytes=mib * 2**20),
        cost_estimate=pl.CostEstimate(flops=flops, bytes_accessed=moved, transcendentals=0),
    )(*ins)


def shards(
    tokens, cotangent, segment, keep_mask, conv_state, lru_state, norm1_gain, conv_weight, lru_bias, decay_rate,
    gate_weight, branch_weight, out_weight, norm2_gain, mlp_in_weight, mlp_out_weight,
):
    here = my_place()
    core = here["core"]
    zero = jnp.zeros_like(core)
    places = jnp.stack(
        [jnp.stack(ring_places(axis, here)) for axis in "xyz"]
        + [jnp.stack([core, zero, zero, zero])]
        + [jnp.stack(pair_places(axis, here)) for axis in "xyz"]
    ).astype(jnp.int32)
    vmem, dma = pltpu.VMEM, pltpu.SemaphoreType.DMA

    tc = jnp.concatenate([tokens[0], cotangent[0]], axis=0)
    tc_other = swap(tc)
    marks = jnp.concatenate([segment, keep_mask], axis=1).astype(F32)
    states = jnp.concatenate([conv_state[0], lru_state], axis=0)
    sent = jnp.concatenate([core_half(states, 1 - core, 2), jnp.pad(marks, ((0, 0), (0, RC - 2 * SEQ)))], axis=0)
    sent = swap(sent)

    mine, theirs, own = kernel(
        pack,
        (places, branch_weight, mlp_in_weight, jnp.stack([norm1_gain, norm2_gain]), out_weight, gate_weight,
         jnp.concatenate([conv_weight, lru_bias, decay_rate[None]], axis=0), mlp_out_weight),
        [SM, HB, HB, VM, HB, HB, VM, HB],
        [((8, DC), BF16, VM)] * 2 + [((16, OWN - DC), BF16, VM)],
        [vmem(v.shape, BF16) for v in (branch_weight, mlp_in_weight, out_weight, gate_weight, mlp_out_weight)]
        + [dma((5,))],
        8,
    )
    (block,) = kernel(join, (places, mine, swap(theirs), own), [SM] + [VM] * 3, [((16, OWN), BF16, VM)], [], 8)

    row = ((64, UNIT), BF16)
    unit_of = ((2, 32, UNIT), BF16)
    p, q = kernel(
        unit,
        (places, *ring_direct(block, "y"), tc_other, sent),
        [SM] + [VM] * 4 + [ANY] * 2,
        [(*unit_of, HB)] * 2,
        [vmem(*row), vmem(*row), vmem((64, DC), F32), vmem((96, D), F32), dma((4,))],
        16,
    )
    early, late = (4, 64, EARLY), (4, 64, LATE)
    stack = ((4, 64, UNIT), BF16)
    p, q = ring_both(p, "z"), ring_both(q, "x")
    stacks = [((*v, n), BF16, HB) for n in (EARLY, LATE) for v in ((2, 4, 32), (2, 2, 2, 32))]
    unit_of = (2, 32, UNIT)
    partial = kernel(
        planes((0, 1, 2)),
        (places, *p[:3], *q[:3]),
        [SM] + [HB] * 6,
        stacks,
        [vmem((6, *unit_of), BF16), dma((6,)), dma((12,))],
        8,
    )
    pe, qe, pl_, ql = kernel(
        planes((3,)),
        (places, p[3], q[3], *partial),
        [SM, ANY, ANY] + [HB] * 4,
        stacks,
        [vmem((2, *unit_of), BF16), dma((2,)), dma((4,))],
        8,
        aliases={3 + i: i for i in range(4)},
    )
    pe, qe, pl_, ql = ring_both(pe, "x"), ring_both(qe, "z"), ring_both(pl_, "x"), ring_both(ql, "z")

    tok = jnp.concatenate([tc[:SEQ], tc_other[:SEQ]], axis=0)
    cot = jnp.concatenate([tc[SEQ:], tc_other[SEQ:]], axis=0)
    states = jnp.stack([core_half(states, core, 2), sent[:4]])
    marks = jnp.concatenate([marks, sent[4:, : 2 * SEQ]], axis=0)
    seg, keep = marks[:, :SEQ], marks[:, SEQ:]
    earlier = [jnp.concatenate([jnp.repeat(seg[:, :1], k, axis=1), seg[:, : SEQ - k]], axis=1) for k in range(1, 4)]
    masks = jnp.stack([keep, (earlier[0] != seg).astype(F32)] + [(e == seg).astype(F32) for e in earlier])
    masks = jnp.broadcast_to(masks.reshape(5, TOK, 1), (5, TOK, LANES))

    wide, wide_low = ((TOK, D), F32), ((TOK, D), BF16)
    act, act_low, padded = ((TOK, RC), F32), ((TOK, RC), BF16), ((2, PAD, RC), F32)
    tables = ((4, 2 * HS, 2 * HS), BF16)
    saved = [wide_low, act_low, padded, act, act_low, act, act, padded, tables]
    part, finals, gains, chans, normed, merged, u, gate_in, conv_low, rate, inp, st, table = kernel(
        rec_forward,
        (places, tok, masks, states[:, :3], states[:, 3:], *pe, *qe),
        [SM] + [VM] * 4 + [HB] * 8,
        [((TOK + 8, D), F32, VM), ((4, RC), F32, VM), ((8, D), F32, VM), ((8, RC), F32, VM)]
        + [(*v, HB) for v in saved],
        [vmem((*ROWS, PB + EARLY), BF16), vmem((*OG_ROWS, OGC), BF16)]
        + [vmem(*v) for v in saved + [act, act]]
        + [dma((2,)), dma((9,))],
        32,
        2 * TOK * (D * BRANCH + RC * (D + 768)),
    )
    half = ((SEQ, D), F32)
    other = swap(part)
    normed2, own, residual = kernel(
        mlp_norm,
        (tok, part, other, gains),
        [VM] * 4,
        [(*wide_low, VM), (*half, VM), (*wide, HB)],
        [vmem(*wide), dma],
        16,
    )
    hidden, ggu, base, back = kernel(
        mlp,
        (places, cot, normed2, own, *pl_, *ql),
        [SM] + [VM] * 3 + [ANY] * 8,
        [((TOK, FC), BF16, VM), ((TOK, INNER), BF16, VM), (*half, HB), ((TOK + SEQ, D), F32, HB)],
        [vmem((*ROWS, INNER), BF16), vmem((*DOWN_ROWS, D), BF16), vmem((2, TOK, 768), F32)]
        + [vmem(*v) for v in (wide, wide, half)]
        + [dma((2,)), dma((3,))],
        32,
        2 * TOK * D * (2 * INNER + 2 * FC),
    )
    back_other = swap(back)
    outs = kernel(
        mlp_grads,
        (places, cot, normed2, hidden, ggu),
        [SM] + [VM] * 4,
        [((2, *late), BF16, HB)] * 4,
        [vmem((4,) + late, BF16), vmem((4,) + late, BF16), dma((12,))],
        32,
        2 * TOK * D * (INNER + FC),
    )
    lp, lq = outs[:2], outs[2:]

    def first_half(p, q, routes):
        return send(p[1], partner(routes[0], 0)), send(q[1], partner(routes[1], 0))

    def second_half(p, q, came, routes, shape, until=(), lands=HB):
        up = kernel(
            pass_on,
            (p[0], came[0], q[0], came[1], *until),
            [HB, lands, HB, lands] + [HB] * len(until),
            [(shape, BF16, HB)] * 2,
            [vmem((4,) + shape, BF16), dma((4,)), dma((2,))],
            16,
        )
        return send(up[0], partner(routes[0], 1)), send(up[1], partner(routes[1], 1))

    late_came = first_half(lp, lq, "xz")
    outs = kernel(
        rec_backward,
        (places, tok, cot, masks, gains, chans, back_other, back, residual, normed, merged, u, gate_in, conv_low, rate,
         inp, st, table, *pe, *qe),
        [SM] + [VM] * 6 + [HB] * 19,
        [(*v, HB) for v in (half, half, half)] + [((2, *early), BF16, HB)] * 4,
        [vmem((*ROWS, BRANCH), BF16), vmem((*OG_ROWS, OGC), BF16)]
        + [vmem(*v) for v in (wide, wide, wide_low, act_low, padded, act, act_low, act, act, padded, tables)]
        + [vmem(*v) for v in (act, wide_low, act, act, act_low, act_low, act, ((TOK, BRANCH), BF16))]
        + [vmem((2, PAD, LANES), F32), vmem((16, D), F32), vmem(*wide), vmem(*half)]
        + [vmem((4,) + early, BF16), vmem((4,) + early, BF16), dma((2,)), dma((11,)), dma((11,))],
        48,
        2 * TOK * D * (2 * BRANCH + 2 * RC),
    )
    grad_residual, mixed_mine, mixed_theirs = outs[:3]
    ep, eq = outs[3:5], outs[5:]
    early_came = first_half(ep, eq, "xz")
    late_up = second_half(lp, lq, late_came, "xz", late, (ep[0],))
    early_up = second_half(ep, eq, early_came, "xz", early)

    summed = kernel(
        half_sums,
        (ep[0], early_came[0], lp[0], late_came[0], eq[0], early_came[1], lq[0], late_came[1]),
        [HB] * 8,
        [(early, BF16, VM), (late, BF16, VM)] * 2,
        [vmem((2, 2) + early, BF16), vmem((2, 2) + late, BF16), dma((8,))],
        16,
    )
    outs = kernel(
        join_sums,
        (places, summed[0], early_up[0], summed[1], late_up[0], summed[2], early_up[1], summed[3], late_up[1]),
        [SM] + [VM] * 8,
        [((2, 64, UNIT), BF16, HB)] * 4,
        [vmem((8, 64, UNIT), BF16), dma((8,))],
        8,
    )
    tp, tq = outs[:2], outs[2:]
    came = first_half(tp, tq, "zx")
    up = second_half(tp, tq, came, "zx", (64, UNIT), lands=ANY)
    sums = kernel(
        cut,
        (places, tp[0], came[0], up[0], tq[0], came[1], up[1]),
        [SM] + [HB, ANY, ANY] * 2,
        [((16, OWN), BF16, VM)] * 4,
        [vmem((6, 64, UNIT), BF16), vmem((64, UNIT), F32), vmem((64, UNIT), F32), vmem((96, D), F32), dma((6,))],
        16,
    )
    mine, theirs, out_grad, gate_grad, chan_grad, down_grad = kernel(
        finish,
        (places, *terms_direct(sums, "y")),
        [SM] + [VM] * 4,
        [((8, DC), F32, VM)] * 2 + [(s, F32, VM) for s in ((12, D), (12, 384), (8, 16), (24, D))],
        [vmem((16, OWN), F32)],
        8,
    )
    branch_grad, in_grad, gain_grads = kernel(
        unpack,
        (places, mine, swap(theirs)),
        [SM] + [VM] * 2,
        [((8, 2 * R), F32, VM), ((8, 2 * F), F32, VM), ((8, LANES), F32, VM)],
        [],
        8,
    )

    output = (base + back_other[TOK:]).astype(BF16)
    grad, _ = rms_back(mixed_mine + swap(mixed_theirs), tok[:SEQ].astype(F32), gains[0])
    input_grad = (grad_residual + grad).astype(BF16)
    theirs = other[TOK : TOK + 4, :RC]
    finals = jnp.stack(
        [v.reshape(1, 4, 2, 384) for v in (jnp.where(core == 0, finals, theirs), jnp.where(core == 0, theirs, finals))],
        axis=3,
    ).reshape(1, 4, R)
    return (
        output[None],
        input_grad[None],
        finals[:, :3],
        finals[:, 3],
        gain_grads[:, 0],
        chan_grad[:4, :12],
        chan_grad[4:7, :12],
        chan_grad[7, :12],
        gate_grad,
        branch_grad,
        out_grad,
        gain_grads[:, 1],
        in_grad,
        down_grad,
    )


def solution(mesh):
    rows, last = P(AXES), P(None, AXES)
    specs = [rows] * 6 + [rows, last, last] + [rows] * 7
    outs = [rows] * 4 + [rows, last, last] + [rows] * 7
    return jax.shard_map(
        shards, mesh=mesh, in_specs=tuple(specs), out_specs=tuple(outs), check_vma=False
    )
```

```python
import jax
import jax.numpy as jnp
from jax import lax
from jax.experimental import pallas as pl
from jax.experimental.pallas import tpu as pltpu
from jax.sharding import PartitionSpec as P

AXES = ("dp", "fsdp")
D, R, F, SEQ = 1024, 1536, 3072, 128
RC, FC = R // 2, F // 2
HS = 192
F32, BF16 = jnp.float32, jnp.bfloat16
BRANCH, INNER = 2 * RC, 2 * FC
TOK, PAD, LANES = 2 * SEQ, SEQ + 8, 128

EARLY, LATE = 1408, 2304
UNIT = EARLY + LATE
OG, PB, PI, QB = 1152, 256, 768, 1280
DC = PB + PI + UNIT
OGC = 1536
DOWN = DC + OGC
OWN = DOWN + D + D // 2


def place_of(device):
    outer, inner = divmod(device, 32)
    x_hi, core = divmod(outer, 2)
    z, rest = divmod(inner, 8)
    x_lo, y = divmod(rest, 4)
    return dict(x=x_hi * 2 + x_lo, y=y, z=z, core=core)


def device_at(x, y, z, core):
    return ((x // 2) * 2 + core) * 32 + z * 8 + (x % 2) * 4 + y


def pairs(move):
    return [(d, device_at(**move(place_of(d)))) for d in range(128)]


def along(axis, steps):
    def move(p):
        sign = 1 if p["core"] == 0 else -1
        return {**p, axis: (p[axis] + sign * steps) % 4}

    return pairs(move)


def other_core(p):
    return {**p, "core": 1 - p["core"]}


def partner(axis, turn):
    def move(p):
        i = p[axis]
        return {**p, axis: i ^ 1 if (p["core"] + turn) % 2 == 0 else 3 - i}

    return pairs(move)


def opposite(axis):
    return pairs(lambda p: {**p, axis: (p[axis] + 2) % 4})


def send(value, route):
    return lax.ppermute(value, AXES, route)


def swap(value):
    return send(value, pairs(other_core))


def my_place():
    device = lax.axis_index(AXES)
    outer, inner = device // 32, device % 32
    return dict(x=(outer // 2) * 2 + (inner // 4) % 2, y=inner % 4, z=inner // 8, core=outer % 2)


def ring_places(axis, here):
    sign, at = 1 - 2 * here["core"], here[axis]
    return [at, (at - sign) % 4, (at + sign) % 4, (at + 2) % 4]


def ring(block, axis):
    one = send(block, along(axis, 1))
    two = send(one, along(axis, 1))
    return block, one, send(two, along(axis, 1)), two


def ring_both(block, axis):
    up, down = send(block, along(axis, 1)), send(block, along(axis, -1))
    return block, up, down, send(up, along(axis, 1))


def pair_places(axis, here):
    i, odd = here[axis], here["core"] == 1
    by_one, by_ends = i + 1 - 2 * (i % 2), 3 - i
    return [i, jnp.where(odd, by_one, by_ends), jnp.where(odd, by_ends, by_one), (i + 2) % 4]


def ring_direct(block, axis):
    return block, send(block, along(axis, 1)), send(block, along(axis, -1)), send(block, opposite(axis))


def terms_direct(terms, axis):
    own, ahead, far, behind = terms
    return own, send(ahead, along(axis, 1)), send(far, opposite(axis)), send(behind, along(axis, -1))


def total(*terms):
    out = terms[0].astype(F32)
    for term in terms[1:]:
        out = out + term.astype(F32)
    return out.astype(BF16)


def core_half(array, core, blocks):
    v = array.reshape(array.shape[:-1] + (blocks, 2, array.shape[-1] // (2 * blocks)))
    v = lax.dynamic_index_in_dim(v, core, v.ndim - 2, keepdims=False)
    return v.reshape(array.shape[:-1] + (array.shape[-1] // 2,))


def dot(a, b, dims):
    return lax.dot_general(a, b, (dims, ((), ())), preferred_element_type=F32)


def nn(a, b):
    return dot(a, b, ((1,), (0,)))


def nt(a, b):
    return dot(a, b, ((1,), (1,)))


def tn(a, b):
    return dot(a, b, ((0,), (0,)))


def inv_rms(v):
    return lax.rsqrt(jnp.mean(v * v, axis=-1, keepdims=True) + 1e-6)


def rms_back(grad, v, gain):
    s = inv_rms(v)
    n = v * s
    g2 = grad * gain
    return s * (g2 - n * jnp.mean(g2 * n, axis=-1, keepdims=True)), grad * n


C0, C1 = 0.7978845608028654, 0.044715


def gelu_both(a):
    t = jnp.tanh(C0 * (a + C1 * (a * a * a)))
    half = 0.5 * (1.0 + t)
    return a * half, half + 0.5 * a * (1.0 - t * t) * (C0 * (1.0 + 3.0 * C1 * (a * a)))


def gates(rate, inp, bias1, bias2, decay, keep, starts):
    rg = jax.nn.sigmoid(rate + bias1)
    ig = jax.nn.sigmoid(inp + bias2)
    sd = jnp.exp(-8.0 * rg * decay)
    q = 1.0 - sd * sd
    root = jnp.sqrt(jnp.maximum(q, 0.001))
    scale = starts + (1.0 - starts) * root
    return rg, ig, sd, q, root, scale


def cols(c):
    return pl.ds(pl.multiple_of(c * LANES, LANES), LANES)


class Saves:
    def __init__(self, sem):
        self.sem, self.copies = sem, []

    def start(self, source, target):
        self.copies.append(pltpu.make_async_copy(source, target, self.sem.at[len(self.copies)]))
        self.copies[-1].start()

    def wait(self):
        for copy in self.copies:
            copy.wait()


def pick(rows, where):
    return jnp.where(lax.broadcasted_iota(jnp.int32, (rows, where.shape[1]), 0) == where, 1.0, 0.0).astype(BF16)


def stand(values, rows):
    v = values.astype(F32)
    i = lax.broadcasted_iota(jnp.int32, (rows, v.shape[1]), 0)
    j = lax.broadcasted_iota(jnp.int32, (rows, v.shape[1]), 1)
    lane = lax.broadcasted_iota(jnp.int32, (rows, LANES), 1)
    out = jnp.zeros((rows, LANES), F32)
    for n in range(v.shape[0]):
        column = jnp.sum(jnp.where(i == j, v[n : n + 1], 0.0), axis=1, keepdims=True)
        out = out + jnp.where(lane == n, column, 0.0)
    return out


def load(sources, targets, sems):
    copies = Saves(sems)
    for source, target in zip(sources, targets):
        copies.start(source, target)
    copies.wait()


def pack(
    places, i_branch, i_inner, gain, i_out, i_gate, perchan, i_down, mine, theirs, own,
    branch, inner, out, gate, down, sems,
):
    load((i_branch, i_inner, i_out, i_gate, i_down), (branch, inner, out, gate, down), sems)

    gains = stand(gain[...], 8).astype(BF16)

    def halves(outs):
        for c, to_core in enumerate(outs):
            for q in range(4):
                v = branch[:, 768 * q + 384 * c : 768 * q + 384 * c + 384]
                if q == 0:
                    to_core[:, 0:PB] = v[:, 0:PB]
                    to_core[:, PB + PI : PB + PI + 128] = v[:, PB:]
                else:
                    to_core[:, PI + 384 * q : PI + 384 * q + 384] = v
                v = inner[:, 1536 * q + 768 * c : 1536 * q + 768 * c + 768]
                to = PB if q == 0 else DC - LATE + 768 * (q - 1)
                to_core[:, to : to + 768] = v
            tile = DC - LATE - LANES
            to_core[:, tile : tile + LANES] = gains

    @pl.when(places[3, 0] == 0)
    def _():
        halves((mine, theirs))

    @pl.when(places[3, 0] == 1)
    def _():
        halves((theirs, mine))

    own[...] = jnp.zeros_like(own)
    own[0:12, 0:D] = out[...]
    own[0:12, D : D + 384] = gate[...]
    own[:, 1408:OGC] = stand(perchan[...], 16).astype(BF16)
    own[:, OGC : OGC + D] = down[0:16]
    own[:, OGC + D :] = jnp.concatenate(
        [down[16:24, 0:512].astype(F32), down[16:24, 512:].astype(F32)], axis=0
    ).astype(BF16)


def join(places, mine, theirs, own, block):
    def rows(low, high):
        block[:, 0:DC] = jnp.concatenate([low[...].astype(F32), high[...].astype(F32)], axis=0).astype(BF16)

    @pl.when(places[3, 0] == 0)
    def _():
        rows(mine, theirs)

    @pl.when(places[3, 0] == 1)
    def _():
        rows(theirs, mine)

    block[:, DC:] = own[...]


def unit(places, p0, p1, p2, p3, *rest):
    o_p, o_q, p, q, d, dn, sems = rest[-7:]
    ogs = []
    s = lax.broadcasted_iota(jnp.int32, (1, 64), 1)
    y = jnp.zeros((1, 64), jnp.int32)
    for j, piece in enumerate((p0, p1, p2, p3)):
        at = places[1, j]
        y = jnp.where(s // 16 == j, at, y)
        v = piece[:, 0:DC].astype(F32)
        for c in range(2):
            d[pl.ds(pl.multiple_of(c * 32 + at * 8, 8), 8)] = v[8 * c : 8 * c + 8]
        ogs.append(piece[:, DC:DOWN])
        v = piece[:, DOWN:].astype(F32)
        dn[pl.ds(pl.multiple_of(at * 24, 8), 16)] = v[:, 0:D]
        for h in range(2):
            dn[pl.ds(pl.multiple_of(at * 24 + 16, 8), 8), 512 * h : 512 * h + 512] = v[8 * h : 8 * h + 8, D:]
    saves = Saves(sems)
    q[...] = d[:, PB + PI :].astype(BF16)
    for c in range(2):
        saves.start(q.at[pl.ds(32 * c, 32)], o_q.at[c])
    p[:, OG:EARLY] = d[:, 0:PB].astype(BF16)
    p[:, UNIT - PI :] = d[:, PB : PB + PI].astype(BF16)
    i = s % 16
    og = nn(pick(48, jnp.where(i < 12, y * 12 + i, 64)), jnp.concatenate(ogs, axis=0)).astype(BF16)
    p[0:48, 0:OG] = og[:, 0:OG]
    for r in range(3):
        p[48:64, 384 * r : 384 * r + 384] = og[16 * r : 16 * r + 16, OG:]
    p[:, EARLY : EARLY + D] = dn[0:64].astype(BF16)
    p[0:32, EARLY + D : EARLY + FC] = dn[64:96, 0:512].astype(BF16)
    p[32:64, EARLY + D : EARLY + FC] = dn[64:96, 512:1024].astype(BF16)
    for c in range(2):
        saves.start(p.at[pl.ds(32 * c, 32)], o_p.at[c])
    saves.wait()


def planes(which):
    def body(places, *refs):
        n = len(which)
        (o_pe, o_qe, o_pl, o_ql), v, in_sems, out_sems = refs[-7:-3], *refs[-3:]
        loads, saves = Saves(in_sems), Saves(out_sems)
        for i, piece in enumerate(refs[: 2 * n]):
            loads.start(piece, v.at[i])
        for i in range(2 * n):
            loads.copies[i].wait()
            j = which[i % n]
            x = places[0, j]
            for first, count, p, q in ((0, EARLY, o_pe, o_qe), (EARLY, LATE, o_pl, o_ql)):
                target = p.at[:, places[2, j]] if i < n else q.at[x // 2, :, x % 2]
                saves.start(v.at[i, :, :, pl.ds(first, count)], target)
        saves.wait()

    return body


ROWS = (2, 2, 4, 2, 32)
OG_ROWS, DOWN_ROWS = (2, 4, 2, 48), (2, 4, 2, 96)


def ring_rows(x, z):
    return (x // 2) * 512 + z * 64 + (x % 2) * 32


def p_copy(piece, places, j, first, count, block, to, sem):
    x = places[0, j]
    target = block.at[x // 2, :, :, x % 2, :, pl.ds(to, count)]
    pltpu.make_async_copy(piece.at[..., pl.ds(first, count)], target, sem).start()


def q_copy(piece, places, j, first, count, block, to, sem):
    target = block.at[:, :, places[2, j], :, :, pl.ds(to, count)]
    pltpu.make_async_copy(piece.at[..., pl.ds(first, count)], target, sem).start()


def og_copy(piece, places, j, block, sem):
    x = places[0, j]
    block = block.at[x // 2, :, x % 2]
    for source, target in (
        (piece.at[0, :, :, pl.ds(0, OG)], block.at[:, pl.ds(0, 32), pl.ds(0, OG)]),
        (piece.at[1, :, pl.ds(0, 16), pl.ds(0, OG)], block.at[:, pl.ds(32, 16), pl.ds(0, OG)]),
    ):
        pltpu.make_async_copy(source, target, sem).start()
    for r in range(3):
        pltpu.make_async_copy(
            piece.at[1, :, pl.ds(16, 16), pl.ds(384 * r, 384)], block.at[:, pl.ds(16 * r, 16), pl.ds(OG, 384)], sem
        ).start()


def down_copy(piece, places, j, block, sem):
    x = places[0, j]
    block = block.at[x // 2, :, x % 2]
    for h in range(2):
        pltpu.make_async_copy(piece.at[h, :, :, pl.ds(0, D)], block.at[:, pl.ds(32 * h, 32)], sem).start()
        pltpu.make_async_copy(
            piece.at[h, :, :, pl.ds(D, 512)], block.at[:, pl.ds(64, 32), pl.ds(512 * h, 512)], sem
        ).start()


def rows_of(block, first, count):
    return block[..., first : first + count].reshape(D, count)


def landed(block, sem):
    pltpu.make_async_copy(block, block, sem).wait()


def turn_matrix():
    i = lax.broadcasted_iota(jnp.int32, (2 * HS, 2 * HS), 0)
    j = lax.broadcasted_iota(jnp.int32, (2 * HS, 2 * HS), 1)
    return jnp.where((i == j + HS) | (j == i + HS), 1.0, 0.0).astype(BF16)


def quarter_masks():
    i = lax.broadcasted_iota(jnp.int32, (2 * HS, 2 * HS), 0) < HS
    j = lax.broadcasted_iota(jnp.int32, (2 * HS, 2 * HS), 1) < HS
    return i, j


def rec_forward(
    places, tok, masks, conv_before, lru_before, p0, p1, p2, p3, q0, q1, q2, q3,
    part, finals, gains, chans, o_normed, o_merged, o_u, o_gate, o_conv, o_rate, o_inp, o_st, o_tables,
    wb, wog, normed, merged, u, gate_in, conv_low, rate, inp, st, tables, coeff, drive, sems, out_sems,
):
    for j, (p, q) in enumerate(((p0, q0), (p1, q1), (p2, q2), (p3, q3))):
        p_copy(p, places, j, OG, PB, wb, 0, sems.at[0])
        q_copy(q, places, j, 0, EARLY, wb, PB, sems.at[0])
    for j, p in enumerate((p0, p1, p2, p3)):
        og_copy(p, places, j, wog, sems.at[1])
    saves = Saves(out_sems)
    t = tok[...].astype(F32)
    scaled = t * inv_rms(t)
    landed(wb, sems.at[0])
    gains[...] = rows_of(wb, BRANCH, LANES).astype(F32).T[:8]
    normed[...] = (scaled * gains[0:1]).astype(BF16)
    saves.start(normed, o_normed)
    for s in range(2):
        u[s, 0:8] = jnp.zeros((8, RC), F32)
        u[s, 5:8] = conv_before[s]
        st[s, 0:8] = jnp.zeros((8, RC), F32)
        st[s, 7:8] = lru_before[s]

    v = nn(normed[...], rows_of(wb, 0, RC))
    for s in range(2):
        rows = slice(s * SEQ, (s + 1) * SEQ)
        for c in range(6):
            u[s, 8:, LANES * c : LANES * c + LANES] = v[rows, LANES * c : LANES * c + LANES] * masks[0, rows]

    saves.start(u, o_u)

    gate_in[...] = nn(normed[...], rows_of(wb, RC, RC))

    saves.start(gate_in, o_gate)
    landed(wog, sems.at[1])
    chans[...] = wog[..., 1408:].reshape(RC, LANES).astype(F32).T[:8]

    @pl.loop(0, 6)
    def _(c):
        at = cols(c)
        for s in range(2):
            rows = slice(s * SEQ, (s + 1) * SEQ)
            v = chans[4:5, at] + chans[0:1, at] * u[s, 8:, at]
            for k in range(1, 4):
                v = v + chans[k : k + 1, at] * (u[s, 8 - k : PAD - k, at] * masks[1 + k, rows])
            conv_low[rows, at] = v.astype(BF16)

    saves.start(conv_low, o_conv)
    turn = turn_matrix()
    top, left = quarter_masks()
    for p in range(2):
        g = wog[p, :, :, :, D : D + 384].reshape(2 * HS, 2 * HS)
        turned = nn(g, turn).astype(BF16)
        zero = jnp.zeros_like(g)
        tables[2 * p] = jnp.where(left, jnp.where(top, g, zero), jnp.where(top, zero, turned))
        tables[2 * p + 1] = jnp.where(left, jnp.where(top, turned, zero), jnp.where(top, zero, g))
        at = slice(2 * HS * p, 2 * HS * (p + 1))
        rate[:, at] = nn(conv_low[:, at], tables[2 * p])
        inp[:, at] = nn(conv_low[:, at], tables[2 * p + 1])
    saves.start(tables, o_tables)
    saves.start(rate, o_rate)
    saves.start(inp, o_inp)

    @pl.loop(0, 6)
    def _(c):
        at = cols(c)
        keep, starts = masks[0], masks[1]
        _, ig, sd, _, _, scale = gates(
            rate[:, at], inp[:, at], chans[5:6, at], chans[6:7, at], chans[7:8, at], keep, starts
        )
        coeff[:, at] = (1.0 - starts) * (keep * sd + (1.0 - keep))
        drive[:, at] = keep * scale * ig * conv_low[:, at].astype(F32)

    row = lax.broadcasted_iota(jnp.int32, (8, RC), 0)

    def forward(i, carry):
        new = []
        for s in range(2):
            at = pl.ds(pl.multiple_of(s * SEQ + i * 8, 8), 8)
            a, b = coeff[at], drive[at]
            for k in (1, 2, 4):
                later = row >= k
                b = jnp.where(later, a * pltpu.roll(b, k, 0) + b, b)
                a = jnp.where(later, a * pltpu.roll(a, k, 0), a)
            h = a * carry[s] + b
            st[s, pl.ds(pl.multiple_of(8 + i * 8, 8), 8)] = h
            new.append(h[7:8])
        return tuple(new)

    last = lax.fori_loop(0, SEQ // 8, forward, (lru_before[0], lru_before[1]))
    saves.start(st, o_st)
    part[TOK:] = jnp.zeros((8, D), F32)
    part[TOK : TOK + 3, 0:RC] = u[1, PAD - 3 :]
    part[TOK + 3 : TOK + 4, 0:RC] = last[1]
    finals[0:3] = u[0, PAD - 3 :]
    finals[3:4] = last[0]

    @pl.loop(0, 6)
    def _(c):
        at = cols(c)
        act, _ = gelu_both(gate_in[:, at])
        for s in range(2):
            rows = slice(s * SEQ, (s + 1) * SEQ)
            merged[rows, at] = (st[s, 8:, at] * act[rows]).astype(BF16)

    saves.start(merged, o_merged)

    part[0:TOK] = nn(merged[...], wog[..., 0:D].reshape(RC, D))

    saves.wait()


def mlp_norm(tok, part, other, gains, normed2, own, o_residual, residual, sem):
    for s in range(2):
        rows, theirs = slice(s * SEQ, (s + 1) * SEQ), slice((1 - s) * SEQ, (2 - s) * SEQ)
        v = tok[rows].astype(F32) + (part[rows] + other[theirs])
        residual[rows] = v
        normed2[rows] = (v * inv_rms(v) * gains[1:2]).astype(BF16)
    copy = pltpu.make_async_copy(residual, o_residual, sem)
    copy.start()
    own[...] = residual[0:SEQ]
    copy.wait()


def mlp(
    places, cot, normed2, own, p0, p1, p2, p3, q0, q1, q2, q3,
    hidden, ggu, o_base, o_back,
    win, wdown, grad_hidden, down, back, base, sems, out_sems,
):
    for j, p in enumerate((p0, p1, p2, p3)):
        down_copy(p, places, j, wdown, sems.at[1])
    for j, (p, q) in enumerate(((p0, q0), (p1, q1), (p2, q2), (p3, q3))):
        p_copy(p, places, j, FC, PI, win, 0, sems.at[0])
        q_copy(q, places, j, 0, LATE, win, PI, sems.at[0])
    saves = Saves(out_sems)
    down[...] = jnp.zeros_like(down)
    back[...] = jnp.zeros_like(back)
    landed(wdown, sems.at[1])

    @pl.loop(0, 2)
    def _(c):
        grad_hidden[c] = nt(cot[...], wdown[c].reshape(768, D))

    landed(win, sems.at[0])

    @pl.loop(0, 2)
    def _(c):
        at = pl.ds(pl.multiple_of(768 * c, 256), 768)
        up = pl.ds(pl.multiple_of(FC + 768 * c, 256), 768)
        wa, wu = win[..., at].reshape(D, 768), win[..., up].reshape(D, 768)
        a = nn(normed2[...], wa)
        b = nn(normed2[...], wu)
        ga, da = gelu_both(a)
        h = (ga * b).astype(BF16)
        hidden[:, at] = h
        gh = grad_hidden[c]
        gg_a = (gh * b * da).astype(BF16)
        gg_b = (gh * ga).astype(BF16)
        ggu[:, at] = gg_a
        ggu[:, up] = gg_b
        down[...] += nn(h, wdown[c].reshape(768, D))
        back[...] += nt(gg_a, wa) + nt(gg_b, wu)

    saves.start(back, o_back.at[pl.ds(0, TOK)])
    saves.start(down.at[pl.ds(SEQ, SEQ)], o_back.at[pl.ds(TOK, SEQ)])
    base[...] = own[...] + down[0:SEQ]
    saves.start(base, o_base)
    saves.wait()


def emit(saves, block, places, axis, outs):
    for j in range(4):
        saves.start(block.at[places[4 + axis, j]], outs[j // 2].at[j % 2])


RINGS = [(x, z) for x in range(4) for z in range(4)]


def emit_columns(saves, block, places, axis, outs, first, count):
    for j in range(4):
        columns = pl.ds(first, count)
        saves.start(block.at[places[4 + axis, j], :, :, columns], outs[j // 2].at[j % 2, :, :, columns])


def mlp_grads(
    places, cot, normed2, hidden, ggu, p0, p1, q0, q1,
    bp, bq, out_sems,
):
    saves = Saves(out_sems)
    @pl.loop(0, 2)
    def _(xh):
        v = tn(hidden[:, pl.ds(pl.multiple_of(768 * xh, 256), 768)], cot[...]).astype(BF16)
        for z in range(4):
            for xl in range(2):
                r = 96 * (2 * z + xl)
                bp[2 * xh + xl, z, :, 0:D] = v[r : r + 64]
                bp[2 * xh + xl, z, 0:32, D:FC] = v[r + 64 : r + 96, 0:512]
                bp[2 * xh + xl, z, 32:64, D:FC] = v[r + 64 : r + 96, 512:1024]

    emit_columns(saves, bp, places, 0, (p0, p1), 0, FC)

    def put(block, order, first, to):
        v = tn(normed2[...], ggu[:, pl.ds(pl.multiple_of(first, 256), 768)]).astype(BF16)
        for x, z in RINGS:
            for half in range(2):
                r = ring_rows(x, z) + 256 * half
                at = (x, z) if order else (z, x)
                columns = pl.ds(pl.multiple_of(to, 256), 768)
                block[(*at, slice(32 * half, 32 * half + 32), columns)] = v[r : r + 32]

    put(bp, True, 0, FC)
    emit_columns(saves, bp, places, 0, (p0, p1), FC, PI)
    q_copies = [(bq.at[places[6, j]], (q0, q1)[j // 2].at[j % 2]) for j in range(4)]

    @pl.loop(0, 3)
    def _(part):
        put(bq, False, 768 * (part + 1), 768 * part)
        columns = pl.ds(pl.multiple_of(768 * part, 256), 768)
        for j, (source, target) in enumerate(q_copies):
            pltpu.make_async_copy(source.at[:, :, columns], target.at[:, :, columns], out_sems.at[8 + j]).start()

    for j, (source, target) in enumerate(q_copies):
        pltpu.make_async_copy(source, target, out_sems.at[8 + j]).wait()
    saves.wait()


def rec_backward(
    places, tok, cot, masks, gains, chans, other, i_back, i_residual, i_normed, i_merged, i_u, i_gate, i_conv, i_rate,
    i_inp, i_st, i_tables, wp0, wp1, wp2, wp3, wq0, wq1, wq2, wq3,
    o_residual, o_mine, o_theirs, p0, p1, q0, q1,
    wb, wog, part, residual, normed, merged, u_in, gate_in, conv_low, rate, inp, st_in, tables,
    coeff, grad_branch, gs, lam, rate_low, inp_low, direct, gmix, rolled, sums, mixed_part, own_residual, bp, bq,
    sems, in_sems, out_sems,
):
    ins = Saves(in_sems)
    for source, target in (
        (i_back.at[pl.ds(0, TOK)], part), (i_residual, residual), (i_merged, merged), (i_gate, gate_in), (i_st, st_in),
        (i_rate, rate), (i_inp, inp), (i_conv, conv_low), (i_tables, tables), (i_u, u_in), (i_normed, normed),
    ):
        ins.start(source, target)
    for j, p in enumerate((wp0, wp1, wp2, wp3)):
        og_copy(p, places, j, wog, sems.at[1])
    for j, (p, q) in enumerate(((wp0, wq0), (wp1, wq1), (wp2, wq2), (wp3, wq3))):
        p_copy(p, places, j, OG, PB, wb, 0, sems.at[0])
        q_copy(q, places, j, 0, QB, wb, PB, sems.at[0])
    saves = Saves(out_sems)
    sums[...] = jnp.zeros_like(sums)
    for copy in ins.copies[0:2]:
        copy.wait()
    for s in range(2):
        rows, theirs = slice(s * SEQ, (s + 1) * SEQ), slice((1 - s) * SEQ, (2 - s) * SEQ)
        grad, term = rms_back(part[rows] + other[theirs], residual[rows], gains[1:2])
        grad = cot[rows].astype(F32) + grad
        grad_branch[rows] = grad.astype(BF16)
        if s == 0:
            own_residual[...] = grad
            sums[9:10] = jnp.sum(term, axis=0, keepdims=True)
    saves.start(own_residual, o_residual)

    def put_og(b, first, v):
        x, z = (b // 8) * 2 + b % 2, (b // 2) % 4
        n = min(max(OG - first, 0), v.shape[1])
        if n:
            bp[x, z, 0:48, first : first + n] = v[:, :n]
        if n < v.shape[1]:
            to = first + n - OG
            for r in range(3):
                bp[x, z, 48:64, 384 * r + to : 384 * r + to + v.shape[1] - n] = v[16 * r : 16 * r + 16, n:]

    ins.copies[2].wait()
    v = tn(merged[...], grad_branch[...]).astype(BF16)
    for b in range(16):
        put_og(b, 0, v[48 * b : 48 * b + 48])
    landed(wog, sems.at[1])
    gs[...] = nt(grad_branch[...], wog[..., 0:D].reshape(RC, D))
    for copy in ins.copies[3:5]:
        copy.wait()

    @pl.loop(0, 6)
    def _(c):
        at = cols(c)
        act, act_grad = gelu_both(gate_in[:, at])
        g = gs[:, at]
        for s in range(2):
            rows = slice(s * SEQ, (s + 1) * SEQ)
            gmix[rows, pl.ds(pl.multiple_of(RC + c * LANES, LANES), LANES)] = (
                g[rows] * st_in[s, 8:, at] * act_grad[rows]
            ).astype(BF16)
        gs[:, at] = g * act

    for copy in ins.copies[5:8]:
        copy.wait()

    @pl.loop(0, 6)
    def _(c):
        at = cols(c)
        keep, starts = masks[0], masks[1]
        rg = jax.nn.sigmoid(rate[:, at] + chans[5:6, at])
        sd = jnp.exp(-8.0 * rg * chans[7:8, at])
        coeff[:, at] = (1.0 - starts) * (keep * sd + (1.0 - keep))

    row = lax.broadcasted_iota(jnp.int32, (8, RC), 0)

    def backward(n, carry):
        i = SEQ // 8 - 1 - n
        new = []
        for s in range(2):
            at = pl.ds(pl.multiple_of(s * SEQ + i * 8, 8), 8)
            own = coeff[at]
            later_a, later_lam = carry[s]
            a = jnp.where(row == 7, later_a, pltpu.roll(own, 7, 0))
            b = gs[at]
            for k in (1, 2, 4):
                here = row < 8 - k
                b = jnp.where(here, b + a * pltpu.roll(b, 8 - k, 0), b)
                a = jnp.where(here, a * pltpu.roll(a, 8 - k, 0), a)
            h = b + a * later_lam
            lam[at] = h
            new.append((own[0:1], h[0:1]))
        return tuple(new)

    zero = jnp.zeros((1, RC), F32)
    lax.fori_loop(0, SEQ // 8, backward, ((zero, zero), (zero, zero)))

    @pl.loop(0, 6)
    def _(c):
        at = cols(c)
        decay = chans[7:8, at]
        for s in range(2):
            rows = slice(s * SEQ, (s + 1) * SEQ)
            keep, starts = masks[0, rows], masks[1, rows]
            rg, ig, sd, q, root, scale = gates(
                rate[rows, at], inp[rows, at], chans[5:6, at], chans[6:7, at], decay, keep, starts
            )
            conv = conv_low[rows, at].astype(F32)
            l = lam[rows, at]
            common = l * keep
            grad_coeff = l * st_in[s, 7 : PAD - 1, at]
            direct[rows, at] = common * scale * ig
            d_ig = common * scale * conv
            d_scale = common * ig * conv
            d_sd = (1.0 - starts) * (grad_coeff * keep - d_scale * jnp.where(q > 0.001, sd / root, 0.0))
            d_log = d_sd * sd * -8.0
            d_rate = d_log * decay * rg * (1.0 - rg)
            d_inp = d_ig * ig * (1.0 - ig)
            rate_low[rows, at] = d_rate.astype(BF16)
            inp_low[rows, at] = d_inp.astype(BF16)
            for n, term in ((5, d_rate), (6, d_inp), (7, d_log * rg)):
                sums[n : n + 1, at] += jnp.sum(term, axis=0, keepdims=True)

    for copy in ins.copies[8:]:
        copy.wait()
    turn = turn_matrix()
    top, left = quarter_masks()
    for p in range(2):
        at = slice(2 * HS * p, 2 * HS * (p + 1))
        direct[:, at] += nt(rate_low[:, at], tables[2 * p]) + nt(inp_low[:, at], tables[2 * p + 1])
        dr = tn(conv_low[:, at], rate_low[:, at]).astype(BF16)
        di = tn(conv_low[:, at], inp_low[:, at]).astype(BF16)
        none = jnp.zeros_like(dr)
        straight = jnp.where(top, jnp.where(left, dr, none), jnp.where(left, none, di))
        crossed = jnp.where(top, jnp.where(left, di, none), jnp.where(left, none, dr))
        g = (straight.astype(F32) + nn(crossed, turn)).astype(BF16)
        for b in range(8):
            put_og(8 * p + b, D, g[48 * b : 48 * b + 48])

    rolled[:, SEQ:] = jnp.zeros((2, 8, LANES), F32)

    @pl.loop(0, 6)
    def _(c):
        at = cols(c)
        for s in range(2):
            rows = slice(s * SEQ, (s + 1) * SEQ)
            g = direct[rows, at]
            gu = chans[0:1, at] * g
            sums[4:5, at] += jnp.sum(g, axis=0, keepdims=True)
            sums[0:1, at] += jnp.sum(g * u_in[s, 8:, at], axis=0, keepdims=True)
            for k in range(1, 4):
                w = g * masks[1 + k, rows]
                sums[k : k + 1, at] += jnp.sum(w * u_in[s, 8 - k : PAD - k, at], axis=0, keepdims=True)
                rolled[s, 0:SEQ] = w
                gu = gu + chans[k : k + 1, at] * rolled[s, k : SEQ + k]
            gmix[rows, at] = (gu * masks[0, rows]).astype(BF16)

    v = jnp.concatenate([sums[0:8, 0:RC], jnp.zeros((LANES - 8, RC), F32)], axis=0).T.astype(BF16)
    for b in range(16):
        put_og(b, 1408, v[48 * b : 48 * b + 48])
    landed(wb, sems.at[0])

    v = tn(normed[...], gmix[:, 0:PB]).astype(BF16)
    for x, z in RINGS:
        for half in range(2):
            r = ring_rows(x, z) + 256 * half
            bp[x, z, 32 * half : 32 * half + 32, OG:EARLY] = v[r : r + 32]
    emit(saves, bp, places, 0, (p0, p1))
    mixed_part[...] = nt(gmix[...], rows_of(wb, 0, BRANCH))
    saves.start(mixed_part.at[pl.ds(0, SEQ)], o_mine)
    saves.start(mixed_part.at[pl.ds(SEQ, SEQ)], o_theirs)
    t = tok[...].astype(F32)
    sums[8:9] = jnp.sum(mixed_part[...] * (t * inv_rms(t)), axis=0, keepdims=True)
    v = jnp.concatenate([sums[8:16], jnp.zeros((LANES - 8, D), F32)], axis=0).T.astype(BF16)
    for x, z in RINGS:
        for half in range(2):
            r = ring_rows(x, z) + 256 * half
            bq[z, x, 32 * half : 32 * half + 32, QB:EARLY] = v[r : r + 32]

    v = tn(normed[...], gmix[:, PB:]).astype(BF16)
    for x, z in RINGS:
        for half in range(2):
            r = ring_rows(x, z) + 256 * half
            bq[z, x, 32 * half : 32 * half + 32, 0:QB] = v[r : r + 32]
    emit(saves, bq, places, 2, (q0, q1))
    saves.wait()


def join_sums(
    places, eo_p, eu_p, lo_p, lu_p, eo_q, eu_q, lo_q, lu_q,
    p0, p1, q0, q1,
    out, out_sems,
):
    saves = Saves(out_sems)
    for n, (axis, outs, a, b, c, d) in enumerate(
        ((2, (p0, p1), eo_p, eu_p, lo_p, lu_p), (0, (q0, q1), eo_q, eu_q, lo_q, lu_q))
    ):
        for j in range(4):
            at, to = places[4 + axis, j], 4 * n + j
            out[to, :, 0:EARLY] = add(a[at], b[at])
            out[to, :, EARLY:] = add(c[at], d[at])
            saves.start(out.at[to], outs[j // 2].at[j % 2])
    saves.wait()


def add(a, b):
    return (a.astype(F32) + b.astype(F32)).astype(BF16)


def half_sums(a_p, b_p, c_p, d_p, a_q, b_q, c_q, d_q, *rest):
    outs, (early, late, in_sems) = rest[-7:-3], rest[-3:]
    loads = Saves(in_sems)
    for n, (a, b, c, d) in enumerate(((a_p, b_p, c_p, d_p), (a_q, b_q, c_q, d_q))):
        for source, target in ((a, early.at[n, 0]), (b, early.at[n, 1]), (c, late.at[n, 0]), (d, late.at[n, 1])):
            loads.start(source.at[0], target)
    for n in range(2):
        for i, v in enumerate((early, late)):
            loads.copies[4 * n + 2 * i].wait()
            loads.copies[4 * n + 2 * i + 1].wait()
            outs[2 * n + i][...] = add(v[n, 0], v[n, 1])


def pass_on(a_p, f_p, a_q, f_q, *rest):
    o_p, o_q, v, in_sems, out_sems = rest[-5:]
    loads, saves = Saves(in_sems), Saves(out_sems)
    for i, source in enumerate((a_p, f_p, a_q, f_q)):
        loads.start(source.at[1], v.at[i])
    for n, out in enumerate((o_p, o_q)):
        loads.copies[2 * n].wait()
        loads.copies[2 * n + 1].wait()
        v[2 * n] = add(v[2 * n], v[2 * n + 1])
        saves.start(v.at[2 * n], out)
    saves.wait()


def cut(
    places, p0, p1, p2, q0, q1, q2,
    o0, o1, o2, o3,
    parts, sp, sq, sd, in_sems,
):
    load((p0.at[0], p1.at[0], p2, q0.at[0], q1.at[0], q2), [parts.at[i] for i in range(6)], in_sems)
    for n, out in enumerate((sp, sq)):
        out[...] = parts[3 * n].astype(F32) + parts[3 * n + 1].astype(F32) + parts[3 * n + 2].astype(F32)
    sd[0:64] = sp[:, EARLY : EARLY + D]
    sd[64:96, 0:512] = sp[0:32, EARLY + D : EARLY + FC]
    sd[64:96, 512:1024] = sp[32:64, EARLY + D : EARLY + FC]
    tail = jnp.concatenate([sp[48:64, 384 * r : 384 * r + 384] for r in range(3)], axis=0)
    og = jnp.concatenate([sp[0:48, 0:OG], tail], axis=1).astype(BF16)
    i = lax.broadcasted_iota(jnp.int32, (16, 48), 0)
    s = lax.broadcasted_iota(jnp.int32, (16, 48), 1)

    def two(rows):
        return jnp.concatenate(rows, axis=0).astype(BF16)

    for j, out in enumerate((o0, o1, o2, o3)):
        y = places[1, (0, 2, 3, 1)[j]]
        rows = [pl.ds(pl.multiple_of(32 * c + y * 8, 8), 8) for c in range(2)]
        out[:, 0:PB] = two([sp[r, OG:EARLY] for r in rows])
        out[:, PB : PB + PI] = two([sp[r, UNIT - PI :] for r in rows])
        out[:, PB + PI : DC] = two([sq[r] for r in rows])
        mine = jnp.where((s == i + y * 12) & (i < 12), 1.0, 0.0).astype(BF16)
        out[:, DC:DOWN] = nn(mine, og).astype(BF16)
        down = sd[pl.ds(pl.multiple_of(y * 24, 8), 24)]
        out[:, DOWN : DOWN + D] = down[0:16].astype(BF16)
        out[:, DOWN + D :] = two([down[16:24, 0:512], down[16:24, 512:]])


def finish(places, o0, o1, o2, o3, mine, theirs, out_grad, gate_grad, chan_grad, down_grad, v):
    v[...] = o0[...].astype(F32) + o1[...].astype(F32) + o2[...].astype(F32) + o3[...].astype(F32)
    core = places[3, 0]
    theirs[...] = v[pl.ds(pl.multiple_of((1 - core) * 8, 8), 8), 0:DC]
    mine[...] = v[pl.ds(pl.multiple_of(core * 8, 8), 8), 0:DC]
    out_grad[...] = v[0:12, DC : DC + D]
    gate_grad[...] = v[0:12, DC + D : DC + D + 384]
    chan_grad[...] = v[:, DC + D + 384 : DOWN].T[0:8]
    down_grad[0:16] = v[:, DOWN : DOWN + D]
    down_grad[16:24, 0:512] = v[0:8, DOWN + D :]
    down_grad[16:24, 512:] = v[8:16, DOWN + D :]


def unpack(places, mine, theirs, branch, inner, gains):
    def halves(ins):
        for c, v in enumerate(ins):
            for q in range(4):
                to = 768 * q + 384 * c
                if q == 0:
                    branch[:, to : to + PB] = v[:, 0:PB]
                    branch[:, to + PB : to + 384] = v[:, PB + PI : PB + PI + 128]
                else:
                    branch[:, to : to + 384] = v[:, PI + 384 * q : PI + 384 * q + 384]
                at = PB if q == 0 else DC - LATE + 768 * (q - 1)
                to = 1536 * q + 768 * c
                inner[:, to : to + 768] = v[:, at : at + 768]

    gains[...] = mine[:, DC - LATE - LANES : DC - LATE] + theirs[:, DC - LATE - LANES : DC - LATE]

    @pl.when(places[3, 0] == 0)
    def _():
        halves((mine, theirs))

    @pl.when(places[3, 0] == 1)
    def _():
        halves((theirs, mine))


VM, HB, SM, ANY = pltpu.VMEM, pltpu.HBM, pltpu.SMEM, pl.ANY


def kernel(body, ins, spaces, outs, scratch, mib, flops=0, aliases={}):
    moved = sum(v.size * v.dtype.itemsize for v in ins)
    ins = [pltpu.with_memory_space_constraint(v, HB) if s is HB else v for v, s in zip(ins, spaces)]
    return pl.pallas_call(
        body,
        out_shape=[HB(s, d) if at is HB else jax.ShapeDtypeStruct(s, d) for s, d, at in outs],
        in_specs=[pl.BlockSpec(memory_space=s) for s in spaces],
        out_specs=[pl.BlockSpec(memory_space=s) for _, _, s in outs],
        scratch_shapes=scratch,
        input_output_aliases=aliases,
        compiler_params=pltpu.CompilerParams(vmem_limit_bytes=mib * 2**20),
        cost_estimate=pl.CostEstimate(flops=flops, bytes_accessed=moved, transcendentals=0),
    )(*ins)


def shards(
    tokens, cotangent, segment, keep_mask, conv_state, lru_state, norm1_gain, conv_weight, lru_bias, decay_rate,
    gate_weight, branch_weight, out_weight, norm2_gain, mlp_in_weight, mlp_out_weight,
):
    here = my_place()
    core = here["core"]
    zero = jnp.zeros_like(core)
    places = jnp.stack(
        [jnp.stack(ring_places(axis, here)) for axis in "xyz"]
        + [jnp.stack([core, zero, zero, zero])]
        + [jnp.stack(pair_places(axis, here)) for axis in "xyz"]
    ).astype(jnp.int32)
    vmem, dma = pltpu.VMEM, pltpu.SemaphoreType.DMA

    tc = jnp.concatenate([tokens[0], cotangent[0]], axis=0)
    tc_other = swap(tc)
    marks = jnp.concatenate([segment, keep_mask], axis=1).astype(F32)
    states = jnp.concatenate([conv_state[0], lru_state], axis=0)
    sent = jnp.concatenate([core_half(states, 1 - core, 2), jnp.pad(marks, ((0, 0), (0, RC - 2 * SEQ)))], axis=0)
    sent = swap(sent)

    mine, theirs, own = kernel(
        pack,
        (places, branch_weight, mlp_in_weight, jnp.stack([norm1_gain, norm2_gain]), out_weight, gate_weight,
         jnp.concatenate([conv_weight, lru_bias, decay_rate[None]], axis=0), mlp_out_weight),
        [SM, HB, HB, VM, HB, HB, VM, HB],
        [((8, DC), BF16, VM)] * 2 + [((16, OWN - DC), BF16, VM)],
        [vmem(v.shape, BF16) for v in (branch_weight, mlp_in_weight, out_weight, gate_weight, mlp_out_weight)]
        + [dma((5,))],
        8,
    )
    (block,) = kernel(join, (places, mine, swap(theirs), own), [SM] + [VM] * 3, [((16, OWN), BF16, VM)], [], 8)

    row = ((64, UNIT), BF16)
    unit_of = ((2, 32, UNIT), BF16)
    p, q = kernel(
        unit,
        (places, *ring_direct(block, "y"), tc_other, sent),
        [SM] + [VM] * 4 + [ANY] * 2,
        [(*unit_of, HB)] * 2,
        [vmem(*row), vmem(*row), vmem((64, DC), F32), vmem((96, D), F32), dma((4,))],
        16,
    )
    early, late = (4, 64, EARLY), (4, 64, LATE)
    stack = ((4, 64, UNIT), BF16)
    p, q = ring_both(p, "z"), ring_both(q, "x")
    stacks = [((*v, n), BF16, HB) for n in (EARLY, LATE) for v in ((2, 4, 32), (2, 2, 2, 32))]
    unit_of = (2, 32, UNIT)
    partial = kernel(
        planes((0, 1, 2)),
        (places, *p[:3], *q[:3]),
        [SM] + [HB] * 6,
        stacks,
        [vmem((6, *unit_of), BF16), dma((6,)), dma((12,))],
        8,
    )
    pe, qe, pl_, ql = kernel(
        planes((3,)),
        (places, p[3], q[3], *partial),
        [SM, ANY, ANY] + [HB] * 4,
        stacks,
        [vmem((2, *unit_of), BF16), dma((2,)), dma((4,))],
        8,
        aliases={3 + i: i for i in range(4)},
    )
    pe, qe, pl_, ql = ring_both(pe, "x"), ring_both(qe, "z"), ring_both(pl_, "x"), ring_both(ql, "z")

    tok = jnp.concatenate([tc[:SEQ], tc_other[:SEQ]], axis=0)
    cot = jnp.concatenate([tc[SEQ:], tc_other[SEQ:]], axis=0)
    states = jnp.stack([core_half(states, core, 2), sent[:4]])
    marks = jnp.concatenate([marks, sent[4:, : 2 * SEQ]], axis=0)
    seg, keep = marks[:, :SEQ], marks[:, SEQ:]
    earlier = [jnp.concatenate([jnp.repeat(seg[:, :1], k, axis=1), seg[:, : SEQ - k]], axis=1) for k in range(1, 4)]
    masks = jnp.stack([keep, (earlier[0] != seg).astype(F32)] + [(e == seg).astype(F32) for e in earlier])
    masks = jnp.broadcast_to(masks.reshape(5, TOK, 1), (5, TOK, LANES))

    wide, wide_low = ((TOK, D), F32), ((TOK, D), BF16)
    act, act_low, padded = ((TOK, RC), F32), ((TOK, RC), BF16), ((2, PAD, RC), F32)
    tables = ((4, 2 * HS, 2 * HS), BF16)
    saved = [wide_low, act_low, padded, act, act_low, act, act, padded, tables]
    part, finals, gains, chans, normed, merged, u, gate_in, conv_low, rate, inp, st, table = kernel(
        rec_forward,
        (places, tok, masks, states[:, :3], states[:, 3:], *pe, *qe),
        [SM] + [VM] * 4 + [HB] * 8,
        [((TOK + 8, D), F32, VM), ((4, RC), F32, VM), ((8, D), F32, VM), ((8, RC), F32, VM)]
        + [(*v, HB) for v in saved],
        [vmem((*ROWS, PB + EARLY), BF16), vmem((*OG_ROWS, OGC), BF16)]
        + [vmem(*v) for v in saved + [act, act]]
        + [dma((2,)), dma((9,))],
        32,
        2 * TOK * (D * BRANCH + RC * (D + 768)),
    )
    half = ((SEQ, D), F32)
    other = swap(part)
    normed2, own, residual = kernel(
        mlp_norm,
        (tok, part, other, gains),
        [VM] * 4,
        [(*wide_low, VM), (*half, VM), (*wide, HB)],
        [vmem(*wide), dma],
        16,
    )
    hidden, ggu, base, back = kernel(
        mlp,
        (places, cot, normed2, own, *pl_, *ql),
        [SM] + [VM] * 3 + [ANY] * 8,
        [((TOK, FC), BF16, VM), ((TOK, INNER), BF16, VM), (*half, HB), ((TOK + SEQ, D), F32, HB)],
        [vmem((*ROWS, INNER), BF16), vmem((*DOWN_ROWS, D), BF16), vmem((2, TOK, 768), F32)]
        + [vmem(*v) for v in (wide, wide, half)]
        + [dma((2,)), dma((3,))],
        32,
        2 * TOK * D * (2 * INNER + 2 * FC),
    )
    back_other = swap(back)
    outs = kernel(
        mlp_grads,
        (places, cot, normed2, hidden, ggu),
        [SM] + [VM] * 4,
        [((2, *late), BF16, HB)] * 4,
        [vmem((4,) + late, BF16), vmem((4,) + late, BF16), dma((12,))],
        32,
        2 * TOK * D * (INNER + FC),
    )
    lp, lq = outs[:2], outs[2:]

    def first_half(p, q, routes):
        return send(p[1], partner(routes[0], 0)), send(q[1], partner(routes[1], 0))

    def second_half(p, q, came, routes, shape, until=(), lands=HB):
        up = kernel(
            pass_on,
            (p[0], came[0], q[0], came[1], *until),
            [HB, lands, HB, lands] + [HB] * len(until),
            [(shape, BF16, HB)] * 2,
            [vmem((4,) + shape, BF16), dma((4,)), dma((2,))],
            16,
        )
        return send(up[0], partner(routes[0], 1)), send(up[1], partner(routes[1], 1))

    late_came = first_half(lp, lq, "xz")
    outs = kernel(
        rec_backward,
        (places, tok, cot, masks, gains, chans, back_other, back, residual, normed, merged, u, gate_in, conv_low, rate,
         inp, st, table, *pe, *qe),
        [SM] + [VM] * 6 + [HB] * 19,
        [(*v, HB) for v in (half, half, half)] + [((2, *early), BF16, HB)] * 4,
        [vmem((*ROWS, BRANCH), BF16), vmem((*OG_ROWS, OGC), BF16)]
        + [vmem(*v) for v in (wide, wide, wide_low, act_low, padded, act, act_low, act, act, padded, tables)]
        + [vmem(*v) for v in (act, wide_low, act, act, act_low, act_low, act, ((TOK, BRANCH), BF16))]
        + [vmem((2, PAD, LANES), F32), vmem((16, D), F32), vmem(*wide), vmem(*half)]
        + [vmem((4,) + early, BF16), vmem((4,) + early, BF16), dma((2,)), dma((11,)), dma((11,))],
        48,
        2 * TOK * D * (2 * BRANCH + 2 * RC),
    )
    grad_residual, mixed_mine, mixed_theirs = outs[:3]
    ep, eq = outs[3:5], outs[5:]
    early_came = first_half(ep, eq, "xz")
    late_up = second_half(lp, lq, late_came, "xz", late, (ep[0],))
    early_up = second_half(ep, eq, early_came, "xz", early)

    summed = kernel(
        half_sums,
        (ep[0], early_came[0], lp[0], late_came[0], eq[0], early_came[1], lq[0], late_came[1]),
        [HB] * 8,
        [(early, BF16, VM), (late, BF16, VM)] * 2,
        [vmem((2, 2) + early, BF16), vmem((2, 2) + late, BF16), dma((8,))],
        16,
    )
    outs = kernel(
        join_sums,
        (places, summed[0], early_up[0], summed[1], late_up[0], summed[2], early_up[1], summed[3], late_up[1]),
        [SM] + [VM] * 8,
        [((2, 64, UNIT), BF16, HB)] * 4,
        [vmem((8, 64, UNIT), BF16), dma((8,))],
        8,
    )
    tp, tq = outs[:2], outs[2:]
    came = first_half(tp, tq, "zx")
    up = second_half(tp, tq, came, "zx", (64, UNIT), lands=ANY)
    sums = kernel(
        cut,
        (places, tp[0], came[0], up[0], tq[0], came[1], up[1]),
        [SM] + [HB, ANY, ANY] * 2,
        [((16, OWN), BF16, VM)] * 4,
        [vmem((6, 64, UNIT), BF16), vmem((64, UNIT), F32), vmem((64, UNIT), F32), vmem((96, D), F32), dma((6,))],
        16,
    )
    mine, theirs, out_grad, gate_grad, chan_grad, down_grad = kernel(
        finish,
        (places, *terms_direct(sums, "y")),
        [SM] + [VM] * 4,
        [((8, DC), F32, VM)] * 2 + [(s, F32, VM) for s in ((12, D), (12, 384), (8, 16), (24, D))],
        [vmem((16, OWN), F32)],
        8,
    )
    branch_grad, in_grad, gain_grads = kernel(
        unpack,
        (places, mine, swap(theirs)),
        [SM] + [VM] * 2,
        [((8, 2 * R), F32, VM), ((8, 2 * F), F32, VM), ((8, LANES), F32, VM)],
        [],
        8,
    )

    output = (base + back_other[TOK:]).astype(BF16)
    grad, _ = rms_back(mixed_mine + swap(mixed_theirs), tok[:SEQ].astype(F32), gains[0])
    input_grad = (grad_residual + grad).astype(BF16)
    theirs = other[TOK : TOK + 4, :RC]
    finals = jnp.stack(
        [v.reshape(1, 4, 2, 384) for v in (jnp.where(core == 0, finals, theirs), jnp.where(core == 0, theirs, finals))],
        axis=3,
    ).reshape(1, 4, R)
    return (
        output[None],
        input_grad[None],
        finals[:, :3],
        finals[:, 3],
        gain_grads[:, 0],
        chan_grad[:4, :12],
        chan_grad[4:7, :12],
        chan_grad[7, :12],
        gate_grad,
        branch_grad,
        out_grad,
        gain_grads[:, 1],
        in_grad,
        down_grad,
    )


def solution(mesh):
    rows, last = P(AXES), P(None, AXES)
    specs = [rows] * 6 + [rows, last, last] + [rows] * 7
    outs = [rows] * 4 + [rows, last, last] + [rows] * 7
    return jax.shard_map(
        shards, mesh=mesh, in_specs=tuple(specs), out_specs=tuple(outs), check_vma=False
    )
```
